32 devices in a mesh: dp: 16 (over z, x, core), seq: 2 (over y).
Axes of the slice: x: 2, y: 2, z: 4, core: 2. Of those that a mesh axis runs over, the one named last changes fastest.
Arguments:
- tokens: float32 [32, 2048, 512], P('dp', 'seq'), may hold values from -6 to 6
- lengths: int32 [32], P('dp'), may hold values from 512 to 2048, as said below
- joint_weight: float32 [512, 1536], P(('dp', 'seq')), may hold values from -0.375 to 0.375
- joint_bias: float32 [1024], P(('dp', 'seq')), may hold values from -2 to 2
- out_weight: float32 [512, 512], P(('dp', 'seq')), may hold values from -1 to 1
- out_bias: float32 [512], P(('dp', 'seq')), may hold values from -2 to 2
- gain_first: float32 [512], P(('dp', 'seq')), may hold values from 0.5 to 1.5
- shift_first: float32 [512], P(('dp', 'seq')), may hold values from -2 to 2
- up_weight: float32 [512, 2048], P(('dp', 'seq')), may hold values from -0.25 to 0.25
- up_bias: float32 [2048], P(('dp', 'seq')), may hold values from -2 to 2
- down_weight: float32 [2048, 512], P(('dp', 'seq')), may hold values from -0.1875 to 0.1875
- down_bias: float32 [512], P(('dp', 'seq')), may hold values from -2 to 2
- gain_second: float32 [512], P(('dp', 'seq')), may hold values from 0.5 to 1.5
- shift_second: float32 [512], P(('dp', 'seq')), may hold values from -2 to 2
- cotangent: float32 [32, 2048, 512], P('dp', 'seq'), may hold values from -6 to 6
Outputs:
- layer_output: float32 [32, 2048, 512], P('dp', 'seq')
- input_grad: float32 [32, 2048, 512], P('dp', 'seq')
- joint_weight_grad: float32 [512, 1536], P(('dp', 'seq'))
- joint_bias_grad: float32 [1024], P(('dp', 'seq'))
- out_weight_grad: float32 [512, 512], P(('dp', 'seq'))
- out_bias_grad: float32 [512], P(('dp', 'seq'))
- gain_first_grad: float32 [512], P(('dp', 'seq'))
- shift_first_grad: float32 [512], P(('dp', 'seq'))
- up_weight_grad: float32 [512, 2048], P(('dp', 'seq'))
- up_bias_grad: float32 [2048], P(('dp', 'seq'))
- down_weight_grad: float32 [2048, 512], P(('dp', 'seq'))
- down_bias_grad: float32 [512], P(('dp', 'seq'))
- gain_second_grad: float32 [512], P(('dp', 'seq'))
- shift_second_grad: float32 [512], P(('dp', 'seq'))
The draws below stay inside these ranges and needn't reach their ends.
Inputs may be any that keep to these rules, and one draw needn't show every extreme that they name: `lengths`: in each aligned block of 2 sequences (those of one index of dp) one sequence has the full length 2048.
All inputs are finite; a program needn't handle non-finite values.
Results may differ from the reference program's by a relative error of at most 0.013.
The reference program's roundings to bfloat16 on the way count: a program that leaves them out, or rounds other values in their place, can miss the bound.
Values may be sent and summed in bfloat16 or wider, within the bound.
A program may use at most 256 MiB of HBM per device.

```python
import math
import jax
import jax.numpy as jnp
from jax import lax

D = 512
H = 8
HEAD = 64
FF = 2048
SLOT = 2048
SEQ_GRP = 2
SEQS = 32


def draw_lengths(key, part):
    key = jax.random.fold_in(key, 7)
    key_lens, key_pick = jax.random.split(key)
    groups = SEQS // SEQ_GRP
    ragged = jax.random.randint(key_lens, (groups, SEQ_GRP), SLOT // 4, SLOT + 1, dtype=jnp.int32)
    chosen = jax.random.randint(key_pick, (groups, 1), 0, SEQ_GRP, dtype=jnp.int32)
    columns = lax.broadcasted_iota(jnp.int32, (groups, SEQ_GRP), 1)
    return jnp.where(columns == chosen, SLOT, ragged).reshape(SEQS).astype(jnp.int32)


def shard_levels(stream_key, dims, cuts, least, largest):
    level, own = 1.0, jax.random.fold_in(stream_key, 6)
    for dim, blocks in cuts:
        draws = jnp.exp(jax.random.uniform(jax.random.fold_in(own, dim), (blocks,), jnp.float32, least / len(cuts), largest / len(cuts)))
        level = level * jnp.repeat(draws, dims[dim] // blocks).reshape([-1 if axis == dim else 1 for axis in range(len(dims))])
    return level


def noise(stream_key, dims, scale, limit, cuts=(), held_as=jnp.bfloat16):
    values = jax.random.normal(stream_key, dims, jnp.float32) * scale
    if len(cuts) > 0:
        values = shard_levels(stream_key, dims, cuts, -0.22, 0.18) * values
    return jnp.clip(values, min=-limit, max=limit).astype(held_as)


def setup_inputs(seed: int = 0) -> dict:
    streams_of = jax.random.split(jax.random.key(seed), 16)
    tokens = noise(streams_of[0], (SEQS, SLOT, D), 1.0, 6.0, ((0, 16), (1, 2)), jnp.float32)
    lengths = draw_lengths(jax.random.fold_in(streams_of[15], 71), 0)
    joint_weight = noise(streams_of[2], (D, 3 * D), (D // 2) ** -0.5, 0.375, ((0, 32),), jnp.float32)
    joint_bias = noise(streams_of[3], (2 * D,), 0.3, 2.0, ((0, 32),), jnp.float32)
    out_weight = noise(streams_of[4], (D, D), (D // 16) ** -0.5, 1.0, ((0, 32),), jnp.float32)
    out_bias = noise(streams_of[5], (D,), 0.3, 2.0, ((0, 32),), jnp.float32)
    gain_first = jnp.clip(1.0 + 0.1 * jax.random.normal(streams_of[6], (D,), jnp.float32), 0.5, 1.5)
    shift_first = noise(streams_of[7], (D,), 0.3, 2.0, ((0, 32),), jnp.float32)
    up_weight = noise(streams_of[8], (D, FF), D ** -0.5, 0.25, ((0, 32),), jnp.float32)
    up_bias = noise(streams_of[9], (FF,), 0.3, 2.0, ((0, 32),), jnp.float32)
    down_weight = noise(streams_of[10], (FF, D), (FF // 2) ** -0.5, 0.1875, ((0, 32),), jnp.float32)
    down_bias = noise(streams_of[11], (D,), 0.3, 2.0, ((0, 32),), jnp.float32)
    gain_second = jnp.clip(1.0 + 0.1 * jax.random.normal(streams_of[12], (D,), jnp.float32), 0.5, 1.5)
    shift_second = noise(streams_of[13], (D,), 0.3, 2.0, ((0, 32),), jnp.float32)
    cotangent = noise(streams_of[14], (SEQS, SLOT, D), 1.0, 6.0, ((0, 16), (1, 2)), jnp.float32)
    return {"tokens": tokens, "lengths": lengths, "joint_weight": joint_weight, "joint_bias": joint_bias, "out_weight": out_weight, "out_bias": out_bias, "gain_first": gain_first, "shift_first": shift_first, "up_weight": up_weight, "up_bias": up_bias, "down_weight": down_weight, "down_bias": down_bias, "gain_second": gain_second, "shift_second": shift_second, "cotangent": cotangent}


@jax.custom_vjp
def low(v):
    return lax.optimization_barrier(v.astype(jnp.bfloat16)).astype(jnp.float32)

@jax.custom_vjp
def low_back(v):
    return v

def low_keep(v):
    return (low(v), None)

def low_pass(kept, grad):
    return (grad,)

def back_keep(v):
    return (v, None)

def back_low(kept, grad):
    return (low(grad),)
low.defvjp(low_keep, low_pass)
low_back.defvjp(back_keep, back_low)

def product(left, right):
    return jnp.dot(left, right, precision=lax.Precision.HIGHEST, preferred_element_type=jnp.float32)

def normed(value, gain, shift):
    centred = value - lax.optimization_barrier(jnp.mean(value, axis=-1, keepdims=True))
    inverse = lax.rsqrt(lax.optimization_barrier(jnp.mean(centred * centred, axis=-1, keepdims=True)) + 1e-05)
    return centred * inverse * gain + shift

def attention(query, keys, values, seq_lens):
    seq_len = query.shape[1]
    block_rows = min(512, seq_len)
    scaling = 1.0 / math.sqrt(HEAD)
    key_valid = jnp.arange(seq_len, dtype=jnp.int32)[None, :] < seq_lens[:, None]

    def one_block(offset):
        picked = lax.dynamic_slice_in_dim(query, offset, block_rows, 1)
        scores = jnp.einsum('bqhd,bkhd->bhqk', picked, keys, precision=lax.Precision.HIGHEST) * scaling
        scores = low_back(scores)
        scores = jnp.where(key_valid[:, None, None, :], scores, -1e+30)
        weights = jax.nn.softmax(scores, axis=-1)
        return jnp.einsum('bhqk,bkhd->bqhd', low(weights), values, precision=lax.Precision.HIGHEST)
    offsets = jnp.arange(seq_len // block_rows, dtype=jnp.int32) * block_rows
    pieces = lax.map(jax.checkpoint(one_block), offsets)
    return jnp.moveaxis(pieces, 0, 1).reshape(query.shape)

def layer(inputs, seq_lens, params):
    joint_weight, joint_bias, out_weight, out_bias, gain_first, shift_first, up_weight, up_bias, down_weight, down_bias, gain_second, shift_second = params
    per_step, seq_len, width = inputs.shape
    flat_rows = inputs.reshape(per_step * seq_len, width)
    bias_pair = low(joint_bias).reshape(H, 2, HEAD)
    bias_full = jnp.stack([bias_pair[:, 0], jnp.zeros_like(bias_pair[:, 0]), bias_pair[:, 1]], axis=1).reshape(3 * width)
    joint = low_back(low(product(low(flat_rows), low(joint_weight)) + bias_full))
    joint = joint.reshape(per_step, seq_len, H, 3, HEAD)
    mixed_out = attention(joint[:, :, :, 0], joint[:, :, :, 1], joint[:, :, :, 2], seq_lens)
    mixed_out = low_back(low(mixed_out.reshape(per_step * seq_len, width)))
    hidden = flat_rows + low_back(product(mixed_out, low(out_weight)) + low(out_bias))
    normal_one = normed(hidden, low(gain_first), low(shift_first))
    inner_pre = low_back(product(low(normal_one), low(up_weight)) + low(up_bias))
    active = low(jax.nn.gelu(inner_pre))
    branch = low_back(product(active, low(down_weight)) + low(down_bias))
    result = normed(normal_one + branch + flat_rows, low(gain_second), low(shift_second))
    return result.reshape(per_step, seq_len, width)

def reference(tokens, lengths, joint_weight, joint_bias, out_weight, out_bias, gain_first, shift_first, up_weight, up_bias, down_weight, down_bias, gain_second, shift_second, cotangent):
    params = (joint_weight, joint_bias, out_weight, out_bias, gain_first, shift_first, up_weight, up_bias, down_weight, down_bias, gain_second, shift_second)
    per_step = math.gcd(SEQS, max(1, 4096 // SLOT))
    rounds = SEQS // per_step

    def accumulate(totals, pieces):
        inputs, seq_lens, grads_in = pieces
        output, pullback = jax.vjp(lambda value, weights: layer(value, seq_lens, weights), inputs, params)
        input_grad, weight_grads = pullback(grads_in)
        return (jax.tree.map(jnp.add, totals, weight_grads), (output, input_grad))
    start_grads = jax.tree.map(jnp.zeros_like, params)
    totals, (outputs, input_grads) = lax.scan(accumulate, start_grads, (tokens.reshape(rounds, per_step, SLOT, D), lengths.reshape(rounds, per_step), cotangent.reshape(rounds, per_step, SLOT, D)))
    return (outputs.reshape(SEQS, SLOT, D), input_grads.reshape(SEQS, SLOT, D), totals[0], totals[1], totals[2], totals[3], totals[4], totals[5], totals[6], totals[7], totals[8], totals[9], totals[10], totals[11])
```

```python
import functools
import math

import jax
import jax.numpy as jnp
from jax import lax
from jax.experimental import pallas as pl
from jax.experimental.pallas import tpu as pltpu
from jax.sharding import PartitionSpec as P

H = 8
HEAD = 64
PAIRS = H // 2
WIDE = 2 * HEAD
BF = jnp.bfloat16
F32 = jnp.float32
EPS = 1e-05
SCALE = 1.0 / math.sqrt(HEAD)
LOG2E = math.log2(math.e)
GELU_A = math.sqrt(2.0 / math.pi)
GELU_B = 0.044715
MESH = pl.DeviceIdType.MESH
MIB = 2**20
FORMS = {
    "nn": (((1,), (0,)), ((), ())),
    "nt": (((1,), (1,)), ((), ())),
    "tn": (((0,), (0,)), ((), ())),
}


def dot(left, right, form="nn"):
    return lax.dot_general(left, right, FORMS[form], preferred_element_type=F32)


def params(limit, steps):
    return pltpu.CompilerParams(
        vmem_limit_bytes=limit * MIB, dimension_semantics=("arbitrary",) * steps
    )


def log2(size):
    return size.bit_length() - 1


def gather_kernel(orders, bits_dp, bits_seq, *refs):
    count = len(orders)
    shards, fulls = refs[:count], refs[count : 2 * count]
    own_sem, send_sem, recv_sem = refs[2 * count :]
    dp, seq = lax.axis_index("dp"), lax.axis_index("seq")
    bits = bits_dp + bits_seq
    mine = [lax.rem(dp // 2 ** (bits_dp - 1 - b), 2) for b in range(bits_dp)]
    mine += [lax.rem(seq // 2 ** (bits_seq - 1 - b), 2) for b in range(bits_seq)]

    def partner(bit):
        if bit < bits_dp:
            return (dp + (1 - 2 * mine[bit]) * 2 ** (bits_dp - 1 - bit), seq)
        return (dp, seq + (1 - 2 * mine[bit]) * 2 ** (bits - 1 - bit))

    barrier = pltpu.get_barrier_semaphore()
    for bit in range(bits):
        pl.semaphore_signal(barrier, inc=1, device_id=partner(bit), device_id_type=MESH)
    local = [
        pltpu.make_async_copy(shard, full.at[tuple(mine)], own_sem.at[i])
        for i, (shard, full) in enumerate(zip(shards, fulls))
    ]
    for copy in local:
        copy.start()
    for copy in local:
        copy.wait()
    pl.semaphore_wait(barrier, bits)
    for stage in range(bits):
        copies = []
        for i, full in enumerate(fulls):
            done = orders[i][:stage]
            place = tuple(slice(None) if b in done else mine[b] for b in range(bits))
            copies.append(
                pltpu.make_async_remote_copy(
                    src_ref=full.at[place],
                    dst_ref=full.at[place],
                    send_sem=send_sem.at[stage, i],
                    recv_sem=recv_sem.at[stage, i],
                    device_id=partner(orders[i][stage]),
                    device_id_type=MESH,
                )
            )
        for copy in copies:
            copy.start()
        for copy in copies:
            copy.wait()


def gather_weights(shards, first):
    bits_dp, bits_seq = log2(lax.axis_size("dp")), log2(lax.axis_size("seq"))
    bits = bits_dp + bits_seq
    upper = list(range(bits_dp - 1))
    beside = list(range(bits_dp, bits))
    plans = (upper + beside + [bits_dp - 1], upper[:-1] + beside + upper[-1:] + [bits_dp - 1])
    orders = tuple(tuple(plans[p]) for p in first)
    count = len(shards)
    fulls = pl.pallas_call(
        functools.partial(gather_kernel, orders, bits_dp, bits_seq),
        out_shape=[jax.ShapeDtypeStruct((2,) * bits + s.shape, s.dtype) for s in shards],
        in_specs=[pl.BlockSpec(memory_space=pl.ANY)] * count,
        out_specs=[pl.BlockSpec(memory_space=pl.ANY)] * count,
        scratch_shapes=[
            pltpu.SemaphoreType.DMA((count,)),
            pltpu.SemaphoreType.DMA((bits, count)),
            pltpu.SemaphoreType.DMA((bits, count)),
        ],
        compiler_params=pltpu.CompilerParams(collective_id=0, has_side_effects=True),
        name="gather_weights",
    )(*shards)
    return [f.reshape((2**bits * s.shape[0],) + s.shape[1:]) for f, s in zip(fulls, shards)]


def owner_sums(arrays):
    size_dp, size_seq = lax.axis_size("dp"), lax.axis_size("seq")
    bits_dp, bits_seq = log2(size_dp), log2(size_seq)
    bits = bits_dp + bits_seq
    dp, seq = lax.axis_index("dp"), lax.axis_index("seq")
    rows = [a.shape[0] // (size_dp * size_seq) for a in arrays]
    arrays = [
        a.reshape((2,) * bits + (r,) + a.shape[1:]) for a, r in zip(arrays, rows)
    ]
    left = list(range(bits))
    order = [bits_dp - 1] + list(range(bits_dp, bits)) + list(range(bits_dp - 2, -1, -1))
    for bit in order:
        axis = left.index(bit)
        left.remove(bit)
        if bit < bits_dp:
            name, size, step, me = "dp", size_dp, 2 ** (bits_dp - 1 - bit), dp
        else:
            name, size, step, me = "seq", size_seq, 2 ** (bits - 1 - bit), seq
        mine = me // step % 2
        pairs = [(i, i ^ step) for i in range(size)]
        sent = [
            lax.dynamic_index_in_dim(a, 1 - mine, axis, keepdims=False).astype(BF) for a in arrays
        ]
        kept = [lax.dynamic_index_in_dim(a, mine, axis, keepdims=False) for a in arrays]
        arrived = [lax.ppermute(s, name, pairs) for s in sent]
        arrays = [k + a.astype(F32) for k, a in zip(kept, arrived)]
    return arrays


def attend_kernel(
    parts,
    groups,
    info,
    query,
    keys_own,
    values_own,
    keys_rest,
    values_rest,
    e_own,
    e_rest,
    mixed,
    mixed_t,
    inverse,
    k_ext,
    v_ext,
):
    local = keys_own.shape[1]
    block = query.shape[1]

    @pl.when(pl.program_id(2) == 0)
    def prepare():
        length = info[pl.program_id(0)]
        for part in range(parts):
            rows = slice(part * local, (part + 1) * local)
            if part == 0:
                keys, values = keys_own[0], values_own[0]
            else:
                inside = slice((part - 1) * local, part * local)
                keys, values = keys_rest[0, inside], values_rest[0, inside]
            k_ext[rows, :WIDE] = keys
            place = lax.broadcasted_iota(jnp.int32, (local, WIDE), 0) + info[groups + part]
            k_ext[rows, WIDE:] = jnp.where(place < length, 0.0, -1e30).astype(BF)
            turned = values.T
            v_ext[0, :HEAD, rows] = turned[:HEAD]
            v_ext[1, :HEAD, rows] = turned[HEAD:]
            v_ext[:, HEAD:, rows] = jnp.ones((2, HEAD, local), BF)

    turned = query[0].T
    zero = jnp.zeros((HEAD, block), BF)
    one = (lax.broadcasted_iota(jnp.int32, (WIDE, block), 0) == 0).astype(F32).astype(BF)
    heads = []
    for head in range(2):
        if head == 0:
            picked = jnp.concatenate([turned[:HEAD], zero, one], axis=0)
        else:
            picked = jnp.concatenate([zero, turned[HEAD:], one], axis=0)
        scores = dot(k_ext[...], picked)
        largest = jnp.max(scores, axis=0, keepdims=True)
        e = jnp.exp2((scores - largest) * (SCALE * LOG2E)).astype(BF)
        e_own[0, head] = e[:local]
        e_rest[0, head] = e[local:]
        out = dot(v_ext[head], e)
        inv = 1.0 / out[HEAD : HEAD + 1]
        inverse[0, 0, head : head + 1] = inv
        heads.append(out[:HEAD] * inv)
    both = jnp.concatenate(heads, axis=0).astype(BF)
    mixed_t[0] = both
    mixed[0] = both.T


def attend(info, joint_own, joint_rest, parts):
    groups, local, _ = joint_own.shape
    rest = joint_rest.shape[1]
    block = min(256, local)
    width = H * HEAD
    grid = (groups, PAIRS, local // block)
    return pl.pallas_call(
        functools.partial(attend_kernel, parts, groups),
        grid=grid,
        in_specs=[
            pl.BlockSpec(memory_space=pltpu.SMEM),
            pl.BlockSpec((1, block, WIDE), lambda g, p, b: (g, b, p)),
            pl.BlockSpec((1, local, WIDE), lambda g, p, b: (g, 0, PAIRS + p)),
            pl.BlockSpec((1, local, WIDE), lambda g, p, b: (g, 0, 2 * PAIRS + p)),
            pl.BlockSpec((1, rest, WIDE), lambda g, p, b: (g, 0, p)),
            pl.BlockSpec((1, rest, WIDE), lambda g, p, b: (g, 0, PAIRS + p)),
        ],
        out_specs=[
            pl.BlockSpec((1, 2, local, block), lambda g, p, b: (g, p, 0, b)),
            pl.BlockSpec((1, 2, rest, block), lambda g, p, b: (g, p, 0, b)),
            pl.BlockSpec((1, block, WIDE), lambda g, p, b: (g, b, p)),
            pl.BlockSpec((1, WIDE, block), lambda g, p, b: (g, p, b)),
            pl.BlockSpec((1, 1, 2, block), lambda g, p, b: (g, p, 0, b)),
        ],
        out_shape=[
            jax.ShapeDtypeStruct((groups, H, local, local), BF),
            jax.ShapeDtypeStruct((groups, H, rest, local), BF),
            jax.ShapeDtypeStruct((groups, local, width), BF),
            jax.ShapeDtypeStruct((groups, width, local), BF),
            jax.ShapeDtypeStruct((groups, PAIRS, 2, local), F32),
        ],
        scratch_shapes=[
            pltpu.VMEM((local + rest, 2 * WIDE), BF),
            pltpu.VMEM((2, WIDE, local + rest), BF),
        ],
        compiler_params=params(56, 3),
        name="attend",
    )(info, joint_own, joint_own, joint_own, joint_rest, joint_rest)


def middle_kernel(
    tokens,
    cotangent,
    mixed,
    out_w,
    up_w,
    down_w,
    rows,
    up_bias,
    result,
    partial,
    mixed_grad,
    out_wg,
    up_wg,
    down_wg,
    row_sums,
    up_bias_sum,
):
    first = pl.program_id(0) == 0

    @pl.when(first)
    def clear():
        out_wg[...] = jnp.zeros_like(out_wg)
        up_wg[...] = jnp.zeros_like(up_wg)
        down_wg[...] = jnp.zeros_like(down_wg)
        row_sums[...] = jnp.zeros_like(row_sums)
        up_bias_sum[...] = jnp.zeros_like(up_bias_sum)

    out_bias, gain_one, shift_one = rows[0:1], rows[1:2], rows[2:3]
    down_bias, gain_two, shift_two = rows[3:4], rows[4:5], rows[5:6]

    def mean(v):
        return jnp.mean(v, axis=-1, keepdims=True)

    def total(v):
        return jnp.sum(v, axis=0, keepdims=True)

    x = tokens[...]
    heads = mixed[...]
    hidden = x + (dot(heads, out_w[...]) + out_bias)
    centred = hidden - mean(hidden)
    r_one = lax.rsqrt(mean(centred * centred) + EPS)
    n_one = centred * r_one
    normal = n_one * gain_one + shift_one
    normal_low = normal.astype(BF)
    inner = dot(normal_low, up_w[...]) + up_bias[...]
    square = inner * inner
    tanh = jnp.tanh(inner * (GELU_A + (GELU_A * GELU_B) * square))
    half = 0.5 + 0.5 * tanh
    active = (inner * half).astype(BF)
    slope = half + (0.5 * inner) * (1.0 - tanh * tanh) * (
        GELU_A + (3.0 * GELU_A * GELU_B) * square
    )
    branch = dot(active, down_w[...]) + down_bias
    last = normal + branch + x
    centred = last - mean(last)
    r_two = lax.rsqrt(mean(centred * centred) + EPS)
    n_two = centred * r_two
    result[...] = n_two * gain_two + shift_two
    grad = cotangent[...]
    e_two = grad * gain_two
    back = r_two * (e_two - mean(e_two) - n_two * mean(e_two * n_two))
    branch_grad = back.astype(BF)
    down_wg[...] += dot(active, branch_grad, "tn")
    inner_grad_wide = slope * dot(branch_grad, down_w[...], "nt")
    inner_grad = inner_grad_wide.astype(BF)
    up_wg[...] += dot(normal_low, inner_grad, "tn")
    up_bias_sum[...] += total(inner_grad.astype(F32))
    norm_grad = back + dot(inner_grad, up_w[...], "nt")
    e_one = norm_grad * gain_one
    hidden_grad = r_one * (e_one - mean(e_one) - n_one * mean(e_one * n_one))
    attn_grad = hidden_grad.astype(BF)
    partial[...] = back + hidden_grad
    out_wg[...] += dot(heads, attn_grad, "tn")
    mixed_grad[...] = dot(attn_grad, out_w[...], "nt").astype(BF)
    row_sums[0:1] += total(attn_grad.astype(F32))
    row_sums[1:2] += total(norm_grad * n_one)
    row_sums[2:3] += total(norm_grad)
    row_sums[3:4] += total(branch_grad.astype(F32))
    row_sums[4:5] += total(grad * n_two)
    row_sums[5:6] += total(grad)


def middle(tokens, cotangent, mixed, out_w, up_w, down_w, rows, up_bias):
    count, width = tokens.shape
    hidden = up_w.shape[1]
    block = min(256, count)

    def moving(columns=width):
        return pl.BlockSpec((block, columns), lambda b: (b, 0))

    def still(*shape):
        return pl.BlockSpec(shape, lambda b: (0, 0), pipeline_mode=pl.Buffered(1))

    return pl.pallas_call(
        middle_kernel,
        grid=(count // block,),
        in_specs=[
            moving(),
            moving(),
            moving(),
            still(width, width),
            still(width, hidden),
            still(hidden, width),
            still(8, width),
            still(1, hidden),
        ],
        out_specs=[
            moving(),
            moving(),
            moving(),
            still(width, width),
            still(width, hidden),
            still(hidden, width),
            still(8, width),
            still(1, hidden),
        ],
        out_shape=[
            jax.ShapeDtypeStruct((count, width), F32),
            jax.ShapeDtypeStruct((count, width), F32),
            jax.ShapeDtypeStruct((count, width), BF),
            jax.ShapeDtypeStruct((width, width), F32),
            jax.ShapeDtypeStruct((width, hidden), F32),
            jax.ShapeDtypeStruct((hidden, width), F32),
            jax.ShapeDtypeStruct((8, width), F32),
            jax.ShapeDtypeStruct((1, hidden), F32),
        ],
        compiler_params=params(58, 1),
        name="middle",
    )(tokens, cotangent, mixed, out_w, up_w, down_w, rows, up_bias)


def pull_kernel(
    own,
    e_part,
    query,
    keys,
    values,
    mixed_grad,
    mixed_t,
    inverse,
    tokens_low,
    weight,
    *rest,
):
    if own:
        partial, dq_before, share, weight_grad, bias_grad, dkv, d_scores, dq_all = rest
    else:
        share, dq_out, weight_grad, bias_grad, dkv, d_scores = rest
    group, pair = pl.program_id(0), pl.program_id(1)
    span = keys.shape[1]
    local = query.shape[1]
    block = min(256, local)
    width = H * HEAD
    turned = mixed_grad[0].astype(F32).T
    heads = mixed_t[0].astype(F32)
    keys_t = keys[0].T
    query_now = query[0]
    lane = lax.broadcasted_iota(jnp.int32, (local, WIDE), 1)
    zero = jnp.zeros((HEAD, local), BF)
    key_sum = jnp.zeros((span, WIDE), F32)
    value_sum = jnp.zeros((span, WIDE), F32)
    query_parts = []
    for head in range(2):
        side = slice(head * HEAD, (head + 1) * HEAD)
        inv = inverse[0, 0, head : head + 1]
        centre = inv * jnp.sum(turned[side] * heads[side], axis=0, keepdims=True)
        scaled = (turned[side] * inv).astype(BF)
        grad_t = jnp.concatenate([scaled, zero] if head == 0 else [zero, scaled], axis=0)
        grad = grad_t.T
        for at in range(0, local, block):
            columns = slice(at, at + block)
            pulled = dot(values[0], grad_t[:, columns])
            e = e_part[0, head, :, columns].astype(F32)
            d_scores[head, :, columns] = (e * (pulled - centre[:, columns])).astype(BF)
            dq = dot(keys_t, d_scores[head, :, columns])[side]
            if own:
                query_parts.append((head, columns, dq))
            else:
                dq_out[0, side, columns] = dq
        kept = lane < HEAD if head == 0 else lane >= HEAD
        query_head = jnp.where(kept, query_now, jnp.zeros_like(query_now))
        key_sum += dot(d_scores[head], query_head)
        value_sum += dot(e_part[0, head], grad)
    at_keys = pl.ds(pl.multiple_of(pair * WIDE, WIDE), WIDE)
    at_values = pl.ds(pl.multiple_of(width + pair * WIDE, WIDE), WIDE)
    dkv[:, at_keys] = (key_sum * SCALE).astype(BF)
    dkv[:, at_values] = value_sum.astype(BF)
    if own:
        for head, columns, dq in query_parts:
            side = slice(head * HEAD, (head + 1) * HEAD)
            row = pl.ds(pl.multiple_of(pair * WIDE + head * HEAD, HEAD), HEAD)
            dq_all[row, columns] = (dq + dq_before[0, side, columns]) * SCALE

    @pl.when(jnp.logical_and(group == 0, pair == 0))
    def clear():
        weight_grad[...] = jnp.zeros_like(weight_grad)
        bias_grad[...] = jnp.zeros_like(bias_grad)

    @pl.when(pair == PAIRS - 1)
    def finish():
        if own:
            dq = dq_all[...].T.astype(BF)
            weight_grad[:, :width] += dot(tokens_low[0], dq, "tn")
            bias_grad[0:1] += jnp.sum(dq.astype(F32), axis=0, keepdims=True)
            share[0] = (
                partial[0]
                + dot(dq, weight[:, :width], "nt")
                + dot(dkv[...], weight[:, width:], "nt")
            )
            weight_grad[:, width:] += dot(tokens_low[0], dkv[...], "tn")
        else:
            share[0] = dot(dkv[...], weight[:, width:], "nt").astype(BF)
            weight_grad[...] += dot(tokens_low[0], dkv[...], "tn")
        bias_grad[1:2] += jnp.sum(dkv[:, width:].astype(F32), axis=0, keepdims=True)


def pull(e_part, joint_own, joint_part, mixed_grad, mixed_t, inverse, tokens_low, weight, extra):
    own = extra is not None
    groups, _, span, local = e_part.shape
    width = H * HEAD
    first = PAIRS if own else 0
    grid = (groups, PAIRS)
    columns = 3 * width if own else 2 * width

    def still(*shape):
        return pl.BlockSpec(shape, lambda g, p: (0,) * len(shape), pipeline_mode=pl.Buffered(1))

    in_specs = [
        pl.BlockSpec((1, 2, span, local), lambda g, p: (g, p, 0, 0)),
        pl.BlockSpec((1, local, WIDE), lambda g, p: (g, 0, p)),
        pl.BlockSpec((1, span, WIDE), lambda g, p: (g, 0, first + p)),
        pl.BlockSpec((1, span, WIDE), lambda g, p: (g, 0, first + PAIRS + p)),
        pl.BlockSpec((1, local, WIDE), lambda g, p: (g, 0, p)),
        pl.BlockSpec((1, WIDE, local), lambda g, p: (g, p, 0)),
        pl.BlockSpec((1, 1, 2, local), lambda g, p: (g, p, 0, 0)),
        pl.BlockSpec((1, span, width), lambda g, p: (g, 0, 0), pipeline_mode=pl.Buffered(1)),
        still(width, 3 * width),
    ]
    scratch = [
        pltpu.VMEM((span, 2 * width), BF),
        pltpu.VMEM((2, span, local), BF),
    ]
    out_specs = [
        pl.BlockSpec((1, span, width), lambda g, p: (g, 0, 0), pipeline_mode=pl.Buffered(1))
    ]
    out_shape = [jax.ShapeDtypeStruct((groups, span, width), F32 if own else BF)]
    if own:
        in_specs += [
            pl.BlockSpec((1, local, width), lambda g, p: (g, 0, 0), pipeline_mode=pl.Buffered(1)),
            pl.BlockSpec((1, WIDE, local), lambda g, p: (g, p, 0)),
        ]
        scratch += [pltpu.VMEM((width, local), F32)]
    else:
        out_specs += [pl.BlockSpec((1, WIDE, local), lambda g, p: (g, p, 0))]
        out_shape += [jax.ShapeDtypeStruct((groups, width, local), F32)]
    out_specs += [still(width, columns), still(8, width)]
    out_shape += [
        jax.ShapeDtypeStruct((width, columns), F32),
        jax.ShapeDtypeStruct((8, width), F32),
    ]
    return pl.pallas_call(
        functools.partial(pull_kernel, own),
        grid=grid,
        in_specs=in_specs,
        out_specs=out_specs,
        out_shape=out_shape,
        scratch_shapes=scratch,
        compiler_params=params(58, 2),
        name="pull_own" if own else "pull_rest",
    )(
        e_part,
        joint_own,
        joint_part,
        joint_part,
        mixed_grad,
        mixed_t,
        inverse,
        tokens_low,
        weight,
        *(extra or ()),
    )


def per_device(
    tokens,
    lengths,
    joint_weight,
    joint_bias,
    out_weight,
    out_bias,
    gain_first,
    shift_first,
    up_weight,
    up_bias,
    down_weight,
    down_bias,
    gain_second,
    shift_second,
    cotangent,
):
    groups, local, width = tokens.shape
    parts = lax.axis_size("seq")
    devices = lax.axis_size("dp") * parts
    me = lax.axis_index("seq")
    rows = groups * local
    tokens_low = tokens.astype(BF)
    others = [
        lax.ppermute(tokens_low, "seq", [(i, (i - shift) % parts) for i in range(parts)])
        for shift in range(1, parts)
    ]
    tokens_rest = others[0] if parts == 2 else jnp.concatenate(others, axis=1)

    own_rows = joint_weight.shape[0]
    joint_shard = (
        joint_weight.astype(BF)
        .reshape(own_rows, H, 3, HEAD)
        .transpose(0, 2, 1, 3)
        .reshape(own_rows, 3 * width)
    )
    vectors = [
        joint_bias,
        out_bias,
        gain_first,
        shift_first,
        up_bias,
        down_bias,
        gain_second,
        shift_second,
    ]
    lens = [v.shape[0] for v in vectors]
    packed = jnp.concatenate([v.astype(BF) for v in vectors])
    room = -packed.shape[0] % 128
    packed = jnp.pad(packed, (0, room)).reshape(1, -1)
    packed = jnp.broadcast_to(packed, (16, packed.shape[1]))
    joint_w, out_w, up_w, down_w, packed = gather_weights(
        [
            joint_shard,
            out_weight.astype(BF),
            up_weight.astype(BF),
            down_weight.astype(BF),
            packed,
        ],
        (0, 1, 0, 1, 1),
    )
    packed = packed.reshape(devices, 16, -1)[:, 0].astype(F32)
    full, at = [], 0
    for size in lens:
        full.append(packed[:, at : at + size].reshape(devices * size))
        at += size
    pair_full, out_b, gain_1, shift_1, up_b, down_b, gain_2, shift_2 = full
    pair_full = pair_full.reshape(H, 2, HEAD)
    bias_kv = jnp.concatenate([jnp.zeros(width, F32), pair_full[:, 1].reshape(width)])
    bias_all = jnp.concatenate([pair_full[:, 0].reshape(width), bias_kv])
    blank = jnp.zeros(width, F32)
    row_stack = jnp.stack([out_b, gain_1, shift_1, down_b, gain_2, shift_2, blank, blank])

    joint_own = (
        jnp.dot(tokens_low.reshape(rows, width), joint_w, preferred_element_type=F32) + bias_all
    )
    joint_own = joint_own.astype(BF).reshape(groups, local, 3 * width)
    joint_rest = (
        jnp.dot(
            tokens_rest.reshape(-1, width), joint_w[:, width:], preferred_element_type=F32
        )
        + bias_kv
    )
    joint_rest = joint_rest.astype(BF).reshape(groups, (parts - 1) * local, 2 * width)

    places = (me + jnp.arange(parts, dtype=jnp.int32)) % parts * local
    info = jnp.concatenate([lengths, places.astype(jnp.int32)])
    e_own, e_rest, mixed, mixed_t, inverse = attend(info, joint_own, joint_rest, parts)

    result, partial, mixed_grad, out_wg, up_wg, down_wg, row_sums, up_bias_sum = middle(
        tokens.reshape(rows, width),
        cotangent.reshape(rows, width),
        mixed.reshape(rows, width),
        out_w,
        up_w,
        down_w,
        row_stack,
        up_b.reshape(1, -1),
    )
    mixed_grad = mixed_grad.reshape(groups, local, width)
    out_sum, up_sum, down_sum = owner_sums([out_wg, up_wg, down_wg])

    share_rest, dq_rest, joint_wg_rest, bias_rest = pull(
        e_rest, joint_own, joint_rest, mixed_grad, mixed_t, inverse, tokens_rest, joint_w, None
    )
    returned = [
        lax.ppermute(
            share_rest[:, (shift - 1) * local : shift * local],
            "seq",
            [(i, (i + shift) % parts) for i in range(parts)],
        )
        for shift in range(1, parts)
    ]
    input_grad, joint_wg, bias_own = pull(
        e_own,
        joint_own,
        joint_own,
        mixed_grad,
        mixed_t,
        inverse,
        tokens_low,
        joint_w,
        (partial.reshape(groups, local, width), dq_rest),
    )
    for piece in returned:
        input_grad = input_grad + piece.astype(F32)
    joint_wg = jnp.concatenate([joint_wg[:, :width], joint_wg[:, width:] + joint_wg_rest], axis=1)

    pair_grad = jnp.stack(
        [
            bias_own[0].reshape(H, HEAD),
            (bias_own[1] + bias_rest[1]).reshape(H, HEAD),
        ],
        axis=1,
    ).reshape(2 * width)
    sums = [
        pair_grad,
        row_sums[0],
        row_sums[1],
        row_sums[2],
        up_bias_sum[0],
        row_sums[3],
        row_sums[4],
        row_sums[5],
    ]
    vec = jnp.concatenate([s.reshape(devices, -1) for s in sums], axis=1)
    joint_sum, vec = owner_sums([joint_wg, vec])
    joint_sum = joint_sum.reshape(own_rows, 3, H, HEAD).transpose(0, 2, 1, 3)
    joint_sum = joint_sum.reshape(own_rows, 3 * width)
    vec = vec.reshape(-1)
    small, at = [], 0
    for size in lens:
        small.append(vec[at : at + size])
        at += size
    return (
        result.reshape(groups, local, width),
        input_grad,
        joint_sum,
        small[0],
        out_sum,
        small[1],
        small[2],
        small[3],
        up_sum,
        small[4],
        down_sum,
        small[5],
        small[6],
        small[7],
    )


def solution(mesh):
    both = ("dp", "seq")
    matrix, vector, whole = P(both, None), P(both), P("dp", "seq", None)
    return jax.shard_map(
        per_device,
        mesh=mesh,
        in_specs=(
            whole,
            P("dp"),
            matrix,
            vector,
            matrix,
            vector,
            vector,
            vector,
            matrix,
            vector,
            matrix,
            vector,
            vector,
            vector,
            whole,
        ),
        out_specs=(
            whole,
            whole,
            matrix,
            vector,
            matrix,
            vector,
            vector,
            vector,
            matrix,
            vector,
            matrix,
            vector,
            vector,
            vector,
        ),
        check_vma=False,
    )
```

```python
import functools
import math

import jax
import jax.numpy as jnp
from jax import lax
from jax.experimental import pallas as pl
from jax.experimental.pallas import tpu as pltpu
from jax.sharding import PartitionSpec as P

H = 8
HEAD = 64
PAIRS = H // 2
WIDE = 2 * HEAD
BF = jnp.bfloat16
F32 = jnp.float32
EPS = 1e-05
SCALE = 1.0 / math.sqrt(HEAD)
LOG2E = math.log2(math.e)
GELU_A = math.sqrt(2.0 / math.pi)
GELU_B = 0.044715
MESH = pl.DeviceIdType.MESH
MIB = 2**20
FORMS = {
    "nn": (((1,), (0,)), ((), ())),
    "nt": (((1,), (1,)), ((), ())),
    "tn": (((0,), (0,)), ((), ())),
}


def dot(left, right, form="nn"):
    return lax.dot_general(left, right, FORMS[form], preferred_element_type=F32)


def params(limit, steps):
    return pltpu.CompilerParams(
        vmem_limit_bytes=limit * MIB, dimension_semantics=("arbitrary",) * steps
    )


def log2(size):
    return size.bit_length() - 1


def place_bits(bits_dp, bits_seq):
    dp, seq = lax.axis_index("dp"), lax.axis_index("seq")
    mine = [lax.rem(dp // 2 ** (bits_dp - 1 - b), 2) for b in range(bits_dp)]
    mine += [lax.rem(seq // 2 ** (bits_seq - 1 - b), 2) for b in range(bits_seq)]

    def partner(bit):
        if bit < bits_dp:
            return (dp + (1 - 2 * mine[bit]) * 2 ** (bits_dp - 1 - bit), seq)
        return (dp, seq + (1 - 2 * mine[bit]) * 2 ** (bits_dp + bits_seq - 1 - bit))

    return mine, partner


def greet(partner, bits):
    barrier = pltpu.get_barrier_semaphore()
    for bit in range(bits):
        pl.semaphore_signal(barrier, inc=1, device_id=partner(bit), device_id_type=MESH)


def own_copies(shards, fulls, mine, sem):
    return [
        pltpu.make_async_copy(shard, full.at[tuple(mine)], sem.at[i])
        for i, (shard, full) in enumerate(zip(shards, fulls))
    ]


def stage_copies(stage, orders, fulls, mine, partner, send_sem, recv_sem):
    copies = []
    for i, full in enumerate(fulls):
        done = orders[i][:stage]
        place = tuple(slice(None) if b in done else mine[b] for b in range(len(mine)))
        copies.append(
            pltpu.make_async_remote_copy(
                src_ref=full.at[place],
                dst_ref=full.at[place],
                send_sem=send_sem.at[stage, i],
                recv_sem=recv_sem.at[stage, i],
                device_id=partner(orders[i][stage]),
                device_id_type=MESH,
            )
        )
    return copies


def gather_plan(first):
    bits_dp, bits_seq = log2(lax.axis_size("dp")), log2(lax.axis_size("seq"))
    bits = bits_dp + bits_seq
    upper = list(range(bits_dp - 1))
    beside = list(range(bits_dp, bits))
    plans = (upper + beside + [bits_dp - 1], upper[:-1] + beside + upper[-1:] + [bits_dp - 1])
    return bits_dp, bits_seq, tuple(tuple(plans[p]) for p in first)


def gather_kernel(orders, bits_dp, bits_seq, *refs):
    count = len(orders)
    shards, fulls = refs[:count], refs[count : 2 * count]
    own_sem, send_sem, recv_sem = refs[2 * count :]
    bits = bits_dp + bits_seq
    mine, partner = place_bits(bits_dp, bits_seq)
    greet(partner, bits)
    local = own_copies(shards, fulls, mine, own_sem)
    for copy in local:
        copy.start()
    for copy in local:
        copy.wait()
    pl.semaphore_wait(pltpu.get_barrier_semaphore(), bits)
    for stage in range(bits):
        copies = stage_copies(stage, orders, fulls, mine, partner, send_sem, recv_sem)
        for copy in copies:
            copy.start()
        for copy in copies:
            copy.wait()


def spread(full):
    return full.reshape((-1,) + full.shape[-1:])


def gather_weights(shards, first):
    bits_dp, bits_seq, orders = gather_plan(first)
    bits = bits_dp + bits_seq
    count = len(shards)
    fulls = pl.pallas_call(
        functools.partial(gather_kernel, orders, bits_dp, bits_seq),
        out_shape=[jax.ShapeDtypeStruct((2,) * bits + s.shape, s.dtype) for s in shards],
        in_specs=[pl.BlockSpec(memory_space=pl.ANY)] * count,
        out_specs=[pl.BlockSpec(memory_space=pl.ANY)] * count,
        scratch_shapes=[
            pltpu.SemaphoreType.DMA((count,)),
            pltpu.SemaphoreType.DMA((bits, count)),
            pltpu.SemaphoreType.DMA((bits, count)),
        ],
        compiler_params=pltpu.CompilerParams(collective_id=0, has_side_effects=True),
        name="gather_weights",
    )(*shards)
    return [spread(f) for f in fulls]


def owner_sums(arrays):
    size_dp, size_seq = lax.axis_size("dp"), lax.axis_size("seq")
    bits_dp, bits_seq = log2(size_dp), log2(size_seq)
    bits = bits_dp + bits_seq
    dp, seq = lax.axis_index("dp"), lax.axis_index("seq")
    rows = [a.shape[0] // (size_dp * size_seq) for a in arrays]
    arrays = [
        a.reshape((2,) * bits + (r,) + a.shape[1:]) for a, r in zip(arrays, rows)
    ]
    left = list(range(bits))
    order = [bits_dp - 1] + list(range(bits_dp, bits)) + list(range(bits_dp - 2, -1, -1))
    for bit in order:
        axis = left.index(bit)
        left.remove(bit)
        if bit < bits_dp:
            name, size, step, me = "dp", size_dp, 2 ** (bits_dp - 1 - bit), dp
        else:
            name, size, step, me = "seq", size_seq, 2 ** (bits - 1 - bit), seq
        mine = me // step % 2
        pairs = [(i, i ^ step) for i in range(size)]
        sent = [
            lax.dynamic_index_in_dim(a, 1 - mine, axis, keepdims=False).astype(BF) for a in arrays
        ]
        kept = [lax.dynamic_index_in_dim(a, mine, axis, keepdims=False) for a in arrays]
        arrived = [lax.ppermute(s, name, pairs) for s in sent]
        arrays = [k + a.astype(F32) for k, a in zip(kept, arrived)]
    return arrays


def project_kernel(own, tokens, weight, bias, *outs):
    x = tokens[...]
    if own:
        query, pair = outs
    else:
        (pair,) = outs
    for p in range(PAIRS):
        start = 3 * WIDE * p + (0 if own else WIDE)
        end = 3 * WIDE * (p + 1)
        joint = (dot(x, weight[:, start:end]) + bias[:, start:end]).astype(BF)
        if own:
            query[:, p * WIDE : (p + 1) * WIDE] = joint[:, :WIDE]
            joint = joint[:, WIDE:]
        pair[:, 2 * p * WIDE : 2 * (p + 1) * WIDE] = joint


def project(tokens, weight, bias, own):
    count, width = tokens.shape
    block = min(512, count)

    def moving(columns):
        return pl.BlockSpec((block, columns), lambda b: (b, 0))

    def still(*shape):
        return pl.BlockSpec(shape, lambda b: (0, 0), pipeline_mode=pl.Buffered(1))

    wide = [width, 2 * width] if own else [2 * width]
    return pl.pallas_call(
        functools.partial(project_kernel, own),
        grid=(count // block,),
        in_specs=[moving(width), still(width, 3 * width), still(1, 3 * width)],
        out_specs=[moving(w) for w in wide],
        out_shape=[jax.ShapeDtypeStruct((count, w), BF) for w in wide],
        compiler_params=params(40, 1),
        name="project_own" if own else "project_rest",
    )(tokens, weight, bias)


def attend_kernel(parts, groups, steps, blocks, orders, bits_dp, bits_seq, *refs):
    count = len(orders)
    info, query, keys_own, keys_rest, values_own, values_rest = refs[:6]
    shards = refs[6 : 6 + count]
    e_out, mixed, mixed_t, inverse = refs[6 + count : 10 + count]
    fulls = refs[10 + count : 10 + 2 * count]
    k_ext, v_ext, kept, tops, own_sem, send_sem, recv_sem = refs[10 + 2 * count :]
    local = keys_own.shape[1]
    block = query.shape[1]
    step = pl.program_id(0)
    chunk = min(256, local)

    bits = bits_dp + bits_seq
    mine, partner = place_bits(bits_dp, bits_seq)
    stages = [
        stage_copies(stage, orders, fulls, mine, partner, send_sem, recv_sem)
        for stage in range(bits)
    ]

    @pl.when(step == 0)
    def enter():
        greet(partner, bits)
        local_copies = own_copies(shards, fulls, mine, own_sem)
        for copy in local_copies:
            copy.start()
        for copy in local_copies:
            copy.wait()
        pl.semaphore_wait(pltpu.get_barrier_semaphore(), bits)
        for copy in stages[0]:
            copy.start()

    for stage in range(1, bits + 1):
        due = max(stage * steps // (bits + 1), 1) if bits <= steps else min(stage, steps)

        @pl.when(step == due)
        def advance():
            for copy in stages[stage - 1]:
                copy.wait()
            if stage < bits:
                for copy in stages[stage]:
                    copy.start()

    @pl.when(jnp.logical_and(step % blocks == 0, step < steps))
    def prepare_keys():
        for group in range(groups):
            @pl.when(step // (blocks * PAIRS) == group)
            def fill():
                length = info[group]
                for part in range(parts):
                    rows = slice(part * local, (part + 1) * local)
                    k_ext[rows, :WIDE] = keys_own[0] if part == 0 else keys_rest[part - 1, 0]
                    place = lax.broadcasted_iota(jnp.int32, (local, WIDE), 0) + info[groups + part]
                    k_ext[rows, WIDE:] = jnp.where(place < length, 0.0, -1e30).astype(BF)

    @pl.when(step % blocks == 1 % blocks)
    def prepare_values():
        for part in range(parts):
            rows = slice(part * local, (part + 1) * local)
            values = values_own[0] if part == 0 else values_rest[part - 1, 0]
            turned = values.T
            v_ext[0, :HEAD, rows] = turned[:HEAD]
            v_ext[1, :HEAD, rows] = turned[HEAD:]
            v_ext[:, HEAD:, rows] = jnp.ones((2, HEAD, local), BF)

    turned = query[0].T
    zero = jnp.zeros((HEAD, block), BF)
    one = (lax.broadcasted_iota(jnp.int32, (WIDE, block), 0) == 0).astype(F32).astype(BF)
    heads = []
    for head in range(2):
        if head == 0:
            picked = jnp.concatenate([turned[:HEAD], zero, one], axis=0)
        else:
            picked = jnp.concatenate([zero, turned[HEAD:], one], axis=0)
        top = tops[head : head + 1]
        out = None
        largest = None
        for at in range(0, parts * local, chunk):
            rows = slice(at, at + chunk)
            inside = slice(at % local, at % local + chunk)
            e = jnp.exp2((kept[head, rows] - top) * (SCALE * LOG2E)).astype(BF)
            e_out[at // local, 0, head, inside] = e
            add = dot(v_ext[head, :, rows], e)
            out = add if out is None else out + add
            scores = dot(k_ext[rows], picked)
            kept[head, rows] = scores
            most = jnp.max(scores.reshape(chunk // 8, 8, block), axis=0)
            largest = most if largest is None else jnp.maximum(largest, most)
        tops[head : head + 1] = jnp.max(largest, axis=0, keepdims=True)
        inv = 1.0 / out[HEAD : HEAD + 1]
        inverse[0, 0, head : head + 1] = inv
        heads.append(out[:HEAD] * inv)
    both = jnp.concatenate(heads, axis=0).astype(BF)
    mixed_t[0] = both
    mixed[0] = both.T


def attend(info, query, pair_own, pair_rest, shards, first):
    groups, local, width = query.shape
    others = pair_rest.shape[0]
    parts = others + 1
    block = min(512, local)
    blocks = local // block
    steps = groups * PAIRS * blocks
    bits_dp, bits_seq, orders = gather_plan(first)
    bits = bits_dp + bits_seq
    count = len(shards)

    def decode(t, place):
        return place(t // (PAIRS * blocks), t // blocks % PAIRS, t % blocks)

    def now(place):
        return lambda t: decode(jnp.minimum(t, steps - 1), place)

    def before(place):
        return lambda t: decode(jnp.maximum(t - 1, 0), place)

    outs = pl.pallas_call(
        functools.partial(
            attend_kernel, parts, groups, steps, blocks, orders, bits_dp, bits_seq
        ),
        grid=(steps + 1,),
        in_specs=[
            pl.BlockSpec(memory_space=pltpu.SMEM),
            pl.BlockSpec((1, block, WIDE), now(lambda g, p, b: (g, b, p))),
            pl.BlockSpec((1, local, WIDE), now(lambda g, p, b: (g, 0, 2 * p))),
            pl.BlockSpec((others, 1, local, WIDE), now(lambda g, p, b: (0, g, 0, 2 * p))),
            pl.BlockSpec((1, local, WIDE), before(lambda g, p, b: (g, 0, 2 * p + 1))),
            pl.BlockSpec((others, 1, local, WIDE), before(lambda g, p, b: (0, g, 0, 2 * p + 1))),
        ]
        + [pl.BlockSpec(memory_space=pl.ANY)] * count,
        out_specs=[
            pl.BlockSpec((parts, 1, 2, local, block), before(lambda g, p, b: (0, g, p, 0, b))),
            pl.BlockSpec((1, block, WIDE), before(lambda g, p, b: (g, b, p))),
            pl.BlockSpec((1, WIDE, block), before(lambda g, p, b: (g, p, b))),
            pl.BlockSpec((1, 1, 2, block), before(lambda g, p, b: (g, p, 0, b))),
        ]
        + [pl.BlockSpec(memory_space=pl.ANY)] * count,
        out_shape=[
            jax.ShapeDtypeStruct((parts, groups, H, local, local), BF),
            jax.ShapeDtypeStruct((groups, local, width), BF),
            jax.ShapeDtypeStruct((groups, width, local), BF),
            jax.ShapeDtypeStruct((groups, PAIRS, 2, local), F32),
        ]
        + [jax.ShapeDtypeStruct((2,) * bits + s.shape, s.dtype) for s in shards],
        scratch_shapes=[
            pltpu.VMEM((parts * local, 2 * WIDE), BF),
            pltpu.VMEM((2, WIDE, parts * local), BF),
            pltpu.VMEM((2, parts * local, block), F32),
            pltpu.VMEM((8, block), F32),
            pltpu.SemaphoreType.DMA((count,)),
            pltpu.SemaphoreType.DMA((bits, count)),
            pltpu.SemaphoreType.DMA((bits, count)),
        ],
        compiler_params=pltpu.CompilerParams(
            vmem_limit_bytes=56 * MIB,
            dimension_semantics=("arbitrary",),
            collective_id=1,
            has_side_effects=True,
        ),
        name="attend",
    )(info, query, pair_own, pair_rest, pair_own, pair_rest, *shards)
    return outs[:4], [spread(f) for f in outs[4:]]


def middle_kernel(
    tokens,
    cotangent,
    mixed,
    out_w,
    up_w,
    down_w,
    rows,
    up_bias,
    result,
    partial,
    mixed_grad,
    out_wg,
    up_wg,
    down_wg,
    row_sums,
    up_bias_sum,
):
    first = pl.program_id(0) == 0

    @pl.when(first)
    def clear():
        out_wg[...] = jnp.zeros_like(out_wg)
        up_wg[...] = jnp.zeros_like(up_wg)
        down_wg[...] = jnp.zeros_like(down_wg)
        row_sums[...] = jnp.zeros_like(row_sums)
        up_bias_sum[...] = jnp.zeros_like(up_bias_sum)

    out_bias, gain_one, shift_one = rows[0:1], rows[1:2], rows[2:3]
    down_bias, gain_two, shift_two = rows[3:4], rows[4:5], rows[5:6]

    def mean(v):
        return jnp.mean(v, axis=-1, keepdims=True)

    def total(v):
        return jnp.sum(v, axis=0, keepdims=True)

    x = tokens[...]
    heads = mixed[...]
    hidden = x + (dot(heads, out_w[...]) + out_bias)
    centred = hidden - mean(hidden)
    r_one = lax.rsqrt(mean(centred * centred) + EPS)
    n_one = centred * r_one
    normal = n_one * gain_one + shift_one
    normal_low = normal.astype(BF)
    inner = dot(normal_low, up_w[...]) + up_bias[...]
    square = inner * inner
    tanh = jnp.tanh(inner * (GELU_A + (GELU_A * GELU_B) * square))
    half = 0.5 + 0.5 * tanh
    active = (inner * half).astype(BF)
    slope = half + (0.5 * inner) * (1.0 - tanh * tanh) * (
        GELU_A + (3.0 * GELU_A * GELU_B) * square
    )
    branch = dot(active, down_w[...]) + down_bias
    last = normal + branch + x
    centred = last - mean(last)
    r_two = lax.rsqrt(mean(centred * centred) + EPS)
    n_two = centred * r_two
    result[...] = n_two * gain_two + shift_two
    grad = cotangent[...]
    e_two = grad * gain_two
    back = r_two * (e_two - mean(e_two) - n_two * mean(e_two * n_two))
    branch_grad = back.astype(BF)
    down_wg[...] += dot(active, branch_grad, "tn")
    inner_grad_wide = slope * dot(branch_grad, down_w[...], "nt")
    inner_grad = inner_grad_wide.astype(BF)
    up_wg[...] += dot(normal_low, inner_grad, "tn")
    up_bias_sum[...] += total(inner_grad.astype(F32))
    norm_grad = back + dot(inner_grad, up_w[...], "nt")
    e_one = norm_grad * gain_one
    hidden_grad = r_one * (e_one - mean(e_one) - n_one * mean(e_one * n_one))
    attn_grad = hidden_grad.astype(BF)
    partial[...] = back + hidden_grad
    out_wg[...] += dot(heads, attn_grad, "tn")
    mixed_grad[...] = dot(attn_grad, out_w[...], "nt").astype(BF)
    row_sums[0:1] += total(attn_grad.astype(F32))
    row_sums[1:2] += total(norm_grad * n_one)
    row_sums[2:3] += total(norm_grad)
    row_sums[3:4] += total(branch_grad.astype(F32))
    row_sums[4:5] += total(grad * n_two)
    row_sums[5:6] += total(grad)


def middle(tokens, cotangent, mixed, out_w, up_w, down_w, rows, up_bias):
    count, width = tokens.shape
    hidden = up_w.shape[1]
    block = min(256, count)

    def moving(columns=width):
        return pl.BlockSpec((block, columns), lambda b: (b, 0))

    def still(*shape):
        return pl.BlockSpec(shape, lambda b: (0, 0), pipeline_mode=pl.Buffered(1))

    return pl.pallas_call(
        middle_kernel,
        grid=(count // block,),
        in_specs=[
            moving(),
            moving(),
            moving(),
            still(width, width),
            still(width, hidden),
            still(hidden, width),
            still(8, width),
            still(1, hidden),
        ],
        out_specs=[
            moving(),
            moving(),
            moving(),
            still(width, width),
            still(width, hidden),
            still(hidden, width),
            still(8, width),
            still(1, hidden),
        ],
        out_shape=[
            jax.ShapeDtypeStruct((count, width), F32),
            jax.ShapeDtypeStruct((count, width), F32),
            jax.ShapeDtypeStruct((count, width), BF),
            jax.ShapeDtypeStruct((width, width), F32),
            jax.ShapeDtypeStruct((width, hidden), F32),
            jax.ShapeDtypeStruct((hidden, width), F32),
            jax.ShapeDtypeStruct((8, width), F32),
            jax.ShapeDtypeStruct((1, hidden), F32),
        ],
        compiler_params=params(58, 1),
        name="middle",
    )(tokens, cotangent, mixed, out_w, up_w, down_w, rows, up_bias)


def pull_kernel(
    parts,
    groups,
    e_part,
    query,
    pair_own,
    pair_rest,
    mixed_grad,
    mixed_t,
    inverse,
    tokens_own,
    tokens_rest,
    weight,
    partial,
    share_rest,
    share_own,
    weight_grad,
    bias_grad,
    d_scores,
    joint_grad,
    total,
    dq_sums,
    dq_turned,
):
    step = pl.program_id(0)
    part = lax.rem(step // (groups * PAIRS) + 1, parts)
    group, pair = lax.rem(step // PAIRS, groups), lax.rem(step, PAIRS)
    own = part == 0
    local = query.shape[1]
    chunk = min(256, local)
    turned = mixed_grad[0].astype(F32).T
    mixed = mixed_t[0].astype(F32)
    values = jnp.where(own, pair_own[0, :, WIDE:], pair_rest[0, 0, :, WIDE:])
    keys_t = jnp.where(own, pair_own[0, :, :WIDE], pair_rest[0, 0, :, :WIDE]).T
    query_now = query[0]
    lane = lax.broadcasted_iota(jnp.int32, (local, WIDE), 1)
    zero = jnp.zeros((HEAD, local), BF)
    grad_t, grad, centre, picked = [], [], [], []
    for head in range(2):
        side = slice(head * HEAD, (head + 1) * HEAD)
        inv = inverse[0, 0, head : head + 1]
        centre.append(inv * jnp.sum(turned[side] * mixed[side], axis=0, keepdims=True))
        scaled = (turned[side] * inv).astype(BF)
        grad_t.append(jnp.concatenate([scaled, zero] if head == 0 else [zero, scaled], axis=0))
        grad.append(grad_t[head].T)
        kept = lane < HEAD if head == 0 else lane >= HEAD
        picked.append(jnp.where(kept, query_now, jnp.zeros_like(query_now)))

    def key_grad(rows):
        sums = dot(d_scores[0, rows], picked[0]) + dot(d_scores[1, rows], picked[1])
        joint_grad[rows, WIDE : 2 * WIDE] = (sums * SCALE).astype(BF)

    last = None
    for at in range(0, local, chunk):
        rows = slice(at, at + chunk)
        for head in range(2):
            pulled = dot(values[rows], grad_t[head])
            e = e_part[0, 0, head, rows].astype(F32)
            d_scores[head, rows] = (e * (pulled - centre[head])).astype(BF)
        sums = dot(e_part[0, 0, 0, rows], grad[0]) + dot(e_part[0, 0, 1, rows], grad[1])
        joint_grad[rows, 2 * WIDE :] = sums.astype(BF)
        if last is not None:
            key_grad(last)
        last = rows
    key_grad(last)
    first_part = part == 1 % parts
    for head in range(2):
        side = slice(head * HEAD, (head + 1) * HEAD)
        dq = dot(keys_t, d_scores[head])[side]
        dq_turned[side] = dq

    @pl.when(step == 0)
    def clear():
        weight_grad[...] = jnp.zeros_like(weight_grad)
        bias_grad[...] = jnp.zeros_like(bias_grad)
        dq_sums[...] = jnp.zeros_like(dq_sums)

    @pl.when(pair == 0)
    def start():
        total[...] = jnp.zeros_like(total)

    side = pl.ds(pl.multiple_of(pair * WIDE, WIDE), WIDE)
    start_at = pair * (3 * WIDE)
    wide = pl.ds(pl.multiple_of(start_at, WIDE), 3 * WIDE)
    last_two = pl.ds(pl.multiple_of(start_at + WIDE, WIDE), 2 * WIDE)
    column = group * PAIRS + pair

    @pl.when(own)
    def near():
        dq = (dq_sums[column] + dq_turned[...]) * SCALE
        dq = dq.T.astype(BF)
        joint_grad[:, :WIDE] = dq
        bias_grad[0:1, side] += jnp.sum(dq.astype(F32), axis=0, keepdims=True)
        total[...] += dot(joint_grad[...], weight[:, wide], "nt")
        weight_grad[:, wide] += dot(tokens_own[0], joint_grad[...], "tn")

    @pl.when(jnp.logical_not(own))
    def far():
        dq_sums[column] += dq_turned[...]
        total[...] += dot(joint_grad[:, WIDE:], weight[:, last_two], "nt")
        weight_grad[:, last_two] += dot(tokens_rest[0, 0], joint_grad[:, WIDE:], "tn")

    bias_grad[1:2, side] += jnp.sum(joint_grad[:, 2 * WIDE :].astype(F32), axis=0, keepdims=True)

    @pl.when(jnp.logical_and(pair == PAIRS - 1, own))
    def finish_near():
        share_own[0] = total[...] + partial[0]

    @pl.when(jnp.logical_and(pair == PAIRS - 1, jnp.logical_not(own)))
    def finish_far():
        share_rest[0, 0] = total[...].astype(BF)


def pull(e_all, query, pair_own, pair_rest, mixed_grad, mixed_t, inverse, own, rest, weight, partial):
    parts, groups, _, local, _ = e_all.shape
    width = H * HEAD
    each = groups * PAIRS

    def at(place):
        return lambda t: place((t // each + 1) % parts, t // PAIRS % groups, t % PAIRS)

    def own_at(place):
        return lambda t: place(
            jnp.where(t // each == parts - 1, t // PAIRS % groups, 0),
            jnp.where(t // each == parts - 1, t % PAIRS, 0),
        )

    def rest_at(place):
        def index(t):
            t = jnp.minimum(t, (parts - 1) * each - 1)
            return place(t // each, t // PAIRS % groups, t % PAIRS)

        return index

    def still(*shape):
        return pl.BlockSpec(shape, lambda t: (0,) * len(shape), pipeline_mode=pl.Buffered(1))

    return pl.pallas_call(
        functools.partial(pull_kernel, parts, groups),
        grid=(parts * each,),
        in_specs=[
            pl.BlockSpec((1, 1, 2, local, local), at(lambda j, g, p: (j, g, p, 0, 0))),
            pl.BlockSpec((1, local, WIDE), at(lambda j, g, p: (g, 0, p))),
            pl.BlockSpec((1, local, 2 * WIDE), own_at(lambda g, p: (g, 0, p))),
            pl.BlockSpec((1, 1, local, 2 * WIDE), rest_at(lambda j, g, p: (j, g, 0, p))),
            pl.BlockSpec((1, local, WIDE), at(lambda j, g, p: (g, 0, p))),
            pl.BlockSpec((1, WIDE, local), at(lambda j, g, p: (g, p, 0))),
            pl.BlockSpec((1, 1, 2, local), at(lambda j, g, p: (g, p, 0, 0))),
            pl.BlockSpec((1, local, width), own_at(lambda g, p: (g, 0, 0))),
            pl.BlockSpec((1, 1, local, width), rest_at(lambda j, g, p: (j, g, 0, 0))),
            still(width, 3 * width),
            pl.BlockSpec((1, local, width), own_at(lambda g, p: (g, 0, 0))),
        ],
        out_specs=[
            pl.BlockSpec((1, 1, local, width), rest_at(lambda j, g, p: (j, g, 0, 0))),
            pl.BlockSpec((1, local, width), own_at(lambda g, p: (g, 0, 0))),
            still(width, 3 * width),
            still(8, width),
        ],
        out_shape=[
            jax.ShapeDtypeStruct((parts - 1, groups, local, width), BF),
            jax.ShapeDtypeStruct((groups, local, width), F32),
            jax.ShapeDtypeStruct((width, 3 * width), F32),
            jax.ShapeDtypeStruct((8, width), F32),
        ],
        scratch_shapes=[
            pltpu.VMEM((2, local, local), BF),
            pltpu.VMEM((local, 3 * WIDE), BF),
            pltpu.VMEM((local, width), F32),
            pltpu.VMEM((each, WIDE, local), F32),
            pltpu.VMEM((WIDE, local), F32),
        ],
        compiler_params=params(60, 1),
        name="pull",
    )(e_all, query, pair_own, pair_rest, mixed_grad, mixed_t, inverse, own, rest, weight, partial)


def per_device(
    tokens,
    lengths,
    joint_weight,
    joint_bias,
    out_weight,
    out_bias,
    gain_first,
    shift_first,
    up_weight,
    up_bias,
    down_weight,
    down_bias,
    gain_second,
    shift_second,
    cotangent,
):
    groups, local, width = tokens.shape
    parts = lax.axis_size("seq")
    devices = lax.axis_size("dp") * parts
    me = lax.axis_index("seq")
    rows = groups * local
    tokens_low = tokens.astype(BF)
    tokens_rest = jnp.stack(
        [
            lax.ppermute(tokens_low, "seq", [(i, (i - shift) % parts) for i in range(parts)])
            for shift in range(1, parts)
        ]
    )

    own_rows = joint_weight.shape[0]
    joint_shard = (
        joint_weight.astype(BF)
        .reshape(own_rows, PAIRS, 2, 3, HEAD)
        .transpose(0, 1, 3, 2, 4)
        .reshape(own_rows, 3 * width)
    )
    vectors = [
        joint_bias,
        out_bias,
        gain_first,
        shift_first,
        up_bias,
        down_bias,
        gain_second,
        shift_second,
    ]
    lens = [v.shape[0] for v in vectors]
    packed = jnp.concatenate([v.astype(BF) for v in vectors])
    room = -packed.shape[0] % 128
    packed = jnp.pad(packed, (0, room)).reshape(1, -1)
    packed = jnp.broadcast_to(packed, (16, packed.shape[1]))
    joint_w, packed = gather_weights([joint_shard, packed], (0, 1))
    packed = packed.reshape(devices, 16, -1)[:, 0].astype(F32)
    full, at = [], 0
    for size in lens:
        full.append(packed[:, at : at + size].reshape(devices * size))
        at += size
    pair_full, out_b, gain_1, shift_1, up_b, down_b, gain_2, shift_2 = full
    pair_full = pair_full.reshape(PAIRS, 2, 2, HEAD)
    bias_all = jnp.stack(
        [pair_full[:, :, 0], jnp.zeros((PAIRS, 2, HEAD), F32), pair_full[:, :, 1]], axis=1
    ).reshape(1, 3 * width)
    blank = jnp.zeros(width, F32)
    row_stack = jnp.stack([out_b, gain_1, shift_1, down_b, gain_2, shift_2, blank, blank])

    query, pair_own = project(tokens_low.reshape(rows, width), joint_w, bias_all, True)
    (pair_rest,) = project(tokens_rest.reshape(-1, width), joint_w, bias_all, False)
    query = query.reshape(groups, local, width)
    pair_own = pair_own.reshape(groups, local, 2 * width)
    pair_rest = pair_rest.reshape(parts - 1, groups, local, 2 * width)

    places = (me + jnp.arange(parts, dtype=jnp.int32)) % parts * local
    info = jnp.concatenate([lengths, places.astype(jnp.int32)])
    (e_all, mixed, mixed_t, inverse), (out_w, up_w, down_w) = attend(
        info,
        query,
        pair_own,
        pair_rest,
        [out_weight.astype(BF), up_weight.astype(BF), down_weight.astype(BF)],
        (0, 0, 1),
    )

    result, partial, mixed_grad, out_wg, up_wg, down_wg, row_sums, up_bias_sum = middle(
        tokens.reshape(rows, width),
        cotangent.reshape(rows, width),
        mixed.reshape(rows, width),
        out_w,
        up_w,
        down_w,
        row_stack,
        up_b.reshape(1, -1),
    )
    mixed_grad = mixed_grad.reshape(groups, local, width)
    out_sum, up_sum, down_sum = owner_sums([out_wg, up_wg, down_wg])

    share_rest, input_grad, joint_wg, bias_grad = pull(
        e_all,
        query,
        pair_own,
        pair_rest,
        mixed_grad,
        mixed_t,
        inverse,
        tokens_low,
        tokens_rest,
        joint_w,
        partial.reshape(groups, local, width),
    )
    for shift in range(1, parts):
        piece = lax.ppermute(
            share_rest[shift - 1], "seq", [(i, (i + shift) % parts) for i in range(parts)]
        )
        input_grad = input_grad + piece.astype(F32)

    pair_grad = jnp.stack(
        [bias_grad[0].reshape(H, HEAD), bias_grad[1].reshape(H, HEAD)], axis=1
    ).reshape(2 * width)
    sums = [
        pair_grad,
        row_sums[0],
        row_sums[1],
        row_sums[2],
        up_bias_sum[0],
        row_sums[3],
        row_sums[4],
        row_sums[5],
    ]
    vec = jnp.concatenate([s.reshape(devices, -1) for s in sums], axis=1)
    joint_sum, vec = owner_sums([joint_wg, vec])
    joint_sum = joint_sum.reshape(own_rows, PAIRS, 3, 2, HEAD).transpose(0, 1, 3, 2, 4)
    joint_sum = joint_sum.reshape(own_rows, 3 * width)
    vec = vec.reshape(-1)
    small, at = [], 0
    for size in lens:
        small.append(vec[at : at + size])
        at += size
    return (
        result.reshape(groups, local, width),
        input_grad,
        joint_sum,
        small[0],
        out_sum,
        small[1],
        small[2],
        small[3],
        up_sum,
        small[4],
        down_sum,
        small[5],
        small[6],
        small[7],
    )


def solution(mesh):
    both = ("dp", "seq")
    matrix, vector, whole = P(both, None), P(both), P("dp", "seq", None)
    return jax.shard_map(
        per_device,
        mesh=mesh,
        in_specs=(
            whole,
            P("dp"),
            matrix,
            vector,
            matrix,
            vector,
            vector,
            vector,
            matrix,
            vector,
            matrix,
            vector,
            vector,
            vector,
            whole,
        ),
        out_specs=(
            whole,
            whole,
            matrix,
            vector,
            matrix,
            vector,
            vector,
            vector,
            matrix,
            vector,
            matrix,
            vector,
            vector,
            vector,
        ),
        check_vma=False,
    )
```

```python
import functools
import math

import jax
import jax.numpy as jnp
from jax import lax
from jax.experimental import pallas as pl
from jax.experimental.pallas import tpu as pltpu
from jax.sharding import PartitionSpec as P

H = 8
HEAD = 64
PAIRS = H // 2
WIDE = 2 * HEAD
BF = jnp.bfloat16
F32 = jnp.float32
EPS = 1e-05
SCALE = 1.0 / math.sqrt(HEAD)
LOG2E = math.log2(math.e)
GELU_A = math.sqrt(2.0 / math.pi)
GELU_B = 0.044715
MESH = pl.DeviceIdType.MESH
MIB = 2**20
FORMS = {
    "nn": (((1,), (0,)), ((), ())),
    "nt": (((1,), (1,)), ((), ())),
    "tn": (((0,), (0,)), ((), ())),
}


def dot(left, right, form="nn"):
    return lax.dot_general(left, right, FORMS[form], preferred_element_type=F32)


def whole_tiles(width, devices):
    return width // devices % 16 == 0


def params(limit, steps):
    return pltpu.CompilerParams(
        vmem_limit_bytes=limit * MIB, dimension_semantics=("arbitrary",) * steps
    )


def log2(size):
    return size.bit_length() - 1


def place_bits(bits_dp, bits_seq):
    dp, seq = lax.axis_index("dp"), lax.axis_index("seq")
    mine = [lax.rem(dp // 2 ** (bits_dp - 1 - b), 2) for b in range(bits_dp)]
    mine += [lax.rem(seq // 2 ** (bits_seq - 1 - b), 2) for b in range(bits_seq)]

    def partner(bit):
        if bit < bits_dp:
            return (dp + (1 - 2 * mine[bit]) * 2 ** (bits_dp - 1 - bit), seq)
        return (dp, seq + (1 - 2 * mine[bit]) * 2 ** (bits_dp + bits_seq - 1 - bit))

    return mine, partner


def greet(partner, bits):
    barrier = pltpu.get_barrier_semaphore()
    for bit in range(bits):
        pl.semaphore_signal(barrier, inc=1, device_id=partner(bit), device_id_type=MESH)


def own_copies(shards, fulls, mine, sem):
    return [
        pltpu.make_async_copy(shard, full.at[tuple(mine)], sem.at[i])
        for i, (shard, full) in enumerate(zip(shards, fulls))
    ]


def stage_copies(stage, orders, fulls, mine, partner, send_sem, recv_sem):
    copies = []
    for i, full in enumerate(fulls):
        done = orders[i][:stage]
        place = tuple(slice(None) if b in done else mine[b] for b in range(len(mine)))
        copies.append(
            pltpu.make_async_remote_copy(
                src_ref=full.at[place],
                dst_ref=full.at[place],
                send_sem=send_sem.at[stage, i],
                recv_sem=recv_sem.at[stage, i],
                device_id=partner(orders[i][stage]),
                device_id_type=MESH,
            )
        )
    return copies


def gather_plan(first):
    bits_dp, bits_seq = log2(lax.axis_size("dp")), log2(lax.axis_size("seq"))
    bits = bits_dp + bits_seq
    upper = list(range(bits_dp - 1))
    beside = list(range(bits_dp, bits))
    plans = (upper + beside + [bits_dp - 1], upper[:-1] + beside + upper[-1:] + [bits_dp - 1])
    return bits_dp, bits_seq, tuple(tuple(plans[p]) for p in first)


def gather_kernel(orders, bits_dp, bits_seq, *refs):
    count = len(orders)
    shards, fulls = refs[:count], refs[count : 2 * count]
    own_sem, send_sem, recv_sem = refs[2 * count :]
    bits = bits_dp + bits_seq
    mine, partner = place_bits(bits_dp, bits_seq)
    greet(partner, bits)
    local = own_copies(shards, fulls, mine, own_sem)
    for copy in local:
        copy.start()
    for copy in local:
        copy.wait()
    pl.semaphore_wait(pltpu.get_barrier_semaphore(), bits)
    for stage in range(bits):
        copies = stage_copies(stage, orders, fulls, mine, partner, send_sem, recv_sem)
        for copy in copies:
            copy.start()
        for copy in copies:
            copy.wait()


def spread(full):
    return full.reshape((-1,) + full.shape[-1:])


def gather_weights(shards, first):
    bits_dp, bits_seq, orders = gather_plan(first)
    bits = bits_dp + bits_seq
    count = len(shards)
    fulls = pl.pallas_call(
        functools.partial(gather_kernel, orders, bits_dp, bits_seq),
        out_shape=[jax.ShapeDtypeStruct((2,) * bits + s.shape, s.dtype) for s in shards],
        in_specs=[pl.BlockSpec(memory_space=pl.ANY)] * count,
        out_specs=[pl.BlockSpec(memory_space=pl.ANY)] * count,
        scratch_shapes=[
            pltpu.SemaphoreType.DMA((count,)),
            pltpu.SemaphoreType.DMA((bits, count)),
            pltpu.SemaphoreType.DMA((bits, count)),
        ],
        compiler_params=pltpu.CompilerParams(collective_id=0, has_side_effects=True),
        name="gather_weights",
    )(*shards)
    return [spread(f) for f in fulls]


def owner_sums(arrays):
    size_dp, size_seq = lax.axis_size("dp"), lax.axis_size("seq")
    bits_dp, bits_seq = log2(size_dp), log2(size_seq)
    bits = bits_dp + bits_seq
    dp, seq = lax.axis_index("dp"), lax.axis_index("seq")
    arrays = [a.reshape((2,) * bits + (-1,) + a.shape[1:]) for a in arrays]
    left = list(range(bits))
    for bit in [bits_dp - 1] + list(range(bits_dp, bits)) + list(range(bits_dp - 2, -1, -1)):
        axis = left.index(bit)
        left.remove(bit)
        if bit < bits_dp:
            name, size, step, me = "dp", size_dp, 2 ** (bits_dp - 1 - bit), dp
        else:
            name, size, step, me = "seq", size_seq, 2 ** (bits - 1 - bit), seq
        mine = me // step % 2
        pairs = [(i, i ^ step) for i in range(size)]
        sent = [
            lax.dynamic_index_in_dim(a, 1 - mine, axis, keepdims=False).astype(BF) for a in arrays
        ]
        kept = [lax.dynamic_index_in_dim(a, mine, axis, keepdims=False) for a in arrays]
        arrived = [lax.ppermute(v, name, pairs) for v in sent]
        arrays = [k + a.astype(F32) for k, a in zip(kept, arrived)]
    return arrays


class Halving:
    def __init__(self, order, held, landing, send_sem, recv_sem, mine, partner, source=None):
        self.order, self.held, self.landing = order, held, landing
        self.send_sem, self.recv_sem = send_sem, recv_sem
        self.mine, self.partner, self.source = mine, partner, source

    def place(self, stage, value):
        at = []
        for bit in range(len(self.mine)):
            if bit in self.order[:stage]:
                at.append(self.mine[bit])
            elif bit == self.order[stage]:
                at.append(value)
            else:
                at.append(slice(None))
        return at

    def copy(self, stage):
        bit = self.order[stage]
        at = self.place(stage, 1 - self.mine[bit])
        source = self.source if stage == 0 and self.source is not None else self.held
        if source is self.held and self.source is not None:
            at = at[: self.order[0]] + at[self.order[0] + 1 :]
        return pltpu.make_async_remote_copy(
            src_ref=source.at[tuple(at)],
            dst_ref=self.landing[stage],
            send_sem=self.send_sem.at[stage],
            recv_sem=self.recv_sem.at[stage],
            device_id=self.partner(bit),
            device_id_type=MESH,
        )

    def add(self, stage, out=None):
        at = self.place(stage, self.mine[self.order[stage]])
        if self.source is not None:
            at = at[: self.order[0]] + at[self.order[0] + 1 :]
        free = [i for i, a in enumerate(at) if isinstance(a, slice)]
        landing = self.landing[stage]

        def one(flat, carry):
            inner = [lax.rem(flat // 2 ** (len(free) - 1 - i), 2) for i in range(len(free))]
            there = list(at)
            for axis, value in zip(free, inner):
                there[axis] = value
            there = tuple(there)
            value = self.held[there].astype(F32) + landing[tuple(inner)].astype(F32)
            if out is None:
                self.held[there] = value.astype(BF)
            else:
                out[...] = value
            return carry

        if free:
            lax.fori_loop(0, 2 ** len(free), one, 0)
        else:
            one(0, 0)


def landing_shapes(bits, rows, width):
    return [pltpu.VMEM((2,) * (bits - 1 - s) + (rows, width), BF) for s in range(bits)]


def project_kernel(own, tokens, weight, bias, *outs):
    x = tokens[...]
    if own:
        query, pair = outs
    else:
        (pair,) = outs
    for p in range(PAIRS):
        start = 3 * WIDE * p + (0 if own else WIDE)
        end = 3 * WIDE * (p + 1)
        joint = (dot(x, weight[:, start:end]) + bias[:, start:end]).astype(BF)
        if own:
            query[:, p * WIDE : (p + 1) * WIDE] = joint[:, :WIDE]
            joint = joint[:, WIDE:]
        pair[:, 2 * p * WIDE : 2 * (p + 1) * WIDE] = joint


def project(tokens, weight, bias, own):
    count, width = tokens.shape
    block = min(512, count)

    def moving(columns):
        return pl.BlockSpec((block, columns), lambda b: (b, 0))

    def still(*shape):
        return pl.BlockSpec(shape, lambda b: (0, 0), pipeline_mode=pl.Buffered(1))

    wide = [width, 2 * width] if own else [2 * width]
    return pl.pallas_call(
        functools.partial(project_kernel, own),
        grid=(count // block,),
        in_specs=[moving(width), still(width, 3 * width), still(1, 3 * width)],
        out_specs=[moving(w) for w in wide],
        out_shape=[jax.ShapeDtypeStruct((count, w), BF) for w in wide],
        compiler_params=params(40, 1),
        name="project_own" if own else "project_rest",
    )(tokens, weight, bias)


def attend_kernel(parts, groups, steps, blocks, orders, bits_dp, bits_seq, *refs):
    count = len(orders)
    info, query, keys_own, keys_rest, values_own, values_rest = refs[:6]
    shards = refs[6 : 6 + count]
    e_out, mixed, mixed_t, inverse = refs[6 + count : 10 + count]
    fulls = refs[10 + count : 10 + 2 * count]
    k_ext, v_ext, kept, tops, own_sem, send_sem, recv_sem = refs[10 + 2 * count :]
    local = keys_own.shape[1]
    block = query.shape[1]
    step = pl.program_id(0)
    chunk = min(256, local)

    bits = bits_dp + bits_seq
    mine, partner = place_bits(bits_dp, bits_seq)
    stages = [
        stage_copies(stage, orders, fulls, mine, partner, send_sem, recv_sem)
        for stage in range(bits)
    ]

    @pl.when(step == 0)
    def enter():
        greet(partner, bits)
        local_copies = own_copies(shards, fulls, mine, own_sem)
        for copy in local_copies:
            copy.start()
        for copy in local_copies:
            copy.wait()
        pl.semaphore_wait(pltpu.get_barrier_semaphore(), bits)
        for copy in stages[0]:
            copy.start()

    for stage in range(1, bits + 1):
        due = max(stage * steps // (bits + 1), 1) if bits <= steps else min(stage, steps)

        @pl.when(step == due)
        def advance():
            for copy in stages[stage - 1]:
                copy.wait()
            if stage < bits:
                for copy in stages[stage]:
                    copy.start()

    @pl.when(jnp.logical_and(step % blocks == 0, step < steps))
    def prepare_keys():
        for group in range(groups):
            @pl.when(step // (blocks * PAIRS) == group)
            def fill():
                length = info[group]
                for part in range(parts):
                    rows = slice(part * local, (part + 1) * local)
                    k_ext[rows, :WIDE] = keys_own[0] if part == 0 else keys_rest[part - 1, 0]
                    place = lax.broadcasted_iota(jnp.int32, (local, WIDE), 0) + info[groups + part]
                    k_ext[rows, WIDE:] = jnp.where(place < length, 0.0, -1e30).astype(BF)

    @pl.when(step % blocks == 1 % blocks)
    def prepare_values():
        for part in range(parts):
            rows = slice(part * local, (part + 1) * local)
            values = values_own[0] if part == 0 else values_rest[part - 1, 0]
            turned = values.T
            v_ext[0, :HEAD, rows] = turned[:HEAD]
            v_ext[1, :HEAD, rows] = turned[HEAD:]
            v_ext[:, HEAD:, rows] = jnp.ones((2, HEAD, local), BF)

    turned = query[0].T
    zero = jnp.zeros((HEAD, block), BF)
    one = (lax.broadcasted_iota(jnp.int32, (WIDE, block), 0) == 0).astype(F32).astype(BF)
    heads = []
    for head in range(2):
        if head == 0:
            picked = jnp.concatenate([turned[:HEAD], zero, one], axis=0)
        else:
            picked = jnp.concatenate([zero, turned[HEAD:], one], axis=0)
        top = tops[head : head + 1]
        out = None
        largest = None
        for at in range(0, parts * local, chunk):
            rows = slice(at, at + chunk)
            inside = slice(at % local, at % local + chunk)
            e = jnp.exp2((kept[head, rows] - top) * (SCALE * LOG2E)).astype(BF)
            e_out[at // local, 0, head, inside] = e
            add = dot(v_ext[head, :, rows], e)
            out = add if out is None else out + add
            scores = dot(k_ext[rows], picked)
            kept[head, rows] = scores
            most = jnp.max(scores.reshape(chunk // 8, 8, block), axis=0)
            largest = most if largest is None else jnp.maximum(largest, most)
        tops[head : head + 1] = jnp.max(largest, axis=0, keepdims=True)
        inv = 1.0 / out[HEAD : HEAD + 1]
        inverse[0, 0, head : head + 1] = inv
        heads.append(out[:HEAD] * inv)
    both = jnp.concatenate(heads, axis=0).astype(BF)
    mixed_t[0] = both
    mixed[0] = both.T


def attend(info, query, pair_own, pair_rest, shards, first):
    groups, local, width = query.shape
    others = pair_rest.shape[0]
    parts = others + 1
    block = min(512, local)
    blocks = local // block
    steps = groups * PAIRS * blocks
    bits_dp, bits_seq, orders = gather_plan(first)
    bits = bits_dp + bits_seq
    count = len(shards)

    def decode(t, place):
        return place(t // (PAIRS * blocks), t // blocks % PAIRS, t % blocks)

    def now(place):
        return lambda t: decode(jnp.minimum(t, steps - 1), place)

    def before(place):
        return lambda t: decode(jnp.maximum(t - 1, 0), place)

    outs = pl.pallas_call(
        functools.partial(
            attend_kernel, parts, groups, steps, blocks, orders, bits_dp, bits_seq
        ),
        grid=(steps + 1,),
        in_specs=[
            pl.BlockSpec(memory_space=pltpu.SMEM),
            pl.BlockSpec((1, block, WIDE), now(lambda g, p, b: (g, b, p))),
            pl.BlockSpec((1, local, WIDE), now(lambda g, p, b: (g, 0, 2 * p))),
            pl.BlockSpec((others, 1, local, WIDE), now(lambda g, p, b: (0, g, 0, 2 * p))),
            pl.BlockSpec((1, local, WIDE), before(lambda g, p, b: (g, 0, 2 * p + 1))),
            pl.BlockSpec((others, 1, local, WIDE), before(lambda g, p, b: (0, g, 0, 2 * p + 1))),
        ]
        + [pl.BlockSpec(memory_space=pl.ANY)] * count,
        out_specs=[
            pl.BlockSpec((parts, 1, 2, local, block), before(lambda g, p, b: (0, g, p, 0, b))),
            pl.BlockSpec((1, block, WIDE), before(lambda g, p, b: (g, b, p))),
            pl.BlockSpec((1, WIDE, block), before(lambda g, p, b: (g, p, b))),
            pl.BlockSpec((1, 1, 2, block), before(lambda g, p, b: (g, p, 0, b))),
        ]
        + [pl.BlockSpec(memory_space=pl.ANY)] * count,
        out_shape=[
            jax.ShapeDtypeStruct((parts, groups, H, local, local), BF),
            jax.ShapeDtypeStruct((groups, local, width), BF),
            jax.ShapeDtypeStruct((groups, width, local), BF),
            jax.ShapeDtypeStruct((groups, PAIRS, 2, local), F32),
        ]
        + [jax.ShapeDtypeStruct((2,) * bits + s.shape, s.dtype) for s in shards],
        scratch_shapes=[
            pltpu.VMEM((parts * local, 2 * WIDE), BF),
            pltpu.VMEM((2, WIDE, parts * local), BF),
            pltpu.VMEM((2, parts * local, block), F32),
            pltpu.VMEM((8, block), F32),
            pltpu.SemaphoreType.DMA((count,)),
            pltpu.SemaphoreType.DMA((bits, count)),
            pltpu.SemaphoreType.DMA((bits, count)),
        ],
        compiler_params=pltpu.CompilerParams(
            vmem_limit_bytes=56 * MIB,
            dimension_semantics=("arbitrary",),
            collective_id=1,
            has_side_effects=True,
        ),
        name="attend",
    )(info, query, pair_own, pair_rest, pair_own, pair_rest, *shards)
    return outs[:4], [spread(f) for f in outs[4:]]


def middle_kernel(
    packed,
    tokens,
    cotangent,
    mixed,
    out_w,
    up_w,
    down_w,
    rows,
    up_bias,
    result,
    partial,
    mixed_grad,
    upper_sums,
    lower_sums,
    vec_sums,
    out_wg,
    up_wg,
    down_wg,
    row_sums,
    up_bias_sum,
):
    first = pl.program_id(0) == 0

    @pl.when(first)
    def clear():
        out_wg[...] = jnp.zeros_like(out_wg)
        up_wg[...] = jnp.zeros_like(up_wg)
        down_wg[...] = jnp.zeros_like(down_wg)
        row_sums[...] = jnp.zeros_like(row_sums)
        up_bias_sum[...] = jnp.zeros_like(up_bias_sum)

    out_bias, gain_one, shift_one = rows[0:1], rows[1:2], rows[2:3]
    down_bias, gain_two, shift_two = rows[3:4], rows[4:5], rows[5:6]

    def mean(v):
        return jnp.mean(v, axis=-1, keepdims=True)

    def total(v):
        return jnp.sum(v, axis=0, keepdims=True)

    x = tokens[...]
    heads = mixed[...]
    hidden = x + (dot(heads, out_w[...]) + out_bias)
    centred = hidden - mean(hidden)
    r_one = lax.rsqrt(mean(centred * centred) + EPS)
    n_one = centred * r_one
    normal = n_one * gain_one + shift_one
    normal_low = normal.astype(BF)
    inner = dot(normal_low, up_w[...]) + up_bias[...]
    square = inner * inner
    tanh = jnp.tanh(inner * (GELU_A + (GELU_A * GELU_B) * square))
    half = 0.5 + 0.5 * tanh
    active = (inner * half).astype(BF)
    slope = half + (0.5 * inner) * (1.0 - tanh * tanh) * (
        GELU_A + (3.0 * GELU_A * GELU_B) * square
    )
    branch = dot(active, down_w[...]) + down_bias
    last = normal + branch + x
    centred = last - mean(last)
    r_two = lax.rsqrt(mean(centred * centred) + EPS)
    n_two = centred * r_two
    result[...] = n_two * gain_two + shift_two
    grad = cotangent[...]
    e_two = grad * gain_two
    back = r_two * (e_two - mean(e_two) - n_two * mean(e_two * n_two))
    branch_grad = back.astype(BF)
    down_wg[...] += dot(active, branch_grad, "tn")
    inner_grad_wide = slope * dot(branch_grad, down_w[...], "nt")
    inner_grad = inner_grad_wide.astype(BF)
    up_wg[...] += dot(normal_low, inner_grad, "tn")
    up_bias_sum[...] += total(inner_grad.astype(F32))
    norm_grad = back + dot(inner_grad, up_w[...], "nt")
    e_one = norm_grad * gain_one
    hidden_grad = r_one * (e_one - mean(e_one) - n_one * mean(e_one * n_one))
    attn_grad = hidden_grad.astype(BF)
    partial[...] = back + hidden_grad
    out_wg[...] += dot(heads, attn_grad, "tn")
    mixed_grad[...] = dot(attn_grad, out_w[...], "nt").astype(BF)
    row_sums[0:1] += total(attn_grad.astype(F32))
    row_sums[1:2] += total(norm_grad * n_one)
    row_sums[2:3] += total(norm_grad)
    row_sums[3:4] += total(branch_grad.astype(F32))
    row_sums[4:5] += total(grad * n_two)
    row_sums[5:6] += total(grad)

    @pl.when(pl.program_id(0) == pl.num_programs(0) - 1)
    def pack():
        width = tokens.shape[1]
        pieces = up_wg.shape[1] // width
        vec_sums[...] = jnp.zeros_like(vec_sums)
        vec_sums[0:8] = row_sums[...]
        for piece in range(pieces):
            columns = slice(piece * width, (piece + 1) * width)
            vec_sums[8 + piece : 9 + piece] = up_bias_sum[:, columns]
        if not packed:
            upper_sums[:, :width] = out_wg[...]
            upper_sums[:, width:] = up_wg[...]
            lower_sums[...] = down_wg[...]
            return
        owners = upper_sums.shape[0]
        rows_out = out_wg.shape[0] // owners
        rows_down = down_wg.shape[0] // owners

        def one(owner, carry):
            near = pl.ds(pl.multiple_of(owner * rows_out, rows_out), rows_out)
            upper_sums[owner, :rows_out] = out_wg[near].astype(BF)
            for piece in range(pieces):
                columns = slice(piece * width, (piece + 1) * width)
                to = slice((piece + 1) * rows_out, (piece + 2) * rows_out)
                upper_sums[owner, to] = up_wg[near, columns].astype(BF)
            far = pl.ds(pl.multiple_of(owner * rows_down, rows_down), rows_down)
            lower_sums[owner] = down_wg[far].astype(BF)
            return carry

        lax.fori_loop(0, owners, one, 0)


def middle(tokens, cotangent, mixed, out_w, up_w, down_w, rows, up_bias, owners):
    count, width = tokens.shape
    hidden = up_w.shape[1]
    block = min(256, count)
    packed = whole_tiles(width, owners)

    def moving(columns=width):
        return pl.BlockSpec((block, columns), lambda b: (b, 0))

    def still(*shape):
        return pl.BlockSpec(shape, lambda b: (0,) * len(shape), pipeline_mode=pl.Buffered(1))

    rows_upper = width // owners * (1 + hidden // width)
    rows_lower = hidden // owners
    if packed:
        sums = [((owners, rows_upper, width), BF), ((owners, rows_lower, width), BF)]
    else:
        sums = [((width, width + hidden), F32), ((hidden, width), F32)]
    return pl.pallas_call(
        functools.partial(middle_kernel, packed),
        grid=(count // block,),
        in_specs=[
            moving(),
            moving(),
            moving(),
            still(width, width),
            still(width, hidden),
            still(hidden, width),
            still(8, width),
            still(1, hidden),
        ],
        out_specs=[
            moving(),
            moving(),
            moving(),
        ]
        + [still(*shape) for shape, _ in sums]
        + [still(16, width)],
        out_shape=[
            jax.ShapeDtypeStruct((count, width), F32),
            jax.ShapeDtypeStruct((count, width), F32),
            jax.ShapeDtypeStruct((count, width), BF),
        ]
        + [jax.ShapeDtypeStruct(shape, kind) for shape, kind in sums]
        + [jax.ShapeDtypeStruct((16, width), F32)],
        scratch_shapes=[
            pltpu.VMEM((width, width), F32),
            pltpu.VMEM((width, hidden), F32),
            pltpu.VMEM((hidden, width), F32),
            pltpu.VMEM((8, width), F32),
            pltpu.VMEM((1, hidden), F32),
        ],
        compiler_params=params(60, 1),
        name="middle",
    )(tokens, cotangent, mixed, out_w, up_w, down_w, rows, up_bias)


def pull_kernel(parts, groups, orders, bits_dp, bits_seq, packed, *refs):
    bits = bits_dp + bits_seq
    lands = 3 * bits if packed else 0
    (
        e_part,
        query,
        pair_own,
        pair_rest,
        mixed_grad,
        mixed_t,
        inverse,
        tokens_own,
        tokens_rest,
        weight,
        partial,
        *sources,
    ) = refs[: 13 if packed else 11]
    vec_in = refs[13 if packed else 11]
    share_own, joint_out, vec_out = refs[14:17] if packed else refs[12:15]
    (
        d_scores,
        joint_grad,
        total,
        dq_sums,
        dq_turned,
        weight_grad,
        bias_grad,
        shares,
        arrived,
        share_send,
        share_recv,
    ) = refs[19:30] if packed else refs[15:26]
    if packed:
        outs = refs[17:19] + (joint_out,)
        helds = refs[30:33]
        vec_landing, own_sem, send_sem, recv_sem, vec_send, vec_recv = refs[33:39]
        landings = [refs[39 + i * bits : 39 + (i + 1) * bits] for i in range(3)]
    step = pl.program_id(0)
    steps = pl.num_programs(0)
    part = lax.rem(step // (groups * PAIRS) + 1, parts)
    group, pair = lax.rem(step // PAIRS, groups), lax.rem(step, PAIRS)
    own = part == 0

    mine, partner = place_bits(bits_dp, bits_seq)
    dp, seq = lax.axis_index("dp"), lax.axis_index("seq")
    streams, halves = [], []
    if packed:
        streams = [
            Halving(
                orders[i],
                helds[i],
                landings[i],
                send_sem.at[i],
                recv_sem.at[i],
                mine,
                partner,
                sources[i] if i < 2 else None,
            )
            for i in range(3)
        ]
        joint = streams.pop()
        for i, stream in enumerate(streams):
            at = tuple(stream.place(0, mine[orders[i][0]]))
            halves.append(
                pltpu.make_async_copy(stream.source.at[at], stream.held, own_sem.at[i])
            )

    def share_copy(other, g):
        return pltpu.make_async_remote_copy(
            src_ref=shares.at[other - 1, g],
            dst_ref=arrived.at[other - 1, g],
            send_sem=share_send.at[other - 1, g],
            recv_sem=share_recv.at[other - 1, g],
            device_id=(dp, lax.rem(seq + other, parts)),
            device_id_type=MESH,
        )

    @pl.when(step == 0)
    def enter():
        barrier = pltpu.get_barrier_semaphore()
        if packed:
            greet(partner, bits)
        for other in range(1, parts):
            pl.semaphore_signal(
                barrier,
                inc=1,
                device_id=(dp, lax.rem(seq + other, parts)),
                device_id_type=MESH,
            )
        for copy in halves:
            copy.start()
        pl.semaphore_wait(barrier, (bits if packed else 0) + parts - 1)
        for stream in streams:
            stream.copy(0).start()

    for stage in range(bits if packed else 0):
        @pl.when(step == (1, 5, 9, 11, 13, 13, 13, 13)[stage])
        def advance():
            if stage == 0:
                for copy in halves:
                    copy.wait()
            for stream, out in zip(streams, outs):
                stream.copy(stage).wait()
                stream.add(stage, out if stage == bits - 1 else None)
                if stage < bits - 1:
                    stream.copy(stage + 1).start()

    local = query.shape[1]
    chunk = min(256, local)
    turned = mixed_grad[0].astype(F32).T
    mixed = mixed_t[0].astype(F32)
    values = jnp.where(own, pair_own[0, :, WIDE:], pair_rest[0, 0, :, WIDE:])
    keys_t = jnp.where(own, pair_own[0, :, :WIDE], pair_rest[0, 0, :, :WIDE]).T
    query_now = query[0]
    lane = lax.broadcasted_iota(jnp.int32, (local, WIDE), 1)
    zero = jnp.zeros((HEAD, local), BF)
    grad_t, grad, centre, picked = [], [], [], []
    for head in range(2):
        side = slice(head * HEAD, (head + 1) * HEAD)
        inv = inverse[0, 0, head : head + 1]
        centre.append(inv * jnp.sum(turned[side] * mixed[side], axis=0, keepdims=True))
        scaled = (turned[side] * inv).astype(BF)
        grad_t.append(jnp.concatenate([scaled, zero] if head == 0 else [zero, scaled], axis=0))
        grad.append(grad_t[head].T)
        kept = lane < HEAD if head == 0 else lane >= HEAD
        picked.append(jnp.where(kept, query_now, jnp.zeros_like(query_now)))

    def key_grad(rows):
        sums = dot(d_scores[0, rows], picked[0]) + dot(d_scores[1, rows], picked[1])
        joint_grad[rows, WIDE : 2 * WIDE] = (sums * SCALE).astype(BF)

    last = None
    for at in range(0, local, chunk):
        rows = slice(at, at + chunk)
        for head in range(2):
            pulled = dot(values[rows], grad_t[head])
            e = e_part[0, 0, head, rows].astype(F32)
            d_scores[head, rows] = (e * (pulled - centre[head])).astype(BF)
        sums = dot(e_part[0, 0, 0, rows], grad[0]) + dot(e_part[0, 0, 1, rows], grad[1])
        joint_grad[rows, 2 * WIDE :] = sums.astype(BF)
        if last is not None:
            key_grad(last)
        last = rows
    key_grad(last)
    first_part = part == 1 % parts
    for head in range(2):
        side = slice(head * HEAD, (head + 1) * HEAD)
        dq = dot(keys_t, d_scores[head])[side]
        dq_turned[side] = dq

    @pl.when(step == 0)
    def clear():
        weight_grad[...] = jnp.zeros_like(weight_grad)
        bias_grad[...] = jnp.zeros_like(bias_grad)
        dq_sums[...] = jnp.zeros_like(dq_sums)

    @pl.when(pair == 0)
    def start():
        total[...] = jnp.zeros_like(total)

    side = pl.ds(pl.multiple_of(pair * WIDE, WIDE), WIDE)
    start_at = pair * (3 * WIDE)
    wide = pl.ds(pl.multiple_of(start_at, WIDE), 3 * WIDE)
    last_two = pl.ds(pl.multiple_of(start_at + WIDE, WIDE), 2 * WIDE)
    column = group * PAIRS + pair

    @pl.when(own)
    def near():
        dq = (dq_sums[column] + dq_turned[...]) * SCALE
        dq = dq.T.astype(BF)
        joint_grad[:, :WIDE] = dq
        bias_grad[0:1, side] += jnp.sum(dq.astype(F32), axis=0, keepdims=True)
        total[...] += dot(joint_grad[...], weight[:, wide], "nt")
        weight_grad[:, wide] += dot(tokens_own[0], joint_grad[...], "tn")

    @pl.when(jnp.logical_not(own))
    def far():
        dq_sums[column] += dq_turned[...]
        total[...] += dot(joint_grad[:, WIDE:], weight[:, last_two], "nt")
        weight_grad[:, last_two] += dot(tokens_rest[0, 0], joint_grad[:, WIDE:], "tn")

    bias_grad[1:2, side] += jnp.sum(joint_grad[:, 2 * WIDE :].astype(F32), axis=0, keepdims=True)

    for other in range(1, parts):
        for g in range(groups):
            @pl.when(step == ((other - 1) * groups + g + 1) * PAIRS - 1)
            def finish_far():
                shares[other - 1, g] = total[...].astype(BF)
                share_copy(other, g).start()

    for g in range(groups):
        @pl.when(step == ((parts - 1) * groups + g + 1) * PAIRS - 1)
        def finish_near():
            value = total[...] + partial[0]
            for other in range(1, parts):
                share_copy(other, g).wait()
                value += arrived[other - 1, g].astype(F32)
            share_own[0] = value

    @pl.when(step == steps - 1)
    def finish():
        vec_out[...] = vec_in[...]
        vec_out[12:14] = bias_grad[0:2]
        if not packed:
            joint_out[...] = weight_grad[...]
            return
        rows_each = weight_grad.shape[0] // 2**bits
        width = total.shape[1]

        def pack(flat, carry):
            place = tuple(lax.rem(flat // 2 ** (bits - 1 - i), 2) for i in range(bits))
            near = pl.ds(pl.multiple_of(flat * rows_each, rows_each), rows_each)
            for piece in range(3):
                columns = slice(piece * width, (piece + 1) * width)
                to = slice(piece * rows_each, (piece + 1) * rows_each)
                joint.held[place + (to,)] = weight_grad[near, columns].astype(BF)
            return carry

        lax.fori_loop(0, 2**bits, pack, 0)
        for stage in range(bits):
            copy = joint.copy(stage)
            vec_landing[stage, 0] = vec_out[...]
            vec_copy = pltpu.make_async_remote_copy(
                src_ref=vec_landing.at[stage, 0],
                dst_ref=vec_landing.at[stage, 1],
                send_sem=vec_send.at[stage],
                recv_sem=vec_recv.at[stage],
                device_id=partner(orders[2][stage]),
                device_id_type=MESH,
            )
            copy.start()
            vec_copy.start()
            vec_copy.wait()
            vec_out[...] += vec_landing[stage, 1]
            copy.wait()
            joint.add(stage, joint_out if stage == bits - 1 else None)


def pull(
    e_all,
    query,
    pair_own,
    pair_rest,
    mixed_grad,
    mixed_t,
    inverse,
    own,
    rest,
    weight,
    partial,
    upper_sums,
    lower_sums,
    vec_sums,
):
    parts, groups, _, local, _ = e_all.shape
    width = H * HEAD
    each = groups * PAIRS
    bits_dp, bits_seq, orders = gather_plan((0, 1, 1))
    orders = tuple(tuple(reversed(order)) for order in orders)
    bits = bits_dp + bits_seq
    packed = whole_tiles(width, 2**bits)
    split = (2,) * bits
    sums, out_blocks, extra = [], [], []
    if packed:
        rows_upper, rows_lower = upper_sums.shape[1], lower_sums.shape[1]
        rows_joint = 3 * width // 2**bits
        sums = [v.reshape(split + v.shape[1:]) for v in (upper_sums, lower_sums)]
        out_blocks = [(rows_joint, width), (16, width), (rows_upper, width), (rows_lower, width)]
        extra = [
            pltpu.VMEM((2,) * (bits - 1) + (rows_upper, width), BF),
            pltpu.VMEM((2,) * (bits - 1) + (rows_lower, width), BF),
            pltpu.VMEM(split + (rows_joint, width), BF),
            pltpu.VMEM((bits, 2, 16, width), F32),
            pltpu.SemaphoreType.DMA((2,)),
            pltpu.SemaphoreType.DMA((3, bits)),
            pltpu.SemaphoreType.DMA((3, bits)),
            pltpu.SemaphoreType.DMA((bits,)),
            pltpu.SemaphoreType.DMA((bits,)),
        ]
        for count in (rows_upper, rows_lower, rows_joint):
            extra += landing_shapes(bits, count, width)
    else:
        out_blocks = [(width, 3 * width), (16, width)]

    def at(place):
        return lambda t: place((t // each + 1) % parts, t // PAIRS % groups, t % PAIRS)

    def own_at(place):
        return lambda t: place(
            jnp.where(t // each == parts - 1, t // PAIRS % groups, 0),
            jnp.where(t // each == parts - 1, t % PAIRS, 0),
        )

    def rest_at(place):
        def index(t):
            t = jnp.minimum(t, (parts - 1) * each - 1)
            return place(t // each, t // PAIRS % groups, t % PAIRS)

        return index

    def still(*shape):
        return pl.BlockSpec(shape, lambda t: (0,) * len(shape), pipeline_mode=pl.Buffered(1))

    once = pl.Buffered(1)
    return pl.pallas_call(
        functools.partial(pull_kernel, parts, groups, orders, bits_dp, bits_seq, packed),
        grid=(parts * each,),
        in_specs=[
            pl.BlockSpec((1, 1, 2, local, local), at(lambda j, g, p: (j, g, p, 0, 0))),
            pl.BlockSpec((1, local, WIDE), at(lambda j, g, p: (g, 0, p))),
            pl.BlockSpec((1, local, 2 * WIDE), own_at(lambda g, p: (g, 0, p))),
            pl.BlockSpec((1, 1, local, 2 * WIDE), rest_at(lambda j, g, p: (j, g, 0, p))),
            pl.BlockSpec((1, local, WIDE), at(lambda j, g, p: (g, 0, p))),
            pl.BlockSpec((1, WIDE, local), at(lambda j, g, p: (g, p, 0))),
            pl.BlockSpec((1, 1, 2, local), at(lambda j, g, p: (g, p, 0, 0))),
            pl.BlockSpec((1, local, width), own_at(lambda g, p: (g, 0, 0)), pipeline_mode=once),
            pl.BlockSpec(
                (1, 1, local, width), rest_at(lambda j, g, p: (j, g, 0, 0)), pipeline_mode=once
            ),
            still(width, 3 * width),
            pl.BlockSpec((1, local, width), own_at(lambda g, p: (g, 0, 0)), pipeline_mode=once),
        ]
        + [pl.BlockSpec(memory_space=pl.ANY)] * len(sums)
        + [still(16, width)],
        out_specs=[
            pl.BlockSpec((1, local, width), own_at(lambda g, p: (g, 0, 0)), pipeline_mode=once),
        ]
        + [still(*shape) for shape in out_blocks],
        out_shape=[jax.ShapeDtypeStruct((groups, local, width), F32)]
        + [jax.ShapeDtypeStruct(shape, F32) for shape in out_blocks],
        scratch_shapes=[
            pltpu.VMEM((2, local, local), BF),
            pltpu.VMEM((local, 3 * WIDE), BF),
            pltpu.VMEM((local, width), F32),
            pltpu.VMEM((each, WIDE, local), F32),
            pltpu.VMEM((WIDE, local), F32),
            pltpu.VMEM((width, 3 * width), F32),
            pltpu.VMEM((8, width), F32),
            pltpu.VMEM((parts - 1, groups, local, width), BF),
            pltpu.VMEM((parts - 1, groups, local, width), BF),
            pltpu.SemaphoreType.DMA((parts - 1, groups)),
            pltpu.SemaphoreType.DMA((parts - 1, groups)),
        ]
        + extra,
        compiler_params=pltpu.CompilerParams(
            vmem_limit_bytes=63 * MIB,
            dimension_semantics=("arbitrary",),
            collective_id=2,
            has_side_effects=True,
        ),
        name="pull",
    )(
        e_all,
        query,
        pair_own,
        pair_rest,
        mixed_grad,
        mixed_t,
        inverse,
        own,
        rest,
        weight,
        partial,
        *sums,
        vec_sums,
    )


def per_device(
    tokens,
    lengths,
    joint_weight,
    joint_bias,
    out_weight,
    out_bias,
    gain_first,
    shift_first,
    up_weight,
    up_bias,
    down_weight,
    down_bias,
    gain_second,
    shift_second,
    cotangent,
):
    groups, local, width = tokens.shape
    parts = lax.axis_size("seq")
    devices = lax.axis_size("dp") * parts
    me = lax.axis_index("seq")
    rows = groups * local
    tokens_low = tokens.astype(BF)
    tokens_rest = jnp.stack(
        [
            lax.ppermute(tokens_low, "seq", [(i, (i - shift) % parts) for i in range(parts)])
            for shift in range(1, parts)
        ]
    )

    own_rows = joint_weight.shape[0]
    joint_shard = (
        joint_weight.astype(BF)
        .reshape(own_rows, PAIRS, 2, 3, HEAD)
        .transpose(0, 1, 3, 2, 4)
        .reshape(own_rows, 3 * width)
    )
    vectors = [
        joint_bias,
        out_bias,
        gain_first,
        shift_first,
        up_bias,
        down_bias,
        gain_second,
        shift_second,
    ]
    lens = [v.shape[0] for v in vectors]
    packed = jnp.concatenate([v.astype(BF) for v in vectors])
    room = -packed.shape[0] % 128
    packed = jnp.pad(packed, (0, room)).reshape(1, -1)
    packed = jnp.broadcast_to(packed, (16, packed.shape[1]))
    joint_w, packed = gather_weights([joint_shard, packed], (0, 1))
    packed = packed.reshape(devices, 16, -1)[:, 0].astype(F32)
    full, at = [], 0
    for size in lens:
        full.append(packed[:, at : at + size].reshape(devices * size))
        at += size
    pair_full, out_b, gain_1, shift_1, up_b, down_b, gain_2, shift_2 = full
    pair_full = pair_full.reshape(PAIRS, 2, 2, HEAD)
    bias_all = jnp.stack(
        [pair_full[:, :, 0], jnp.zeros((PAIRS, 2, HEAD), F32), pair_full[:, :, 1]], axis=1
    ).reshape(1, 3 * width)
    blank = jnp.zeros(width, F32)
    row_stack = jnp.stack([out_b, gain_1, shift_1, down_b, gain_2, shift_2, blank, blank])

    query, pair_own = project(tokens_low.reshape(rows, width), joint_w, bias_all, True)
    (pair_rest,) = project(tokens_rest.reshape(-1, width), joint_w, bias_all, False)
    query = query.reshape(groups, local, width)
    pair_own = pair_own.reshape(groups, local, 2 * width)
    pair_rest = pair_rest.reshape(parts - 1, groups, local, 2 * width)

    places = (me + jnp.arange(parts, dtype=jnp.int32)) % parts * local
    info = jnp.concatenate([lengths, places.astype(jnp.int32)])
    (e_all, mixed, mixed_t, inverse), (out_w, up_w, down_w) = attend(
        info,
        query,
        pair_own,
        pair_rest,
        [out_weight.astype(BF), up_weight.astype(BF), down_weight.astype(BF)],
        (0, 0, 1),
    )

    result, partial, mixed_grad, upper_sums, lower_sums, vec_sums = middle(
        tokens.reshape(rows, width),
        cotangent.reshape(rows, width),
        mixed.reshape(rows, width),
        out_w,
        up_w,
        down_w,
        row_stack,
        up_b.reshape(1, -1),
        devices,
    )
    mixed_grad = mixed_grad.reshape(groups, local, width)
    input_grad, joint, vec, *owned = pull(
        e_all,
        query,
        pair_own,
        pair_rest,
        mixed_grad,
        mixed_t,
        inverse,
        tokens_low,
        tokens_rest,
        joint_w,
        partial.reshape(groups, local, width),
        upper_sums,
        lower_sums,
        vec_sums,
    )
    pieces = up_weight.shape[1] // width
    if owned:
        upper, lower = owned
        out_sum = upper[:own_rows]
        up_sum = upper[own_rows:].reshape(pieces, own_rows, width).transpose(1, 0, 2)
        up_sum = up_sum.reshape(own_rows, pieces * width)
        joint_sum = joint.reshape(3, own_rows, width).transpose(1, 0, 2)
    else:
        joint_sum, upper, lower = owner_sums([joint, upper_sums, lower_sums])
        out_sum, up_sum = upper[:, :width], upper[:, width:]
        vec = lax.psum(vec, ("dp", "seq"))
    joint_sum = joint_sum.reshape(own_rows, PAIRS, 3, 2, HEAD).transpose(0, 1, 3, 2, 4)
    joint_sum = joint_sum.reshape(own_rows, 3 * width)
    pair_grad = jnp.stack(
        [vec[12].reshape(H, HEAD), vec[13].reshape(H, HEAD)], axis=1
    ).reshape(2 * width)
    device = lax.axis_index("dp") * parts + me
    sums = [
        pair_grad,
        vec[0],
        vec[1],
        vec[2],
        vec[8 : 8 + pieces].reshape(-1),
        vec[3],
        vec[4],
        vec[5],
    ]
    small = [
        lax.dynamic_slice_in_dim(v, device * size, size, 0) for v, size in zip(sums, lens)
    ]
    return (
        result.reshape(groups, local, width),
        input_grad,
        joint_sum,
        small[0],
        out_sum,
        small[1],
        small[2],
        small[3],
        up_sum,
        small[4],
        lower,
        small[5],
        small[6],
        small[7],
    )


def solution(mesh):
    both = ("dp", "seq")
    matrix, vector, whole = P(both, None), P(both), P("dp", "seq", None)
    return jax.shard_map(
        per_device,
        mesh=mesh,
        in_specs=(
            whole,
            P("dp"),
            matrix,
            vector,
            matrix,
            vector,
            vector,
            vector,
            matrix,
            vector,
            matrix,
            vector,
            vector,
            vector,
            whole,
        ),
        out_specs=(
            whole,
            whole,
            matrix,
            vector,
            matrix,
            vector,
            vector,
            vector,
            matrix,
            vector,
            matrix,
            vector,
            vector,
            vector,
        ),
        check_vma=False,
    )
```

```python
import functools
import math

import jax
import jax.numpy as jnp
from jax import lax
from jax.experimental import pallas as pl
from jax.experimental.pallas import tpu as pltpu
from jax.sharding import PartitionSpec as P

H = 8
HEAD = 64
PAIRS = H // 2
WIDE = 2 * HEAD
BF = jnp.bfloat16
F32 = jnp.float32
EPS = 1e-05
SCALE = 1.0 / math.sqrt(HEAD)
LOG2E = math.log2(math.e)
GELU_A = math.sqrt(2.0 / math.pi)
GELU_B = 0.044715
MESH = pl.DeviceIdType.MESH
MIB = 2**20
FORMS = {
    "nn": (((1,), (0,)), ((), ())),
    "nt": (((1,), (1,)), ((), ())),
    "tn": (((0,), (0,)), ((), ())),
}


def dot(left, right, form="nn"):
    return lax.dot_general(left, right, FORMS[form], preferred_element_type=F32)


def whole_tiles(width, devices):
    return width // devices % 16 == 0


def params(limit, steps):
    return pltpu.CompilerParams(
        vmem_limit_bytes=limit * MIB, dimension_semantics=("arbitrary",) * steps
    )


def log2(size):
    return size.bit_length() - 1


class Net:
    def __init__(self, bits_dp, bits_seq):
        self.bits_dp, self.bits_seq = bits_dp, bits_seq
        self.bits = bits_dp + bits_seq
        self.dp, self.seq = lax.axis_index("dp"), lax.axis_index("seq")
        self.mine = [lax.rem(self.dp // 2 ** (bits_dp - 1 - b), 2) for b in range(bits_dp)]
        self.mine += [lax.rem(self.seq // 2 ** (bits_seq - 1 - b), 2) for b in range(bits_seq)]

    def partner(self, flips):
        dp, seq = self.dp, self.seq
        for bit in flips:
            turn = 1 - 2 * self.mine[bit]
            if bit < self.bits_dp:
                dp = dp + turn * 2 ** (self.bits_dp - 1 - bit)
            else:
                seq = seq + turn * 2 ** (self.bits - 1 - bit)
        return (dp, seq)

    def place(self, done, turned=()):
        at = []
        for bit in range(self.bits):
            if bit in done:
                at.append(slice(None))
            else:
                at.append(1 - self.mine[bit] if bit in turned else self.mine[bit])
        return tuple(at)

    def signal(self, device):
        pl.semaphore_signal(
            pltpu.get_barrier_semaphore(), inc=1, device_id=device, device_id_type=MESH
        )

    def greet(self, groups):
        count = 0
        for group in groups:
            for flips in subsets(group):
                self.signal(self.partner(flips))
                count += 1
        return count


def subsets(group):
    return [
        tuple(b for i, b in enumerate(group) if pick >> i & 1)
        for pick in range(1, 2 ** len(group))
    ]


def stages_of(bits_dp, bits_seq):
    bits = bits_dp + bits_seq

    def twos(numbers):
        return [tuple(numbers[i : i + 2]) for i in range(0, len(numbers), 2)]

    beside = twos(list(range(bits_dp, bits)))
    upper = twos(list(range(bits_dp - 2)))
    return beside, upper, [(bits_dp - 2,)], [(bits_dp - 1,)]


def mesh_bits():
    return log2(lax.axis_size("dp")), log2(lax.axis_size("seq"))


class Links:
    def __init__(self, net, send_sem, recv_sem):
        self.net, self.send_sem, self.recv_sem, self.used = net, send_sem, recv_sem, 0

    def copy(self, source, target, device):
        at = self.used
        self.used += 1
        return pltpu.make_async_remote_copy(
            src_ref=source,
            dst_ref=target,
            send_sem=self.send_sem.at[at],
            recv_sem=self.recv_sem.at[at],
            device_id=device,
            device_id_type=MESH,
        )

    def spread(self, full, done, group):
        place = self.net.place(done)
        return [
            self.copy(full.at[place], full.at[place], self.net.partner(flips))
            for flips in subsets(group)
        ]


def start(copies):
    for copy in copies:
        copy.start()


def wait(copies):
    for copy in copies:
        copy.wait()


def flat(groups):
    return tuple(b for group in groups for b in group)


def ring(net, parts, other):
    return (net.dp, lax.rem(net.seq + parts - other, parts))


def owned_row(vector, row, device):
    size, width = vector.shape[1], H * HEAD
    shift = log2(size)
    entry = lax.broadcasted_iota(jnp.int32, (size, width), 0)
    column = lax.broadcasted_iota(jnp.int32, (size, width), 1) + row * width
    here = (column >> shift == device) & (column & (size - 1) == entry)
    return dot(vector.astype(BF), here.astype(F32).astype(BF))


def owned_pair(vector, row, device):
    size, width = vector.shape[1], H * HEAD
    shift = log2(size)
    entry = lax.broadcasted_iota(jnp.int32, (size, width), 0)
    column = lax.broadcasted_iota(jnp.int32, (1, width), 1) + row * width
    pair = column * 0
    for p in range(1, PAIRS):
        pair += (column >= 3 * WIDE * p).astype(jnp.int32)
    inside = column - 3 * WIDE * pair
    kind = inside >> log2(WIDE)
    head = 2 * pair + (inside >> log2(HEAD) & 1)
    index = (2 * head + (kind >> 1)) * HEAD + (inside & (HEAD - 1))
    index = jnp.where(kind == 1, -1, index)
    here = (index >> shift == device) & (index & (size - 1) == entry)
    return dot(vector.astype(BF), here.astype(F32).astype(BF))


def begin_kernel(bits_dp, bits_seq, parts, packed, *refs):
    (
        tokens,
        joint_wide,
        up_wide,
        down_wide,
        out_wide,
        pair_bias,
        out_bias,
        gain_one,
        shift_one,
        up_bias,
        down_bias,
        gain_two,
        shift_two,
        tokens_low,
        tokens_rest,
        joint_out,
        vec,
        up_w,
        down_w,
        out_w,
        query,
        pair_own,
        wide,
        narrow,
        joint_here,
        joint_shard,
        up_shard,
        down_shard,
        out_shard,
        vec_sent,
        vec_landing,
        query_here,
        pair_here,
        own_sem,
        send_sem,
        recv_sem,
    ) = refs
    joint_w = joint_here if packed else joint_out
    net = Net(bits_dp, bits_seq)
    links = Links(net, send_sem, recv_sem)
    beside, upper, next_to, cores = stages_of(bits_dp, bits_seq)
    order = beside + upper + next_to + cores
    groups, local, width = tokens.shape
    due = net.greet(order)
    for other in range(1, parts):
        net.signal(ring(net, parts, other))
        due += 1
    loads = [
        pltpu.make_async_copy(tokens.at[g], wide.at[g], own_sem.at[g]) for g in range(groups)
    ]
    stores = [
        pltpu.make_async_copy(narrow.at[g], tokens_low.at[g], own_sem.at[groups + g])
        for g in range(groups)
    ]
    mine = net.place(())
    placed = [
        pltpu.make_async_copy(shard, full.at[mine], own_sem.at[2 * groups + i])
        for i, (shard, full) in enumerate(
            ((joint_shard, joint_w), (up_shard, up_w), (down_shard, down_w), (out_shard, out_w))
        )
    ]
    start(loads)
    joint = joint_wide[...]
    turned = []
    for head in range(0, H, 2):
        for kind in range(3):
            for at in (head, head + 1):
                turned.append(joint[:, (3 * at + kind) * HEAD : (3 * at + kind + 1) * HEAD])
    joint_shard[...] = jnp.concatenate(turned, axis=1).astype(BF)
    start(placed[:1])
    up_shard[...] = up_wide[...].astype(BF)
    down_shard[...] = down_wide[...].astype(BF)
    out_shard[...] = out_wide[...].astype(BF)
    start(placed[1:])
    device = net.dp * parts + net.seq
    vec[...] = jnp.zeros_like(vec)
    lines = (out_bias, gain_one, shift_one, down_bias, gain_two, shift_two)
    for row, vector in enumerate(lines):
        vec[row : row + 1] = owned_row(vector[...], 0, device)
    for row in range(4):
        vec[6 + row : 7 + row] = owned_row(up_bias[...], row, device)
    for row in range(3):
        vec[10 + row : 11 + row] = owned_pair(pair_bias[...], row, device)
    wait(placed)
    pl.semaphore_wait(pltpu.get_barrier_semaphore(), due)

    def narrowed(g):
        wait(loads[g : g + 1])
        narrow[g] = wide[g].astype(BF)
        start(stores[g : g + 1])

    late = []
    exchange = []
    for stage, group in enumerate(order):
        done = flat(order[:stage])
        joint = links.spread(joint_w, done, group)
        vec_sent[stage] = vec[...]
        small = [
            links.copy(vec_sent.at[stage], vec_landing.at[stage, i], net.partner(flips))
            for i, flips in enumerate(subsets(group))
        ]
        start(joint)
        start(small)
        if stage < len(beside):
            rest = [links.spread(full, done, group) for full in (up_w, down_w, out_w)]
            for copies in rest:
                start(copies)
        if stage == len(beside) - 1:
            narrowed(0)
            exchange = [
                links.copy(narrow.at[0], tokens_rest.at[other - 1, 0], ring(net, parts, other))
                for other in range(1, parts)
            ]
            start(exchange)
        elif stage == len(beside):
            for g in range(1, groups):
                narrowed(g)
        wait(joint)
        wait(small)
        for i in range(len(small)):
            vec[...] += vec_landing[stage, i]
        if stage < len(beside):
            for copies in rest:
                wait(copies)
        elif stage < len(beside) + len(upper):
            wait(late)
            late = links.spread(up_w, done, group)
            start(late)
    wait(late)
    if packed:
        whole = pltpu.make_async_copy(joint_here, joint_out, own_sem.at[4 * groups + 4])
        whole.start()
        weight = joint_w.shape[-1]
        bias = jnp.concatenate([vec[10 + i : 11 + i] for i in range(3)], axis=1)
        block = min(256, local)
        results = []
        for g in range(groups):

            def rows_of(b, carry):
                rows = pl.ds(pl.multiple_of(b * block, block), block)
                full = joint_w[...].reshape(width, weight)
                joint = (dot(narrow[g, rows], full) + bias).astype(BF)
                for p in range(PAIRS):
                    at = 3 * WIDE * p
                    query_here[g, rows, p * WIDE : (p + 1) * WIDE] = joint[:, at : at + WIDE]
                    pair_here[g, rows, 2 * p * WIDE : 2 * (p + 1) * WIDE] = joint[
                        :, at + WIDE : at + 3 * WIDE
                    ]
                return carry

            lax.fori_loop(0, local // block, rows_of, 0)
            results.append(
                pltpu.make_async_copy(query_here.at[g], query.at[g], own_sem.at[2 * groups + 4 + g])
            )
            results.append(
                pltpu.make_async_copy(
                    pair_here.at[g], pair_own.at[g], own_sem.at[3 * groups + 4 + g]
                )
            )
            start(results[-2:])
        wait(results)
        whole.wait()
    wait(exchange)
    wait(stores)


def begin(tokens, joint, up, down, out, vectors, parts):
    bits_dp, bits_seq = mesh_bits()
    bits = bits_dp + bits_seq
    groups, local, width = tokens.shape
    packed = joint.shape[0] % 16 == 0
    beside, upper, next_to, cores = stages_of(bits_dp, bits_seq)
    order = beside + upper + next_to + cores
    sends = sum(2 ** len(group) - 1 for group in order)
    copies = 2 * sends + 4 * sends + parts
    split = (2,) * bits
    hbm = pl.BlockSpec(memory_space=pl.ANY)
    vmem = pl.BlockSpec(memory_space=pltpu.VMEM)
    return pl.pallas_call(
        functools.partial(begin_kernel, bits_dp, bits_seq, parts, packed),
        in_specs=[hbm] + [vmem] * (4 + len(vectors)),
        out_specs=[hbm, hbm, hbm, vmem] + [hbm] * 5,
        out_shape=[
            jax.ShapeDtypeStruct((groups, local, width), BF),
            jax.ShapeDtypeStruct((parts - 1, groups, local, width), BF),
            jax.ShapeDtypeStruct(split + joint.shape, BF),
            jax.ShapeDtypeStruct((16, width), F32),
            jax.ShapeDtypeStruct(split + up.shape, BF),
            jax.ShapeDtypeStruct(split + down.shape, BF),
            jax.ShapeDtypeStruct(split + out.shape, BF),
            jax.ShapeDtypeStruct((groups, local, width), BF),
            jax.ShapeDtypeStruct((groups, local, 2 * width), BF),
        ],
        scratch_shapes=[
            pltpu.VMEM((groups, local, width), F32),
            pltpu.VMEM((groups, local, width), BF),
            pltpu.VMEM(split + joint.shape if packed else (16, 128), BF),
            pltpu.VMEM(joint.shape, BF),
            pltpu.VMEM(up.shape, BF),
            pltpu.VMEM(down.shape, BF),
            pltpu.VMEM(out.shape, BF),
            pltpu.VMEM((len(order), 16, width), F32),
            pltpu.VMEM((len(order), 3, 16, width), F32),
            pltpu.VMEM((groups, local, width), BF),
            pltpu.VMEM((groups, local, 2 * width), BF),
            pltpu.SemaphoreType.DMA((4 * groups + 5,)),
            pltpu.SemaphoreType.DMA((copies,)),
            pltpu.SemaphoreType.DMA((copies,)),
        ],
        compiler_params=pltpu.CompilerParams(
            vmem_limit_bytes=62 * MIB, collective_id=0, has_side_effects=True
        ),
        name="begin",
    )(tokens, joint, up, down, out, *vectors)


def matrix_of(full):
    return full.reshape((-1,) + full.shape[-1:])


def owner_sums(arrays):
    size_dp, size_seq = lax.axis_size("dp"), lax.axis_size("seq")
    bits_dp, bits_seq = log2(size_dp), log2(size_seq)
    bits = bits_dp + bits_seq
    dp, seq = lax.axis_index("dp"), lax.axis_index("seq")
    arrays = [a.reshape((2,) * bits + (-1,) + a.shape[1:]) for a in arrays]
    left = list(range(bits))
    for bit in [bits_dp - 1] + list(range(bits_dp, bits)) + list(range(bits_dp - 2, -1, -1)):
        axis = left.index(bit)
        left.remove(bit)
        if bit < bits_dp:
            name, size, step, me = "dp", size_dp, 2 ** (bits_dp - 1 - bit), dp
        else:
            name, size, step, me = "seq", size_seq, 2 ** (bits - 1 - bit), seq
        mine = me // step % 2
        pairs = [(i, i ^ step) for i in range(size)]
        sent = [
            lax.dynamic_index_in_dim(a, 1 - mine, axis, keepdims=False).astype(BF) for a in arrays
        ]
        kept = [lax.dynamic_index_in_dim(a, mine, axis, keepdims=False) for a in arrays]
        arrived = [lax.ppermute(v, name, pairs) for v in sent]
        arrays = [k + a.astype(F32) for k, a in zip(kept, arrived)]
    return arrays


class Halving:
    def __init__(self, net, links, groups, held, landing, source=None):
        self.net, self.groups, self.held, self.landing = net, groups, held, landing
        self.gone = groups[0] if source is not None else ()
        self.rounds = []
        for stage, group in enumerate(groups):
            copies = []
            for i, flips in enumerate(subsets(group)):
                at = self.place(stage, flips)
                part = source.at[at] if stage == 0 and source is not None else held.at[self.cut(at)]
                copies.append(links.copy(part, landing[stage].at[i], net.partner(flips)))
            self.rounds.append(copies)

    def place(self, stage, turned):
        done, group = flat(self.groups[:stage]), self.groups[stage]
        at = []
        for bit, mine in enumerate(self.net.mine):
            if bit in done or bit in group:
                at.append(1 - mine if bit in turned else mine)
            else:
                at.append(slice(None))
        return tuple(at)

    def cut(self, at):
        return tuple(a for bit, a in enumerate(at) if bit not in self.gone)

    def start(self, stage):
        start(self.rounds[stage])

    def add(self, stage, out=None):
        wait(self.rounds[stage])
        at = self.cut(self.place(stage, ()))
        free = [i for i, a in enumerate(at) if isinstance(a, slice)]
        landing = self.landing[stage]

        def one(flat_index, carry):
            inner = [lax.rem(flat_index // 2 ** (len(free) - 1 - i), 2) for i in range(len(free))]
            there = list(at)
            for axis, value in zip(free, inner):
                there[axis] = value
            there = tuple(there)
            value = self.held[there].astype(F32)
            for i in range(landing.shape[0]):
                value += landing[(i,) + tuple(inner)].astype(F32)
            if out is None:
                self.held[there] = value.astype(BF)
            else:
                out[...] = value
            return carry

        if free:
            lax.fori_loop(0, 2 ** len(free), one, 0)
        else:
            one(0, 0)


class Everywhere:
    def __init__(self, net, links, groups, value, sent, landing):
        self.value, self.sent, self.landing = value, sent, landing
        self.rounds = [
            [
                links.copy(sent.at[stage], landing.at[stage, i], net.partner(flips))
                for i, flips in enumerate(subsets(group))
            ]
            for stage, group in enumerate(groups)
        ]

    def start(self, stage):
        self.sent[stage] = self.value[...]
        start(self.rounds[stage])

    def add(self, stage, out=None):
        wait(self.rounds[stage])
        for i in range(len(self.rounds[stage])):
            self.value[...] += self.landing[stage, i]


def landing_shapes(groups, bits, rows, width):
    shapes, left = [], bits
    for group in groups:
        left -= len(group)
        shapes.append(pltpu.VMEM((2 ** len(group) - 1,) + (2,) * left + (rows, width), BF))
    return shapes


def sum_orders(bits_dp, bits_seq):
    beside, upper, next_to, cores = stages_of(bits_dp, bits_seq)
    far = upper[::-1]
    if len(beside) == 1 and len(beside[0]) == 1:
        near = [beside[0] + next_to[0]]
    else:
        near = beside + next_to
    return cores + beside + next_to + far, cores + next_to + beside + far, cores + near + far


def project_kernel(tokens, weight, bias, query, pair):
    x = tokens[...]
    for p in range(PAIRS):
        columns = slice(3 * WIDE * p, 3 * WIDE * (p + 1))
        joint = (dot(x, weight[:, columns]) + bias[:, columns]).astype(BF)
        query[:, p * WIDE : (p + 1) * WIDE] = joint[:, :WIDE]
        pair[:, 2 * p * WIDE : 2 * (p + 1) * WIDE] = joint[:, WIDE:]


def project(tokens, weight, bias):
    count, width = tokens.shape
    block = min(512, count)

    def moving(columns):
        return pl.BlockSpec((block, columns), lambda b: (b, 0))

    def still(*shape):
        return pl.BlockSpec(shape, lambda b: (0, 0), pipeline_mode=pl.Buffered(1))

    return pl.pallas_call(
        project_kernel,
        grid=(count // block,),
        in_specs=[moving(width), still(width, 3 * width), still(1, 3 * width)],
        out_specs=[moving(width), moving(2 * width)],
        out_shape=[
            jax.ShapeDtypeStruct((count, width), BF),
            jax.ShapeDtypeStruct((count, 2 * width), BF),
        ],
        compiler_params=params(40, 1),
        name="project",
    )(tokens, weight, bias)


def attend_kernel(parts, groups, steps, blocks, bits_dp, bits_seq, *refs):
    (
        lengths,
        query,
        keys_own,
        values_own,
        weight,
        vec,
        tokens_low,
        _,
        _,
        _,
        _,
        e_out,
        mixed,
        mixed_t,
        inverse,
        pair_rest,
        tokens_rest,
        up_w,
        down_w,
        out_w,
        k_ext,
        v_ext,
        kept,
        tops,
        rest_here,
        pair_here,
        own_sem,
        send_sem,
        recv_sem,
    ) = refs
    local = keys_own.shape[1]
    block = query.shape[1]
    step = pl.program_id(0)
    chunk = min(256, local)

    net = Net(bits_dp, bits_seq)
    links = Links(net, send_sem, recv_sem)
    beside, upper, next_to, cores = stages_of(bits_dp, bits_seq)
    order = beside + upper + next_to + cores
    first, last = len(beside), len(order)
    lead = len(upper)
    rounds = []
    for stage in range(first, last):
        copies = []
        for full in (down_w, out_w):
            copies += links.spread(full, flat(order[:stage]), order[stage])
        ahead = stage + lead
        if ahead < last:
            copies += links.spread(up_w, flat(order[:ahead]), order[ahead])
        rounds.append(copies)
    times = [0, 7, 12, 14, 15, 16]
    if len(rounds) > 3:
        times = [i * steps // (len(rounds) + 1) for i in range(len(rounds) + 1)]
    else:
        times = [0, steps * 7 // 16, steps * 12 // 16, steps * 14 // 16]
    exchange = [
        [
            links.copy(
                tokens_low.at[g], tokens_rest.at[other - 1, g], ring(net, parts, other)
            )
            for other in range(1, parts)
        ]
        for g in range(1, groups)
    ]

    @pl.when(step == 0)
    def enter():
        due = net.greet(order[first:])
        for other in range(1, parts):
            net.signal(ring(net, parts, other))
            due += 1
        pl.semaphore_wait(pltpu.get_barrier_semaphore(), due)
        for copies in exchange:
            start(copies)
        start(rounds[0])

    for i in range(len(rounds)):
        @pl.when(step == times[i + 1])
        def advance():
            wait(rounds[i])
            if i + 1 < len(rounds):
                start(rounds[i + 1])

    @pl.when(step % blocks == 1 % blocks)
    def prepare_values():
        for part in range(parts):
            rows = slice(part * local, (part + 1) * local)
            values = values_own[0] if part == 0 else pair_here[part - 1, :, WIDE:]
            turned = values.T
            v_ext[0, :HEAD, rows] = turned[:HEAD]
            v_ext[1, :HEAD, rows] = turned[HEAD:]
            v_ext[:, HEAD:, rows] = jnp.ones((2, HEAD, local), BF)

    for group in range(groups):
        @pl.when(step == group * blocks * PAIRS)
        def fetch():
            if group > 0:
                wait(exchange[group - 1])
            copy = pltpu.make_async_copy(tokens_rest.at[:, group], rest_here, own_sem.at[group])
            copy.start()
            copy.wait()

    @pl.when(jnp.logical_and(step % blocks == 0, step < steps))
    def prepare_keys():
        pair = lax.rem(step // blocks, PAIRS)
        columns = pl.ds(pl.multiple_of(pair * (3 * WIDE) + WIDE, WIDE), 2 * WIDE)
        bias = jnp.zeros((1, 2 * WIDE), F32)
        flat_bias = jnp.concatenate([vec[10 + i : 11 + i] for i in range(3)], axis=1)
        for p in range(PAIRS):
            at = 3 * WIDE * p + WIDE
            bias = jnp.where(pair == p, flat_bias[:, at : at + 2 * WIDE], bias)
        for part in range(1, parts):
            both = (dot(rest_here[part - 1], weight[:, columns]) + bias).astype(BF)
            pair_here[part - 1] = both
            pair_rest[part - 1, 0] = both
        for group in range(groups):
            @pl.when(step // (blocks * PAIRS) == group)
            def fill():
                length = lengths[group]
                for part in range(parts):
                    rows = slice(part * local, (part + 1) * local)
                    k_ext[rows, :WIDE] = keys_own[0] if part == 0 else pair_here[part - 1, :, :WIDE]
                    first_key = lax.rem(net.seq + part, parts) * local
                    place = lax.broadcasted_iota(jnp.int32, (local, WIDE), 0) + first_key
                    k_ext[rows, WIDE:] = jnp.where(place < length, 0.0, -1e30).astype(BF)

    turned = query[0].T
    zero = jnp.zeros((HEAD, block), BF)
    one = (lax.broadcasted_iota(jnp.int32, (WIDE, block), 0) == 0).astype(F32).astype(BF)
    heads = []
    for head in range(2):
        if head == 0:
            picked = jnp.concatenate([turned[:HEAD], zero, one], axis=0)
        else:
            picked = jnp.concatenate([zero, turned[HEAD:], one], axis=0)
        top = tops[head : head + 1]
        out = None
        largest = None
        for at in range(0, parts * local, chunk):
            rows = slice(at, at + chunk)
            inside = slice(at % local, at % local + chunk)
            e = jnp.exp2((kept[head, rows] - top) * (SCALE * LOG2E)).astype(BF)
            e_out[at // local, 0, head, inside] = e
            add = dot(v_ext[head, :, rows], e)
            out = add if out is None else out + add
            scores = dot(k_ext[rows], picked)
            kept[head, rows] = scores
            most = jnp.max(scores.reshape(chunk // 8, 8, block), axis=0)
            largest = most if largest is None else jnp.maximum(largest, most)
        tops[head : head + 1] = jnp.max(largest, axis=0, keepdims=True)
        inv = 1.0 / out[HEAD : HEAD + 1]
        inverse[0, 0, head : head + 1] = inv
        heads.append(out[:HEAD] * inv)
    both = jnp.concatenate(heads, axis=0).astype(BF)
    mixed_t[0] = both
    mixed[0] = both.T


def attend(lengths, query, pair_own, weight, vec, tokens_low, tokens_rest, up_w, down_w, out_w):
    groups, local, width = query.shape
    others = tokens_rest.shape[0]
    parts = others + 1
    block = min(512, local)
    blocks = local // block
    steps = groups * PAIRS * blocks
    bits_dp, bits_seq = mesh_bits()
    beside, upper, next_to, cores = stages_of(bits_dp, bits_seq)
    sends = sum(2 ** len(group) - 1 for group in upper + next_to + cores)
    copies = 3 * sends + groups * others

    def decode(t, place):
        return place(t // (PAIRS * blocks), t // blocks % PAIRS, t % blocks)

    def now(place):
        return lambda t: decode(jnp.minimum(t, steps - 1), place)

    def before(place):
        return lambda t: decode(jnp.maximum(t - 1, 0), place)

    def still(*shape):
        return pl.BlockSpec(shape, lambda t: (0,) * len(shape), pipeline_mode=pl.Buffered(1))

    hbm = pl.BlockSpec(memory_space=pl.ANY)
    passed = (tokens_rest, up_w, down_w, out_w)
    return pl.pallas_call(
        functools.partial(attend_kernel, parts, groups, steps, blocks, bits_dp, bits_seq),
        grid=(steps + 1,),
        in_specs=[
            pl.BlockSpec(memory_space=pltpu.SMEM),
            pl.BlockSpec((1, block, WIDE), now(lambda g, p, b: (g, b, p))),
            pl.BlockSpec((1, local, WIDE), now(lambda g, p, b: (g, 0, 2 * p))),
            pl.BlockSpec((1, local, WIDE), before(lambda g, p, b: (g, 0, 2 * p + 1))),
            still(width, 3 * width),
            still(*vec.shape),
        ]
        + [hbm] * 5,
        out_specs=[
            pl.BlockSpec((parts, 1, 2, local, block), before(lambda g, p, b: (0, g, p, 0, b))),
            pl.BlockSpec((1, block, WIDE), before(lambda g, p, b: (g, b, p))),
            pl.BlockSpec((1, WIDE, block), before(lambda g, p, b: (g, p, b))),
            pl.BlockSpec((1, 1, 2, block), before(lambda g, p, b: (g, p, 0, b))),
            pl.BlockSpec((others, 1, local, 2 * WIDE), now(lambda g, p, b: (0, g, 0, p))),
        ]
        + [hbm] * 4,
        out_shape=[
            jax.ShapeDtypeStruct((parts, groups, H, local, local), BF),
            jax.ShapeDtypeStruct((groups, local, width), BF),
            jax.ShapeDtypeStruct((groups, width, local), BF),
            jax.ShapeDtypeStruct((groups, PAIRS, 2, local), F32),
            jax.ShapeDtypeStruct((others, groups, local, 2 * width), BF),
        ]
        + [jax.ShapeDtypeStruct(v.shape, v.dtype) for v in passed],
        input_output_aliases={7: 5, 8: 6, 9: 7, 10: 8},
        scratch_shapes=[
            pltpu.VMEM((parts * local, 2 * WIDE), BF),
            pltpu.VMEM((2, WIDE, parts * local), BF),
            pltpu.VMEM((2, parts * local, block), F32),
            pltpu.VMEM((8, block), F32),
            pltpu.VMEM((others, local, width), BF),
            pltpu.VMEM((others, local, 2 * WIDE), BF),
            pltpu.SemaphoreType.DMA((groups,)),
            pltpu.SemaphoreType.DMA((copies,)),
            pltpu.SemaphoreType.DMA((copies,)),
        ],
        compiler_params=pltpu.CompilerParams(
            vmem_limit_bytes=62 * MIB,
            dimension_semantics=("arbitrary",),
            collective_id=1,
            has_side_effects=True,
        ),
        name="attend",
    )(lengths, query, pair_own, pair_own, weight, vec, tokens_low, *passed)


def middle_kernel(
    packed,
    tokens,
    cotangent,
    mixed,
    out_w,
    up_w,
    down_w,
    rows,
    result,
    partial,
    mixed_grad,
    upper_sums,
    lower_sums,
    vec_sums,
    out_wg,
    up_wg,
    down_wg,
    row_sums,
    up_bias_sum,
):
    first = pl.program_id(0) == 0

    @pl.when(first)
    def clear():
        out_wg[...] = jnp.zeros_like(out_wg)
        up_wg[...] = jnp.zeros_like(up_wg)
        down_wg[...] = jnp.zeros_like(down_wg)
        row_sums[...] = jnp.zeros_like(row_sums)
        up_bias_sum[...] = jnp.zeros_like(up_bias_sum)

    pieces = up_w.shape[1] // tokens.shape[1]
    up_bias = jnp.concatenate([rows[6 + i : 7 + i] for i in range(pieces)], axis=1)
    out_bias, gain_one, shift_one = rows[0:1], rows[1:2], rows[2:3]
    down_bias, gain_two, shift_two = rows[3:4], rows[4:5], rows[5:6]

    def mean(v):
        return jnp.mean(v, axis=-1, keepdims=True)

    def total(v):
        return jnp.sum(v, axis=0, keepdims=True)

    x = tokens[...]
    heads = mixed[...]
    hidden = x + (dot(heads, out_w[...]) + out_bias)
    centred = hidden - mean(hidden)
    r_one = lax.rsqrt(mean(centred * centred) + EPS)
    n_one = centred * r_one
    normal = n_one * gain_one + shift_one
    normal_low = normal.astype(BF)
    inner = dot(normal_low, up_w[...]) + up_bias
    square = inner * inner
    tanh = jnp.tanh(inner * (GELU_A + (GELU_A * GELU_B) * square))
    half = 0.5 + 0.5 * tanh
    active = (inner * half).astype(BF)
    slope = half + (0.5 * inner) * (1.0 - tanh * tanh) * (
        GELU_A + (3.0 * GELU_A * GELU_B) * square
    )
    branch = dot(active, down_w[...]) + down_bias
    last = normal + branch + x
    centred = last - mean(last)
    r_two = lax.rsqrt(mean(centred * centred) + EPS)
    n_two = centred * r_two
    result[...] = n_two * gain_two + shift_two
    grad = cotangent[...]
    e_two = grad * gain_two
    back = r_two * (e_two - mean(e_two) - n_two * mean(e_two * n_two))
    branch_grad = back.astype(BF)
    down_wg[...] += dot(active, branch_grad, "tn")
    inner_grad_wide = slope * dot(branch_grad, down_w[...], "nt")
    inner_grad = inner_grad_wide.astype(BF)
    up_wg[...] += dot(normal_low, inner_grad, "tn")
    up_bias_sum[...] += total(inner_grad.astype(F32))
    norm_grad = back + dot(inner_grad, up_w[...], "nt")
    e_one = norm_grad * gain_one
    hidden_grad = r_one * (e_one - mean(e_one) - n_one * mean(e_one * n_one))
    attn_grad = hidden_grad.astype(BF)
    partial[...] = back + hidden_grad
    out_wg[...] += dot(heads, attn_grad, "tn")
    mixed_grad[...] = dot(attn_grad, out_w[...], "nt").astype(BF)
    row_sums[0:1] += total(attn_grad.astype(F32))
    row_sums[1:2] += total(norm_grad * n_one)
    row_sums[2:3] += total(norm_grad)
    row_sums[3:4] += total(branch_grad.astype(F32))
    row_sums[4:5] += total(grad * n_two)
    row_sums[5:6] += total(grad)

    @pl.when(pl.program_id(0) == pl.num_programs(0) - 1)
    def pack():
        width = tokens.shape[1]
        pieces = up_wg.shape[1] // width
        vec_sums[...] = jnp.zeros_like(vec_sums)
        vec_sums[0:8] = row_sums[...]
        for piece in range(pieces):
            columns = slice(piece * width, (piece + 1) * width)
            vec_sums[8 + piece : 9 + piece] = up_bias_sum[:, columns]
        if not packed:
            upper_sums[:, :width] = out_wg[...]
            upper_sums[:, width:] = up_wg[...]
            lower_sums[...] = down_wg[...]
            return
        owners = upper_sums.shape[0]
        rows_out = out_wg.shape[0] // owners
        rows_down = down_wg.shape[0] // owners

        def one(owner, carry):
            near = pl.ds(pl.multiple_of(owner * rows_out, rows_out), rows_out)
            upper_sums[owner, :rows_out] = out_wg[near].astype(BF)
            for piece in range(pieces):
                columns = slice(piece * width, (piece + 1) * width)
                to = slice((piece + 1) * rows_out, (piece + 2) * rows_out)
                upper_sums[owner, to] = up_wg[near, columns].astype(BF)
            far = pl.ds(pl.multiple_of(owner * rows_down, rows_down), rows_down)
            lower_sums[owner] = down_wg[far].astype(BF)
            return carry

        lax.fori_loop(0, owners, one, 0)


def middle(tokens, cotangent, mixed, out_w, up_w, down_w, rows, owners):
    count, width = tokens.shape
    hidden = up_w.shape[1]
    block = min(256, count)
    packed = whole_tiles(width, owners)

    def moving(columns=width):
        return pl.BlockSpec((block, columns), lambda b: (b, 0))

    def still(*shape):
        return pl.BlockSpec(shape, lambda b: (0,) * len(shape), pipeline_mode=pl.Buffered(1))

    rows_upper = width // owners * (1 + hidden // width)
    rows_lower = hidden // owners
    if packed:
        sums = [((owners, rows_upper, width), BF), ((owners, rows_lower, width), BF)]
    else:
        sums = [((width, width + hidden), F32), ((hidden, width), F32)]
    return pl.pallas_call(
        functools.partial(middle_kernel, packed),
        grid=(count // block,),
        in_specs=[
            moving(),
            moving(),
            moving(),
            still(width, width),
            still(width, hidden),
            still(hidden, width),
            still(16, width),
        ],
        out_specs=[
            moving(),
            moving(),
            moving(),
        ]
        + [still(*shape) for shape, _ in sums]
        + [still(16, width)],
        out_shape=[
            jax.ShapeDtypeStruct((count, width), F32),
            jax.ShapeDtypeStruct((count, width), F32),
            jax.ShapeDtypeStruct((count, width), BF),
        ]
        + [jax.ShapeDtypeStruct(shape, kind) for shape, kind in sums]
        + [jax.ShapeDtypeStruct((16, width), F32)],
        scratch_shapes=[
            pltpu.VMEM((width, width), F32),
            pltpu.VMEM((width, hidden), F32),
            pltpu.VMEM((hidden, width), F32),
            pltpu.VMEM((8, width), F32),
            pltpu.VMEM((1, hidden), F32),
        ],
        compiler_params=params(62, 1),
        name="middle",
    )(tokens, cotangent, mixed, out_w, up_w, down_w, rows)


def pull_kernel(parts, groups, bits_dp, bits_seq, packed, *refs):
    taken = 0

    def take(count):
        nonlocal taken
        taken += count
        return refs[taken - count : taken]

    e_part, query, pair_own, pair_rest, mixed_grad, mixed_t, inverse = take(7)
    tokens_own, tokens_rest, weight, partial = take(4)
    sources = take(2) if packed else ()
    (vec_in,) = take(1)
    share_own, arrived, joint_out, vec_out = take(4)
    owned = take(2) if packed else ()
    d_scores, joint_grad, total, dq_sums, dq_turned, weight_grad, bias_grad, shares = take(8)
    share_send, share_recv, own_sem = take(3)
    step = pl.program_id(0)
    steps = pl.num_programs(0)
    each = groups * PAIRS
    part = lax.rem(step // each + 1, parts)
    own = part == 0
    inside = lax.rem(step, each)
    group = jnp.where(own, lax.rem(inside, groups), inside // PAIRS)
    pair = jnp.where(own, inside // groups, lax.rem(inside, PAIRS))

    net = Net(bits_dp, bits_seq)
    bits = net.bits
    orders = sum_orders(bits_dp, bits_seq)
    streams, loads = [], []
    if packed:
        upper_held, lower_held, early_held, late_held = take(4)
        vec_sent, vec_landing, bias_sent, bias_landing = take(4)
        send_sem, recv_sem = take(2)
        links = Links(net, send_sem, recv_sem)
        upper, lower = streams = [
            Halving(net, links, orders[i], held, take(len(orders[i])), sources[i])
            for i, held in enumerate((upper_held, lower_held))
        ]
        early, late = [
            Halving(net, links, orders[2], held, take(len(orders[2])))
            for held in (early_held, late_held)
        ]
        early_vec = Everywhere(net, links, orders[2], vec_out.at[0:16], vec_sent, vec_landing)
        late_vec = Everywhere(net, links, orders[2], bias_grad, bias_sent, bias_landing)
        for i, stream in enumerate(streams):
            at = stream.place(0, ())
            loads.append(pltpu.make_async_copy(sources[i].at[at], stream.held, own_sem.at[i]))
    stores = [
        pltpu.make_async_copy(total.at[g], share_own.at[g], own_sem.at[2 + g])
        for g in range(groups)
    ]

    def share_copy(other, g):
        return pltpu.make_async_remote_copy(
            src_ref=shares.at[other - 1, g],
            dst_ref=arrived.at[other - 1, g],
            send_sem=share_send.at[other - 1, g],
            recv_sem=share_recv.at[other - 1, g],
            device_id=(net.dp, lax.rem(net.seq + other, parts)),
            device_id_type=MESH,
        )

    @pl.when(step == 0)
    def enter():
        due = parts - 1
        for other in range(1, parts):
            net.signal((net.dp, lax.rem(net.seq + other, parts)))
        if packed:
            due += net.greet(orders[0]) + net.greet(orders[2])
        start(loads)
        pl.semaphore_wait(pltpu.get_barrier_semaphore(), due)
        for stream in streams:
            stream.start(0)

    def advance(streams, stage, outs, count):
        for stream, out in zip(streams, outs):
            stream.add(stage, out if stage == count - 1 else None)
            if stage < count - 1:
                stream.start(stage + 1)

    def pack(held, first, columns):
        rows_each = weight_grad.shape[0] // 2**bits

        def one(flat_index, carry):
            place = tuple(lax.rem(flat_index // 2 ** (bits - 1 - i), 2) for i in range(bits))
            near = pl.ds(pl.multiple_of(flat_index * rows_each, rows_each), rows_each)
            held[place] = weight_grad[near, first : first + columns].astype(BF)
            return carry

        lax.fori_loop(0, 2**bits, one, 0)

    split_at = 3 * WIDE * (PAIRS - 1)
    if packed:
        for stage, when in enumerate((1, 5, 9, 12)):
            @pl.when(step == when)
            def ffn():
                if stage == 0:
                    wait(loads)
                advance(streams, stage, owned, len(orders[0]))

        joint_early = joint_out.at[:, :split_at]

        @pl.when(step == steps - groups)
        def joint_first():
            pack(early.held, 0, split_at)
            vec_out[...] = vec_in[...]
            for stream in (early, early_vec):
                stream.start(0)

        @pl.when(step == steps - 1)
        def joint_second():
            advance((early, early_vec), 0, (joint_early, None), len(orders[2]))

    local = query.shape[1]
    chunk = min(256, local)
    turned = mixed_grad[0].astype(F32).T
    mixed = mixed_t[0].astype(F32)
    values = jnp.where(own, pair_own[0, :, WIDE:], pair_rest[0, 0, :, WIDE:])
    keys_t = jnp.where(own, pair_own[0, :, :WIDE], pair_rest[0, 0, :, :WIDE]).T
    query_now = query[0]
    lane = lax.broadcasted_iota(jnp.int32, (local, WIDE), 1)
    zero = jnp.zeros((HEAD, local), BF)
    grad_t, grad, centre, picked = [], [], [], []
    for head in range(2):
        side = slice(head * HEAD, (head + 1) * HEAD)
        inv = inverse[0, 0, head : head + 1]
        centre.append(inv * jnp.sum(turned[side] * mixed[side], axis=0, keepdims=True))
        scaled = (turned[side] * inv).astype(BF)
        grad_t.append(jnp.concatenate([scaled, zero] if head == 0 else [zero, scaled], axis=0))
        grad.append(grad_t[head].T)
        kept = lane < HEAD if head == 0 else lane >= HEAD
        picked.append(jnp.where(kept, query_now, jnp.zeros_like(query_now)))

    def key_grad(rows):
        sums = dot(d_scores[0, rows], picked[0]) + dot(d_scores[1, rows], picked[1])
        joint_grad[rows, WIDE : 2 * WIDE] = (sums * SCALE).astype(BF)

    last = None
    for at in range(0, local, chunk):
        rows = slice(at, at + chunk)
        for head in range(2):
            pulled = dot(values[rows], grad_t[head])
            e = e_part[0, 0, head, rows].astype(F32)
            d_scores[head, rows] = (e * (pulled - centre[head])).astype(BF)
        sums = dot(e_part[0, 0, 0, rows], grad[0]) + dot(e_part[0, 0, 1, rows], grad[1])
        joint_grad[rows, 2 * WIDE :] = sums.astype(BF)
        if last is not None:
            key_grad(last)
        last = rows
    key_grad(last)
    first_part = part == 1 % parts
    for head in range(2):
        side = slice(head * HEAD, (head + 1) * HEAD)
        dq = dot(keys_t, d_scores[head])[side]
        dq_turned[side] = dq

    @pl.when(step == 0)
    def clear():
        weight_grad[...] = jnp.zeros_like(weight_grad)
        bias_grad[...] = jnp.zeros_like(bias_grad)
        dq_sums[...] = jnp.zeros_like(dq_sums)

    @pl.when(jnp.logical_and(pair == 0, own))
    def start_near():
        total[group] = partial[0]

    @pl.when(jnp.logical_and(pair == 0, jnp.logical_not(own)))
    def start_far():
        total[group] = jnp.zeros(total.shape[1:], F32)

    side = pl.ds(pl.multiple_of(pair * WIDE, WIDE), WIDE)
    start_at = pair * (3 * WIDE)
    wide = pl.ds(pl.multiple_of(start_at, WIDE), 3 * WIDE)
    last_two = pl.ds(pl.multiple_of(start_at + WIDE, WIDE), 2 * WIDE)
    column = group * PAIRS + pair

    @pl.when(own)
    def near():
        dq = (dq_sums[column] + dq_turned[...]) * SCALE
        dq = dq.T.astype(BF)
        joint_grad[:, :WIDE] = dq
        bias_grad[0:1, side] += jnp.sum(dq.astype(F32), axis=0, keepdims=True)
        total[group] += dot(joint_grad[...], weight[:, wide], "nt")
        weight_grad[:, wide] += dot(tokens_own[group], joint_grad[...], "tn")

    @pl.when(jnp.logical_not(own))
    def far():
        dq_sums[column] += dq_turned[...]
        total[group] += dot(joint_grad[:, WIDE:], weight[:, last_two], "nt")
        weight_grad[:, last_two] += dot(tokens_rest[0, 0], joint_grad[:, WIDE:], "tn")

    bias_grad[1:2, side] += jnp.sum(joint_grad[:, 2 * WIDE :].astype(F32), axis=0, keepdims=True)

    for other in range(1, parts):
        for g in range(groups):
            @pl.when(step == ((other - 1) * groups + g + 1) * PAIRS - 1)
            def finish_far():
                shares[other - 1, g] = total[g].astype(BF)
                share_copy(other, g).start()

    for g in range(groups):
        @pl.when(step == steps - groups + g)
        def finish_near():
            start(stores[g : g + 1])

    @pl.when(step == steps - 1)
    def finish():
        if packed:
            last = len(orders[2])
            pack(late.held, split_at, 3 * WIDE)
            pairs = ((early, early_vec), (late, late_vec))
            outs = (joint_early, None), (joint_out.at[:, split_at:], None)
            for stream in pairs[1]:
                stream.start(0)
            for stage in range(last):
                if stage + 1 < last:
                    advance(pairs[0], stage + 1, outs[0], last)
                advance(pairs[1], stage, outs[1], last)
        else:
            vec_out[...] = vec_in[...]
            joint_out[...] = weight_grad[...]
        vec_out[12:14] = bias_grad[0:2]
        for g in range(groups):
            for other in range(1, parts):
                share_copy(other, g).wait()
        wait(stores)


def pull(
    e_all,
    query,
    pair_own,
    pair_rest,
    mixed_grad,
    mixed_t,
    inverse,
    own,
    rest,
    weight,
    partial,
    upper_sums,
    lower_sums,
    vec_sums,
):
    parts, groups, _, local, _ = e_all.shape
    width = H * HEAD
    each = groups * PAIRS
    bits_dp, bits_seq = mesh_bits()
    bits = bits_dp + bits_seq
    orders = sum_orders(bits_dp, bits_seq)
    packed = whole_tiles(width, 2**bits)
    split = (2,) * bits
    sums, out_blocks, extra = [], [], []
    if packed:
        rows_upper, rows_lower = upper_sums.shape[1], lower_sums.shape[1]
        rows_joint = width // 2**bits
        sums = [v.reshape(split + v.shape[1:]) for v in (upper_sums, lower_sums)]
        out_blocks = [(rows_joint, 3 * width), (16, width), (rows_upper, width), (rows_lower, width)]
        early = 3 * WIDE * (PAIRS - 1)
        late = 3 * WIDE
        last = len(orders[2])
        sends = sum(2 ** len(g) - 1 for order in orders for g in order)
        sends += 3 * sum(2 ** len(g) - 1 for g in orders[2])
        extra = [
            pltpu.VMEM((2,) * (bits - 1) + (rows_upper, width), BF),
            pltpu.VMEM((2,) * (bits - 1) + (rows_lower, width), BF),
            pltpu.VMEM(split + (rows_joint, early), BF),
            pltpu.VMEM(split + (rows_joint, late), BF),
            pltpu.VMEM((last, 16, width), F32),
            pltpu.VMEM((last, 3, 16, width), F32),
            pltpu.VMEM((last, 8, width), F32),
            pltpu.VMEM((last, 3, 8, width), F32),
            pltpu.SemaphoreType.DMA((sends,)),
            pltpu.SemaphoreType.DMA((sends,)),
        ]
        extra += landing_shapes(orders[0], bits, rows_upper, width)
        extra += landing_shapes(orders[1], bits, rows_lower, width)
        extra += landing_shapes(orders[2], bits, rows_joint, early)
        extra += landing_shapes(orders[2], bits, rows_joint, late)
    else:
        out_blocks = [(width, 3 * width), (16, width)]

    def decode(t):
        part, inside = (t // each + 1) % parts, t % each
        own = part == 0
        group = jnp.where(own, inside % groups, inside // PAIRS)
        pair = jnp.where(own, inside // groups, inside % PAIRS)
        return part, group, pair

    def at(place):
        return lambda t: place(*decode(t))

    def own_at(place):
        def index(t):
            part, group, pair = decode(t)
            return place(jnp.where(part == 0, group, 0), jnp.where(part == 0, pair, 0))

        return index

    def once_at(t):
        return jnp.clip(t - (parts - 1) * each, 0, groups - 1), 0, 0

    def rest_at(place):
        def index(t):
            t = jnp.minimum(t, (parts - 1) * each - 1)
            return place(t // each, t // PAIRS % groups, t % PAIRS)

        return index

    def still(*shape):
        return pl.BlockSpec(shape, lambda t: (0,) * len(shape), pipeline_mode=pl.Buffered(1))

    once = pl.Buffered(1)
    return pl.pallas_call(
        functools.partial(pull_kernel, parts, groups, bits_dp, bits_seq, packed),
        grid=(parts * each,),
        in_specs=[
            pl.BlockSpec((1, 1, 2, local, local), at(lambda j, g, p: (j, g, p, 0, 0))),
            pl.BlockSpec((1, local, WIDE), at(lambda j, g, p: (g, 0, p))),
            pl.BlockSpec((1, local, 2 * WIDE), own_at(lambda g, p: (g, 0, p))),
            pl.BlockSpec((1, 1, local, 2 * WIDE), rest_at(lambda j, g, p: (j, g, 0, p))),
            pl.BlockSpec((1, local, WIDE), at(lambda j, g, p: (g, 0, p))),
            pl.BlockSpec((1, WIDE, local), at(lambda j, g, p: (g, p, 0))),
            pl.BlockSpec((1, 1, 2, local), at(lambda j, g, p: (g, p, 0, 0))),
            still(groups, local, width),
            pl.BlockSpec(
                (1, 1, local, width), rest_at(lambda j, g, p: (j, g, 0, 0)), pipeline_mode=once
            ),
            still(width, 3 * width),
            pl.BlockSpec((1, local, width), once_at, pipeline_mode=once),
        ]
        + [pl.BlockSpec(memory_space=pl.ANY)] * len(sums)
        + [still(16, width)],
        out_specs=[
            pl.BlockSpec(memory_space=pl.ANY),
            pl.BlockSpec(memory_space=pl.ANY),
        ]
        + [still(*shape) for shape in out_blocks],
        out_shape=[
            jax.ShapeDtypeStruct((groups, local, width), F32),
            jax.ShapeDtypeStruct((parts - 1, groups, local, width), BF),
        ]
        + [jax.ShapeDtypeStruct(shape, F32) for shape in out_blocks],
        scratch_shapes=[
            pltpu.VMEM((2, local, local), BF),
            pltpu.VMEM((local, 3 * WIDE), BF),
            pltpu.VMEM((groups, local, width), F32),
            pltpu.VMEM((each, WIDE, local), F32),
            pltpu.VMEM((WIDE, local), F32),
            pltpu.VMEM((width, 3 * width), F32),
            pltpu.VMEM((8, width), F32),
            pltpu.VMEM((parts - 1, groups, local, width), BF),
            pltpu.SemaphoreType.DMA((parts - 1, groups)),
            pltpu.SemaphoreType.DMA((parts - 1, groups)),
            pltpu.SemaphoreType.DMA((2 + groups,)),
        ]
        + extra,
        compiler_params=pltpu.CompilerParams(
            vmem_limit_bytes=63 * MIB,
            dimension_semantics=("arbitrary",),
            collective_id=2,
            has_side_effects=True,
        ),
        name="pull",
    )(
        e_all,
        query,
        pair_own,
        pair_rest,
        mixed_grad,
        mixed_t,
        inverse,
        own,
        rest,
        weight,
        partial,
        *sums,
        vec_sums,
    )


def finish_kernel(bits_dp, bits_seq, share, arrived, joint, vec, upper, lower, *outs):
    (
        input_grad,
        joint_sum,
        pair_sum,
        out_sum,
        out_bias,
        gain_one,
        shift_one,
        up_sum,
        up_bias,
        down_sum,
        down_bias,
        gain_two,
        shift_two,
    ) = outs
    value = share[...]
    for other in range(arrived.shape[0]):
        value += arrived[other].astype(F32)
    input_grad[...] = value

    @pl.when(pl.program_id(0) == 0)
    def small():
        net = Net(bits_dp, bits_seq)
        device = net.dp * 2**bits_seq + net.seq
        rows, width = out_sum.shape
        summed = joint[...]
        turned = []
        for head in range(H):
            for kind in range(3):
                at = ((head // 2 * 3 + kind) * 2 + head % 2) * HEAD
                turned.append(summed[:, at : at + HEAD])
        joint_sum[...] = jnp.concatenate(turned, axis=1)
        out_sum[...] = upper[:rows]
        for piece in range(up_sum.shape[1] // width):
            up_sum[:, piece * width : (piece + 1) * width] = upper[
                (piece + 1) * rows : (piece + 2) * rows
            ]
        down_sum[...] = lower[...]
        lines = vec[...]
        which = lax.broadcasted_iota(jnp.int32, lines.shape, 0)

        def entries(out, row, column):
            line = jnp.sum(jnp.where(which == row, lines, 0.0), axis=0, keepdims=True)
            line = jnp.broadcast_to(line, (8, width))
            out[...] = pltpu.roll(line, lax.rem(width - column, width), 1)[:1, : out.shape[1]]

        plain = (out_bias, gain_one, shift_one, down_bias, gain_two, shift_two)
        for row, out in enumerate(plain):
            entries(out, row, device * out.shape[1])
        first = device * up_bias.shape[1]
        entries(up_bias, 8 + first // width, lax.rem(first, width))
        first = device * pair_sum.shape[1]
        kind = lax.rem(first // HEAD, 2)
        entries(pair_sum, 12 + kind, first // WIDE * HEAD + lax.rem(first, HEAD))


def finish(share, arrived, joint, vec, upper, lower, shards):
    groups, local, width = share.shape
    block = min(512, local)
    each = local // block

    def moving(*lead):
        return pl.BlockSpec(
            (1,) * len(lead) + (block, width), lambda b: (b // each, b % each, 0)
        )

    def still(shape):
        return pl.BlockSpec(shape, lambda b: (0,) * len(shape), pipeline_mode=pl.Buffered(1))

    bits_dp, bits_seq = mesh_bits()
    others = arrived.shape[0]
    small = (joint, vec, upper, lower)
    outs = pl.pallas_call(
        functools.partial(finish_kernel, bits_dp, bits_seq),
        grid=(groups * each,),
        in_specs=[
            moving(1),
            pl.BlockSpec((others, 1, block, width), lambda b: (0, b // each, b % each, 0)),
        ]
        + [still(v.shape) for v in small],
        out_specs=[moving(1)] + [still(shape) for shape in shards],
        out_shape=[jax.ShapeDtypeStruct(share.shape, F32)]
        + [jax.ShapeDtypeStruct(shape, F32) for shape in shards],
        compiler_params=params(62, 1),
        name="finish",
    )(share, arrived, *small)
    return [outs[0]] + [
        v.reshape(v.shape[1:]) if v.shape[0] == 1 else v for v in outs[1:]
    ]


def per_device(
    tokens,
    lengths,
    joint_weight,
    joint_bias,
    out_weight,
    out_bias,
    gain_first,
    shift_first,
    up_weight,
    up_bias,
    down_weight,
    down_bias,
    gain_second,
    shift_second,
    cotangent,
):
    groups, local, width = tokens.shape
    parts = lax.axis_size("seq")
    devices = lax.axis_size("dp") * parts
    me = lax.axis_index("seq")
    rows = groups * local
    own_rows = joint_weight.shape[0]
    vectors = [
        joint_bias,
        out_bias,
        gain_first,
        shift_first,
        up_bias,
        down_bias,
        gain_second,
        shift_second,
    ]
    lens = [v.shape[0] for v in vectors]
    tokens_low, tokens_rest, joint_w, vec, up_w, down_w, out_w, query, pair_own = begin(
        tokens,
        joint_weight,
        up_weight,
        down_weight,
        out_weight,
        [v.reshape(1, -1) for v in vectors],
        parts,
    )
    joint_w = matrix_of(joint_w)
    pieces = up_weight.shape[1] // width
    if not whole_tiles(width, devices):
        query, pair_own = project(
            tokens_low.reshape(rows, width), joint_w, vec[10:13].reshape(1, -1)
        )
        query = query.reshape(groups, local, width)
        pair_own = pair_own.reshape(groups, local, 2 * width)

    e_all, mixed, mixed_t, inverse, pair_rest, tokens_rest, up_w, down_w, out_w = attend(
        lengths, query, pair_own, joint_w, vec, tokens_low, tokens_rest, up_w, down_w, out_w
    )
    out_w, up_w, down_w = matrix_of(out_w), matrix_of(up_w), matrix_of(down_w)

    result, partial, mixed_grad, upper_sums, lower_sums, vec_sums = middle(
        tokens.reshape(rows, width),
        cotangent.reshape(rows, width),
        mixed.reshape(rows, width),
        out_w,
        up_w,
        down_w,
        vec,
        devices,
    )
    mixed_grad = mixed_grad.reshape(groups, local, width)
    share, arrived, joint, vec, *owned = pull(
        e_all,
        query,
        pair_own,
        pair_rest,
        mixed_grad,
        mixed_t,
        inverse,
        tokens_low,
        tokens_rest,
        joint_w,
        partial.reshape(groups, local, width),
        upper_sums,
        lower_sums,
        vec_sums,
    )
    if owned:
        upper, lower = owned
        shards = [
            (1, v.shape[0]) if v.ndim == 1 else v.shape
            for v in (
                joint_weight,
                joint_bias,
                out_weight,
                out_bias,
                gain_first,
                shift_first,
                up_weight,
                up_bias,
                down_weight,
                down_bias,
                gain_second,
                shift_second,
            )
        ]
        outs = finish(share, arrived, joint, vec, upper, lower, shards)
        return (result.reshape(groups, local, width), *outs)
    input_grad = share + jnp.sum(arrived.astype(F32), axis=0)
    joint_sum, upper, lower = owner_sums([joint, upper_sums, lower_sums])
    out_sum, up_sum = upper[:, :width], upper[:, width:]
    vec = lax.psum(vec, ("dp", "seq"))
    device = lax.axis_index("dp") * parts + me
    joint_sum = joint_sum.reshape(own_rows, PAIRS, 3, 2, HEAD).transpose(0, 1, 3, 2, 4)
    joint_sum = joint_sum.reshape(own_rows, 3 * width)
    pair_grad = jnp.stack(
        [vec[12].reshape(H, HEAD), vec[13].reshape(H, HEAD)], axis=1
    ).reshape(2 * width)
    sums = [
        pair_grad,
        vec[0],
        vec[1],
        vec[2],
        vec[8 : 8 + pieces].reshape(-1),
        vec[3],
        vec[4],
        vec[5],
    ]
    small = [
        lax.dynamic_slice_in_dim(v, device * size, size, 0) for v, size in zip(sums, lens)
    ]
    return (
        result.reshape(groups, local, width),
        input_grad,
        joint_sum,
        small[0],
        out_sum,
        small[1],
        small[2],
        small[3],
        up_sum,
        small[4],
        lower,
        small[5],
        small[6],
        small[7],
    )


def solution(mesh):
    both = ("dp", "seq")
    matrix, vector, whole = P(both, None), P(both), P("dp", "seq", None)
    return jax.shard_map(
        per_device,
        mesh=mesh,
        in_specs=(
            whole,
            P("dp"),
            matrix,
            vector,
            matrix,
            vector,
            vector,
            vector,
            matrix,
            vector,
            matrix,
            vector,
            vector,
            vector,
            whole,
        ),
        out_specs=(
            whole,
            whole,
            matrix,
            vector,
            matrix,
            vector,
            vector,
            vector,
            matrix,
            vector,
            matrix,
            vector,
            vector,
            vector,
        ),
        check_vma=False,
    )
```

```python
import functools
import math

import jax
import jax.numpy as jnp
from jax import lax
from jax.experimental import pallas as pl
from jax.experimental.pallas import tpu as pltpu
from jax.sharding import PartitionSpec as P

H = 8
HEAD = 64
PAIRS = H // 2
WIDE = 2 * HEAD
JOINT_PARTS = ((0, 2), (2, 1), (3, 1))
AHEAD = 16
BF = jnp.bfloat16
F32 = jnp.float32
EPS = 1e-05
SCALE = 1.0 / math.sqrt(HEAD)
LOG2E = math.log2(math.e)
GELU_A = math.sqrt(2.0 / math.pi)
GELU_B = 0.044715
MESH = pl.DeviceIdType.MESH
MIB = 2**20
FORMS = {
    "nn": (((1,), (0,)), ((), ())),
    "nt": (((1,), (1,)), ((), ())),
    "tn": (((0,), (0,)), ((), ())),
}


def dot(left, right, form="nn"):
    return lax.dot_general(left, right, FORMS[form], preferred_element_type=F32)


def whole_tiles(width, devices):
    return width // devices % 16 == 0


def params(limit, steps):
    return pltpu.CompilerParams(
        vmem_limit_bytes=limit * MIB, dimension_semantics=("arbitrary",) * steps
    )


def log2(size):
    return size.bit_length() - 1


class Net:
    def __init__(self, bits_dp, bits_seq):
        self.bits_dp, self.bits_seq = bits_dp, bits_seq
        self.bits = bits_dp + bits_seq
        self.dp, self.seq = lax.axis_index("dp"), lax.axis_index("seq")
        self.mine = [lax.rem(self.dp // 2 ** (bits_dp - 1 - b), 2) for b in range(bits_dp)]
        self.mine += [lax.rem(self.seq // 2 ** (bits_seq - 1 - b), 2) for b in range(bits_seq)]

    def partner(self, flips):
        dp, seq = self.dp, self.seq
        for bit in flips:
            turn = 1 - 2 * self.mine[bit]
            if bit < self.bits_dp:
                dp = dp + turn * 2 ** (self.bits_dp - 1 - bit)
            else:
                seq = seq + turn * 2 ** (self.bits - 1 - bit)
        return (dp, seq)

    def place(self, done, turned=()):
        at = []
        for bit in range(self.bits):
            if bit in done:
                at.append(slice(None))
            else:
                at.append(1 - self.mine[bit] if bit in turned else self.mine[bit])
        return tuple(at)

    def signal(self, device):
        pl.semaphore_signal(
            pltpu.get_barrier_semaphore(), inc=1, device_id=device, device_id_type=MESH
        )

    def greet(self, groups):
        count = 0
        for group in groups:
            for flips in subsets(group):
                self.signal(self.partner(flips))
                count += 1
        return count


def subsets(group):
    return [
        tuple(b for i, b in enumerate(group) if pick >> i & 1)
        for pick in range(1, 2 ** len(group))
    ]


def stages_of(bits_dp, bits_seq):
    bits = bits_dp + bits_seq

    def twos(numbers):
        return [tuple(numbers[i : i + 2]) for i in range(0, len(numbers), 2)]

    beside = twos(list(range(bits_dp, bits)))
    upper = twos(list(range(bits_dp - 2)))
    return beside, upper, [(bits_dp - 2,)], [(bits_dp - 1,)]


def mesh_bits():
    return log2(lax.axis_size("dp")), log2(lax.axis_size("seq"))


class Links:
    def __init__(self, net, send_sem, recv_sem):
        self.net, self.send_sem, self.recv_sem, self.used = net, send_sem, recv_sem, 0

    def copy(self, source, target, device):
        at = self.used
        self.used += 1
        return pltpu.make_async_remote_copy(
            src_ref=source,
            dst_ref=target,
            send_sem=self.send_sem.at[at],
            recv_sem=self.recv_sem.at[at],
            device_id=device,
            device_id_type=MESH,
        )

    def spread(self, full, done, group, columns=slice(None), shard=None):
        place = self.net.place(done) + (slice(None), columns)
        source = full.at[place] if shard is None else shard.at[:, columns]
        return [
            self.copy(source, full.at[place], self.net.partner(flips))
            for flips in subsets(group)
        ]


def start(copies):
    for copy in copies:
        copy.start()


def wait(copies):
    for copy in copies:
        copy.wait()


def flat(groups):
    return tuple(b for group in groups for b in group)


def ring(net, parts, other):
    return (net.dp, lax.rem(net.seq + parts - other, parts))


def owned_row(vector, row, device):
    size, width = vector.shape[1], H * HEAD
    shift = log2(size)
    entry = lax.broadcasted_iota(jnp.int32, (size, width), 0)
    column = lax.broadcasted_iota(jnp.int32, (size, width), 1) + row * width
    here = (column >> shift == device) & (column & (size - 1) == entry)
    return dot(vector.astype(BF), here.astype(F32).astype(BF))


def owned_pair(vector, row, device):
    size, width = vector.shape[1], H * HEAD
    shift = log2(size)
    entry = lax.broadcasted_iota(jnp.int32, (size, width), 0)
    column = lax.broadcasted_iota(jnp.int32, (1, width), 1)
    if row > 0:
        column += (row - 1) * width
        head = 2 * (column >> log2(2 * WIDE)) + (column >> log2(HEAD) & 1)
        index = (2 * head + 1) * HEAD + (column & (HEAD - 1))
        index = jnp.where(column & WIDE == 0, -1, index)
    else:
        index = 2 * (column >> log2(HEAD)) * HEAD + (column & (HEAD - 1))
    here = (index >> shift == device) & (index & (size - 1) == entry)
    return dot(vector.astype(BF), here.astype(F32).astype(BF))


def joint_columns():
    blocks = [3 * head for head in range(H)]
    for pair in range(PAIRS):
        blocks += [3 * head + kind for kind in (1, 2) for head in (2 * pair, 2 * pair + 1)]
    return blocks


def begin_kernel(bits_dp, bits_seq, parts, packed, *refs):
    (
        tokens,
        joint_wide,
        up_wide,
        down_wide,
        out_wide,
        pair_bias,
        out_bias,
        gain_one,
        shift_one,
        up_bias,
        down_bias,
        gain_two,
        shift_two,
        tokens_low,
        tokens_rest,
        joint_out,
        vec,
        up_w,
        down_w,
        out_w,
        query,
        pair_own,
        wide,
        narrow,
        joint_here,
        joint_shard,
        up_shard,
        down_shard,
        out_shard,
        vec_sent,
        vec_landing,
        query_here,
        pair_here,
        own_sem,
        send_sem,
        recv_sem,
    ) = refs
    joint_w = joint_here if packed else joint_out
    net = Net(bits_dp, bits_seq)
    links = Links(net, send_sem, recv_sem)
    beside, upper, next_to, cores = stages_of(bits_dp, bits_seq)
    order = beside + upper + next_to + cores
    groups, local, width = tokens.shape
    due = net.greet(order)
    for other in range(1, parts):
        net.signal(ring(net, parts, other))
        due += 1
    loads = [
        pltpu.make_async_copy(tokens.at[g], wide.at[g], own_sem.at[g]) for g in range(groups)
    ]
    stores = [
        pltpu.make_async_copy(narrow.at[g], tokens_low.at[g], own_sem.at[groups + g])
        for g in range(groups)
    ]
    mine = net.place(())
    placed = [
        pltpu.make_async_copy(shard, full.at[mine], own_sem.at[2 * groups + i])
        for i, (shard, full) in enumerate(
            ((joint_shard, joint_w), (up_shard, up_w), (down_shard, down_w), (out_shard, out_w))
        )
    ]
    start(loads)
    joint = joint_wide[...]
    turned = [joint[:, b * HEAD : (b + 1) * HEAD] for b in joint_columns()]
    joint_shard[...] = jnp.concatenate(turned, axis=1).astype(BF)
    start(placed[:1])
    pl.semaphore_wait(pltpu.get_barrier_semaphore(), due)

    def prepare():
        up_shard[...] = up_wide[...].astype(BF)
        down_shard[...] = down_wide[...].astype(BF)
        out_shard[...] = out_wide[...].astype(BF)
        start(placed[1:])
        device = net.dp * parts + net.seq
        vec[...] = jnp.zeros_like(vec)
        lines = (out_bias, gain_one, shift_one, down_bias, gain_two, shift_two)
        for row, vector in enumerate(lines):
            vec[row : row + 1] = owned_row(vector[...], 0, device)
        for row in range(4):
            vec[6 + row : 7 + row] = owned_row(up_bias[...], row, device)
        for row in range(3):
            vec[10 + row : 11 + row] = owned_pair(pair_bias[...], row, device)
        wait(placed)

    def narrowed(g):
        wait(loads[g : g + 1])
        narrow[g] = wide[g].astype(BF)
        start(stores[g : g + 1])

    cut = width + 2 * WIDE
    columns = (slice(0, cut), slice(cut, 3 * width))
    dones = [flat(order[:stage]) for stage in range(len(order))]
    ahead, behind = [
        [
            links.spread(joint_w, done, group, c, None if done else joint_shard)
            for done, group in zip(dones, order)
        ]
        for c in columns
    ]
    small = [
        [
            links.copy(vec_sent.at[stage], vec_landing.at[stage, i], net.partner(flips))
            for i, flips in enumerate(subsets(group))
        ]
        for stage, group in enumerate(order)
    ]

    def small_start(stage):
        vec_sent[stage] = vec[...]
        start(small[stage])

    def small_add(stage):
        wait(small[stage])
        for i in range(len(small[stage])):
            vec[...] += vec_landing[stage, i]

    exchange = [
        links.copy(narrow.at[0], tokens_rest.at[other - 1, 0], ring(net, parts, other))
        for other in range(1, parts)
    ]
    some = slice(0, local // AHEAD)
    exchange_next = [
        links.copy(narrow.at[1, some], tokens_rest.at[other - 1, 1, some], ring(net, parts, other))
        for other in range(1, parts)
    ]

    def projected(part):
        bias = jnp.concatenate([vec[10 + i : 11 + i] for i in range(3)], axis=1)[:, columns[part]]
        block = min(256, local)
        for g in range(groups):

            def rows_of(b, carry):
                rows = pl.ds(pl.multiple_of(b * block, block), block)
                full = joint_w[..., columns[part]].reshape(width, -1)
                joint = (dot(narrow[g, rows], full) + bias).astype(BF)
                if part == 0:
                    query_here[g, rows] = joint[:, :width]
                    pair_here[g, rows, : cut - width] = joint[:, width:]
                else:
                    pair_here[g, rows, cut - width :] = joint
                return carry

            lax.fori_loop(0, local // block, rows_of, 0)

    late, rest = [], []
    last = len(order) - 1
    start(ahead[0])
    start(behind[0])
    prepare()
    small_start(0)
    for stage in range(last):
        done, group = dones[stage], order[stage]
        if stage < len(beside):
            rest = [links.spread(full, done, group) for full in (up_w, down_w, out_w)]
            for copies in rest:
                start(copies)
        if stage == len(beside) - 1:
            narrowed(0)
            start(exchange)
        elif stage == len(beside):
            for g in range(1, groups):
                narrowed(g)
            start(exchange_next)
        wait(ahead[stage])
        small_add(stage)
        start(ahead[stage + 1])
        small_start(stage + 1)
        if stage + 1 < last:
            wait(behind[stage])
            start(behind[stage + 1])
        for copies in rest:
            wait(copies)
        rest = []
        if len(beside) <= stage < len(beside) + len(upper):
            wait(late)
            late = links.spread(up_w, done, group)
            start(late)
    wait(ahead[last])
    small_add(last)
    if packed:
        projected(0)
    wait(behind[last - 1])
    start(behind[last])
    wait(behind[last])
    if packed:
        results = [
            pltpu.make_async_copy(joint_here, joint_out, own_sem.at[4 * groups + 4]),
            pltpu.make_async_copy(query_here, query, own_sem.at[4 * groups + 5]),
        ]
        start(results)
        projected(1)
        results.append(pltpu.make_async_copy(pair_here, pair_own, own_sem.at[4 * groups + 6]))
        start(results[2:])
        wait(results)
    wait(late)
    wait(exchange)
    wait(exchange_next)
    wait(stores)


def begin(tokens, joint, up, down, out, vectors, parts):
    bits_dp, bits_seq = mesh_bits()
    bits = bits_dp + bits_seq
    groups, local, width = tokens.shape
    packed = joint.shape[0] % 16 == 0
    beside, upper, next_to, cores = stages_of(bits_dp, bits_seq)
    order = beside + upper + next_to + cores
    sends = sum(2 ** len(group) - 1 for group in order)
    copies = 3 * sends + 4 * sends + 2 * parts
    split = (2,) * bits
    hbm = pl.BlockSpec(memory_space=pl.ANY)
    vmem = pl.BlockSpec(memory_space=pltpu.VMEM)
    return pl.pallas_call(
        functools.partial(begin_kernel, bits_dp, bits_seq, parts, packed),
        in_specs=[hbm] + [vmem] * (4 + len(vectors)),
        out_specs=[hbm, hbm, hbm, vmem] + [hbm] * 5,
        out_shape=[
            jax.ShapeDtypeStruct((groups, local, width), BF),
            jax.ShapeDtypeStruct((parts - 1, groups, local, width), BF),
            jax.ShapeDtypeStruct(split + joint.shape, BF),
            jax.ShapeDtypeStruct((16, width), F32),
            jax.ShapeDtypeStruct(split + up.shape, BF),
            jax.ShapeDtypeStruct(split + down.shape, BF),
            jax.ShapeDtypeStruct(split + out.shape, BF),
            jax.ShapeDtypeStruct((groups, local, width), BF),
            jax.ShapeDtypeStruct((groups, local, 2 * width), BF),
        ],
        scratch_shapes=[
            pltpu.VMEM((groups, local, width), F32),
            pltpu.VMEM((groups, local, width), BF),
            pltpu.VMEM(split + joint.shape if packed else (16, 128), BF),
            pltpu.VMEM(joint.shape, BF),
            pltpu.VMEM(up.shape, BF),
            pltpu.VMEM(down.shape, BF),
            pltpu.VMEM(out.shape, BF),
            pltpu.VMEM((len(order), 16, width), F32),
            pltpu.VMEM((len(order), 3, 16, width), F32),
            pltpu.VMEM((groups, local, width), BF),
            pltpu.VMEM((groups, local, 2 * width), BF),
            pltpu.SemaphoreType.DMA((4 * groups + 7,)),
            pltpu.SemaphoreType.DMA((copies,)),
            pltpu.SemaphoreType.DMA((copies,)),
        ],
        compiler_params=pltpu.CompilerParams(
            vmem_limit_bytes=62 * MIB, collective_id=0, has_side_effects=True
        ),
        name="begin",
    )(tokens, joint, up, down, out, *vectors)


def matrix_of(full):
    return full.reshape((-1,) + full.shape[-1:])


def owner_sums(arrays):
    size_dp, size_seq = lax.axis_size("dp"), lax.axis_size("seq")
    bits_dp, bits_seq = log2(size_dp), log2(size_seq)
    bits = bits_dp + bits_seq
    dp, seq = lax.axis_index("dp"), lax.axis_index("seq")
    arrays = [a.reshape((2,) * bits + (-1,) + a.shape[1:]) for a in arrays]
    left = list(range(bits))
    for bit in [bits_dp - 1] + list(range(bits_dp, bits)) + list(range(bits_dp - 2, -1, -1)):
        axis = left.index(bit)
        left.remove(bit)
        if bit < bits_dp:
            name, size, step, me = "dp", size_dp, 2 ** (bits_dp - 1 - bit), dp
        else:
            name, size, step, me = "seq", size_seq, 2 ** (bits - 1 - bit), seq
        mine = me // step % 2
        pairs = [(i, i ^ step) for i in range(size)]
        sent = [
            lax.dynamic_index_in_dim(a, 1 - mine, axis, keepdims=False).astype(BF) for a in arrays
        ]
        kept = [lax.dynamic_index_in_dim(a, mine, axis, keepdims=False) for a in arrays]
        arrived = [lax.ppermute(v, name, pairs) for v in sent]
        arrays = [k + a.astype(F32) for k, a in zip(kept, arrived)]
    return arrays


class Halving:
    def __init__(self, net, links, groups, held, landing, source=None):
        self.net, self.groups, self.held, self.landing = net, groups, held, landing
        self.gone = groups[0] if source is not None else ()
        self.rounds = []
        for stage, group in enumerate(groups):
            copies = []
            for i, flips in enumerate(subsets(group)):
                at = self.place(stage, flips)
                part = source.at[at] if stage == 0 and source is not None else held.at[self.cut(at)]
                copies.append(links.copy(part, landing[stage].at[i], net.partner(flips)))
            self.rounds.append(copies)

    def place(self, stage, turned):
        done, group = flat(self.groups[:stage]), self.groups[stage]
        at = []
        for bit, mine in enumerate(self.net.mine):
            if bit in done or bit in group:
                at.append(1 - mine if bit in turned else mine)
            else:
                at.append(slice(None))
        return tuple(at)

    def cut(self, at):
        return tuple(a for bit, a in enumerate(at) if bit not in self.gone)

    def start(self, stage):
        start(self.rounds[stage])

    def add(self, stage, out=None):
        wait(self.rounds[stage])
        at = self.cut(self.place(stage, ()))
        free = [i for i, a in enumerate(at) if isinstance(a, slice)]
        landing = self.landing[stage]

        def one(flat_index, carry):
            inner = [lax.rem(flat_index // 2 ** (len(free) - 1 - i), 2) for i in range(len(free))]
            there = list(at)
            for axis, value in zip(free, inner):
                there[axis] = value
            there = tuple(there)
            value = self.held[there].astype(F32)
            for i in range(landing.shape[0]):
                value += landing[(i,) + tuple(inner)].astype(F32)
            if out is None:
                self.held[there] = value.astype(BF)
            else:
                out[...] = value
            return carry

        if free:
            lax.fori_loop(0, 2 ** len(free), one, 0)
        else:
            one(0, 0)


class Everywhere:
    def __init__(self, net, links, groups, value, sent, landing):
        self.value, self.sent, self.landing = value, sent, landing
        self.rounds = [
            [
                links.copy(sent.at[stage], landing.at[stage, i], net.partner(flips))
                for i, flips in enumerate(subsets(group))
            ]
            for stage, group in enumerate(groups)
        ]

    def start(self, stage):
        self.sent[stage] = self.value[...]
        start(self.rounds[stage])

    def add(self, stage, out=None):
        wait(self.rounds[stage])
        for i in range(len(self.rounds[stage])):
            self.value[...] += self.landing[stage, i]


def landing_shapes(groups, bits, rows, width):
    shapes, left = [], bits
    for group in groups:
        left -= len(group)
        shapes.append(pltpu.VMEM((2 ** len(group) - 1,) + (2,) * left + (rows, width), BF))
    return shapes


def sum_orders(bits_dp, bits_seq):
    beside, upper, next_to, cores = stages_of(bits_dp, bits_seq)
    far = upper[::-1]
    if len(beside) == 1 and len(beside[0]) == 1:
        near = [beside[0] + next_to[0]]
    else:
        near = beside + next_to
    return cores + beside + next_to + far, cores + next_to + beside + far, cores + near + far


def project_kernel(tokens, weight, bias, query, pair):
    x = tokens[...]
    width = x.shape[1]
    query[...] = (dot(x, weight[:, :width]) + bias[:, :width]).astype(BF)
    pair[...] = (dot(x, weight[:, width:]) + bias[:, width:]).astype(BF)


def project(tokens, weight, bias):
    count, width = tokens.shape
    block = min(512, count)

    def moving(columns):
        return pl.BlockSpec((block, columns), lambda b: (b, 0))

    def still(*shape):
        return pl.BlockSpec(shape, lambda b: (0, 0), pipeline_mode=pl.Buffered(1))

    return pl.pallas_call(
        project_kernel,
        grid=(count // block,),
        in_specs=[moving(width), still(width, 3 * width), still(1, 3 * width)],
        out_specs=[moving(width), moving(2 * width)],
        out_shape=[
            jax.ShapeDtypeStruct((count, width), BF),
            jax.ShapeDtypeStruct((count, 2 * width), BF),
        ],
        compiler_params=params(40, 1),
        name="project",
    )(tokens, weight, bias)


def attend_kernel(parts, groups, steps, blocks, bits_dp, bits_seq, *refs):
    (
        lengths,
        query,
        keys_own,
        values_own,
        weight,
        vec,
        tokens_low,
        _,
        _,
        _,
        _,
        e_out,
        mixed,
        mixed_t,
        inverse,
        pair_rest,
        tokens_rest,
        up_w,
        down_w,
        out_w,
        k_mask,
        v_ext,
        kept,
        tops,
        rest_here,
        pair_here,
        own_sem,
        send_sem,
        recv_sem,
    ) = refs
    local = keys_own.shape[1]
    block = query.shape[1]
    step = pl.program_id(0)
    chunk = min(256, local)

    net = Net(bits_dp, bits_seq)
    links = Links(net, send_sem, recv_sem)
    beside, upper, next_to, cores = stages_of(bits_dp, bits_seq)
    order = beside + upper + next_to + cores
    first, last = len(beside), len(order)
    lead = len(upper)
    rounds = []
    for stage in range(first, last):
        copies = []
        for full in (down_w, out_w):
            copies += links.spread(full, flat(order[:stage]), order[stage])
        ahead = stage + lead
        if ahead < last:
            copies += links.spread(up_w, flat(order[:ahead]), order[ahead])
        rounds.append(copies)
    if len(rounds) > 3:
        times = [i * steps // (len(rounds) + 1) for i in range(len(rounds) + 1)]
    else:
        times = [0, steps * 6 // 16, steps * 12 // 16, steps * 14 // 16]
    exchange = []
    for g in range(1, groups):
        left = slice(local // AHEAD if g == 1 else 0, local)
        exchange.append(
            [
                links.copy(
                    tokens_low.at[g, left],
                    tokens_rest.at[other - 1, g, left],
                    ring(net, parts, other),
                )
                for other in range(1, parts)
            ]
        )

    @pl.when(step == 0)
    def enter():
        due = net.greet(order[first:])
        for other in range(1, parts):
            net.signal(ring(net, parts, other))
            due += 1
        pl.semaphore_wait(pltpu.get_barrier_semaphore(), due)
        for copies in exchange:
            start(copies)
        start(rounds[0])

    for i in range(len(rounds)):
        @pl.when(step == times[i + 1])
        def advance():
            wait(rounds[i])
            if i + 1 < len(rounds):
                start(rounds[i + 1])

    stores = [
        pltpu.make_async_copy(pair_here.at[:, g], pair_rest.at[:, g], own_sem.at[groups + g])
        for g in range(groups)
    ]
    for group in range(groups):
        @pl.when(step == group * blocks * PAIRS)
        def other_keys():
            if group > 0:
                wait(exchange[group - 1])
            copy = pltpu.make_async_copy(tokens_rest.at[:, group], rest_here, own_sem.at[group])
            copy.start()
            width = weight.shape[0]
            bias = jnp.concatenate([vec[11:12], vec[12:13]], axis=1)
            for part in range(parts):
                rows = slice(part * local, (part + 1) * local)
                first_key = lax.rem(net.seq + part, parts) * local
                place = lax.broadcasted_iota(jnp.int32, (local, WIDE), 0) + first_key
                k_mask[rows] = jnp.where(place < lengths[group], 0.0, -1e30).astype(BF)
            copy.wait()
            for part in range(1, parts):
                for p in range(PAIRS):
                    columns = slice(2 * WIDE * p, 2 * WIDE * (p + 1))
                    both = dot(rest_here[part - 1], weight[:, width:][:, columns])
                    pair_here[part - 1, group, p] = (both + bias[:, columns]).astype(BF)
            start(stores[group : group + 1])

    @pl.when(step == steps)
    def leave():
        wait(stores)

    def decode(t):
        return t // (PAIRS * blocks), lax.rem(t // blocks, PAIRS)

    group_then, pair_then = decode(jnp.maximum(step - 1, 0))

    @pl.when(step % blocks == 1 % blocks)
    def prepare_values():
        for part in range(parts):
            rows = slice(part * local, (part + 1) * local)
            if part == 0:
                values = values_own[0]
            else:
                values = pair_here[part - 1, group_then, pair_then, :, WIDE:]
            turned = values.T
            v_ext[0, :HEAD, rows] = turned[:HEAD]
            v_ext[1, :HEAD, rows] = turned[HEAD:]

    @pl.when(step == 0)
    def ones():
        v_ext[:, HEAD:] = jnp.ones((2, HEAD, parts * local), BF)

    group_now, pair_now = decode(jnp.minimum(step, steps - 1))

    turned = query[0].T
    zero = jnp.zeros((HEAD, block), BF)
    one = (lax.broadcasted_iota(jnp.int32, (WIDE, block), 0) == 0).astype(F32).astype(BF)
    heads = []
    for head in range(2):
        if head == 0:
            picked = jnp.concatenate([turned[:HEAD], zero, one], axis=0)
        else:
            picked = jnp.concatenate([zero, turned[HEAD:], one], axis=0)
        top = tops[head : head + 1]
        out = None
        largest = None
        for at in range(0, parts * local, chunk):
            rows = slice(at, at + chunk)
            inside = slice(at % local, at % local + chunk)
            e = jnp.exp2((kept[head, rows] - top) * (SCALE * LOG2E)).astype(BF)
            e_out[at // local, 0, head, inside] = e
            add = dot(v_ext[head, :, rows], e)
            out = add if out is None else out + add
            if at < local:
                keys = keys_own[0, inside]
            else:
                keys = pair_here[at // local - 1, group_now, pair_now, inside, :WIDE]
            scores = dot(jnp.concatenate([keys, k_mask[rows]], axis=1), picked)
            kept[head, rows] = scores
            most = jnp.max(scores.reshape(chunk // 8, 8, block), axis=0)
            largest = most if largest is None else jnp.maximum(largest, most)
        tops[head : head + 1] = jnp.max(largest, axis=0, keepdims=True)
        inv = 1.0 / out[HEAD : HEAD + 1]
        inverse[0, 0, head : head + 1] = inv
        heads.append(out[:HEAD] * inv)
    both = jnp.concatenate(heads, axis=0).astype(BF)
    mixed_t[0] = both
    mixed[0] = both.T


def attend(lengths, query, pair_own, weight, vec, tokens_low, tokens_rest, up_w, down_w, out_w):
    groups, local, width = query.shape
    others = tokens_rest.shape[0]
    parts = others + 1
    block = min(512, local)
    blocks = local // block
    steps = groups * PAIRS * blocks
    bits_dp, bits_seq = mesh_bits()
    beside, upper, next_to, cores = stages_of(bits_dp, bits_seq)
    sends = sum(2 ** len(group) - 1 for group in upper + next_to + cores)
    copies = 3 * sends + groups * others

    def decode(t, place):
        return place(t // (PAIRS * blocks), t // blocks % PAIRS, t % blocks)

    def now(place):
        return lambda t: decode(jnp.minimum(t, steps - 1), place)

    def before(place):
        return lambda t: decode(jnp.maximum(t - 1, 0), place)

    def still(*shape):
        return pl.BlockSpec(shape, lambda t: (0,) * len(shape), pipeline_mode=pl.Buffered(1))

    hbm = pl.BlockSpec(memory_space=pl.ANY)
    passed = (tokens_rest, up_w, down_w, out_w)
    return pl.pallas_call(
        functools.partial(attend_kernel, parts, groups, steps, blocks, bits_dp, bits_seq),
        grid=(steps + 1,),
        in_specs=[
            pl.BlockSpec(memory_space=pltpu.SMEM),
            pl.BlockSpec((1, block, WIDE), now(lambda g, p, b: (g, b, p))),
            pl.BlockSpec((1, local, WIDE), now(lambda g, p, b: (g, 0, 2 * p))),
            pl.BlockSpec((1, local, WIDE), before(lambda g, p, b: (g, 0, 2 * p + 1))),
            still(width, 3 * width),
            still(*vec.shape),
        ]
        + [hbm] * 5,
        out_specs=[
            pl.BlockSpec((parts, 1, 2, local, block), before(lambda g, p, b: (0, g, p, 0, b))),
            pl.BlockSpec((1, block, WIDE), before(lambda g, p, b: (g, b, p))),
            pl.BlockSpec((1, WIDE, block), before(lambda g, p, b: (g, p, b))),
            pl.BlockSpec((1, 1, 2, block), before(lambda g, p, b: (g, p, 0, b))),
            hbm,
        ]
        + [hbm] * 4,
        out_shape=[
            jax.ShapeDtypeStruct((parts, groups, H, local, local), BF),
            jax.ShapeDtypeStruct((groups, local, width), BF),
            jax.ShapeDtypeStruct((groups, width, local), BF),
            jax.ShapeDtypeStruct((groups, PAIRS, 2, local), F32),
            jax.ShapeDtypeStruct((others, groups, PAIRS, local, 2 * WIDE), BF),
        ]
        + [jax.ShapeDtypeStruct(v.shape, v.dtype) for v in passed],
        input_output_aliases={7: 5, 8: 6, 9: 7, 10: 8},
        scratch_shapes=[
            pltpu.VMEM((parts * local, WIDE), BF),
            pltpu.VMEM((2, WIDE, parts * local), BF),
            pltpu.VMEM((2, parts * local, block), F32),
            pltpu.VMEM((8, block), F32),
            pltpu.VMEM((others, local, width), BF),
            pltpu.VMEM((others, groups, PAIRS, local, 2 * WIDE), BF),
            pltpu.SemaphoreType.DMA((2 * groups,)),
            pltpu.SemaphoreType.DMA((copies,)),
            pltpu.SemaphoreType.DMA((copies,)),
        ],
        compiler_params=pltpu.CompilerParams(
            vmem_limit_bytes=62 * MIB,
            dimension_semantics=("arbitrary",),
            collective_id=1,
            has_side_effects=True,
        ),
        name="attend",
    )(lengths, query, pair_own, pair_own, weight, vec, tokens_low, *passed)


def middle_kernel(
    packed,
    tokens,
    cotangent,
    mixed,
    out_w,
    up_w,
    down_w,
    rows,
    result,
    partial,
    mixed_grad,
    upper_sums,
    lower_sums,
    vec_sums,
    out_wg,
    up_wg,
    down_wg,
    row_sums,
    up_bias_sum,
):
    first = pl.program_id(0) == 0

    @pl.when(first)
    def clear():
        out_wg[...] = jnp.zeros_like(out_wg)
        up_wg[...] = jnp.zeros_like(up_wg)
        down_wg[...] = jnp.zeros_like(down_wg)
        row_sums[...] = jnp.zeros_like(row_sums)
        up_bias_sum[...] = jnp.zeros_like(up_bias_sum)

    pieces = up_w.shape[1] // tokens.shape[1]
    up_bias = jnp.concatenate([rows[6 + i : 7 + i] for i in range(pieces)], axis=1)
    out_bias, gain_one, shift_one = rows[0:1], rows[1:2], rows[2:3]
    down_bias, gain_two, shift_two = rows[3:4], rows[4:5], rows[5:6]

    def mean(v):
        return jnp.mean(v, axis=-1, keepdims=True)

    def total(v):
        return jnp.sum(v, axis=0, keepdims=True)

    x = tokens[...]
    heads = mixed[...]
    hidden = x + (dot(heads, out_w[...]) + out_bias)
    centred = hidden - mean(hidden)
    r_one = lax.rsqrt(mean(centred * centred) + EPS)
    n_one = centred * r_one
    normal = n_one * gain_one + shift_one
    normal_low = normal.astype(BF)
    inner = dot(normal_low, up_w[...]) + up_bias
    square = inner * inner
    tanh = jnp.tanh(inner * (GELU_A + (GELU_A * GELU_B) * square))
    half = 0.5 + 0.5 * tanh
    active = (inner * half).astype(BF)
    slope = half + (0.5 * inner) * (1.0 - tanh * tanh) * (
        GELU_A + (3.0 * GELU_A * GELU_B) * square
    )
    branch = dot(active, down_w[...]) + down_bias
    last = normal + branch + x
    centred = last - mean(last)
    r_two = lax.rsqrt(mean(centred * centred) + EPS)
    n_two = centred * r_two
    result[...] = n_two * gain_two + shift_two
    grad = cotangent[...]
    e_two = grad * gain_two
    back = r_two * (e_two - mean(e_two) - n_two * mean(e_two * n_two))
    branch_grad = back.astype(BF)
    down_wg[...] += dot(active, branch_grad, "tn")
    inner_grad_wide = slope * dot(branch_grad, down_w[...], "nt")
    inner_grad = inner_grad_wide.astype(BF)
    up_wg[...] += dot(normal_low, inner_grad, "tn")
    up_bias_sum[...] += total(inner_grad.astype(F32))
    norm_grad = back + dot(inner_grad, up_w[...], "nt")
    e_one = norm_grad * gain_one
    hidden_grad = r_one * (e_one - mean(e_one) - n_one * mean(e_one * n_one))
    attn_grad = hidden_grad.astype(BF)
    partial[...] = back + hidden_grad
    out_wg[...] += dot(heads, attn_grad, "tn")
    mixed_grad[...] = dot(attn_grad, out_w[...], "nt").astype(BF)
    row_sums[0:1] += total(attn_grad.astype(F32))
    row_sums[1:2] += total(norm_grad * n_one)
    row_sums[2:3] += total(norm_grad)
    row_sums[3:4] += total(branch_grad.astype(F32))
    row_sums[4:5] += total(grad * n_two)
    row_sums[5:6] += total(grad)

    @pl.when(pl.program_id(0) == pl.num_programs(0) - 1)
    def pack():
        width = tokens.shape[1]
        pieces = up_wg.shape[1] // width
        vec_sums[...] = jnp.zeros_like(vec_sums)
        vec_sums[0:8] = row_sums[...]
        for piece in range(pieces):
            columns = slice(piece * width, (piece + 1) * width)
            vec_sums[8 + piece : 9 + piece] = up_bias_sum[:, columns]
        if not packed:
            upper_sums[:, :width] = out_wg[...]
            upper_sums[:, width:] = up_wg[...]
            lower_sums[...] = down_wg[...]
            return
        owners = upper_sums.shape[0]
        rows_out = out_wg.shape[0] // owners
        rows_down = down_wg.shape[0] // owners

        def one(owner, carry):
            near = pl.ds(pl.multiple_of(owner * rows_out, rows_out), rows_out)
            upper_sums[owner, :rows_out] = out_wg[near].astype(BF)
            for piece in range(pieces):
                columns = slice(piece * width, (piece + 1) * width)
                to = slice((piece + 1) * rows_out, (piece + 2) * rows_out)
                upper_sums[owner, to] = up_wg[near, columns].astype(BF)
            far = pl.ds(pl.multiple_of(owner * rows_down, rows_down), rows_down)
            lower_sums[owner] = down_wg[far].astype(BF)
            return carry

        lax.fori_loop(0, owners, one, 0)


def middle(tokens, cotangent, mixed, out_w, up_w, down_w, rows, owners):
    count, width = tokens.shape
    hidden = up_w.shape[1]
    block = min(512, count)
    packed = whole_tiles(width, owners)

    def moving(columns=width):
        return pl.BlockSpec((block, columns), lambda b: (b, 0))

    def still(*shape):
        return pl.BlockSpec(shape, lambda b: (0,) * len(shape), pipeline_mode=pl.Buffered(1))

    rows_upper = width // owners * (1 + hidden // width)
    rows_lower = hidden // owners
    if packed:
        sums = [((owners, rows_upper, width), BF), ((owners, rows_lower, width), BF)]
    else:
        sums = [((width, width + hidden), F32), ((hidden, width), F32)]
    return pl.pallas_call(
        functools.partial(middle_kernel, packed),
        grid=(count // block,),
        in_specs=[
            moving(),
            moving(),
            moving(),
            still(width, width),
            still(width, hidden),
            still(hidden, width),
            still(16, width),
        ],
        out_specs=[
            moving(),
            moving(),
            moving(),
        ]
        + [still(*shape) for shape, _ in sums]
        + [still(16, width)],
        out_shape=[
            jax.ShapeDtypeStruct((count, width), F32),
            jax.ShapeDtypeStruct((count, width), F32),
            jax.ShapeDtypeStruct((count, width), BF),
        ]
        + [jax.ShapeDtypeStruct(shape, kind) for shape, kind in sums]
        + [jax.ShapeDtypeStruct((16, width), F32)],
        scratch_shapes=[
            pltpu.VMEM((width, width), F32),
            pltpu.VMEM((width, hidden), F32),
            pltpu.VMEM((hidden, width), F32),
            pltpu.VMEM((8, width), F32),
            pltpu.VMEM((1, hidden), F32),
        ],
        compiler_params=params(62, 1),
        name="middle",
    )(tokens, cotangent, mixed, out_w, up_w, down_w, rows)


def pull_kernel(parts, groups, bits_dp, bits_seq, packed, *refs):
    taken = 0

    def take(count):
        nonlocal taken
        taken += count
        return refs[taken - count : taken]

    e_part, query, pair_own, pair_rest, mixed_grad, mixed_t, inverse = take(7)
    tokens_own, tokens_rest, weight, partial = take(4)
    sources = take(2) if packed else ()
    (vec_in,) = take(1)
    share_own, arrived, joint_out, vec_out = take(4)
    owned = take(2) if packed else ()
    d_scores, joint_grad, total, dq_sums, dq_turned, weight_grad, bias_grad, shares = take(8)
    share_send, share_recv, own_sem = take(3)
    step = pl.program_id(0)
    steps = pl.num_programs(0)
    each = groups * PAIRS
    part = lax.rem(step // each + 1, parts)
    own = part == 0
    inside = lax.rem(step, each)
    group = jnp.where(own, lax.rem(inside, groups), inside // PAIRS)
    pair = jnp.where(own, inside // groups, lax.rem(inside, PAIRS))

    net = Net(bits_dp, bits_seq)
    bits = net.bits
    orders = sum_orders(bits_dp, bits_seq)
    streams, loads = [], []
    if packed:
        upper_held, lower_held = take(2)
        joint_helds = take(len(JOINT_PARTS))
        vec_sent, vec_landing, bias_sent, bias_landing = take(4)
        send_sem, recv_sem = take(2)
        links = Links(net, send_sem, recv_sem)
        upper, lower = streams = [
            Halving(net, links, orders[i], held, take(len(orders[i])), sources[i])
            for i, held in enumerate((upper_held, lower_held))
        ]
        joint = [Halving(net, links, orders[2], h, take(len(orders[2]))) for h in joint_helds]
        early_vec = Everywhere(net, links, orders[2], vec_out.at[0:16], vec_sent, vec_landing)
        late_vec = Everywhere(net, links, orders[2], bias_grad, bias_sent, bias_landing)
        for i, stream in enumerate(streams):
            at = stream.place(0, ())
            loads.append(pltpu.make_async_copy(sources[i].at[at], stream.held, own_sem.at[i]))
    stores = [
        pltpu.make_async_copy(total.at[g], share_own.at[g], own_sem.at[2 + g])
        for g in range(groups)
    ]
    partials = [
        pltpu.make_async_copy(partial.at[g], total.at[g], own_sem.at[2 + groups + g])
        for g in range(groups)
    ]

    def share_copy(other, g):
        return pltpu.make_async_remote_copy(
            src_ref=shares.at[other - 1, g],
            dst_ref=arrived.at[other - 1, g],
            send_sem=share_send.at[other - 1, g],
            recv_sem=share_recv.at[other - 1, g],
            device_id=(net.dp, lax.rem(net.seq + other, parts)),
            device_id_type=MESH,
        )

    @pl.when(step == 0)
    def enter():
        due = parts - 1
        for other in range(1, parts):
            net.signal((net.dp, lax.rem(net.seq + other, parts)))
        if packed:
            due += net.greet(orders[0]) + net.greet(orders[2])
        start(loads)
        start(partials)
        pl.semaphore_wait(pltpu.get_barrier_semaphore(), due)
        for stream in streams:
            stream.start(0)

    def advance(streams, stage, outs, count):
        for stream, out in zip(streams, outs):
            stream.add(stage, out if stage == count - 1 else None)
            if stage < count - 1:
                stream.start(stage + 1)

    def pack(index):
        first, count = JOINT_PARTS[index]
        held = joint[index].held
        rows_each, width = weight_grad.shape[0] // 2**bits, weight_grad.shape[0]
        columns = slice(first * WIDE, (first + count) * WIDE)
        doubled = slice(width + 2 * first * WIDE, width + 2 * (first + count) * WIDE)

        def one(flat_index, carry):
            place = tuple(lax.rem(flat_index // 2 ** (bits - 1 - i), 2) for i in range(bits))
            near = pl.ds(pl.multiple_of(flat_index * rows_each, rows_each), rows_each)
            held[place + (slice(None), slice(0, count * WIDE))] = weight_grad[near, columns].astype(BF)
            held[place + (slice(None), slice(count * WIDE, 3 * count * WIDE))] = weight_grad[
                near, doubled
            ].astype(BF)
            return carry

        lax.fori_loop(0, 2**bits, one, 0)

    def joint_place(index):
        first, count = JOINT_PARTS[index]
        return joint_out.at[:, 3 * first * WIDE : 3 * (first + count) * WIDE]

    if packed:
        last = len(orders[2])
        for stage, when in enumerate((1, 5, 9, 12)):
            @pl.when(step == when)
            def ffn():
                if stage == 0:
                    wait(loads)
                advance(streams, stage, owned, len(orders[0]))

        @pl.when(step == steps - 2 * groups)
        def joint_early():
            pack(0)
            vec_out[...] = vec_in[...]
            joint[0].start(0)
            early_vec.start(0)

        @pl.when(step == steps - 2 * groups + 1)
        def joint_early_near():
            advance((joint[0], early_vec), 0, (None, None), last)

        @pl.when(step == steps - groups)
        def joint_middle():
            pack(1)
            joint[1].start(0)

        @pl.when(step == steps - 1)
        def joint_middle_near():
            advance((joint[0], early_vec), 1, (None, None), last)
            advance((joint[1],), 0, (None,), last)

    local = query.shape[1]
    chunk = min(256, local)
    turned = mixed_grad[0].astype(F32).T
    mixed = mixed_t[0].astype(F32)
    values = jnp.where(own, pair_own[0, :, WIDE:], pair_rest[0, 0, 0, :, WIDE:])
    keys_t = jnp.where(own, pair_own[0, :, :WIDE], pair_rest[0, 0, 0, :, :WIDE]).T
    query_now = query[0]
    lane = lax.broadcasted_iota(jnp.int32, (local, WIDE), 1)
    zero = jnp.zeros((HEAD, local), BF)
    grad_t, grad, centre, picked = [], [], [], []
    for head in range(2):
        side = slice(head * HEAD, (head + 1) * HEAD)
        inv = inverse[0, 0, head : head + 1]
        centre.append(inv * jnp.sum(turned[side] * mixed[side], axis=0, keepdims=True))
        scaled = (turned[side] * inv).astype(BF)
        grad_t.append(jnp.concatenate([scaled, zero] if head == 0 else [zero, scaled], axis=0))
        grad.append(grad_t[head].T)
        kept = lane < HEAD if head == 0 else lane >= HEAD
        picked.append(jnp.where(kept, query_now, jnp.zeros_like(query_now)))

    width = weight.shape[0]
    at_queries = pl.ds(pl.multiple_of(pair * WIDE, WIDE), WIDE)
    start_at = width + pair * (2 * WIDE)
    at_keys = pl.ds(pl.multiple_of(start_at, WIDE), WIDE)
    at_values = pl.ds(pl.multiple_of(start_at + WIDE, WIDE), WIDE)
    at_both = pl.ds(pl.multiple_of(start_at, WIDE), 2 * WIDE)

    def key_grad(rows):
        sums = dot(d_scores[0, rows], picked[0]) + dot(d_scores[1, rows], picked[1])
        joint_grad[group, rows, at_keys] = (sums * SCALE).astype(BF)

    last_rows = None
    for at in range(0, local, chunk):
        rows = slice(at, at + chunk)
        for head in range(2):
            pulled = dot(values[rows], grad_t[head])
            e = e_part[0, 0, head, rows].astype(F32)
            d_scores[head, rows] = (e * (pulled - centre[head])).astype(BF)
        sums = dot(e_part[0, 0, 0, rows], grad[0]) + dot(e_part[0, 0, 1, rows], grad[1])
        joint_grad[group, rows, at_values] = sums.astype(BF)
        if last_rows is not None:
            key_grad(last_rows)
        last_rows = rows
    key_grad(last_rows)
    for head in range(2):
        side = slice(head * HEAD, (head + 1) * HEAD)
        dq = dot(keys_t, d_scores[head])[side]
        dq_turned[side] = dq

    @pl.when(step == 0)
    def clear():
        weight_grad[...] = jnp.zeros_like(weight_grad)
        bias_grad[...] = jnp.zeros_like(bias_grad)
        dq_sums[...] = jnp.zeros_like(dq_sums)

    column = group * PAIRS + pair

    @pl.when(own)
    def near():
        dq = (dq_sums[column] + dq_turned[...]) * SCALE
        dq = dq.T.astype(BF)
        joint_grad[group, :, at_queries] = dq
        bias_grad[0:1, at_queries] += jnp.sum(dq.astype(F32), axis=0, keepdims=True)
        weight_grad[:, at_queries] += dot(tokens_own[group], dq, "tn")
        weight_grad[:, at_both] += dot(tokens_own[group], joint_grad[group, :, at_both], "tn")

    @pl.when(jnp.logical_not(own))
    def far():
        dq_sums[column] += dq_turned[...]
        weight_grad[:, at_both] += dot(tokens_rest[0, 0], joint_grad[group, :, at_both], "tn")

    value_sums = jnp.sum(joint_grad[group, :, at_values].astype(F32), axis=0, keepdims=True)
    bias_grad[1:2, at_queries] += value_sums

    for other in range(1, parts):
        for g in range(groups):
            @pl.when(step == ((other - 1) * groups + g + 1) * PAIRS - 1)
            def finish_far():
                for at in range(0, local, chunk):
                    rows = slice(at, at + chunk)
                    part_share = dot(joint_grad[g, rows, width:], weight[:, width:], "nt")
                    shares[other - 1, g, rows] = part_share.astype(BF)
                share_copy(other, g).start()

    def input_grads(g):
        for at in range(0, local, chunk):
            rows = slice(at, at + chunk)
            total[g, rows] += dot(joint_grad[g, rows], weight[...], "nt")
        start(stores[g : g + 1])

    @pl.when(step == steps - 1)
    def finish():
        work = list(range(groups))
        if packed:
            pack(2)
            joint[2].start(0)
            late_vec.start(0)
            advance((joint[1],), 1, (None,), last)
        wait(partials)
        if packed:
            for stage in range(last):
                if work:
                    input_grads(work.pop(0))
                outs = (joint_place(2), None)
                advance((joint[2], late_vec), stage, outs, last)
                if stage == 0:
                    advance((joint[0], early_vec), last - 1, (joint_place(0), None), last)
            joint[1].add(last - 1, joint_place(1))
        else:
            vec_out[...] = vec_in[...]
            joint_out[...] = weight_grad[...]
        for g in work:
            input_grads(g)
        vec_out[12:14] = bias_grad[0:2]
        for g in range(groups):
            for other in range(1, parts):
                share_copy(other, g).wait()
        wait(stores)


def pull(
    e_all,
    query,
    pair_own,
    pair_rest,
    mixed_grad,
    mixed_t,
    inverse,
    own,
    rest,
    weight,
    partial,
    upper_sums,
    lower_sums,
    vec_sums,
):
    parts, groups, _, local, _ = e_all.shape
    width = H * HEAD
    each = groups * PAIRS
    bits_dp, bits_seq = mesh_bits()
    bits = bits_dp + bits_seq
    orders = sum_orders(bits_dp, bits_seq)
    packed = whole_tiles(width, 2**bits)
    split = (2,) * bits
    sums, out_blocks, extra = [], [], []
    if packed:
        rows_upper, rows_lower = upper_sums.shape[1], lower_sums.shape[1]
        rows_joint = width // 2**bits
        sums = [v.reshape(split + v.shape[1:]) for v in (upper_sums, lower_sums)]
        out_blocks = [(rows_joint, 3 * width), (16, width), (rows_upper, width), (rows_lower, width)]
        joint_widths = [3 * count * WIDE for _, count in JOINT_PARTS]
        last = len(orders[2])
        sends = sum(2 ** len(g) - 1 for order in orders for g in order)
        sends += 4 * sum(2 ** len(g) - 1 for g in orders[2])
        extra = [
            pltpu.VMEM((2,) * (bits - 1) + (rows_upper, width), BF),
            pltpu.VMEM((2,) * (bits - 1) + (rows_lower, width), BF),
        ]
        extra += [pltpu.VMEM(split + (rows_joint, columns), BF) for columns in joint_widths]
        extra += [
            pltpu.VMEM((last, 16, width), F32),
            pltpu.VMEM((last, 3, 16, width), F32),
            pltpu.VMEM((last, 8, width), F32),
            pltpu.VMEM((last, 3, 8, width), F32),
            pltpu.SemaphoreType.DMA((sends,)),
            pltpu.SemaphoreType.DMA((sends,)),
        ]
        extra += landing_shapes(orders[0], bits, rows_upper, width)
        extra += landing_shapes(orders[1], bits, rows_lower, width)
        for columns in joint_widths:
            extra += landing_shapes(orders[2], bits, rows_joint, columns)
    else:
        out_blocks = [(width, 3 * width), (16, width)]

    def decode(t):
        part, inside = (t // each + 1) % parts, t % each
        own = part == 0
        group = jnp.where(own, inside % groups, inside // PAIRS)
        pair = jnp.where(own, inside // groups, inside % PAIRS)
        return part, group, pair

    def at(place):
        return lambda t: place(*decode(t))

    def own_at(place):
        def index(t):
            part, group, pair = decode(t)
            return place(jnp.where(part == 0, group, 0), jnp.where(part == 0, pair, 0))

        return index

    def rest_at(place):
        def index(t):
            t = jnp.minimum(t, (parts - 1) * each - 1)
            return place(t // each, t // PAIRS % groups, t % PAIRS)

        return index

    def still(*shape):
        return pl.BlockSpec(shape, lambda t: (0,) * len(shape), pipeline_mode=pl.Buffered(1))

    once = pl.Buffered(1)
    return pl.pallas_call(
        functools.partial(pull_kernel, parts, groups, bits_dp, bits_seq, packed),
        grid=(parts * each,),
        in_specs=[
            pl.BlockSpec((1, 1, 2, local, local), at(lambda j, g, p: (j, g, p, 0, 0))),
            pl.BlockSpec((1, local, WIDE), at(lambda j, g, p: (g, 0, p))),
            pl.BlockSpec((1, local, 2 * WIDE), own_at(lambda g, p: (g, 0, p))),
            pl.BlockSpec((1, 1, 1, local, 2 * WIDE), rest_at(lambda j, g, p: (j, g, p, 0, 0))),
            pl.BlockSpec((1, local, WIDE), at(lambda j, g, p: (g, 0, p))),
            pl.BlockSpec((1, WIDE, local), at(lambda j, g, p: (g, p, 0))),
            pl.BlockSpec((1, 1, 2, local), at(lambda j, g, p: (g, p, 0, 0))),
            still(groups, local, width),
            pl.BlockSpec(
                (1, 1, local, width), rest_at(lambda j, g, p: (j, g, 0, 0)), pipeline_mode=once
            ),
            still(width, 3 * width),
            pl.BlockSpec(memory_space=pl.ANY),
        ]
        + [pl.BlockSpec(memory_space=pl.ANY)] * len(sums)
        + [still(16, width)],
        out_specs=[
            pl.BlockSpec(memory_space=pl.ANY),
            pl.BlockSpec(memory_space=pl.ANY),
        ]
        + [still(*shape) for shape in out_blocks],
        out_shape=[
            jax.ShapeDtypeStruct((groups, local, width), F32),
            jax.ShapeDtypeStruct((parts - 1, groups, local, width), BF),
        ]
        + [jax.ShapeDtypeStruct(shape, F32) for shape in out_blocks],
        scratch_shapes=[
            pltpu.VMEM((2, local, local), BF),
            pltpu.VMEM((groups, local, 3 * width), BF),
            pltpu.VMEM((groups, local, width), F32),
            pltpu.VMEM((each, WIDE, local), F32),
            pltpu.VMEM((WIDE, local), F32),
            pltpu.VMEM((width, 3 * width), F32),
            pltpu.VMEM((8, width), F32),
            pltpu.VMEM((parts - 1, groups, local, width), BF),
            pltpu.SemaphoreType.DMA((parts - 1, groups)),
            pltpu.SemaphoreType.DMA((parts - 1, groups)),
            pltpu.SemaphoreType.DMA((2 + 2 * groups,)),
        ]
        + extra,
        compiler_params=pltpu.CompilerParams(
            vmem_limit_bytes=63 * MIB,
            dimension_semantics=("arbitrary",),
            collective_id=2,
            has_side_effects=True,
        ),
        name="pull",
    )(
        e_all,
        query,
        pair_own,
        pair_rest,
        mixed_grad,
        mixed_t,
        inverse,
        own,
        rest,
        weight,
        partial,
        *sums,
        vec_sums,
    )


def finish_kernel(bits_dp, bits_seq, share, arrived, joint, vec, upper, lower, *outs):
    (
        input_grad,
        joint_sum,
        pair_sum,
        out_sum,
        out_bias,
        gain_one,
        shift_one,
        up_sum,
        up_bias,
        down_sum,
        down_bias,
        gain_two,
        shift_two,
    ) = outs
    value = share[...]
    for other in range(arrived.shape[0]):
        value += arrived[other].astype(F32)
    input_grad[...] = value

    @pl.when(pl.program_id(0) == 0)
    def small():
        net = Net(bits_dp, bits_seq)
        device = net.dp * 2**bits_seq + net.seq
        rows, width = out_sum.shape
        summed = joint[...]
        turned = []
        for head in range(H):
            pair = head // 2
            for first, count in JOINT_PARTS:
                if first <= pair < first + count:
                    base = 3 * first * WIDE + head % 2 * HEAD
                    both = base + (count + 2 * (pair - first)) * WIDE
                    for at in (base + (pair - first) * WIDE, both, both + WIDE):
                        turned.append(summed[:, at : at + HEAD])
        joint_sum[...] = jnp.concatenate(turned, axis=1)
        out_sum[...] = upper[:rows]
        for piece in range(up_sum.shape[1] // width):
            up_sum[:, piece * width : (piece + 1) * width] = upper[
                (piece + 1) * rows : (piece + 2) * rows
            ]
        down_sum[...] = lower[...]
        lines = vec[...]
        which = lax.broadcasted_iota(jnp.int32, lines.shape, 0)

        def entries(out, row, column):
            line = jnp.sum(jnp.where(which == row, lines, 0.0), axis=0, keepdims=True)
            line = jnp.broadcast_to(line, (8, width))
            out[...] = pltpu.roll(line, lax.rem(width - column, width), 1)[:1, : out.shape[1]]

        plain = (out_bias, gain_one, shift_one, down_bias, gain_two, shift_two)
        for row, out in enumerate(plain):
            entries(out, row, device * out.shape[1])
        first = device * up_bias.shape[1]
        entries(up_bias, 8 + first // width, lax.rem(first, width))
        first = device * pair_sum.shape[1]
        kind = lax.rem(first // HEAD, 2)
        entries(pair_sum, 12 + kind, first // WIDE * HEAD + lax.rem(first, HEAD))


def finish(share, arrived, joint, vec, upper, lower, shards):
    groups, local, width = share.shape
    block = min(512, local)
    each = local // block

    def moving(*lead):
        return pl.BlockSpec(
            (1,) * len(lead) + (block, width), lambda b: (b // each, b % each, 0)
        )

    def still(shape):
        return pl.BlockSpec(shape, lambda b: (0,) * len(shape), pipeline_mode=pl.Buffered(1))

    bits_dp, bits_seq = mesh_bits()
    others = arrived.shape[0]
    small = (joint, vec, upper, lower)
    outs = pl.pallas_call(
        functools.partial(finish_kernel, bits_dp, bits_seq),
        grid=(groups * each,),
        in_specs=[
            moving(1),
            pl.BlockSpec((others, 1, block, width), lambda b: (0, b // each, b % each, 0)),
        ]
        + [still(v.shape) for v in small],
        out_specs=[moving(1)] + [still(shape) for shape in shards],
        out_shape=[jax.ShapeDtypeStruct(share.shape, F32)]
        + [jax.ShapeDtypeStruct(shape, F32) for shape in shards],
        compiler_params=params(62, 1),
        name="finish",
    )(share, arrived, *small)
    return [outs[0]] + [
        v.reshape(v.shape[1:]) if v.shape[0] == 1 else v for v in outs[1:]
    ]


def per_device(
    tokens,
    lengths,
    joint_weight,
    joint_bias,
    out_weight,
    out_bias,
    gain_first,
    shift_first,
    up_weight,
    up_bias,
    down_weight,
    down_bias,
    gain_second,
    shift_second,
    cotangent,
):
    groups, local, width = tokens.shape
    parts = lax.axis_size("seq")
    devices = lax.axis_size("dp") * parts
    me = lax.axis_index("seq")
    rows = groups * local
    own_rows = joint_weight.shape[0]
    vectors = [
        joint_bias,
        out_bias,
        gain_first,
        shift_first,
        up_bias,
        down_bias,
        gain_second,
        shift_second,
    ]
    lens = [v.shape[0] for v in vectors]
    tokens_low, tokens_rest, joint_w, vec, up_w, down_w, out_w, query, pair_own = begin(
        tokens,
        joint_weight,
        up_weight,
        down_weight,
        out_weight,
        [v.reshape(1, -1) for v in vectors],
        parts,
    )
    joint_w = matrix_of(joint_w)
    pieces = up_weight.shape[1] // width
    if not whole_tiles(width, devices):
        query, pair_own = project(
            tokens_low.reshape(rows, width), joint_w, vec[10:13].reshape(1, -1)
        )
        query = query.reshape(groups, local, width)
        pair_own = pair_own.reshape(groups, local, 2 * width)

    e_all, mixed, mixed_t, inverse, pair_rest, tokens_rest, up_w, down_w, out_w = attend(
        lengths, query, pair_own, joint_w, vec, tokens_low, tokens_rest, up_w, down_w, out_w
    )
    out_w, up_w, down_w = matrix_of(out_w), matrix_of(up_w), matrix_of(down_w)

    result, partial, mixed_grad, upper_sums, lower_sums, vec_sums = middle(
        tokens.reshape(rows, width),
        cotangent.reshape(rows, width),
        mixed.reshape(rows, width),
        out_w,
        up_w,
        down_w,
        vec,
        devices,
    )
    mixed_grad = mixed_grad.reshape(groups, local, width)
    share, arrived, joint, vec, *owned = pull(
        e_all,
        query,
        pair_own,
        pair_rest,
        mixed_grad,
        mixed_t,
        inverse,
        tokens_low,
        tokens_rest,
        joint_w,
        partial.reshape(groups, local, width),
        upper_sums,
        lower_sums,
        vec_sums,
    )
    if owned:
        upper, lower = owned
        shards = [
            (1, v.shape[0]) if v.ndim == 1 else v.shape
            for v in (
                joint_weight,
                joint_bias,
                out_weight,
                out_bias,
                gain_first,
                shift_first,
                up_weight,
                up_bias,
                down_weight,
                down_bias,
                gain_second,
                shift_second,
            )
        ]
        outs = finish(share, arrived, joint, vec, upper, lower, shards)
        return (result.reshape(groups, local, width), *outs)
    input_grad = share + jnp.sum(arrived.astype(F32), axis=0)
    joint_sum, upper, lower = owner_sums([joint, upper_sums, lower_sums])
    out_sum, up_sum = upper[:, :width], upper[:, width:]
    vec = lax.psum(vec, ("dp", "seq"))
    device = lax.axis_index("dp") * parts + me
    back = [joint_columns().index(block) for block in range(3 * H)]
    joint_sum = joint_sum.reshape(own_rows, 3 * H, HEAD)
    joint_sum = jnp.stack([joint_sum[:, b] for b in back], axis=1).reshape(own_rows, 3 * width)
    pair_grad = jnp.stack(
        [vec[12].reshape(H, HEAD), vec[13].reshape(H, HEAD)], axis=1
    ).reshape(2 * width)
    sums = [
        pair_grad,
        vec[0],
        vec[1],
        vec[2],
        vec[8 : 8 + pieces].reshape(-1),
        vec[3],
        vec[4],
        vec[5],
    ]
    small = [
        lax.dynamic_slice_in_dim(v, device * size, size, 0) for v, size in zip(sums, lens)
    ]
    return (
        result.reshape(groups, local, width),
        input_grad,
        joint_sum,
        small[0],
        out_sum,
        small[1],
        small[2],
        small[3],
        up_sum,
        small[4],
        lower,
        small[5],
        small[6],
        small[7],
    )


def solution(mesh):
    both = ("dp", "seq")
    matrix, vector, whole = P(both, None), P(both), P("dp", "seq", None)
    return jax.shard_map(
        per_device,
        mesh=mesh,
        in_specs=(
            whole,
            P("dp"),
            matrix,
            vector,
            matrix,
            vector,
            vector,
            vector,
            matrix,
            vector,
            matrix,
            vector,
            vector,
            vector,
            whole,
        ),
        out_specs=(
            whole,
            whole,
            matrix,
            vector,
            matrix,
            vector,
            vector,
            vector,
            matrix,
            vector,
            matrix,
            vector,
            vector,
            vector,
        ),
        check_vma=False,
    )
```

```python
import functools
import math

import jax
import jax.numpy as jnp
from jax import lax
from jax.experimental import pallas as pl
from jax.experimental.pallas import tpu as pltpu
from jax.sharding import PartitionSpec as P

H = 8
HEAD = 64
PAIRS = H // 2
WIDE = 2 * HEAD
JOINT_PARTS = ((0, 2), (2, 1), (3, 1))
AHEAD = 16
BF = jnp.bfloat16
F32 = jnp.float32
EPS = 1e-05
SCALE = 1.0 / math.sqrt(HEAD)
LOG2E = math.log2(math.e)
GELU_A = math.sqrt(2.0 / math.pi)
GELU_B = 0.044715
MESH = pl.DeviceIdType.MESH
MIB = 2**20
FORMS = {
    "nn": (((1,), (0,)), ((), ())),
    "nt": (((1,), (1,)), ((), ())),
    "tn": (((0,), (0,)), ((), ())),
}


def dot(left, right, form="nn"):
    return lax.dot_general(left, right, FORMS[form], preferred_element_type=F32)


def whole_tiles(width, devices):
    return width // devices % 16 == 0


def params(limit, steps):
    return pltpu.CompilerParams(
        vmem_limit_bytes=limit * MIB, dimension_semantics=("arbitrary",) * steps
    )


def log2(size):
    return size.bit_length() - 1


class Net:
    def __init__(self, bits_dp, bits_seq):
        self.bits_dp, self.bits_seq = bits_dp, bits_seq
        self.bits = bits_dp + bits_seq
        self.dp, self.seq = lax.axis_index("dp"), lax.axis_index("seq")
        self.mine = [lax.rem(lax.div(self.dp, 2 ** (bits_dp - 1 - b)), 2) for b in range(bits_dp)]
        self.mine += [lax.rem(lax.div(self.seq, 2 ** (bits_seq - 1 - b)), 2) for b in range(bits_seq)]

    def partner(self, flips):
        dp, seq = self.dp, self.seq
        for bit in flips:
            turn = 1 - 2 * self.mine[bit]
            if bit < self.bits_dp:
                dp = dp + turn * 2 ** (self.bits_dp - 1 - bit)
            else:
                seq = seq + turn * 2 ** (self.bits - 1 - bit)
        return (dp, seq)

    def place(self, done, turned=()):
        at = []
        for bit in range(self.bits):
            if bit in done:
                at.append(slice(None))
            else:
                at.append(1 - self.mine[bit] if bit in turned else self.mine[bit])
        return tuple(at)

    def signal(self, device):
        pl.semaphore_signal(
            pltpu.get_barrier_semaphore(), inc=1, device_id=device, device_id_type=MESH
        )

    def greet(self, groups):
        count = 0
        for group in groups:
            for flips in subsets(group):
                self.signal(self.partner(flips))
                count += 1
        return count


def subsets(group):
    return [
        tuple(b for i, b in enumerate(group) if pick >> i & 1)
        for pick in range(1, 2 ** len(group))
    ]


def stages_of(bits_dp, bits_seq):
    bits = bits_dp + bits_seq

    def twos(numbers):
        return [tuple(numbers[i : i + 2]) for i in range(0, len(numbers), 2)]

    beside = twos(list(range(bits_dp, bits)))
    upper = twos(list(range(bits_dp - 2)))
    return beside, upper, [(bits_dp - 2,)], [(bits_dp - 1,)]


def mesh_bits():
    return log2(lax.axis_size("dp")), log2(lax.axis_size("seq"))


class Later:
    def __init__(self, make):
        self.make = make

    def start(self):
        self.make().start()

    def wait(self):
        self.make().wait()


class Links:
    def __init__(self, net, send_sem, recv_sem):
        self.net, self.send_sem, self.recv_sem, self.used = net, send_sem, recv_sem, 0

    def copy(self, source, target, device):
        at = self.used
        self.used += 1
        return Later(
            lambda: pltpu.make_async_remote_copy(
                src_ref=source(),
                dst_ref=target(),
                send_sem=self.send_sem.at[at],
                recv_sem=self.recv_sem.at[at],
                device_id=device(),
                device_id_type=MESH,
            )
        )

    def spread(self, full, done, group, columns=slice(None), shard=None):
        def target():
            return full.at[self.net.place(done) + (slice(None), columns)]

        def source():
            return target() if shard is None else shard.at[:, columns]

        return [
            self.copy(source, target, functools.partial(self.net.partner, flips))
            for flips in subsets(group)
        ]


def start(copies):
    for copy in copies:
        copy.start()


def wait(copies):
    for copy in copies:
        copy.wait()


def flat(groups):
    return tuple(b for group in groups for b in group)


def ring(net, parts, other):
    return (net.dp, lax.rem(net.seq + parts - other, parts))


def owned_row(vector, row, device):
    size, width = vector.shape[1], H * HEAD
    shift = log2(size)
    entry = lax.broadcasted_iota(jnp.int32, (size, width), 0)
    column = lax.broadcasted_iota(jnp.int32, (size, width), 1) + row * width
    here = (column >> shift == device) & (column & (size - 1) == entry)
    return dot(vector.astype(BF), here.astype(F32).astype(BF))


def owned_pair(vector, row, device):
    size, width = vector.shape[1], H * HEAD
    shift = log2(size)
    entry = lax.broadcasted_iota(jnp.int32, (size, width), 0)
    column = lax.broadcasted_iota(jnp.int32, (1, width), 1)
    if row > 0:
        column += (row - 1) * width
        head = 2 * (column >> log2(2 * WIDE)) + (column >> log2(HEAD) & 1)
        index = (2 * head + 1) * HEAD + (column & (HEAD - 1))
        index = jnp.where(column & WIDE == 0, -1, index)
    else:
        index = 2 * (column >> log2(HEAD)) * HEAD + (column & (HEAD - 1))
    here = (index >> shift == device) & (index & (size - 1) == entry)
    return dot(vector.astype(BF), here.astype(F32).astype(BF))


def joint_columns():
    blocks = [3 * head for head in range(H)]
    for pair in range(PAIRS):
        blocks += [3 * head + kind for kind in (1, 2) for head in (2 * pair, 2 * pair + 1)]
    return blocks


def begin_kernel(bits_dp, bits_seq, parts, packed, *refs):
    (
        tokens,
        joint_wide,
        up_wide,
        down_wide,
        out_wide,
        pair_bias,
        out_bias,
        gain_one,
        shift_one,
        up_bias,
        down_bias,
        gain_two,
        shift_two,
        tokens_low,
        tokens_t,
        tokens_rest,
        joint_out,
        vec,
        up_w,
        down_w,
        out_w,
        query,
        pair_own,
        wide,
        narrow,
        narrow_t,
        joint_here,
        joint_shard,
        up_shard,
        down_shard,
        out_shard,
        vec_sent,
        vec_landing,
        query_here,
        pair_here,
        own_sem,
        send_sem,
        recv_sem,
    ) = refs
    joint_w = joint_here if packed else joint_out
    net = Net(bits_dp, bits_seq)
    links = Links(net, send_sem, recv_sem)
    beside, upper, next_to, cores = stages_of(bits_dp, bits_seq)
    order = beside + upper + next_to + cores
    groups, local, width = tokens.shape
    due = net.greet(order)
    for other in range(1, parts):
        net.signal(ring(net, parts, other))
        due += 1
    loads = [
        pltpu.make_async_copy(tokens.at[g], wide.at[g], own_sem.at[g]) for g in range(groups)
    ]
    stores = [
        pltpu.make_async_copy(narrow.at[g], tokens_low.at[g], own_sem.at[groups + g])
        for g in range(groups)
    ]
    turned_stores = [pltpu.make_async_copy(narrow_t, tokens_t, own_sem.at[4 * groups + 7])]
    mine = net.place(())
    placed = [
        pltpu.make_async_copy(shard, full.at[mine], own_sem.at[2 * groups + i])
        for i, (shard, full) in enumerate(
            ((joint_shard, joint_w), (up_shard, up_w), (down_shard, down_w), (out_shard, out_w))
        )
    ]
    start(loads)
    joint = joint_wide[...]
    turned = [joint[:, b * HEAD : (b + 1) * HEAD] for b in joint_columns()]
    joint_shard[...] = jnp.concatenate(turned, axis=1).astype(BF)
    start(placed[:1])
    pl.semaphore_wait(pltpu.get_barrier_semaphore(), due)

    def prepare():
        up_shard[...] = up_wide[...].astype(BF)
        down_shard[...] = down_wide[...].astype(BF)
        out_shard[...] = out_wide[...].astype(BF)
        start(placed[1:])
        device = net.dp * parts + net.seq
        vec[...] = jnp.zeros_like(vec)
        lines = (out_bias, gain_one, shift_one, down_bias, gain_two, shift_two)
        for row, vector in enumerate(lines):
            vec[row : row + 1] = owned_row(vector[...], 0, device)
        for row in range(4):
            vec[6 + row : 7 + row] = owned_row(up_bias[...], row, device)
        for row in range(3):
            vec[10 + row : 11 + row] = owned_pair(pair_bias[...], row, device)
        wait(placed)

    def narrowed(g):
        wait(loads[g : g + 1])
        narrow[g] = wide[g].astype(BF)
        start(stores[g : g + 1])

    def turned_tokens():
        block = min(256, local)
        for g in range(groups):
            for at in range(0, local, block):
                rows = slice(at, at + block)
                narrow_t[g, :, rows] = narrow[g, rows].T
        start(turned_stores)

    cut = width + 2 * WIDE
    columns = (slice(0, cut), slice(cut, 3 * width))
    dones = [flat(order[:stage]) for stage in range(len(order))]
    ahead, behind = [
        [
            links.spread(joint_w, done, group, c, None if done else joint_shard)
            for done, group in zip(dones, order)
        ]
        for c in columns
    ]
    small = [
        [
            links.copy(
                functools.partial(Everywhere.line, vec_sent, stage),
                functools.partial(Everywhere.line, vec_landing, stage, i),
                functools.partial(net.partner, flips),
            )
            for i, flips in enumerate(subsets(group))
        ]
        for stage, group in enumerate(order)
    ]

    def small_start(stage):
        vec_sent[stage] = vec[...]
        start(small[stage])

    def small_add(stage):
        wait(small[stage])
        for i in range(len(small[stage])):
            vec[...] += vec_landing[stage, i]

    exchange = [
        links.copy(
            functools.partial(Everywhere.line, narrow, 0),
            functools.partial(Everywhere.line, tokens_rest, other - 1, 0),
            functools.partial(ring, net, parts, other),
        )
        for other in range(1, parts)
    ]
    some = slice(0, local // AHEAD)
    exchange_next = [
        links.copy(
            functools.partial(Everywhere.line, narrow, 1, some),
            functools.partial(Everywhere.line, tokens_rest, other - 1, 1, some),
            functools.partial(ring, net, parts, other),
        )
        for other in range(1, parts)
    ]

    def projected(part):
        bias = jnp.concatenate([vec[10 + i : 11 + i] for i in range(3)], axis=1)[:, columns[part]]
        block = min(256, local)
        for g in range(groups):

            def rows_of(b, carry):
                rows = pl.ds(pl.multiple_of(b * block, block), block)
                full = joint_w[..., columns[part]].reshape(width, -1)
                joint = (dot(narrow[g, rows], full) + bias).astype(BF)
                if part == 0:
                    query_here[g, rows] = joint[:, :width]
                    pair_here[g, rows, : cut - width] = joint[:, width:]
                else:
                    pair_here[g, rows, cut - width :] = joint
                return carry

            lax.fori_loop(0, local // block, rows_of, 0)

    late, rest = [], []
    last = len(order) - 1
    start(ahead[0])
    start(behind[0])
    prepare()
    small_start(0)
    for stage in range(last):
        done, group = dones[stage], order[stage]
        if stage < len(beside):
            rest = [links.spread(full, done, group) for full in (up_w, down_w, out_w)]
            for copies in rest:
                start(copies)
        if stage == len(beside) - 1:
            narrowed(0)
            start(exchange)
        elif stage == len(beside):
            for g in range(1, groups):
                narrowed(g)
            start(exchange_next)
            turned_tokens()
        wait(ahead[stage])
        small_add(stage)
        start(ahead[stage + 1])
        small_start(stage + 1)
        if stage + 1 < last:
            wait(behind[stage])
            start(behind[stage + 1])
        for copies in rest:
            wait(copies)
        rest = []
        if len(beside) <= stage < len(beside) + len(upper):
            wait(late)
            late = links.spread(up_w, done, group)
            start(late)
    wait(ahead[last])
    small_add(last)
    if packed:
        projected(0)
    wait(behind[last - 1])
    start(behind[last])
    wait(behind[last])
    if packed:
        results = [
            pltpu.make_async_copy(joint_here, joint_out, own_sem.at[4 * groups + 4]),
            pltpu.make_async_copy(query_here, query, own_sem.at[4 * groups + 5]),
        ]
        start(results)
        projected(1)
        results.append(pltpu.make_async_copy(pair_here, pair_own, own_sem.at[4 * groups + 6]))
        start(results[2:])
        wait(results)
    wait(late)
    wait(exchange)
    wait(exchange_next)
    wait(stores)
    wait(turned_stores)


def begin(tokens, joint, up, down, out, vectors, parts):
    bits_dp, bits_seq = mesh_bits()
    bits = bits_dp + bits_seq
    groups, local, width = tokens.shape
    packed = joint.shape[0] % 16 == 0
    beside, upper, next_to, cores = stages_of(bits_dp, bits_seq)
    order = beside + upper + next_to + cores
    sends = sum(2 ** len(group) - 1 for group in order)
    copies = 3 * sends + 4 * sends + 2 * parts
    split = (2,) * bits
    hbm = pl.BlockSpec(memory_space=pl.ANY)
    vmem = pl.BlockSpec(memory_space=pltpu.VMEM)
    return pl.pallas_call(
        functools.partial(begin_kernel, bits_dp, bits_seq, parts, packed),
        in_specs=[hbm] + [vmem] * (4 + len(vectors)),
        out_specs=[hbm, hbm, hbm, hbm, vmem] + [hbm] * 5,
        out_shape=[
            jax.ShapeDtypeStruct((groups, local, width), BF),
            jax.ShapeDtypeStruct((groups, width, local), BF),
            jax.ShapeDtypeStruct((parts - 1, groups, local, width), BF),
            jax.ShapeDtypeStruct(split + joint.shape, BF),
            jax.ShapeDtypeStruct((16, width), F32),
            jax.ShapeDtypeStruct(split + up.shape, BF),
            jax.ShapeDtypeStruct(split + down.shape, BF),
            jax.ShapeDtypeStruct(split + out.shape, BF),
            jax.ShapeDtypeStruct((groups, local, width), BF),
            jax.ShapeDtypeStruct((groups, local, 2 * width), BF),
        ],
        scratch_shapes=[
            pltpu.VMEM((groups, local, width), F32),
            pltpu.VMEM((groups, local, width), BF),
            pltpu.VMEM((groups, width, local), BF),
            pltpu.VMEM(split + joint.shape if packed else (16, 128), BF),
            pltpu.VMEM(joint.shape, BF),
            pltpu.VMEM(up.shape, BF),
            pltpu.VMEM(down.shape, BF),
            pltpu.VMEM(out.shape, BF),
            pltpu.VMEM((len(order), 16, width), F32),
            pltpu.VMEM((len(order), 3, 16, width), F32),
            pltpu.VMEM((groups, local, width), BF),
            pltpu.VMEM((groups, local, 2 * width), BF),
            pltpu.SemaphoreType.DMA((4 * groups + 8,)),
            pltpu.SemaphoreType.DMA((copies,)),
            pltpu.SemaphoreType.DMA((copies,)),
        ],
        compiler_params=pltpu.CompilerParams(
            vmem_limit_bytes=62 * MIB, collective_id=0, has_side_effects=True
        ),
        name="begin",
    )(tokens, joint, up, down, out, *vectors)


def matrix_of(full):
    return full.reshape((-1,) + full.shape[-1:])


def owner_sums(arrays):
    size_dp, size_seq = lax.axis_size("dp"), lax.axis_size("seq")
    bits_dp, bits_seq = log2(size_dp), log2(size_seq)
    bits = bits_dp + bits_seq
    dp, seq = lax.axis_index("dp"), lax.axis_index("seq")
    arrays = [a.reshape((2,) * bits + (-1,) + a.shape[1:]) for a in arrays]
    left = list(range(bits))
    for bit in [bits_dp - 1] + list(range(bits_dp, bits)) + list(range(bits_dp - 2, -1, -1)):
        axis = left.index(bit)
        left.remove(bit)
        if bit < bits_dp:
            name, size, step, me = "dp", size_dp, 2 ** (bits_dp - 1 - bit), dp
        else:
            name, size, step, me = "seq", size_seq, 2 ** (bits - 1 - bit), seq
        mine = me // step % 2
        pairs = [(i, i ^ step) for i in range(size)]
        sent = [
            lax.dynamic_index_in_dim(a, 1 - mine, axis, keepdims=False).astype(BF) for a in arrays
        ]
        kept = [lax.dynamic_index_in_dim(a, mine, axis, keepdims=False) for a in arrays]
        arrived = [lax.ppermute(v, name, pairs) for v in sent]
        arrays = [k + a.astype(F32) for k, a in zip(kept, arrived)]
    return arrays


class Halving:
    def __init__(self, net, links, groups, held, landing, source=None):
        self.net, self.groups, self.held, self.landing = net, groups, held, landing
        self.gone = groups[0] if source is not None else ()
        self.rounds = []
        for stage, group in enumerate(groups):
            copies = []
            for i, flips in enumerate(subsets(group)):
                copies.append(
                    links.copy(
                        functools.partial(self.part, stage, flips, source),
                        functools.partial(self.slot, stage, i),
                        functools.partial(net.partner, flips),
                    )
                )
            self.rounds.append(copies)

    def place(self, stage, turned):
        done, group = flat(self.groups[:stage]), self.groups[stage]
        at = []
        for bit, mine in enumerate(self.net.mine):
            if bit in done or bit in group:
                at.append(1 - mine if bit in turned else mine)
            else:
                at.append(slice(None))
        return tuple(at)

    def part(self, stage, flips, source):
        at = self.place(stage, flips)
        return source.at[at] if stage == 0 and source is not None else self.held.at[self.cut(at)]

    def slot(self, stage, i):
        return self.landing[stage].at[i]

    def cut(self, at):
        return tuple(a for bit, a in enumerate(at) if bit not in self.gone)

    def start(self, stage):
        start(self.rounds[stage])

    def add(self, stage, out=None):
        wait(self.rounds[stage])
        at = self.cut(self.place(stage, ()))
        free = [i for i, a in enumerate(at) if isinstance(a, slice)]
        landing = self.landing[stage]

        def one(flat_index, carry):
            inner = [lax.rem(flat_index // 2 ** (len(free) - 1 - i), 2) for i in range(len(free))]
            there = list(at)
            for axis, value in zip(free, inner):
                there[axis] = value
            there = tuple(there)
            value = self.held[there].astype(F32)
            for i in range(landing.shape[0]):
                value += landing[(i,) + tuple(inner)].astype(F32)
            if out is None:
                self.held[there] = value.astype(BF)
            else:
                out[...] = value
            return carry

        if free:
            lax.fori_loop(0, 2 ** len(free), one, 0)
        else:
            one(0, 0)


class Everywhere:
    def __init__(self, net, links, groups, value, sent, landing):
        self.value, self.sent, self.landing = value, sent, landing
        self.rounds = [
            [
                links.copy(
                    functools.partial(self.line, sent, stage),
                    functools.partial(self.line, landing, stage, i),
                    functools.partial(net.partner, flips),
                )
                for i, flips in enumerate(subsets(group))
            ]
            for stage, group in enumerate(groups)
        ]

    @staticmethod
    def line(ref, *at):
        return ref.at[at]

    def start(self, stage):
        self.sent[stage] = self.value[...]
        start(self.rounds[stage])

    def add(self, stage, out=None):
        wait(self.rounds[stage])
        for i in range(len(self.rounds[stage])):
            self.value[...] += self.landing[stage, i]


def landing_shapes(groups, bits, rows, width):
    shapes, left = [], bits
    for group in groups:
        left -= len(group)
        shapes.append(pltpu.VMEM((2 ** len(group) - 1,) + (2,) * left + (rows, width), BF))
    return shapes


def sum_orders(bits_dp, bits_seq):
    beside, upper, next_to, cores = stages_of(bits_dp, bits_seq)
    far = upper[::-1]
    if len(beside) == 1 and len(beside[0]) == 1:
        near = [beside[0] + next_to[0]]
    else:
        near = beside + next_to
    return cores + beside + next_to + far, cores + next_to + beside + far, cores + near + far


def project_kernel(tokens, weight, bias, query, pair):
    x = tokens[...]
    width = x.shape[1]
    query[...] = (dot(x, weight[:, :width]) + bias[:, :width]).astype(BF)
    pair[...] = (dot(x, weight[:, width:]) + bias[:, width:]).astype(BF)


def project(tokens, weight, bias):
    count, width = tokens.shape
    block = min(512, count)

    def moving(columns):
        return pl.BlockSpec((block, columns), lambda b: (b, 0))

    def still(*shape):
        return pl.BlockSpec(shape, lambda b: (0, 0), pipeline_mode=pl.Buffered(1))

    return pl.pallas_call(
        project_kernel,
        grid=(count // block,),
        in_specs=[moving(width), still(width, 3 * width), still(1, 3 * width)],
        out_specs=[moving(width), moving(2 * width)],
        out_shape=[
            jax.ShapeDtypeStruct((count, width), BF),
            jax.ShapeDtypeStruct((count, 2 * width), BF),
        ],
        compiler_params=params(40, 1),
        name="project",
    )(tokens, weight, bias)


def attend_kernel(parts, groups, steps, blocks, bits_dp, bits_seq, *refs):
    (
        lengths,
        query,
        keys_own,
        values_own,
        weight,
        vec,
        tokens_low,
        _,
        _,
        _,
        _,
        e_out,
        mixed,
        mixed_t,
        inverse,
        pair_rest,
        tokens_rest,
        up_w,
        down_w,
        out_w,
        k_mask,
        v_ext,
        kept,
        tops,
        rest_here,
        pair_here,
        own_sem,
        send_sem,
        recv_sem,
    ) = refs
    local = keys_own.shape[1]
    block = query.shape[1]
    step = pl.program_id(0)
    chunk = min(256, local)

    net = Net(bits_dp, bits_seq)
    links = Links(net, send_sem, recv_sem)
    beside, upper, next_to, cores = stages_of(bits_dp, bits_seq)
    order = beside + upper + next_to + cores
    first, last = len(beside), len(order)
    lead = len(upper)
    rounds = []
    for stage in range(first, last):
        copies = []
        for full in (down_w, out_w):
            copies += links.spread(full, flat(order[:stage]), order[stage])
        ahead = stage + lead
        if ahead < last:
            copies += links.spread(up_w, flat(order[:ahead]), order[ahead])
        rounds.append(copies)
    if len(rounds) > 3:
        times = [i * steps // (len(rounds) + 1) for i in range(len(rounds) + 1)]
    else:
        times = [0, steps * 6 // 16, steps * 12 // 16, steps * 14 // 16]
    exchange = []
    for g in range(1, groups):
        left = slice(local // AHEAD if g == 1 else 0, local)
        exchange.append(
            [
                links.copy(
                    functools.partial(Everywhere.line, tokens_low, g, left),
                    functools.partial(Everywhere.line, tokens_rest, other - 1, g, left),
                    functools.partial(ring, net, parts, other),
                )
                for other in range(1, parts)
            ]
        )

    @pl.when(step == 0)
    def enter():
        due = net.greet(order[first:])
        for other in range(1, parts):
            net.signal(ring(net, parts, other))
            due += 1
        pl.semaphore_wait(pltpu.get_barrier_semaphore(), due)
        for copies in exchange:
            start(copies)
        start(rounds[0])

    for i in range(len(rounds)):
        @pl.when(step == times[i + 1])
        def advance():
            wait(rounds[i])
            if i + 1 < len(rounds):
                start(rounds[i + 1])

    stores = [
        pltpu.make_async_copy(pair_here.at[:, g], pair_rest.at[:, g], own_sem.at[groups + g])
        for g in range(groups)
    ]
    for group in range(groups):
        @pl.when(step == group * blocks * PAIRS)
        def other_keys():
            if group > 0:
                wait(exchange[group - 1])
            copy = pltpu.make_async_copy(tokens_rest.at[:, group], rest_here, own_sem.at[group])
            copy.start()
            width = weight.shape[0]
            bias = jnp.concatenate([vec[11:12], vec[12:13]], axis=1)
            for part in range(parts):
                rows = slice(part * local, (part + 1) * local)
                first_key = lax.rem(net.seq + part, parts) * local
                place = lax.broadcasted_iota(jnp.int32, (local, WIDE), 0) + first_key
                k_mask[rows] = jnp.where(place < lengths[group], 0.0, -1e30).astype(BF)
            copy.wait()
            for part in range(1, parts):
                for p in range(PAIRS):
                    columns = slice(2 * WIDE * p, 2 * WIDE * (p + 1))
                    both = dot(rest_here[part - 1], weight[:, width:][:, columns])
                    pair_here[part - 1, group, p] = (both + bias[:, columns]).astype(BF)
            start(stores[group : group + 1])

    @pl.when(step == steps)
    def leave():
        wait(stores)

    def decode(t):
        return lax.div(t, PAIRS * blocks), lax.rem(lax.div(t, blocks), PAIRS)

    group_then, pair_then = decode(jnp.maximum(step - 1, 0))

    @pl.when(lax.rem(step, blocks) == 1 % blocks)
    def prepare_values():
        for part in range(parts):
            rows = slice(part * local, (part + 1) * local)
            if part == 0:
                values = values_own[0]
            else:
                values = pair_here[part - 1, group_then, pair_then, :, WIDE:]
            turned = values.T
            v_ext[0, :HEAD, rows] = turned[:HEAD]
            v_ext[1, :HEAD, rows] = turned[HEAD:]

    @pl.when(step == 0)
    def ones():
        v_ext[:, HEAD:] = jnp.ones((2, HEAD, parts * local), BF)

    group_now, pair_now = decode(jnp.minimum(step, steps - 1))

    turned = query[0].T
    zero = jnp.zeros((HEAD, block), BF)
    one = (lax.broadcasted_iota(jnp.int32, (WIDE, block), 0) == 0).astype(F32).astype(BF)
    heads = []
    for head in range(2):
        if head == 0:
            picked = jnp.concatenate([turned[:HEAD], zero, one], axis=0)
        else:
            picked = jnp.concatenate([zero, turned[HEAD:], one], axis=0)
        top = tops[head : head + 1]
        out = None
        largest = None
        for at in range(0, parts * local, chunk):
            rows = slice(at, at + chunk)
            inside = slice(at % local, at % local + chunk)
            e = jnp.exp2((kept[head, rows] - top) * (SCALE * LOG2E)).astype(BF)
            e_out[at // local, 0, head, inside] = e
            add = dot(v_ext[head, :, rows], e)
            out = add if out is None else out + add
            if at < local:
                keys = keys_own[0, inside]
            else:
                keys = pair_here[at // local - 1, group_now, pair_now, inside, :WIDE]
            scores = dot(jnp.concatenate([keys, k_mask[rows]], axis=1), picked)
            kept[head, rows] = scores
            most = jnp.max(scores.reshape(chunk // 8, 8, block), axis=0)
            largest = most if largest is None else jnp.maximum(largest, most)
        tops[head : head + 1] = jnp.max(largest, axis=0, keepdims=True)
        inv = 1.0 / out[HEAD : HEAD + 1]
        inverse[0, 0, head : head + 1] = inv
        heads.append(out[:HEAD] * inv)
    both = jnp.concatenate(heads, axis=0).astype(BF)
    mixed_t[0] = both
    mixed[0] = both.T


def attend(lengths, query, pair_own, weight, vec, tokens_low, tokens_rest, up_w, down_w, out_w):
    groups, local, width = query.shape
    others = tokens_rest.shape[0]
    parts = others + 1
    block = min(512, local)
    blocks = local // block
    steps = groups * PAIRS * blocks
    bits_dp, bits_seq = mesh_bits()
    beside, upper, next_to, cores = stages_of(bits_dp, bits_seq)
    sends = sum(2 ** len(group) - 1 for group in upper + next_to + cores)
    copies = 3 * sends + groups * others

    def decode(t, place):
        return place(
            lax.div(t, PAIRS * blocks), lax.rem(lax.div(t, blocks), PAIRS), lax.rem(t, blocks)
        )

    def now(place):
        return lambda t: decode(jnp.minimum(t, steps - 1), place)

    def before(place):
        return lambda t: decode(jnp.maximum(t - 1, 0), place)

    def still(*shape):
        return pl.BlockSpec(shape, lambda t: (0,) * len(shape), pipeline_mode=pl.Buffered(1))

    hbm = pl.BlockSpec(memory_space=pl.ANY)
    passed = (tokens_rest, up_w, down_w, out_w)
    return pl.pallas_call(
        functools.partial(attend_kernel, parts, groups, steps, blocks, bits_dp, bits_seq),
        grid=(steps + 1,),
        in_specs=[
            pl.BlockSpec(memory_space=pltpu.SMEM),
            pl.BlockSpec((1, block, WIDE), now(lambda g, p, b: (g, b, p))),
            pl.BlockSpec((1, local, WIDE), now(lambda g, p, b: (g, 0, 2 * p))),
            pl.BlockSpec((1, local, WIDE), before(lambda g, p, b: (g, 0, 2 * p + 1))),
            still(width, 3 * width),
            still(*vec.shape),
        ]
        + [hbm] * 5,
        out_specs=[
            pl.BlockSpec((parts, 1, 2, local, block), before(lambda g, p, b: (0, g, p, 0, b))),
            pl.BlockSpec((1, block, WIDE), before(lambda g, p, b: (g, b, p))),
            pl.BlockSpec((1, WIDE, block), before(lambda g, p, b: (g, p, b))),
            pl.BlockSpec((1, 1, 2, block), before(lambda g, p, b: (g, p, 0, b))),
            hbm,
        ]
        + [hbm] * 4,
        out_shape=[
            jax.ShapeDtypeStruct((parts, groups, H, local, local), BF),
            jax.ShapeDtypeStruct((groups, local, width), BF),
            jax.ShapeDtypeStruct((groups, width, local), BF),
            jax.ShapeDtypeStruct((groups, PAIRS, 2, local), F32),
            jax.ShapeDtypeStruct((others, groups, PAIRS, local, 2 * WIDE), BF),
        ]
        + [jax.ShapeDtypeStruct(v.shape, v.dtype) for v in passed],
        input_output_aliases={7: 5, 8: 6, 9: 7, 10: 8},
        scratch_shapes=[
            pltpu.VMEM((parts * local, WIDE), BF),
            pltpu.VMEM((2, WIDE, parts * local), BF),
            pltpu.VMEM((2, parts * local, block), F32),
            pltpu.VMEM((8, block), F32),
            pltpu.VMEM((others, local, width), BF),
            pltpu.VMEM((others, groups, PAIRS, local, 2 * WIDE), BF),
            pltpu.SemaphoreType.DMA((2 * groups,)),
            pltpu.SemaphoreType.DMA((copies,)),
            pltpu.SemaphoreType.DMA((copies,)),
        ],
        compiler_params=pltpu.CompilerParams(
            vmem_limit_bytes=62 * MIB,
            dimension_semantics=("arbitrary",),
            collective_id=1,
            has_side_effects=True,
        ),
        name="attend",
    )(lengths, query, pair_own, pair_own, weight, vec, tokens_low, *passed)


def middle_kernel(
    packed,
    tokens,
    cotangent,
    mixed,
    out_w,
    up_w,
    down_w,
    rows,
    result,
    partial,
    mixed_grad,
    upper_sums,
    lower_sums,
    vec_sums,
    out_wg,
    up_wg,
    down_wg,
    row_sums,
    up_bias_sum,
):
    first = pl.program_id(0) == 0

    @pl.when(first)
    def clear():
        out_wg[...] = jnp.zeros_like(out_wg)
        up_wg[...] = jnp.zeros_like(up_wg)
        down_wg[...] = jnp.zeros_like(down_wg)
        row_sums[...] = jnp.zeros_like(row_sums)
        up_bias_sum[...] = jnp.zeros_like(up_bias_sum)

    pieces = up_w.shape[1] // tokens.shape[1]
    up_bias = jnp.concatenate([rows[6 + i : 7 + i] for i in range(pieces)], axis=1)
    out_bias, gain_one, shift_one = rows[0:1], rows[1:2], rows[2:3]
    down_bias, gain_two, shift_two = rows[3:4], rows[4:5], rows[5:6]

    def mean(v):
        return jnp.mean(v, axis=-1, keepdims=True)

    def total(v):
        return jnp.sum(v, axis=0, keepdims=True)

    x = tokens[...]
    heads = mixed[...]
    hidden = x + (dot(heads, out_w[...]) + out_bias)
    centred = hidden - mean(hidden)
    r_one = lax.rsqrt(mean(centred * centred) + EPS)
    n_one = centred * r_one
    normal = n_one * gain_one + shift_one
    normal_low = normal.astype(BF)
    inner = dot(normal_low, up_w[...]) + up_bias
    square = inner * inner
    tanh = jnp.tanh(inner * (GELU_A + (GELU_A * GELU_B) * square))
    half = 0.5 + 0.5 * tanh
    active = (inner * half).astype(BF)
    slope = half + (0.5 * inner) * (1.0 - tanh * tanh) * (
        GELU_A + (3.0 * GELU_A * GELU_B) * square
    )
    branch = dot(active, down_w[...]) + down_bias
    last = normal + branch + x
    centred = last - mean(last)
    r_two = lax.rsqrt(mean(centred * centred) + EPS)
    n_two = centred * r_two
    result[...] = n_two * gain_two + shift_two
    grad = cotangent[...]
    e_two = grad * gain_two
    back = r_two * (e_two - mean(e_two) - n_two * mean(e_two * n_two))
    branch_grad = back.astype(BF)
    down_wg[...] += dot(active, branch_grad, "tn")
    inner_grad_wide = slope * dot(branch_grad, down_w[...], "nt")
    inner_grad = inner_grad_wide.astype(BF)
    up_wg[...] += dot(normal_low, inner_grad, "tn")
    up_bias_sum[...] += total(inner_grad.astype(F32))
    norm_grad = back + dot(inner_grad, up_w[...], "nt")
    e_one = norm_grad * gain_one
    hidden_grad = r_one * (e_one - mean(e_one) - n_one * mean(e_one * n_one))
    attn_grad = hidden_grad.astype(BF)
    partial[...] = back + hidden_grad
    out_wg[...] += dot(heads, attn_grad, "tn")
    mixed_grad[...] = dot(attn_grad, out_w[...], "nt").astype(BF)
    row_sums[0:1] += total(attn_grad.astype(F32))
    row_sums[1:2] += total(norm_grad * n_one)
    row_sums[2:3] += total(norm_grad)
    row_sums[3:4] += total(branch_grad.astype(F32))
    row_sums[4:5] += total(grad * n_two)
    row_sums[5:6] += total(grad)

    @pl.when(pl.program_id(0) == pl.num_programs(0) - 1)
    def pack():
        width = tokens.shape[1]
        pieces = up_wg.shape[1] // width
        vec_sums[...] = jnp.zeros_like(vec_sums)
        vec_sums[0:8] = row_sums[...]
        for piece in range(pieces):
            columns = slice(piece * width, (piece + 1) * width)
            vec_sums[8 + piece : 9 + piece] = up_bias_sum[:, columns]
        if not packed:
            upper_sums[:, :width] = out_wg[...]
            upper_sums[:, width:] = up_wg[...]
            lower_sums[...] = down_wg[...]
            return
        owners = upper_sums.shape[0]
        rows_out = out_wg.shape[0] // owners
        rows_down = down_wg.shape[0] // owners

        def one(owner, carry):
            near = pl.ds(pl.multiple_of(owner * rows_out, rows_out), rows_out)
            upper_sums[owner, :rows_out] = out_wg[near].astype(BF)
            for piece in range(pieces):
                columns = slice(piece * width, (piece + 1) * width)
                to = slice((piece + 1) * rows_out, (piece + 2) * rows_out)
                upper_sums[owner, to] = up_wg[near, columns].astype(BF)
            far = pl.ds(pl.multiple_of(owner * rows_down, rows_down), rows_down)
            lower_sums[owner] = down_wg[far].astype(BF)
            return carry

        lax.fori_loop(0, owners, one, 0)


def middle(tokens, cotangent, mixed, out_w, up_w, down_w, rows, owners):
    count, width = tokens.shape
    hidden = up_w.shape[1]
    block = min(512, count)
    packed = whole_tiles(width, owners)

    def moving(columns=width):
        return pl.BlockSpec((block, columns), lambda b: (b, 0))

    def still(*shape):
        return pl.BlockSpec(shape, lambda b: (0,) * len(shape), pipeline_mode=pl.Buffered(1))

    rows_upper = width // owners * (1 + hidden // width)
    rows_lower = hidden // owners
    if packed:
        sums = [((owners, rows_upper, width), BF), ((owners, rows_lower, width), BF)]
    else:
        sums = [((width, width + hidden), F32), ((hidden, width), F32)]
    return pl.pallas_call(
        functools.partial(middle_kernel, packed),
        grid=(count // block,),
        in_specs=[
            moving(),
            moving(),
            moving(),
            still(width, width),
            still(width, hidden),
            still(hidden, width),
            still(16, width),
        ],
        out_specs=[
            moving(),
            moving(),
            moving(),
        ]
        + [still(*shape) for shape, _ in sums]
        + [still(16, width)],
        out_shape=[
            jax.ShapeDtypeStruct((count, width), F32),
            jax.ShapeDtypeStruct((count, width), F32),
            jax.ShapeDtypeStruct((count, width), BF),
        ]
        + [jax.ShapeDtypeStruct(shape, kind) for shape, kind in sums]
        + [jax.ShapeDtypeStruct((16, width), F32)],
        scratch_shapes=[
            pltpu.VMEM((width, width), F32),
            pltpu.VMEM((width, hidden), F32),
            pltpu.VMEM((hidden, width), F32),
            pltpu.VMEM((8, width), F32),
            pltpu.VMEM((1, hidden), F32),
        ],
        compiler_params=params(62, 1),
        name="middle",
    )(tokens, cotangent, mixed, out_w, up_w, down_w, rows)


def pull_kernel(parts, groups, bits_dp, bits_seq, packed, *refs):
    taken = 0

    def take(count):
        nonlocal taken
        taken += count
        return refs[taken - count : taken]

    e_part, query, pair_own, pair_rest, mixed_grad, mixed_t, inverse = take(7)
    tokens_t, tokens_rest, weight, partial = take(4)
    sources = take(2) if packed else ()
    (vec_in,) = take(1)
    share_own, arrived, joint_out, vec_out = take(4)
    owned = take(2) if packed else ()
    d_scores, joint_grad, total, dq_sums, dq_turned, weight_grad, bias_grad, shares = take(8)
    share_send, share_recv, own_sem = take(3)
    step = pl.program_id(0)
    steps = pl.num_programs(0)
    each = groups * PAIRS
    part = lax.rem(lax.div(step, each) + 1, parts)
    own = part == 0
    inside = lax.rem(step, each)
    group = jnp.where(own, lax.rem(inside, groups), lax.div(inside, PAIRS))
    pair = jnp.where(own, lax.div(inside, groups), lax.rem(inside, PAIRS))

    net = Net(bits_dp, bits_seq)
    bits = net.bits
    orders = sum_orders(bits_dp, bits_seq)
    streams, loads = [], []
    if packed:
        upper_held, lower_held = take(2)
        joint_helds = take(len(JOINT_PARTS))
        vec_sent, vec_landing, bias_sent, bias_landing = take(4)
        send_sem, recv_sem = take(2)
        links = Links(net, send_sem, recv_sem)
        upper, lower = streams = [
            Halving(net, links, orders[i], held, take(len(orders[i])), sources[i])
            for i, held in enumerate((upper_held, lower_held))
        ]
        joint = [Halving(net, links, orders[2], h, take(len(orders[2]))) for h in joint_helds]
        early_vec = Everywhere(net, links, orders[2], vec_out.at[0:16], vec_sent, vec_landing)
        late_vec = Everywhere(net, links, orders[2], bias_grad, bias_sent, bias_landing)
        for i, stream in enumerate(streams):
            at = stream.place(0, ())
            loads.append(pltpu.make_async_copy(sources[i].at[at], stream.held, own_sem.at[i]))
    stores = [
        pltpu.make_async_copy(total.at[g], share_own.at[g], own_sem.at[2 + g])
        for g in range(groups)
    ]
    partials = [
        pltpu.make_async_copy(partial.at[g], total.at[g], own_sem.at[2 + groups + g])
        for g in range(groups)
    ]

    def share_copy(other, g):
        return pltpu.make_async_remote_copy(
            src_ref=shares.at[other - 1, g],
            dst_ref=arrived.at[other - 1, g],
            send_sem=share_send.at[other - 1, g],
            recv_sem=share_recv.at[other - 1, g],
            device_id=(net.dp, lax.rem(net.seq + other, parts)),
            device_id_type=MESH,
        )

    @pl.when(step == 0)
    def enter():
        due = parts - 1
        for other in range(1, parts):
            net.signal((net.dp, lax.rem(net.seq + other, parts)))
        if packed:
            due += net.greet(orders[0]) + net.greet(orders[2])
        start(loads)
        start(partials)
        pl.semaphore_wait(pltpu.get_barrier_semaphore(), due)
        for stream in streams:
            stream.start(0)

    def advance(streams, stage, outs, count):
        for stream, out in zip(streams, outs):
            stream.add(stage, out if stage == count - 1 else None)
            if stage < count - 1:
                stream.start(stage + 1)

    def pack(index):
        first, count = JOINT_PARTS[index]
        held = joint[index].held
        rows_each, width = weight_grad.shape[0] // 2**bits, weight_grad.shape[0]
        columns = slice(first * WIDE, (first + count) * WIDE)
        doubled = slice(width + 2 * first * WIDE, width + 2 * (first + count) * WIDE)

        def one(flat_index, carry):
            place = tuple(lax.rem(flat_index // 2 ** (bits - 1 - i), 2) for i in range(bits))
            near = pl.ds(pl.multiple_of(flat_index * rows_each, rows_each), rows_each)
            held[place + (slice(None), slice(0, count * WIDE))] = weight_grad[near, columns].astype(BF)
            held[place + (slice(None), slice(count * WIDE, 3 * count * WIDE))] = weight_grad[
                near, doubled
            ].astype(BF)
            return carry

        lax.fori_loop(0, 2**bits, one, 0)

    def joint_place(index):
        first, count = JOINT_PARTS[index]
        return joint_out.at[:, 3 * first * WIDE : 3 * (first + count) * WIDE]

    if packed:
        last = len(orders[2])
        for stage, when in enumerate((1, 5, 9, 12)):
            @pl.when(step == when)
            def ffn():
                if stage == 0:
                    wait(loads)
                advance(streams, stage, owned, len(orders[0]))

        @pl.when(step == steps - 2 * groups)
        def joint_early():
            pack(0)
            vec_out[...] = vec_in[...]
            joint[0].start(0)
            early_vec.start(0)

        @pl.when(step == steps - 2 * groups + 1)
        def joint_early_near():
            advance((joint[0], early_vec), 0, (None, None), last)

        @pl.when(step == steps - groups)
        def joint_middle():
            pack(1)
            joint[1].start(0)

        @pl.when(step == steps - 1)
        def joint_middle_near():
            advance((joint[0], early_vec), 1, (None, None), last)
            advance((joint[1],), 0, (None,), last)

    local = query.shape[1]
    chunk = min(256, local)
    turned = mixed_grad[0].astype(F32).T
    mixed = mixed_t[0].astype(F32)
    values = jnp.where(own, pair_own[0, :, WIDE:], pair_rest[0, 0, 0, :, WIDE:])
    keys_t = jnp.where(own, pair_own[0, :, :WIDE], pair_rest[0, 0, 0, :, :WIDE]).T
    query_now = query[0]
    lane = lax.broadcasted_iota(jnp.int32, (local, WIDE), 1)
    zero = jnp.zeros((HEAD, local), BF)
    grad_t, grad, centre, picked = [], [], [], []
    for head in range(2):
        side = slice(head * HEAD, (head + 1) * HEAD)
        inv = inverse[0, 0, head : head + 1]
        centre.append(inv * jnp.sum(turned[side] * mixed[side], axis=0, keepdims=True))
        scaled = (turned[side] * inv).astype(BF)
        grad_t.append(jnp.concatenate([scaled, zero] if head == 0 else [zero, scaled], axis=0))
        grad.append(grad_t[head].T)
        kept = lane < HEAD if head == 0 else lane >= HEAD
        picked.append(jnp.where(kept, query_now, jnp.zeros_like(query_now)))

    width = weight.shape[0]
    at_queries = pl.ds(pl.multiple_of(pair * WIDE, WIDE), WIDE)
    start_at = width + pair * (2 * WIDE)
    at_keys = pl.ds(pl.multiple_of(start_at, WIDE), WIDE)
    at_values = pl.ds(pl.multiple_of(start_at + WIDE, WIDE), WIDE)
    at_both = pl.ds(pl.multiple_of(start_at, WIDE), 2 * WIDE)

    def key_grad(rows):
        sums = dot(d_scores[0, rows], picked[0]) + dot(d_scores[1, rows], picked[1])
        joint_grad[group, rows, at_keys] = (sums * SCALE).astype(BF)

    last_rows = None
    for at in range(0, local, chunk):
        rows = slice(at, at + chunk)
        for head in range(2):
            pulled = dot(values[rows], grad_t[head])
            e = e_part[0, 0, head, rows].astype(F32)
            d_scores[head, rows] = (e * (pulled - centre[head])).astype(BF)
        sums = dot(e_part[0, 0, 0, rows], grad[0]) + dot(e_part[0, 0, 1, rows], grad[1])
        joint_grad[group, rows, at_values] = sums.astype(BF)
        if last_rows is not None:
            key_grad(last_rows)
        last_rows = rows
    key_grad(last_rows)
    for head in range(2):
        side = slice(head * HEAD, (head + 1) * HEAD)
        dq = dot(keys_t, d_scores[head])[side]
        dq_turned[side] = dq

    @pl.when(step == 0)
    def clear():
        weight_grad[...] = jnp.zeros_like(weight_grad)
        bias_grad[...] = jnp.zeros_like(bias_grad)
        dq_sums[...] = jnp.zeros_like(dq_sums)

    column = group * PAIRS + pair

    @pl.when(own)
    def near():
        dq = (dq_sums[column] + dq_turned[...]) * SCALE
        dq = dq.T.astype(BF)
        joint_grad[group, :, at_queries] = dq
        bias_grad[0:1, at_queries] += jnp.sum(dq.astype(F32), axis=0, keepdims=True)
        weight_grad[:, at_queries] += dot(tokens_t[group], dq)
        weight_grad[:, at_both] += dot(tokens_t[group], joint_grad[group, :, at_both])

    @pl.when(jnp.logical_not(own))
    def far():
        dq_sums[column] += dq_turned[...]

    value_sums = jnp.sum(joint_grad[group, :, at_values].astype(F32), axis=0, keepdims=True)
    bias_grad[1:2, at_queries] += value_sums

    for other in range(1, parts):
        for g in range(groups):
            @pl.when(step == ((other - 1) * groups + g + 1) * PAIRS - 1)
            def finish_far():
                for at in range(0, local, chunk):
                    rows = slice(at, at + chunk)
                    part_share = dot(joint_grad[g, rows, width:], weight[:, width:], "nt")
                    shares[other - 1, g, rows] = part_share.astype(BF)
                share_copy(other, g).start()
                weight_grad[:, width:] += dot(tokens_rest[0, 0], joint_grad[g, :, width:], "tn")

    def input_grads(g):
        for at in range(0, local, chunk):
            rows = slice(at, at + chunk)
            total[g, rows] += dot(joint_grad[g, rows], weight[...], "nt")
        start(stores[g : g + 1])

    @pl.when(step == steps - 1)
    def finish():
        work = list(range(groups))
        if packed:
            pack(2)
            joint[2].start(0)
            late_vec.start(0)
            advance((joint[1],), 1, (None,), last)
        wait(partials)
        if packed:
            for stage in range(last):
                if work:
                    input_grads(work.pop(0))
                outs = (joint_place(2), None)
                advance((joint[2], late_vec), stage, outs, last)
                if stage == 0:
                    advance((joint[0], early_vec), last - 1, (joint_place(0), None), last)
            joint[1].add(last - 1, joint_place(1))
        else:
            vec_out[...] = vec_in[...]
            joint_out[...] = weight_grad[...]
        for g in work:
            input_grads(g)
        vec_out[12:14] = bias_grad[0:2]
        for g in range(groups):
            for other in range(1, parts):
                share_copy(other, g).wait()
        wait(stores)


def pull(
    e_all,
    query,
    pair_own,
    pair_rest,
    mixed_grad,
    mixed_t,
    inverse,
    own,
    rest,
    weight,
    partial,
    upper_sums,
    lower_sums,
    vec_sums,
):
    parts, groups, _, local, _ = e_all.shape
    width = H * HEAD
    each = groups * PAIRS
    bits_dp, bits_seq = mesh_bits()
    bits = bits_dp + bits_seq
    orders = sum_orders(bits_dp, bits_seq)
    packed = whole_tiles(width, 2**bits)
    split = (2,) * bits
    sums, out_blocks, extra = [], [], []
    if packed:
        rows_upper, rows_lower = upper_sums.shape[1], lower_sums.shape[1]
        rows_joint = width // 2**bits
        sums = [v.reshape(split + v.shape[1:]) for v in (upper_sums, lower_sums)]
        out_blocks = [(rows_joint, 3 * width), (16, width), (rows_upper, width), (rows_lower, width)]
        joint_widths = [3 * count * WIDE for _, count in JOINT_PARTS]
        last = len(orders[2])
        sends = sum(2 ** len(g) - 1 for order in orders for g in order)
        sends += 4 * sum(2 ** len(g) - 1 for g in orders[2])
        extra = [
            pltpu.VMEM((2,) * (bits - 1) + (rows_upper, width), BF),
            pltpu.VMEM((2,) * (bits - 1) + (rows_lower, width), BF),
        ]
        extra += [pltpu.VMEM(split + (rows_joint, columns), BF) for columns in joint_widths]
        extra += [
            pltpu.VMEM((last, 16, width), F32),
            pltpu.VMEM((last, 3, 16, width), F32),
            pltpu.VMEM((last, 8, width), F32),
            pltpu.VMEM((last, 3, 8, width), F32),
            pltpu.SemaphoreType.DMA((sends,)),
            pltpu.SemaphoreType.DMA((sends,)),
        ]
        extra += landing_shapes(orders[0], bits, rows_upper, width)
        extra += landing_shapes(orders[1], bits, rows_lower, width)
        for columns in joint_widths:
            extra += landing_shapes(orders[2], bits, rows_joint, columns)
    else:
        out_blocks = [(width, 3 * width), (16, width)]

    def decode(t):
        part, inside = lax.rem(lax.div(t, each) + 1, parts), lax.rem(t, each)
        own = part == 0
        group = jnp.where(own, lax.rem(inside, groups), lax.div(inside, PAIRS))
        pair = jnp.where(own, lax.div(inside, groups), lax.rem(inside, PAIRS))
        return part, group, pair

    def at(place):
        return lambda t: place(*decode(t))

    def own_at(place):
        def index(t):
            part, group, pair = decode(t)
            return place(jnp.where(part == 0, group, 0), jnp.where(part == 0, pair, 0))

        return index

    def rest_at(place):
        def index(t):
            t = jnp.minimum(t, (parts - 1) * each - 1)
            return place(
                lax.div(t, each), lax.rem(lax.div(t, PAIRS), groups), lax.rem(t, PAIRS)
            )

        return index

    def still(*shape):
        return pl.BlockSpec(shape, lambda t: (0,) * len(shape), pipeline_mode=pl.Buffered(1))

    once = pl.Buffered(1)
    return pl.pallas_call(
        functools.partial(pull_kernel, parts, groups, bits_dp, bits_seq, packed),
        grid=(parts * each,),
        in_specs=[
            pl.BlockSpec((1, 1, 2, local, local), at(lambda j, g, p: (j, g, p, 0, 0))),
            pl.BlockSpec((1, local, WIDE), at(lambda j, g, p: (g, 0, p))),
            pl.BlockSpec((1, local, 2 * WIDE), own_at(lambda g, p: (g, 0, p))),
            pl.BlockSpec((1, 1, 1, local, 2 * WIDE), rest_at(lambda j, g, p: (j, g, p, 0, 0))),
            pl.BlockSpec((1, local, WIDE), at(lambda j, g, p: (g, 0, p))),
            pl.BlockSpec((1, WIDE, local), at(lambda j, g, p: (g, p, 0))),
            pl.BlockSpec((1, 1, 2, local), at(lambda j, g, p: (g, p, 0, 0))),
            still(groups, width, local),
            pl.BlockSpec(
                (1, 1, local, width), rest_at(lambda j, g, p: (j, g, 0, 0)), pipeline_mode=once
            ),
            still(width, 3 * width),
            pl.BlockSpec(memory_space=pl.ANY),
        ]
        + [pl.BlockSpec(memory_space=pl.ANY)] * len(sums)
        + [still(16, width)],
        out_specs=[
            pl.BlockSpec(memory_space=pl.ANY),
            pl.BlockSpec(memory_space=pl.ANY),
        ]
        + [still(*shape) for shape in out_blocks],
        out_shape=[
            jax.ShapeDtypeStruct((groups, local, width), F32),
            jax.ShapeDtypeStruct((parts - 1, groups, local, width), BF),
        ]
        + [jax.ShapeDtypeStruct(shape, F32) for shape in out_blocks],
        scratch_shapes=[
            pltpu.VMEM((2, local, local), BF),
            pltpu.VMEM((groups, local, 3 * width), BF),
            pltpu.VMEM((groups, local, width), F32),
            pltpu.VMEM((each, WIDE, local), F32),
            pltpu.VMEM((WIDE, local), F32),
            pltpu.VMEM((width, 3 * width), F32),
            pltpu.VMEM((8, width), F32),
            pltpu.VMEM((parts - 1, groups, local, width), BF),
            pltpu.SemaphoreType.DMA((parts - 1, groups)),
            pltpu.SemaphoreType.DMA((parts - 1, groups)),
            pltpu.SemaphoreType.DMA((2 + 2 * groups,)),
        ]
        + extra,
        compiler_params=pltpu.CompilerParams(
            vmem_limit_bytes=63 * MIB,
            dimension_semantics=("arbitrary",),
            collective_id=2,
            has_side_effects=True,
        ),
        name="pull",
    )(
        e_all,
        query,
        pair_own,
        pair_rest,
        mixed_grad,
        mixed_t,
        inverse,
        own,
        rest,
        weight,
        partial,
        *sums,
        vec_sums,
    )


def finish_kernel(bits_dp, bits_seq, share, arrived, joint, vec, upper, lower, *outs):
    (
        input_grad,
        joint_sum,
        pair_sum,
        out_sum,
        out_bias,
        gain_one,
        shift_one,
        up_sum,
        up_bias,
        down_sum,
        down_bias,
        gain_two,
        shift_two,
    ) = outs
    value = share[...]
    for other in range(arrived.shape[0]):
        value += arrived[other].astype(F32)
    input_grad[...] = value

    @pl.when(pl.program_id(0) == 0)
    def small():
        net = Net(bits_dp, bits_seq)
        device = net.dp * 2**bits_seq + net.seq
        rows, width = out_sum.shape
        summed = joint[...]
        turned = []
        for head in range(H):
            pair = head // 2
            for first, count in JOINT_PARTS:
                if first <= pair < first + count:
                    base = 3 * first * WIDE + head % 2 * HEAD
                    both = base + (count + 2 * (pair - first)) * WIDE
                    for at in (base + (pair - first) * WIDE, both, both + WIDE):
                        turned.append(summed[:, at : at + HEAD])
        joint_sum[...] = jnp.concatenate(turned, axis=1)
        out_sum[...] = upper[:rows]
        for piece in range(up_sum.shape[1] // width):
            up_sum[:, piece * width : (piece + 1) * width] = upper[
                (piece + 1) * rows : (piece + 2) * rows
            ]
        down_sum[...] = lower[...]
        lines = vec[...]
        which = lax.broadcasted_iota(jnp.int32, lines.shape, 0)

        def entries(out, row, column):
            line = jnp.sum(jnp.where(which == row, lines, 0.0), axis=0, keepdims=True)
            line = jnp.broadcast_to(line, (8, width))
            out[...] = pltpu.roll(line, lax.rem(width - column, width), 1)[:1, : out.shape[1]]

        plain = (out_bias, gain_one, shift_one, down_bias, gain_two, shift_two)
        for row, out in enumerate(plain):
            entries(out, row, device * out.shape[1])
        first = device * up_bias.shape[1]
        entries(up_bias, 8 + first // width, lax.rem(first, width))
        first = device * pair_sum.shape[1]
        kind = lax.rem(first // HEAD, 2)
        entries(pair_sum, 12 + kind, first // WIDE * HEAD + lax.rem(first, HEAD))


def finish(share, arrived, joint, vec, upper, lower, shards):
    groups, local, width = share.shape
    block = min(512, local)
    each = local // block

    def moving(*lead):
        return pl.BlockSpec(
            (1,) * len(lead) + (block, width), lambda b: (b // each, b % each, 0)
        )

    def still(shape):
        return pl.BlockSpec(shape, lambda b: (0,) * len(shape), pipeline_mode=pl.Buffered(1))

    bits_dp, bits_seq = mesh_bits()
    others = arrived.shape[0]
    small = (joint, vec, upper, lower)
    outs = pl.pallas_call(
        functools.partial(finish_kernel, bits_dp, bits_seq),
        grid=(groups * each,),
        in_specs=[
            moving(1),
            pl.BlockSpec((others, 1, block, width), lambda b: (0, b // each, b % each, 0)),
        ]
        + [still(v.shape) for v in small],
        out_specs=[moving(1)] + [still(shape) for shape in shards],
        out_shape=[jax.ShapeDtypeStruct(share.shape, F32)]
        + [jax.ShapeDtypeStruct(shape, F32) for shape in shards],
        compiler_params=params(62, 1),
        name="finish",
    )(share, arrived, *small)
    return [outs[0]] + [
        v.reshape(v.shape[1:]) if v.shape[0] == 1 else v for v in outs[1:]
    ]


def per_device(
    tokens,
    lengths,
    joint_weight,
    joint_bias,
    out_weight,
    out_bias,
    gain_first,
    shift_first,
    up_weight,
    up_bias,
    down_weight,
    down_bias,
    gain_second,
    shift_second,
    cotangent,
):
    groups, local, width = tokens.shape
    parts = lax.axis_size("seq")
    devices = lax.axis_size("dp") * parts
    me = lax.axis_index("seq")
    rows = groups * local
    own_rows = joint_weight.shape[0]
    vectors = [
        joint_bias,
        out_bias,
        gain_first,
        shift_first,
        up_bias,
        down_bias,
        gain_second,
        shift_second,
    ]
    lens = [v.shape[0] for v in vectors]
    tokens_low, tokens_t, tokens_rest, joint_w, vec, up_w, down_w, out_w, query, pair_own = begin(
        tokens,
        joint_weight,
        up_weight,
        down_weight,
        out_weight,
        [v.reshape(1, -1) for v in vectors],
        parts,
    )
    joint_w = matrix_of(joint_w)
    pieces = up_weight.shape[1] // width
    if not whole_tiles(width, devices):
        query, pair_own = project(
            tokens_low.reshape(rows, width), joint_w, vec[10:13].reshape(1, -1)
        )
        query = query.reshape(groups, local, width)
        pair_own = pair_own.reshape(groups, local, 2 * width)

    e_all, mixed, mixed_t, inverse, pair_rest, tokens_rest, up_w, down_w, out_w = attend(
        lengths, query, pair_own, joint_w, vec, tokens_low, tokens_rest, up_w, down_w, out_w
    )
    out_w, up_w, down_w = matrix_of(out_w), matrix_of(up_w), matrix_of(down_w)

    result, partial, mixed_grad, upper_sums, lower_sums, vec_sums = middle(
        tokens.reshape(rows, width),
        cotangent.reshape(rows, width),
        mixed.reshape(rows, width),
        out_w,
        up_w,
        down_w,
        vec,
        devices,
    )
    mixed_grad = mixed_grad.reshape(groups, local, width)
    share, arrived, joint, vec, *owned = pull(
        e_all,
        query,
        pair_own,
        pair_rest,
        mixed_grad,
        mixed_t,
        inverse,
        tokens_t,
        tokens_rest,
        joint_w,
        partial.reshape(groups, local, width),
        upper_sums,
        lower_sums,
        vec_sums,
    )
    if owned:
        upper, lower = owned
        shards = [
            (1, v.shape[0]) if v.ndim == 1 else v.shape
            for v in (
                joint_weight,
                joint_bias,
                out_weight,
                out_bias,
                gain_first,
                shift_first,
                up_weight,
                up_bias,
                down_weight,
                down_bias,
                gain_second,
                shift_second,
            )
        ]
        outs = finish(share, arrived, joint, vec, upper, lower, shards)
        return (result.reshape(groups, local, width), *outs)
    input_grad = share + jnp.sum(arrived.astype(F32), axis=0)
    joint_sum, upper, lower = owner_sums([joint, upper_sums, lower_sums])
    out_sum, up_sum = upper[:, :width], upper[:, width:]
    vec = lax.psum(vec, ("dp", "seq"))
    device = lax.axis_index("dp") * parts + me
    back = [joint_columns().index(block) for block in range(3 * H)]
    joint_sum = joint_sum.reshape(own_rows, 3 * H, HEAD)
    joint_sum = jnp.stack([joint_sum[:, b] for b in back], axis=1).reshape(own_rows, 3 * width)
    pair_grad = jnp.stack(
        [vec[12].reshape(H, HEAD), vec[13].reshape(H, HEAD)], axis=1
    ).reshape(2 * width)
    sums = [
        pair_grad,
        vec[0],
        vec[1],
        vec[2],
        vec[8 : 8 + pieces].reshape(-1),
        vec[3],
        vec[4],
        vec[5],
    ]
    small = [
        lax.dynamic_slice_in_dim(v, device * size, size, 0) for v, size in zip(sums, lens)
    ]
    return (
        result.reshape(groups, local, width),
        input_grad,
        joint_sum,
        small[0],
        out_sum,
        small[1],
        small[2],
        small[3],
        up_sum,
        small[4],
        lower,
        small[5],
        small[6],
        small[7],
    )


def solution(mesh):
    both = ("dp", "seq")
    matrix, vector, whole = P(both, None), P(both), P("dp", "seq", None)
    return jax.shard_map(
        per_device,
        mesh=mesh,
        in_specs=(
            whole,
            P("dp"),
            matrix,
            vector,
            matrix,
            vector,
            vector,
            vector,
            matrix,
            vector,
            matrix,
            vector,
            vector,
            vector,
            whole,
        ),
        out_specs=(
            whole,
            whole,
            matrix,
            vector,
            matrix,
            vector,
            vector,
            vector,
            matrix,
            vector,
            matrix,
            vector,
            vector,
            vector,
        ),
        check_vma=False,
    )
```

```python
import functools
import math

import jax
import jax.numpy as jnp
from jax import lax
from jax.experimental import pallas as pl
from jax.experimental.pallas import tpu as pltpu
from jax.sharding import PartitionSpec as P

H = 8
HEAD = 64
PAIRS = H // 2
WIDE = 2 * HEAD
JOINT_PARTS = ((0, 2), (2, 1), (3, 1))
AHEAD = 16
BF = jnp.bfloat16
F32 = jnp.float32
EPS = 1e-05
SCALE = 1.0 / math.sqrt(HEAD)
LOG2E = math.log2(math.e)
GELU_A = math.sqrt(2.0 / math.pi)
GELU_B = 0.044715
MESH = pl.DeviceIdType.MESH
MIB = 2**20
FORMS = {
    "nn": (((1,), (0,)), ((), ())),
    "nt": (((1,), (1,)), ((), ())),
    "tn": (((0,), (0,)), ((), ())),
}


def dot(left, right, form="nn"):
    return lax.dot_general(left, right, FORMS[form], preferred_element_type=F32)


def whole_tiles(width, devices):
    return width // devices % 16 == 0


def params(limit, steps):
    return pltpu.CompilerParams(
        vmem_limit_bytes=limit * MIB, dimension_semantics=("arbitrary",) * steps
    )


def log2(size):
    return size.bit_length() - 1


class Net:
    def __init__(self, bits_dp, bits_seq):
        self.bits_dp, self.bits_seq = bits_dp, bits_seq
        self.bits = bits_dp + bits_seq
        self.dp, self.seq = lax.axis_index("dp"), lax.axis_index("seq")
        self.mine = [lax.rem(lax.div(self.dp, 2 ** (bits_dp - 1 - b)), 2) for b in range(bits_dp)]
        self.mine += [lax.rem(lax.div(self.seq, 2 ** (bits_seq - 1 - b)), 2) for b in range(bits_seq)]

    def partner(self, flips):
        dp, seq = self.dp, self.seq
        for bit in flips:
            turn = 1 - 2 * self.mine[bit]
            if bit < self.bits_dp:
                dp = dp + turn * 2 ** (self.bits_dp - 1 - bit)
            else:
                seq = seq + turn * 2 ** (self.bits - 1 - bit)
        return (dp, seq)

    def place(self, done, turned=()):
        at = []
        for bit in range(self.bits):
            if bit in done:
                at.append(slice(None))
            else:
                at.append(1 - self.mine[bit] if bit in turned else self.mine[bit])
        return tuple(at)

    def signal(self, device):
        pl.semaphore_signal(
            pltpu.get_barrier_semaphore(), inc=1, device_id=device, device_id_type=MESH
        )

    def greet(self, groups):
        count = 0
        for group in groups:
            for flips in subsets(group):
                self.signal(self.partner(flips))
                count += 1
        return count


def subsets(group):
    return [
        tuple(b for i, b in enumerate(group) if pick >> i & 1)
        for pick in range(1, 2 ** len(group))
    ]


def stages_of(bits_dp, bits_seq):
    bits = bits_dp + bits_seq

    def twos(numbers):
        return [tuple(numbers[i : i + 2]) for i in range(0, len(numbers), 2)]

    beside = twos(list(range(bits_dp, bits)))
    upper = twos(list(range(bits_dp - 2)))
    return beside, upper, [(bits_dp - 2,)], [(bits_dp - 1,)]


def mesh_bits():
    return log2(lax.axis_size("dp")), log2(lax.axis_size("seq"))


class Later:
    def __init__(self, make):
        self.make = make

    def start(self):
        self.make().start()

    def wait(self):
        self.make().wait()


class Links:
    def __init__(self, net, send_sem, recv_sem):
        self.net, self.send_sem, self.recv_sem, self.used = net, send_sem, recv_sem, 0

    def copy(self, source, target, device):
        at = self.used
        self.used += 1
        return Later(
            lambda: pltpu.make_async_remote_copy(
                src_ref=source(),
                dst_ref=target(),
                send_sem=self.send_sem.at[at],
                recv_sem=self.recv_sem.at[at],
                device_id=device(),
                device_id_type=MESH,
            )
        )

    def spread(self, full, done, group, columns=slice(None), shard=None):
        def target():
            return full.at[self.net.place(done) + (slice(None), columns)]

        def source():
            return target() if shard is None else shard.at[:, columns]

        return [
            self.copy(source, target, functools.partial(self.net.partner, flips))
            for flips in subsets(group)
        ]


def start(copies):
    for copy in copies:
        copy.start()


def wait(copies):
    for copy in copies:
        copy.wait()


def flat(groups):
    return tuple(b for group in groups for b in group)


def ring(net, parts, other):
    return (net.dp, lax.rem(net.seq + parts - other, parts))


def owned_row(vector, row, device):
    size, width = vector.shape[1], H * HEAD
    shift = log2(size)
    entry = lax.broadcasted_iota(jnp.int32, (size, width), 0)
    column = lax.broadcasted_iota(jnp.int32, (size, width), 1) + row * width
    here = (column >> shift == device) & (column & (size - 1) == entry)
    return dot(vector.astype(BF), here.astype(F32).astype(BF))


def owned_pair(vector, row, device):
    size, width = vector.shape[1], H * HEAD
    shift = log2(size)
    entry = lax.broadcasted_iota(jnp.int32, (size, width), 0)
    column = lax.broadcasted_iota(jnp.int32, (1, width), 1)
    if row > 0:
        column += (row - 1) * width
        head = 2 * (column >> log2(2 * WIDE)) + (column >> log2(HEAD) & 1)
        index = (2 * head + 1) * HEAD + (column & (HEAD - 1))
        index = jnp.where(column & WIDE == 0, -1, index)
    else:
        index = 2 * (column >> log2(HEAD)) * HEAD + (column & (HEAD - 1))
    here = (index >> shift == device) & (index & (size - 1) == entry)
    return dot(vector.astype(BF), here.astype(F32).astype(BF))


def joint_columns():
    blocks = [3 * head for head in range(H)]
    for pair in range(PAIRS):
        blocks += [3 * head + kind for kind in (1, 2) for head in (2 * pair, 2 * pair + 1)]
    return blocks


def begin_kernel(bits_dp, bits_seq, parts, packed, *refs):
    (
        tokens,
        joint_wide,
        up_wide,
        down_wide,
        out_wide,
        pair_bias,
        out_bias,
        gain_one,
        shift_one,
        up_bias,
        down_bias,
        gain_two,
        shift_two,
        tokens_low,
        tokens_t,
        tokens_rest,
        joint_out,
        vec,
        up_w,
        down_w,
        out_w,
        query,
        pair_own,
        wide,
        narrow,
        narrow_t,
        joint_here,
        joint_shard,
        up_shard,
        down_shard,
        out_shard,
        vec_sent,
        vec_landing,
        query_here,
        pair_here,
        own_sem,
        send_sem,
        recv_sem,
    ) = refs
    joint_w = joint_here if packed else joint_out
    net = Net(bits_dp, bits_seq)
    links = Links(net, send_sem, recv_sem)
    beside, upper, next_to, cores = stages_of(bits_dp, bits_seq)
    order = beside + upper + next_to + cores
    groups, local, width = tokens.shape
    due = net.greet(order)
    for other in range(1, parts):
        net.signal(ring(net, parts, other))
        due += 1
    loads = [
        pltpu.make_async_copy(tokens.at[g], wide.at[g], own_sem.at[g]) for g in range(groups)
    ]
    stores = [
        pltpu.make_async_copy(narrow.at[g], tokens_low.at[g], own_sem.at[groups + g])
        for g in range(groups)
    ]
    turned_stores = [pltpu.make_async_copy(narrow_t, tokens_t, own_sem.at[4 * groups + 7])]
    mine = net.place(())
    placed = [
        pltpu.make_async_copy(shard, full.at[mine], own_sem.at[2 * groups + i])
        for i, (shard, full) in enumerate(
            ((joint_shard, joint_w), (up_shard, up_w), (down_shard, down_w), (out_shard, out_w))
        )
    ]
    start(loads)
    joint = joint_wide[...]
    turned = [joint[:, b * HEAD : (b + 1) * HEAD] for b in joint_columns()]
    joint_shard[...] = jnp.concatenate(turned, axis=1).astype(BF)
    start(placed[:1])
    pl.semaphore_wait(pltpu.get_barrier_semaphore(), due)

    def prepare():
        up_shard[...] = up_wide[...].astype(BF)
        down_shard[...] = down_wide[...].astype(BF)
        out_shard[...] = out_wide[...].astype(BF)
        start(placed[1:])
        device = net.dp * parts + net.seq
        vec[...] = jnp.zeros_like(vec)
        lines = (out_bias, gain_one, shift_one, down_bias, gain_two, shift_two)
        for row, vector in enumerate(lines):
            vec[row : row + 1] = owned_row(vector[...], 0, device)
        for row in range(4):
            vec[6 + row : 7 + row] = owned_row(up_bias[...], row, device)
        for row in range(3):
            vec[10 + row : 11 + row] = owned_pair(pair_bias[...], row, device)
        wait(placed)

    def narrowed(g):
        wait(loads[g : g + 1])
        narrow[g] = wide[g].astype(BF)
        start(stores[g : g + 1])

    def turned_tokens():
        block = min(256, local)
        for g in range(groups):
            for at in range(0, local, block):
                rows = slice(at, at + block)
                narrow_t[g, :, rows] = narrow[g, rows].T
        start(turned_stores)

    cut = width + 2 * WIDE
    columns = (slice(0, cut), slice(cut, 3 * width))
    dones = [flat(order[:stage]) for stage in range(len(order))]
    ahead, behind = [
        [
            links.spread(joint_w, done, group, c, None if done else joint_shard)
            for done, group in zip(dones, order)
        ]
        for c in columns
    ]
    small = [
        [
            links.copy(
                functools.partial(Everywhere.line, vec_sent, stage),
                functools.partial(Everywhere.line, vec_landing, stage, i),
                functools.partial(net.partner, flips),
            )
            for i, flips in enumerate(subsets(group))
        ]
        for stage, group in enumerate(order)
    ]

    def small_start(stage):
        vec_sent[stage] = vec[...].astype(BF)
        start(small[stage])

    def small_add(stage):
        wait(small[stage])
        for i in range(len(small[stage])):
            vec[...] += vec_landing[stage, i].astype(F32)

    exchange = [
        links.copy(
            functools.partial(Everywhere.line, narrow, 0),
            functools.partial(Everywhere.line, tokens_rest, other - 1, 0),
            functools.partial(ring, net, parts, other),
        )
        for other in range(1, parts)
    ]
    some = slice(0, local // AHEAD)
    exchange_next = [
        links.copy(
            functools.partial(Everywhere.line, narrow, 1, some),
            functools.partial(Everywhere.line, tokens_rest, other - 1, 1, some),
            functools.partial(ring, net, parts, other),
        )
        for other in range(1, parts)
    ]

    def projected(part):
        bias = jnp.concatenate([vec[10 + i : 11 + i] for i in range(3)], axis=1)[:, columns[part]]
        block = min(256, local)
        for g in range(groups):

            def rows_of(b, carry):
                rows = pl.ds(pl.multiple_of(b * block, block), block)
                full = joint_w[..., columns[part]].reshape(width, -1)
                joint = (dot(narrow[g, rows], full) + bias).astype(BF)
                if part == 0:
                    query_here[g, rows] = joint[:, :width]
                    pair_here[g, rows, : cut - width] = joint[:, width:]
                else:
                    pair_here[g, rows, cut - width :] = joint
                return carry

            lax.fori_loop(0, local // block, rows_of, 0)

    late, rest = [], []
    last = len(order) - 1
    start(ahead[0])
    start(behind[0])
    prepare()
    small_start(0)
    for stage in range(last):
        done, group = dones[stage], order[stage]
        if stage < len(beside):
            rest = [links.spread(full, done, group) for full in (up_w, down_w, out_w)]
            for copies in rest:
                start(copies)
        if stage == len(beside) - 1:
            narrowed(0)
            start(exchange)
        elif stage == len(beside):
            for g in range(1, groups):
                narrowed(g)
            start(exchange_next)
            turned_tokens()
        wait(ahead[stage])
        small_add(stage)
        start(ahead[stage + 1])
        small_start(stage + 1)
        if stage + 1 < last:
            wait(behind[stage])
            start(behind[stage + 1])
        for copies in rest:
            wait(copies)
        rest = []
        if len(beside) <= stage < len(beside) + len(upper):
            wait(late)
            late = links.spread(up_w, done, group)
            start(late)
    wait(ahead[last])
    small_add(last)
    if packed:
        projected(0)
    wait(behind[last - 1])
    start(behind[last])
    wait(behind[last])
    if packed:
        results = [
            pltpu.make_async_copy(joint_here, joint_out, own_sem.at[4 * groups + 4]),
            pltpu.make_async_copy(query_here, query, own_sem.at[4 * groups + 5]),
        ]
        start(results)
        projected(1)
        results.append(pltpu.make_async_copy(pair_here, pair_own, own_sem.at[4 * groups + 6]))
        start(results[2:])
        wait(results)
    wait(late)
    wait(exchange)
    wait(exchange_next)
    wait(stores)
    wait(turned_stores)


def begin(tokens, joint, up, down, out, vectors, parts):
    bits_dp, bits_seq = mesh_bits()
    bits = bits_dp + bits_seq
    groups, local, width = tokens.shape
    packed = joint.shape[0] % 16 == 0
    beside, upper, next_to, cores = stages_of(bits_dp, bits_seq)
    order = beside + upper + next_to + cores
    sends = sum(2 ** len(group) - 1 for group in order)
    copies = 3 * sends + 4 * sends + 2 * parts
    split = (2,) * bits
    hbm = pl.BlockSpec(memory_space=pl.ANY)
    vmem = pl.BlockSpec(memory_space=pltpu.VMEM)
    return pl.pallas_call(
        functools.partial(begin_kernel, bits_dp, bits_seq, parts, packed),
        in_specs=[hbm] + [vmem] * (4 + len(vectors)),
        out_specs=[hbm, hbm, hbm, hbm, vmem] + [hbm] * 5,
        out_shape=[
            jax.ShapeDtypeStruct((groups, local, width), BF),
            jax.ShapeDtypeStruct((groups, width, local), BF),
            jax.ShapeDtypeStruct((parts - 1, groups, local, width), BF),
            jax.ShapeDtypeStruct(split + joint.shape, BF),
            jax.ShapeDtypeStruct((16, width), F32),
            jax.ShapeDtypeStruct(split + up.shape, BF),
            jax.ShapeDtypeStruct(split + down.shape, BF),
            jax.ShapeDtypeStruct(split + out.shape, BF),
            jax.ShapeDtypeStruct((groups, local, width), BF),
            jax.ShapeDtypeStruct((groups, local, 2 * width), BF),
        ],
        scratch_shapes=[
            pltpu.VMEM((groups, local, width), F32),
            pltpu.VMEM((groups, local, width), BF),
            pltpu.VMEM((groups, width, local), BF),
            pltpu.VMEM(split + joint.shape if packed else (16, 128), BF),
            pltpu.VMEM(joint.shape, BF),
            pltpu.VMEM(up.shape, BF),
            pltpu.VMEM(down.shape, BF),
            pltpu.VMEM(out.shape, BF),
            pltpu.VMEM((len(order), 16, width), BF),
            pltpu.VMEM((len(order), 3, 16, width), BF),
            pltpu.VMEM((groups, local, width), BF),
            pltpu.VMEM((groups, local, 2 * width), BF),
            pltpu.SemaphoreType.DMA((4 * groups + 8,)),
            pltpu.SemaphoreType.DMA((copies,)),
            pltpu.SemaphoreType.DMA((copies,)),
        ],
        compiler_params=pltpu.CompilerParams(
            vmem_limit_bytes=62 * MIB, collective_id=0, has_side_effects=True
        ),
        name="begin",
    )(tokens, joint, up, down, out, *vectors)


def matrix_of(full):
    return full.reshape((-1,) + full.shape[-1:])


def owner_sums(arrays):
    size_dp, size_seq = lax.axis_size("dp"), lax.axis_size("seq")
    bits_dp, bits_seq = log2(size_dp), log2(size_seq)
    bits = bits_dp + bits_seq
    dp, seq = lax.axis_index("dp"), lax.axis_index("seq")
    arrays = [a.reshape((2,) * bits + (-1,) + a.shape[1:]) for a in arrays]
    left = list(range(bits))
    for bit in [bits_dp - 1] + list(range(bits_dp, bits)) + list(range(bits_dp - 2, -1, -1)):
        axis = left.index(bit)
        left.remove(bit)
        if bit < bits_dp:
            name, size, step, me = "dp", size_dp, 2 ** (bits_dp - 1 - bit), dp
        else:
            name, size, step, me = "seq", size_seq, 2 ** (bits - 1 - bit), seq
        mine = me // step % 2
        pairs = [(i, i ^ step) for i in range(size)]
        sent = [
            lax.dynamic_index_in_dim(a, 1 - mine, axis, keepdims=False).astype(BF) for a in arrays
        ]
        kept = [lax.dynamic_index_in_dim(a, mine, axis, keepdims=False) for a in arrays]
        arrived = [lax.ppermute(v, name, pairs) for v in sent]
        arrays = [k + a.astype(F32) for k, a in zip(kept, arrived)]
    return arrays


class Halving:
    def __init__(self, net, links, groups, held, landing, source=None):
        self.net, self.groups, self.held, self.landing = net, groups, held, landing
        self.gone = groups[0] if source is not None else ()
        self.rounds = []
        for stage, group in enumerate(groups):
            copies = []
            for i, flips in enumerate(subsets(group)):
                copies.append(
                    links.copy(
                        functools.partial(self.part, stage, flips, source),
                        functools.partial(self.slot, stage, i),
                        functools.partial(net.partner, flips),
                    )
                )
            self.rounds.append(copies)

    def place(self, stage, turned):
        done, group = flat(self.groups[:stage]), self.groups[stage]
        at = []
        for bit, mine in enumerate(self.net.mine):
            if bit in done or bit in group:
                at.append(1 - mine if bit in turned else mine)
            else:
                at.append(slice(None))
        return tuple(at)

    def part(self, stage, flips, source):
        at = self.place(stage, flips)
        return source.at[at] if stage == 0 and source is not None else self.held.at[self.cut(at)]

    def slot(self, stage, i):
        return self.landing[stage].at[i]

    def cut(self, at):
        return tuple(a for bit, a in enumerate(at) if bit not in self.gone)

    def start(self, stage):
        start(self.rounds[stage])

    def add(self, stage, out=None):
        wait(self.rounds[stage])
        at = self.cut(self.place(stage, ()))
        free = [i for i, a in enumerate(at) if isinstance(a, slice)]
        landing = self.landing[stage]

        def one(flat_index, carry):
            inner = [lax.rem(flat_index // 2 ** (len(free) - 1 - i), 2) for i in range(len(free))]
            there = list(at)
            for axis, value in zip(free, inner):
                there[axis] = value
            there = tuple(there)
            value = self.held[there].astype(F32)
            for i in range(landing.shape[0]):
                value += landing[(i,) + tuple(inner)].astype(F32)
            if out is None:
                self.held[there] = value.astype(BF)
            else:
                out[...] = value
            return carry

        if free:
            lax.fori_loop(0, 2 ** len(free), one, 0)
        else:
            one(0, 0)


class Everywhere:
    def __init__(self, net, links, groups, value, sent, landing):
        self.value, self.sent, self.landing = value, sent, landing
        self.rounds = [
            [
                links.copy(
                    functools.partial(self.line, sent, stage),
                    functools.partial(self.line, landing, stage, i),
                    functools.partial(net.partner, flips),
                )
                for i, flips in enumerate(subsets(group))
            ]
            for stage, group in enumerate(groups)
        ]

    @staticmethod
    def line(ref, *at):
        return ref.at[at]

    def start(self, stage):
        self.sent[stage] = self.value[...]
        start(self.rounds[stage])

    def add(self, stage, out=None):
        wait(self.rounds[stage])
        for i in range(len(self.rounds[stage])):
            self.value[...] += self.landing[stage, i]


def landing_shapes(groups, bits, rows, width):
    shapes, left = [], bits
    for group in groups:
        left -= len(group)
        shapes.append(pltpu.VMEM((2 ** len(group) - 1,) + (2,) * left + (rows, width), BF))
    return shapes


def sum_orders(bits_dp, bits_seq):
    beside, upper, next_to, cores = stages_of(bits_dp, bits_seq)
    far = upper[::-1]
    if len(beside) == 1 and len(beside[0]) == 1:
        near = [beside[0] + next_to[0]]
    else:
        near = beside + next_to
    return cores + beside + next_to + far, cores + next_to + beside + far, cores + near + far


def project_kernel(tokens, weight, bias, query, pair):
    x = tokens[...]
    width = x.shape[1]
    query[...] = (dot(x, weight[:, :width]) + bias[:, :width]).astype(BF)
    pair[...] = (dot(x, weight[:, width:]) + bias[:, width:]).astype(BF)


def project(tokens, weight, bias):
    count, width = tokens.shape
    block = min(512, count)

    def moving(columns):
        return pl.BlockSpec((block, columns), lambda b: (b, 0))

    def still(*shape):
        return pl.BlockSpec(shape, lambda b: (0, 0), pipeline_mode=pl.Buffered(1))

    return pl.pallas_call(
        project_kernel,
        grid=(count // block,),
        in_specs=[moving(width), still(width, 3 * width), still(1, 3 * width)],
        out_specs=[moving(width), moving(2 * width)],
        out_shape=[
            jax.ShapeDtypeStruct((count, width), BF),
            jax.ShapeDtypeStruct((count, 2 * width), BF),
        ],
        compiler_params=params(40, 1),
        name="project",
    )(tokens, weight, bias)


def attend_kernel(parts, groups, steps, blocks, bits_dp, bits_seq, *refs):
    (
        lengths,
        query,
        keys_own,
        values_own,
        weight,
        vec,
        tokens_low,
        _,
        _,
        _,
        _,
        e_out,
        mixed,
        mixed_t,
        inverse,
        pair_rest,
        tokens_rest,
        up_w,
        down_w,
        out_w,
        k_mask,
        v_ext,
        kept,
        tops,
        rest_here,
        pair_here,
        own_sem,
        send_sem,
        recv_sem,
    ) = refs
    local = keys_own.shape[1]
    block = query.shape[1]
    step = pl.program_id(0)
    chunk = min(256, local)

    net = Net(bits_dp, bits_seq)
    links = Links(net, send_sem, recv_sem)
    beside, upper, next_to, cores = stages_of(bits_dp, bits_seq)
    order = beside + upper + next_to + cores
    first, last = len(beside), len(order)
    lead = len(upper)
    rounds = []
    for stage in range(first, last):
        copies = []
        for full in (down_w, out_w):
            copies += links.spread(full, flat(order[:stage]), order[stage])
        ahead = stage + lead
        if ahead < last:
            copies += links.spread(up_w, flat(order[:ahead]), order[ahead])
        rounds.append(copies)
    if len(rounds) > 3:
        times = [i * steps // (len(rounds) + 1) for i in range(len(rounds) + 1)]
    else:
        times = [0, steps * 6 // 16, steps * 12 // 16, steps * 14 // 16]
    exchange = []
    for g in range(1, groups):
        left = slice(local // AHEAD if g == 1 else 0, local)
        exchange.append(
            [
                links.copy(
                    functools.partial(Everywhere.line, tokens_low, g, left),
                    functools.partial(Everywhere.line, tokens_rest, other - 1, g, left),
                    functools.partial(ring, net, parts, other),
                )
                for other in range(1, parts)
            ]
        )

    @pl.when(step == 0)
    def enter():
        due = net.greet(order[first:])
        for other in range(1, parts):
            net.signal(ring(net, parts, other))
            due += 1
        pl.semaphore_wait(pltpu.get_barrier_semaphore(), due)
        for copies in exchange:
            start(copies)
        start(rounds[0])

    for i in range(len(rounds)):
        @pl.when(step == times[i + 1])
        def advance():
            wait(rounds[i])
            if i + 1 < len(rounds):
                start(rounds[i + 1])

    stores = [
        pltpu.make_async_copy(pair_here.at[:, g], pair_rest.at[:, g], own_sem.at[groups + g])
        for g in range(groups)
    ]
    for group in range(groups):
        @pl.when(step == group * blocks * PAIRS)
        def other_keys():
            if group > 0:
                wait(exchange[group - 1])
            copy = pltpu.make_async_copy(tokens_rest.at[:, group], rest_here, own_sem.at[group])
            copy.start()
            width = weight.shape[0]
            bias = jnp.concatenate([vec[11:12], vec[12:13]], axis=1)
            for part in range(parts):
                rows = slice(part * local, (part + 1) * local)
                first_key = lax.rem(net.seq + part, parts) * local
                place = lax.broadcasted_iota(jnp.int32, (local, WIDE), 0) + first_key
                k_mask[rows] = jnp.where(place < lengths[group], 0.0, -1e30).astype(BF)
            copy.wait()
            for part in range(1, parts):
                for p in range(PAIRS):
                    columns = slice(2 * WIDE * p, 2 * WIDE * (p + 1))
                    both = dot(rest_here[part - 1], weight[:, width:][:, columns])
                    pair_here[part - 1, group, p] = (both + bias[:, columns]).astype(BF)
            start(stores[group : group + 1])

    @pl.when(step == steps)
    def leave():
        wait(stores)

    def decode(t):
        return lax.div(t, PAIRS * blocks), lax.rem(lax.div(t, blocks), PAIRS)

    group_then, pair_then = decode(jnp.maximum(step - 1, 0))

    @pl.when(lax.rem(step, blocks) == 1 % blocks)
    def prepare_values():
        for part in range(parts):
            rows = slice(part * local, (part + 1) * local)
            if part == 0:
                values = values_own[0]
            else:
                values = pair_here[part - 1, group_then, pair_then, :, WIDE:]
            turned = values.T
            v_ext[0, :HEAD, rows] = turned[:HEAD]
            v_ext[1, :HEAD, rows] = turned[HEAD:]

    @pl.when(step == 0)
    def ones():
        v_ext[:, HEAD:] = jnp.ones((2, HEAD, parts * local), BF)

    group_now, pair_now = decode(jnp.minimum(step, steps - 1))

    turned = query[0].T
    zero = jnp.zeros((HEAD, block), BF)
    one = (lax.broadcasted_iota(jnp.int32, (WIDE, block), 0) == 0).astype(F32).astype(BF)
    heads = []
    for head in range(2):
        if head == 0:
            picked = jnp.concatenate([turned[:HEAD], zero, one], axis=0)
        else:
            picked = jnp.concatenate([zero, turned[HEAD:], one], axis=0)
        top = tops[head : head + 1]
        out = None
        largest = None
        for at in range(0, parts * local, chunk):
            rows = slice(at, at + chunk)
            inside = slice(at % local, at % local + chunk)
            e = jnp.exp2((kept[head, rows] - top) * (SCALE * LOG2E)).astype(BF)
            e_out[at // local, 0, head, inside] = e
            add = dot(v_ext[head, :, rows], e)
            out = add if out is None else out + add
            if at < local:
                keys = keys_own[0, inside]
            else:
                keys = pair_here[at // local - 1, group_now, pair_now, inside, :WIDE]
            scores = dot(jnp.concatenate([keys, k_mask[rows]], axis=1), picked)
            kept[head, rows] = scores
            most = jnp.max(scores.reshape(chunk // 8, 8, block), axis=0)
            largest = most if largest is None else jnp.maximum(largest, most)
        tops[head : head + 1] = jnp.max(largest, axis=0, keepdims=True)
        inv = 1.0 / out[HEAD : HEAD + 1]
        inverse[0, 0, head : head + 1] = inv
        heads.append(out[:HEAD] * inv)
    both = jnp.concatenate(heads, axis=0).astype(BF)
    mixed_t[0] = both
    mixed[0] = both.T


def attend(lengths, query, pair_own, weight, vec, tokens_low, tokens_rest, up_w, down_w, out_w):
    groups, local, width = query.shape
    others = tokens_rest.shape[0]
    parts = others + 1
    block = min(512, local)
    blocks = local // block
    steps = groups * PAIRS * blocks
    bits_dp, bits_seq = mesh_bits()
    beside, upper, next_to, cores = stages_of(bits_dp, bits_seq)
    sends = sum(2 ** len(group) - 1 for group in upper + next_to + cores)
    copies = 3 * sends + groups * others

    def decode(t, place):
        return place(
            lax.div(t, PAIRS * blocks), lax.rem(lax.div(t, blocks), PAIRS), lax.rem(t, blocks)
        )

    def now(place):
        return lambda t: decode(jnp.minimum(t, steps - 1), place)

    def before(place):
        return lambda t: decode(jnp.maximum(t - 1, 0), place)

    def still(*shape):
        return pl.BlockSpec(shape, lambda t: (0,) * len(shape), pipeline_mode=pl.Buffered(1))

    hbm = pl.BlockSpec(memory_space=pl.ANY)
    passed = (tokens_rest, up_w, down_w, out_w)
    return pl.pallas_call(
        functools.partial(attend_kernel, parts, groups, steps, blocks, bits_dp, bits_seq),
        grid=(steps + 1,),
        in_specs=[
            pl.BlockSpec(memory_space=pltpu.SMEM),
            pl.BlockSpec((1, block, WIDE), now(lambda g, p, b: (g, b, p))),
            pl.BlockSpec((1, local, WIDE), now(lambda g, p, b: (g, 0, 2 * p))),
            pl.BlockSpec((1, local, WIDE), before(lambda g, p, b: (g, 0, 2 * p + 1))),
            still(width, 3 * width),
            still(*vec.shape),
        ]
        + [hbm] * 5,
        out_specs=[
            pl.BlockSpec((parts, 1, 2, local, block), before(lambda g, p, b: (0, g, p, 0, b))),
            pl.BlockSpec((1, block, WIDE), before(lambda g, p, b: (g, b, p))),
            pl.BlockSpec((1, WIDE, block), before(lambda g, p, b: (g, p, b))),
            pl.BlockSpec((1, 1, 2, block), before(lambda g, p, b: (g, p, 0, b))),
            hbm,
        ]
        + [hbm] * 4,
        out_shape=[
            jax.ShapeDtypeStruct((parts, groups, H, local, local), BF),
            jax.ShapeDtypeStruct((groups, local, width), BF),
            jax.ShapeDtypeStruct((groups, width, local), BF),
            jax.ShapeDtypeStruct((groups, PAIRS, 2, local), F32),
            jax.ShapeDtypeStruct((others, groups, PAIRS, local, 2 * WIDE), BF),
        ]
        + [jax.ShapeDtypeStruct(v.shape, v.dtype) for v in passed],
        input_output_aliases={7: 5, 8: 6, 9: 7, 10: 8},
        scratch_shapes=[
            pltpu.VMEM((parts * local, WIDE), BF),
            pltpu.VMEM((2, WIDE, parts * local), BF),
            pltpu.VMEM((2, parts * local, block), F32),
            pltpu.VMEM((8, block), F32),
            pltpu.VMEM((others, local, width), BF),
            pltpu.VMEM((others, groups, PAIRS, local, 2 * WIDE), BF),
            pltpu.SemaphoreType.DMA((2 * groups,)),
            pltpu.SemaphoreType.DMA((copies,)),
            pltpu.SemaphoreType.DMA((copies,)),
        ],
        compiler_params=pltpu.CompilerParams(
            vmem_limit_bytes=62 * MIB,
            dimension_semantics=("arbitrary",),
            collective_id=1,
            has_side_effects=True,
        ),
        name="attend",
    )(lengths, query, pair_own, pair_own, weight, vec, tokens_low, *passed)


def middle_kernel(
    packed,
    tokens,
    cotangent,
    mixed,
    out_w,
    up_w,
    down_w,
    rows,
    result,
    partial,
    mixed_grad,
    upper_sums,
    lower_sums,
    vec_sums,
    out_wg,
    up_wg,
    down_wg,
    row_sums,
    up_bias_sum,
):
    first = pl.program_id(0) == 0

    @pl.when(first)
    def clear():
        out_wg[...] = jnp.zeros_like(out_wg)
        up_wg[...] = jnp.zeros_like(up_wg)
        down_wg[...] = jnp.zeros_like(down_wg)
        row_sums[...] = jnp.zeros_like(row_sums)
        up_bias_sum[...] = jnp.zeros_like(up_bias_sum)

    pieces = up_w.shape[1] // tokens.shape[1]
    up_bias = jnp.concatenate([rows[6 + i : 7 + i] for i in range(pieces)], axis=1)
    out_bias, gain_one, shift_one = rows[0:1], rows[1:2], rows[2:3]
    down_bias, gain_two, shift_two = rows[3:4], rows[4:5], rows[5:6]

    def mean(v):
        return jnp.mean(v, axis=-1, keepdims=True)

    def total(v):
        return jnp.sum(v, axis=0, keepdims=True)

    x = tokens[...]
    heads = mixed[...]
    hidden = x + (dot(heads, out_w[...]) + out_bias)
    centred = hidden - mean(hidden)
    r_one = lax.rsqrt(mean(centred * centred) + EPS)
    n_one = centred * r_one
    normal = n_one * gain_one + shift_one
    normal_low = normal.astype(BF)
    inner = dot(normal_low, up_w[...]) + up_bias
    square = inner * inner
    tanh = jnp.tanh(inner * (GELU_A + (GELU_A * GELU_B) * square))
    half = 0.5 + 0.5 * tanh
    active = (inner * half).astype(BF)
    slope = half + (0.5 * inner) * (1.0 - tanh * tanh) * (
        GELU_A + (3.0 * GELU_A * GELU_B) * square
    )
    branch = dot(active, down_w[...]) + down_bias
    last = normal + branch + x
    centred = last - mean(last)
    r_two = lax.rsqrt(mean(centred * centred) + EPS)
    n_two = centred * r_two
    result[...] = n_two * gain_two + shift_two
    grad = cotangent[...]
    e_two = grad * gain_two
    back = r_two * (e_two - mean(e_two) - n_two * mean(e_two * n_two))
    branch_grad = back.astype(BF)
    down_wg[...] += dot(active, branch_grad, "tn")
    inner_grad_wide = slope * dot(branch_grad, down_w[...], "nt")
    inner_grad = inner_grad_wide.astype(BF)
    up_wg[...] += dot(normal_low, inner_grad, "tn")
    up_bias_sum[...] += total(inner_grad.astype(F32))
    norm_grad = back + dot(inner_grad, up_w[...], "nt")
    e_one = norm_grad * gain_one
    hidden_grad = r_one * (e_one - mean(e_one) - n_one * mean(e_one * n_one))
    attn_grad = hidden_grad.astype(BF)
    partial[...] = back + hidden_grad
    out_wg[...] += dot(heads, attn_grad, "tn")
    mixed_grad[...] = dot(attn_grad, out_w[...], "nt").astype(BF)
    row_sums[0:1] += total(attn_grad.astype(F32))
    row_sums[1:2] += total(norm_grad * n_one)
    row_sums[2:3] += total(norm_grad)
    row_sums[3:4] += total(branch_grad.astype(F32))
    row_sums[4:5] += total(grad * n_two)
    row_sums[5:6] += total(grad)

    @pl.when(pl.program_id(0) == pl.num_programs(0) - 1)
    def pack():
        width = tokens.shape[1]
        pieces = up_wg.shape[1] // width
        vec_sums[...] = jnp.zeros_like(vec_sums)
        vec_sums[0:8] = row_sums[...]
        for piece in range(pieces):
            columns = slice(piece * width, (piece + 1) * width)
            vec_sums[8 + piece : 9 + piece] = up_bias_sum[:, columns]
        if not packed:
            upper_sums[:, :width] = out_wg[...]
            upper_sums[:, width:] = up_wg[...]
            lower_sums[...] = down_wg[...]
            return
        owners = upper_sums.shape[0]
        rows_out = out_wg.shape[0] // owners
        rows_down = down_wg.shape[0] // owners

        def one(owner, carry):
            near = pl.ds(pl.multiple_of(owner * rows_out, rows_out), rows_out)
            upper_sums[owner, :rows_out] = out_wg[near].astype(BF)
            for piece in range(pieces):
                columns = slice(piece * width, (piece + 1) * width)
                to = slice((piece + 1) * rows_out, (piece + 2) * rows_out)
                upper_sums[owner, to] = up_wg[near, columns].astype(BF)
            far = pl.ds(pl.multiple_of(owner * rows_down, rows_down), rows_down)
            lower_sums[owner] = down_wg[far].astype(BF)
            return carry

        lax.fori_loop(0, owners, one, 0)


def middle(tokens, cotangent, mixed, out_w, up_w, down_w, rows, owners):
    count, width = tokens.shape
    hidden = up_w.shape[1]
    block = min(512, count)
    packed = whole_tiles(width, owners)

    def moving(columns=width):
        return pl.BlockSpec((block, columns), lambda b: (b, 0))

    def still(*shape):
        return pl.BlockSpec(shape, lambda b: (0,) * len(shape), pipeline_mode=pl.Buffered(1))

    rows_upper = width // owners * (1 + hidden // width)
    rows_lower = hidden // owners
    if packed:
        sums = [((owners, rows_upper, width), BF), ((owners, rows_lower, width), BF)]
    else:
        sums = [((width, width + hidden), F32), ((hidden, width), F32)]
    return pl.pallas_call(
        functools.partial(middle_kernel, packed),
        grid=(count // block,),
        in_specs=[
            moving(),
            moving(),
            moving(),
            still(width, width),
            still(width, hidden),
            still(hidden, width),
            still(16, width),
        ],
        out_specs=[
            moving(),
            moving(),
            moving(),
        ]
        + [still(*shape) for shape, _ in sums]
        + [still(16, width)],
        out_shape=[
            jax.ShapeDtypeStruct((count, width), F32),
            jax.ShapeDtypeStruct((count, width), F32),
            jax.ShapeDtypeStruct((count, width), BF),
        ]
        + [jax.ShapeDtypeStruct(shape, kind) for shape, kind in sums]
        + [jax.ShapeDtypeStruct((16, width), F32)],
        scratch_shapes=[
            pltpu.VMEM((width, width), F32),
            pltpu.VMEM((width, hidden), F32),
            pltpu.VMEM((hidden, width), F32),
            pltpu.VMEM((8, width), F32),
            pltpu.VMEM((1, hidden), F32),
        ],
        compiler_params=params(62, 1),
        name="middle",
    )(tokens, cotangent, mixed, out_w, up_w, down_w, rows)


def pull_kernel(parts, groups, bits_dp, bits_seq, packed, *refs):
    taken = 0

    def take(count):
        nonlocal taken
        taken += count
        return refs[taken - count : taken]

    e_part, query, pair_own, pair_rest, mixed_grad, mixed_t, inverse = take(7)
    tokens_t, tokens_rest, weight, partial = take(4)
    sources = take(2) if packed else ()
    (vec_in,) = take(1)
    share_own, arrived, joint_out, vec_out = take(4)
    owned = take(2) if packed else ()
    d_scores, joint_grad, total, dq_sums, weight_grad, bias_grad, shares = take(7)
    share_send, share_recv, own_sem = take(3)
    step = pl.program_id(0)
    steps = pl.num_programs(0)
    each = groups * PAIRS
    part = lax.rem(lax.div(step, each) + 1, parts)
    own = part == 0
    inside = lax.rem(step, each)
    group = jnp.where(own, lax.rem(inside, groups), lax.div(inside, PAIRS))
    pair = jnp.where(own, lax.div(inside, groups), lax.rem(inside, PAIRS))

    net = Net(bits_dp, bits_seq)
    bits = net.bits
    orders = sum_orders(bits_dp, bits_seq)
    streams, loads = [], []
    if packed:
        upper_held, lower_held = take(2)
        joint_helds = take(len(JOINT_PARTS))
        vec_sent, vec_landing, bias_sent, bias_landing = take(4)
        send_sem, recv_sem = take(2)
        links = Links(net, send_sem, recv_sem)
        upper, lower = streams = [
            Halving(net, links, orders[i], held, take(len(orders[i])), sources[i])
            for i, held in enumerate((upper_held, lower_held))
        ]
        joint = [Halving(net, links, orders[2], h, take(len(orders[2]))) for h in joint_helds]
        early_vec = Everywhere(net, links, orders[2], vec_out.at[0:16], vec_sent, vec_landing)
        late_vec = Everywhere(net, links, orders[2], bias_grad, bias_sent, bias_landing)
        for i, stream in enumerate(streams):
            at = stream.place(0, ())
            loads.append(pltpu.make_async_copy(sources[i].at[at], stream.held, own_sem.at[i]))
    stores = [
        pltpu.make_async_copy(total.at[g], share_own.at[g], own_sem.at[2 + g])
        for g in range(groups)
    ]
    partials = [
        pltpu.make_async_copy(partial.at[g], total.at[g], own_sem.at[2 + groups + g])
        for g in range(groups)
    ]

    def share_copy(other, g):
        return pltpu.make_async_remote_copy(
            src_ref=shares.at[other - 1, g],
            dst_ref=arrived.at[other - 1, g],
            send_sem=share_send.at[other - 1, g],
            recv_sem=share_recv.at[other - 1, g],
            device_id=(net.dp, lax.rem(net.seq + other, parts)),
            device_id_type=MESH,
        )

    @pl.when(step == 0)
    def enter():
        due = parts - 1
        for other in range(1, parts):
            net.signal((net.dp, lax.rem(net.seq + other, parts)))
        if packed:
            due += net.greet(orders[0]) + net.greet(orders[2])
        start(loads)
        start(partials)
        pl.semaphore_wait(pltpu.get_barrier_semaphore(), due)
        for stream in streams:
            stream.start(0)

    def advance(streams, stage, outs, count):
        for stream, out in zip(streams, outs):
            stream.add(stage, out if stage == count - 1 else None)
            if stage < count - 1:
                stream.start(stage + 1)

    def pack(index):
        first, count = JOINT_PARTS[index]
        held = joint[index].held
        rows_each, width = weight_grad.shape[0] // 2**bits, weight_grad.shape[0]
        columns = slice(first * WIDE, (first + count) * WIDE)
        doubled = slice(width + 2 * first * WIDE, width + 2 * (first + count) * WIDE)

        def one(flat_index, carry):
            place = tuple(lax.rem(flat_index // 2 ** (bits - 1 - i), 2) for i in range(bits))
            near = pl.ds(pl.multiple_of(flat_index * rows_each, rows_each), rows_each)
            held[place + (slice(None), slice(0, count * WIDE))] = weight_grad[near, columns].astype(BF)
            held[place + (slice(None), slice(count * WIDE, 3 * count * WIDE))] = weight_grad[
                near, doubled
            ].astype(BF)
            return carry

        lax.fori_loop(0, 2**bits, one, 0)

    def joint_place(index):
        first, count = JOINT_PARTS[index]
        return joint_out.at[:, 3 * first * WIDE : 3 * (first + count) * WIDE]

    if packed:
        last = len(orders[2])
        for stage, when in enumerate((1, 5, 9, 12)):
            @pl.when(step == when)
            def ffn():
                if stage == 0:
                    wait(loads)
                advance(streams, stage, owned, len(orders[0]))

        @pl.when(step == steps - 2 * groups)
        def joint_early():
            pack(0)
            vec_out[...] = vec_in[...]
            joint[0].start(0)
            early_vec.start(0)

        @pl.when(step == steps - 2 * groups + 1)
        def joint_early_near():
            advance((joint[0], early_vec), 0, (None, None), last)

        @pl.when(step == steps - groups)
        def joint_middle():
            pack(1)
            joint[1].start(0)

        @pl.when(step == steps - 1)
        def joint_middle_near():
            advance((joint[0], early_vec), 1, (None, None), last)
            advance((joint[1],), 0, (None,), last)

    local = query.shape[1]
    chunk = min(256, local)
    turned = mixed_grad[0].astype(F32).T
    mixed = mixed_t[0].astype(F32)
    values = jnp.where(own, pair_own[0, :, WIDE:], pair_rest[0, 0, 0, :, WIDE:])
    keys_t = jnp.where(own, pair_own[0, :, :WIDE], pair_rest[0, 0, 0, :, :WIDE]).T
    query_now = query[0]
    lane = lax.broadcasted_iota(jnp.int32, (local, WIDE), 1)
    zero = jnp.zeros((HEAD, local), BF)
    grad_t, grad, centre, picked = [], [], [], []
    for head in range(2):
        side = slice(head * HEAD, (head + 1) * HEAD)
        inv = inverse[0, 0, head : head + 1]
        centre.append(inv * jnp.sum(turned[side] * mixed[side], axis=0, keepdims=True))
        scaled = (turned[side] * inv).astype(BF)
        grad_t.append(jnp.concatenate([scaled, zero] if head == 0 else [zero, scaled], axis=0))
        grad.append(grad_t[head].T)
        kept = lane < HEAD if head == 0 else lane >= HEAD
        picked.append(jnp.where(kept, query_now, jnp.zeros_like(query_now)))

    width = weight.shape[0]
    at_queries = pl.ds(pl.multiple_of(pair * WIDE, WIDE), WIDE)
    start_at = width + pair * (2 * WIDE)
    at_keys = pl.ds(pl.multiple_of(start_at, WIDE), WIDE)
    at_values = pl.ds(pl.multiple_of(start_at + WIDE, WIDE), WIDE)
    at_both = pl.ds(pl.multiple_of(start_at, WIDE), 2 * WIDE)

    def key_grad(rows):
        sums = dot(d_scores[0, rows], picked[0]) + dot(d_scores[1, rows], picked[1])
        joint_grad[group, rows, at_keys] = (sums * SCALE).astype(BF)

    @pl.when(step == 0)
    def clear():
        weight_grad[...] = jnp.zeros_like(weight_grad)
        bias_grad[...] = jnp.zeros_like(bias_grad)
        dq_sums[...] = jnp.zeros_like(dq_sums)

    column = group * PAIRS + pair
    value_sums = jnp.zeros((1, WIDE), F32)
    last_rows = None
    for at in range(0, local, chunk):
        rows = slice(at, at + chunk)
        for head in range(2):
            pulled = dot(values[rows], grad_t[head])
            e = e_part[0, 0, head, rows].astype(F32)
            d_scores[head, rows] = (e * (pulled - centre[head])).astype(BF)
        sums = dot(e_part[0, 0, 0, rows], grad[0]) + dot(e_part[0, 0, 1, rows], grad[1])
        sums = sums.astype(BF)
        joint_grad[group, rows, at_values] = sums
        value_sums += jnp.sum(sums.astype(F32), axis=0, keepdims=True)
        if last_rows is not None:
            key_grad(last_rows)
        last_rows = rows
    key_grad(last_rows)
    for head in range(2):
        side = slice(head * HEAD, (head + 1) * HEAD)
        dq_sums[column, side] += dot(keys_t, d_scores[head])[side]
    bias_grad[1:2, at_queries] += value_sums

    @pl.when(own)
    def near():
        dq = (dq_sums[column] * SCALE).astype(BF).T
        joint_grad[group, :, at_queries] = dq
        bias_grad[0:1, at_queries] += jnp.sum(dq.astype(F32), axis=0, keepdims=True)
        weight_grad[:, at_queries] += dot(tokens_t[group], dq)
        weight_grad[:, at_both] += dot(tokens_t[group], joint_grad[group, :, at_both])

    for other in range(1, parts):
        for g in range(groups):
            @pl.when(step == ((other - 1) * groups + g + 1) * PAIRS - 1)
            def finish_far():
                for at in range(0, local, chunk):
                    rows = slice(at, at + chunk)
                    part_share = dot(joint_grad[g, rows, width:], weight[:, width:], "nt")
                    shares[other - 1, g, rows] = part_share.astype(BF)
                share_copy(other, g).start()
                weight_grad[:, width:] += dot(tokens_rest[0, 0], joint_grad[g, :, width:], "tn")

    def input_grads(g):
        for at in range(0, local, chunk):
            rows = slice(at, at + chunk)
            total[g, rows] += dot(joint_grad[g, rows], weight[...], "nt")
        start(stores[g : g + 1])

    @pl.when(step == steps - 1)
    def finish():
        work = list(range(groups))
        if packed:
            pack(2)
            joint[2].start(0)
            late_vec.start(0)
            advance((joint[1],), 1, (None,), last)
        wait(partials)
        if packed:
            for stage in range(last):
                if work:
                    input_grads(work.pop(0))
                outs = (joint_place(2), None)
                advance((joint[2], late_vec), stage, outs, last)
                if stage == 0:
                    advance((joint[0], early_vec), last - 1, (joint_place(0), None), last)
            joint[1].add(last - 1, joint_place(1))
        else:
            vec_out[...] = vec_in[...]
            joint_out[...] = weight_grad[...]
        for g in work:
            input_grads(g)
        vec_out[12:14] = bias_grad[0:2]
        for g in range(groups):
            for other in range(1, parts):
                share_copy(other, g).wait()
        wait(stores)


def pull(
    e_all,
    query,
    pair_own,
    pair_rest,
    mixed_grad,
    mixed_t,
    inverse,
    own,
    rest,
    weight,
    partial,
    upper_sums,
    lower_sums,
    vec_sums,
):
    parts, groups, _, local, _ = e_all.shape
    width = H * HEAD
    each = groups * PAIRS
    bits_dp, bits_seq = mesh_bits()
    bits = bits_dp + bits_seq
    orders = sum_orders(bits_dp, bits_seq)
    packed = whole_tiles(width, 2**bits)
    split = (2,) * bits
    sums, out_blocks, extra = [], [], []
    if packed:
        rows_upper, rows_lower = upper_sums.shape[1], lower_sums.shape[1]
        rows_joint = width // 2**bits
        sums = [v.reshape(split + v.shape[1:]) for v in (upper_sums, lower_sums)]
        out_blocks = [(rows_joint, 3 * width), (16, width), (rows_upper, width), (rows_lower, width)]
        joint_widths = [3 * count * WIDE for _, count in JOINT_PARTS]
        last = len(orders[2])
        sends = sum(2 ** len(g) - 1 for order in orders for g in order)
        sends += 4 * sum(2 ** len(g) - 1 for g in orders[2])
        extra = [
            pltpu.VMEM((2,) * (bits - 1) + (rows_upper, width), BF),
            pltpu.VMEM((2,) * (bits - 1) + (rows_lower, width), BF),
        ]
        extra += [pltpu.VMEM(split + (rows_joint, columns), BF) for columns in joint_widths]
        extra += [
            pltpu.VMEM((last, 16, width), F32),
            pltpu.VMEM((last, 3, 16, width), F32),
            pltpu.VMEM((last, 8, width), F32),
            pltpu.VMEM((last, 3, 8, width), F32),
            pltpu.SemaphoreType.DMA((sends,)),
            pltpu.SemaphoreType.DMA((sends,)),
        ]
        extra += landing_shapes(orders[0], bits, rows_upper, width)
        extra += landing_shapes(orders[1], bits, rows_lower, width)
        for columns in joint_widths:
            extra += landing_shapes(orders[2], bits, rows_joint, columns)
    else:
        out_blocks = [(width, 3 * width), (16, width)]

    def decode(t):
        part, inside = lax.rem(lax.div(t, each) + 1, parts), lax.rem(t, each)
        own = part == 0
        group = jnp.where(own, lax.rem(inside, groups), lax.div(inside, PAIRS))
        pair = jnp.where(own, lax.div(inside, groups), lax.rem(inside, PAIRS))
        return part, group, pair

    def at(place):
        return lambda t: place(*decode(t))

    def own_at(place):
        def index(t):
            part, group, pair = decode(t)
            return place(jnp.where(part == 0, group, 0), jnp.where(part == 0, pair, 0))

        return index

    def rest_at(place):
        def index(t):
            t = jnp.minimum(t, (parts - 1) * each - 1)
            return place(
                lax.div(t, each), lax.rem(lax.div(t, PAIRS), groups), lax.rem(t, PAIRS)
            )

        return index

    def still(*shape):
        return pl.BlockSpec(shape, lambda t: (0,) * len(shape), pipeline_mode=pl.Buffered(1))

    once = pl.Buffered(1)
    return pl.pallas_call(
        functools.partial(pull_kernel, parts, groups, bits_dp, bits_seq, packed),
        grid=(parts * each,),
        in_specs=[
            pl.BlockSpec((1, 1, 2, local, local), at(lambda j, g, p: (j, g, p, 0, 0))),
            pl.BlockSpec((1, local, WIDE), at(lambda j, g, p: (g, 0, p))),
            pl.BlockSpec((1, local, 2 * WIDE), own_at(lambda g, p: (g, 0, p))),
            pl.BlockSpec((1, 1, 1, local, 2 * WIDE), rest_at(lambda j, g, p: (j, g, p, 0, 0))),
            pl.BlockSpec((1, local, WIDE), at(lambda j, g, p: (g, 0, p))),
            pl.BlockSpec((1, WIDE, local), at(lambda j, g, p: (g, p, 0))),
            pl.BlockSpec((1, 1, 2, local), at(lambda j, g, p: (g, p, 0, 0))),
            still(groups, width, local),
            pl.BlockSpec(
                (1, 1, local, width), rest_at(lambda j, g, p: (j, g, 0, 0)), pipeline_mode=once
            ),
            still(width, 3 * width),
            pl.BlockSpec(memory_space=pl.ANY),
        ]
        + [pl.BlockSpec(memory_space=pl.ANY)] * len(sums)
        + [still(16, width)],
        out_specs=[
            pl.BlockSpec(memory_space=pl.ANY),
            pl.BlockSpec(memory_space=pl.ANY),
        ]
        + [still(*shape) for shape in out_blocks],
        out_shape=[
            jax.ShapeDtypeStruct((groups, local, width), F32),
            jax.ShapeDtypeStruct((parts - 1, groups, local, width), BF),
        ]
        + [jax.ShapeDtypeStruct(shape, F32) for shape in out_blocks],
        scratch_shapes=[
            pltpu.VMEM((2, local, local), BF),
            pltpu.VMEM((groups, local, 3 * width), BF),
            pltpu.VMEM((groups, local, width), F32),
            pltpu.VMEM((each, WIDE, local), F32),
            pltpu.VMEM((width, 3 * width), F32),
            pltpu.VMEM((8, width), F32),
            pltpu.VMEM((parts - 1, groups, local, width), BF),
            pltpu.SemaphoreType.DMA((parts - 1, groups)),
            pltpu.SemaphoreType.DMA((parts - 1, groups)),
            pltpu.SemaphoreType.DMA((2 + 2 * groups,)),
        ]
        + extra,
        compiler_params=pltpu.CompilerParams(
            vmem_limit_bytes=63 * MIB,
            dimension_semantics=("arbitrary",),
            collective_id=2,
            has_side_effects=True,
        ),
        name="pull",
    )(
        e_all,
        query,
        pair_own,
        pair_rest,
        mixed_grad,
        mixed_t,
        inverse,
        own,
        rest,
        weight,
        partial,
        *sums,
        vec_sums,
    )


def finish_kernel(bits_dp, bits_seq, share, arrived, joint, vec, upper, lower, *outs):
    (
        input_grad,
        joint_sum,
        pair_sum,
        out_sum,
        out_bias,
        gain_one,
        shift_one,
        up_sum,
        up_bias,
        down_sum,
        down_bias,
        gain_two,
        shift_two,
    ) = outs
    value = share[...]
    for other in range(arrived.shape[0]):
        value += arrived[other].astype(F32)
    input_grad[...] = value

    @pl.when(pl.program_id(0) == 0)
    def small():
        net = Net(bits_dp, bits_seq)
        device = net.dp * 2**bits_seq + net.seq
        rows, width = out_sum.shape
        summed = joint[...]
        turned = []
        for head in range(H):
            pair = head // 2
            for first, count in JOINT_PARTS:
                if first <= pair < first + count:
                    base = 3 * first * WIDE + head % 2 * HEAD
                    both = base + (count + 2 * (pair - first)) * WIDE
                    for at in (base + (pair - first) * WIDE, both, both + WIDE):
                        turned.append(summed[:, at : at + HEAD])
        joint_sum[...] = jnp.concatenate(turned, axis=1)
        out_sum[...] = upper[:rows]
        for piece in range(up_sum.shape[1] // width):
            up_sum[:, piece * width : (piece + 1) * width] = upper[
                (piece + 1) * rows : (piece + 2) * rows
            ]
        down_sum[...] = lower[...]
        lines = vec[...]
        which = lax.broadcasted_iota(jnp.int32, lines.shape, 0)

        def entries(out, row, column):
            line = jnp.sum(jnp.where(which == row, lines, 0.0), axis=0, keepdims=True)
            line = jnp.broadcast_to(line, (8, width))
            out[...] = pltpu.roll(line, lax.rem(width - column, width), 1)[:1, : out.shape[1]]

        plain = (out_bias, gain_one, shift_one, down_bias, gain_two, shift_two)
        for row, out in enumerate(plain):
            entries(out, row, device * out.shape[1])
        first = device * up_bias.shape[1]
        entries(up_bias, 8 + first // width, lax.rem(first, width))
        first = device * pair_sum.shape[1]
        kind = lax.rem(first // HEAD, 2)
        entries(pair_sum, 12 + kind, first // WIDE * HEAD + lax.rem(first, HEAD))


def finish(share, arrived, joint, vec, upper, lower, shards):
    groups, local, width = share.shape
    block = min(1024, local)
    each = local // block

    def moving(*lead):
        return pl.BlockSpec(
            (1,) * len(lead) + (block, width), lambda b: (b // each, b % each, 0)
        )

    def still(shape):
        return pl.BlockSpec(shape, lambda b: (0,) * len(shape), pipeline_mode=pl.Buffered(1))

    bits_dp, bits_seq = mesh_bits()
    others = arrived.shape[0]
    small = (joint, vec, upper, lower)
    outs = pl.pallas_call(
        functools.partial(finish_kernel, bits_dp, bits_seq),
        grid=(groups * each,),
        in_specs=[
            moving(1),
            pl.BlockSpec((others, 1, block, width), lambda b: (0, b // each, b % each, 0)),
        ]
        + [still(v.shape) for v in small],
        out_specs=[moving(1)] + [still(shape) for shape in shards],
        out_shape=[jax.ShapeDtypeStruct(share.shape, F32)]
        + [jax.ShapeDtypeStruct(shape, F32) for shape in shards],
        compiler_params=params(62, 1),
        name="finish",
    )(share, arrived, *small)
    return [outs[0]] + [
        v.reshape(v.shape[1:]) if v.shape[0] == 1 else v for v in outs[1:]
    ]


def per_device(
    tokens,
    lengths,
    joint_weight,
    joint_bias,
    out_weight,
    out_bias,
    gain_first,
    shift_first,
    up_weight,
    up_bias,
    down_weight,
    down_bias,
    gain_second,
    shift_second,
    cotangent,
):
    groups, local, width = tokens.shape
    parts = lax.axis_size("seq")
    devices = lax.axis_size("dp") * parts
    me = lax.axis_index("seq")
    rows = groups * local
    own_rows = joint_weight.shape[0]
    vectors = [
        joint_bias,
        out_bias,
        gain_first,
        shift_first,
        up_bias,
        down_bias,
        gain_second,
        shift_second,
    ]
    lens = [v.shape[0] for v in vectors]
    tokens_low, tokens_t, tokens_rest, joint_w, vec, up_w, down_w, out_w, query, pair_own = begin(
        tokens,
        joint_weight,
        up_weight,
        down_weight,
        out_weight,
        [v.reshape(1, -1) for v in vectors],
        parts,
    )
    joint_w = matrix_of(joint_w)
    pieces = up_weight.shape[1] // width
    if not whole_tiles(width, devices):
        query, pair_own = project(
            tokens_low.reshape(rows, width), joint_w, vec[10:13].reshape(1, -1)
        )
        query = query.reshape(groups, local, width)
        pair_own = pair_own.reshape(groups, local, 2 * width)

    e_all, mixed, mixed_t, inverse, pair_rest, tokens_rest, up_w, down_w, out_w = attend(
        lengths, query, pair_own, joint_w, vec, tokens_low, tokens_rest, up_w, down_w, out_w
    )
    out_w, up_w, down_w = matrix_of(out_w), matrix_of(up_w), matrix_of(down_w)

    result, partial, mixed_grad, upper_sums, lower_sums, vec_sums = middle(
        tokens.reshape(rows, width),
        cotangent.reshape(rows, width),
        mixed.reshape(rows, width),
        out_w,
        up_w,
        down_w,
        vec,
        devices,
    )
    mixed_grad = mixed_grad.reshape(groups, local, width)
    share, arrived, joint, vec, *owned = pull(
        e_all,
        query,
        pair_own,
        pair_rest,
        mixed_grad,
        mixed_t,
        inverse,
        tokens_t,
        tokens_rest,
        joint_w,
        partial.reshape(groups, local, width),
        upper_sums,
        lower_sums,
        vec_sums,
    )
    if owned:
        upper, lower = owned
        shards = [
            (1, v.shape[0]) if v.ndim == 1 else v.shape
            for v in (
                joint_weight,
                joint_bias,
                out_weight,
                out_bias,
                gain_first,
                shift_first,
                up_weight,
                up_bias,
                down_weight,
                down_bias,
                gain_second,
                shift_second,
            )
        ]
        outs = finish(share, arrived, joint, vec, upper, lower, shards)
        return (result.reshape(groups, local, width), *outs)
    input_grad = share + jnp.sum(arrived.astype(F32), axis=0)
    joint_sum, upper, lower = owner_sums([joint, upper_sums, lower_sums])
    out_sum, up_sum = upper[:, :width], upper[:, width:]
    vec = lax.psum(vec, ("dp", "seq"))
    device = lax.axis_index("dp") * parts + me
    back = [joint_columns().index(block) for block in range(3 * H)]
    joint_sum = joint_sum.reshape(own_rows, 3 * H, HEAD)
    joint_sum = jnp.stack([joint_sum[:, b] for b in back], axis=1).reshape(own_rows, 3 * width)
    pair_grad = jnp.stack(
        [vec[12].reshape(H, HEAD), vec[13].reshape(H, HEAD)], axis=1
    ).reshape(2 * width)
    sums = [
        pair_grad,
        vec[0],
        vec[1],
        vec[2],
        vec[8 : 8 + pieces].reshape(-1),
        vec[3],
        vec[4],
        vec[5],
    ]
    small = [
        lax.dynamic_slice_in_dim(v, device * size, size, 0) for v, size in zip(sums, lens)
    ]
    return (
        result.reshape(groups, local, width),
        input_grad,
        joint_sum,
        small[0],
        out_sum,
        small[1],
        small[2],
        small[3],
        up_sum,
        small[4],
        lower,
        small[5],
        small[6],
        small[7],
    )


def solution(mesh):
    both = ("dp", "seq")
    matrix, vector, whole = P(both, None), P(both), P("dp", "seq", None)
    return jax.shard_map(
        per_device,
        mesh=mesh,
        in_specs=(
            whole,
            P("dp"),
            matrix,
            vector,
            matrix,
            vector,
            vector,
            vector,
            matrix,
            vector,
            matrix,
            vector,
            vector,
            vector,
            whole,
        ),
        out_specs=(
            whole,
            whole,
            matrix,
            vector,
            matrix,
            vector,
            vector,
            vector,
            matrix,
            vector,
            matrix,
            vector,
            vector,
            vector,
        ),
        check_vma=False,
    )
```

```python
import functools
import math

import jax
import jax.numpy as jnp
from jax import lax
from jax.experimental import pallas as pl
from jax.experimental.pallas import tpu as pltpu
from jax.sharding import PartitionSpec as P

H = 8
HEAD = 64
PAIRS = H // 2
WIDE = 2 * HEAD
JOINT_PARTS = ((0, 2), (2, 1), (3, 1))
AHEAD = 16
BF = jnp.bfloat16
F32 = jnp.float32
EPS = 1e-05
SCALE = 1.0 / math.sqrt(HEAD)
LOG2E = math.log2(math.e)
GELU_A = math.sqrt(2.0 / math.pi)
GELU_B = 0.044715
MESH = pl.DeviceIdType.MESH
MIB = 2**20
FORMS = {
    "nn": (((1,), (0,)), ((), ())),
    "nt": (((1,), (1,)), ((), ())),
    "tn": (((0,), (0,)), ((), ())),
}


def dot(left, right, form="nn"):
    return lax.dot_general(left, right, FORMS[form], preferred_element_type=F32)


def whole_tiles(width, devices):
    return width // devices % 16 == 0


def params(limit, steps):
    return pltpu.CompilerParams(
        vmem_limit_bytes=limit * MIB, dimension_semantics=("arbitrary",) * steps
    )


def log2(size):
    return size.bit_length() - 1


class Net:
    def __init__(self, bits_dp, bits_seq):
        self.bits_dp, self.bits_seq = bits_dp, bits_seq
        self.bits = bits_dp + bits_seq
        self.dp, self.seq = lax.axis_index("dp"), lax.axis_index("seq")
        self.mine = [lax.rem(lax.div(self.dp, 2 ** (bits_dp - 1 - b)), 2) for b in range(bits_dp)]
        self.mine += [lax.rem(lax.div(self.seq, 2 ** (bits_seq - 1 - b)), 2) for b in range(bits_seq)]

    def partner(self, flips):
        dp, seq = self.dp, self.seq
        for bit in flips:
            turn = 1 - 2 * self.mine[bit]
            if bit < self.bits_dp:
                dp = dp + turn * 2 ** (self.bits_dp - 1 - bit)
            else:
                seq = seq + turn * 2 ** (self.bits - 1 - bit)
        return (dp, seq)

    def place(self, done, turned=()):
        at = []
        for bit in range(self.bits):
            if bit in done:
                at.append(slice(None))
            else:
                at.append(1 - self.mine[bit] if bit in turned else self.mine[bit])
        return tuple(at)

    def signal(self, device):
        pl.semaphore_signal(
            pltpu.get_barrier_semaphore(), inc=1, device_id=device, device_id_type=MESH
        )

    def greet(self, groups):
        count = 0
        for group in groups:
            for flips in subsets(group):
                self.signal(self.partner(flips))
                count += 1
        return count


def subsets(group):
    return [
        tuple(b for i, b in enumerate(group) if pick >> i & 1)
        for pick in range(1, 2 ** len(group))
    ]


def stages_of(bits_dp, bits_seq):
    bits = bits_dp + bits_seq

    def twos(numbers):
        return [tuple(numbers[i : i + 2]) for i in range(0, len(numbers), 2)]

    beside = twos(list(range(bits_dp, bits)))
    upper = twos(list(range(bits_dp - 2)))
    return beside, upper, [(bits_dp - 2,)], [(bits_dp - 1,)]


def mesh_bits():
    return log2(lax.axis_size("dp")), log2(lax.axis_size("seq"))


class Later:
    def __init__(self, make):
        self.make = make

    def start(self):
        self.make().start()

    def wait(self):
        self.make().wait()


class Links:
    def __init__(self, net, send_sem, recv_sem):
        self.net, self.send_sem, self.recv_sem, self.used = net, send_sem, recv_sem, 0

    def copy(self, source, target, device):
        at = self.used
        self.used += 1
        return Later(
            lambda: pltpu.make_async_remote_copy(
                src_ref=source(),
                dst_ref=target(),
                send_sem=self.send_sem.at[at],
                recv_sem=self.recv_sem.at[at],
                device_id=device(),
                device_id_type=MESH,
            )
        )

    def spread(self, full, done, group, columns=slice(None), shard=None):
        def target():
            return full.at[self.net.place(done) + (slice(None), columns)]

        def source():
            return target() if shard is None else shard.at[:, columns]

        return [
            self.copy(source, target, functools.partial(self.net.partner, flips))
            for flips in subsets(group)
        ]


def start(copies):
    for copy in copies:
        copy.start()


def wait(copies):
    for copy in copies:
        copy.wait()


def flat(groups):
    return tuple(b for group in groups for b in group)


def ring(net, parts, other):
    return (net.dp, lax.rem(net.seq + parts - other, parts))


def owned_row(vector, row, device):
    size, width = vector.shape[1], H * HEAD
    shift = log2(size)
    entry = lax.broadcasted_iota(jnp.int32, (size, width), 0)
    column = lax.broadcasted_iota(jnp.int32, (size, width), 1) + row * width
    here = (column >> shift == device) & (column & (size - 1) == entry)
    return dot(vector.astype(BF), here.astype(F32).astype(BF))


def owned_pair(vector, row, device):
    size, width = vector.shape[1], H * HEAD
    shift = log2(size)
    entry = lax.broadcasted_iota(jnp.int32, (size, width), 0)
    column = lax.broadcasted_iota(jnp.int32, (1, width), 1)
    if row > 0:
        column += (row - 1) * width
        head = 2 * (column >> log2(2 * WIDE)) + (column >> log2(HEAD) & 1)
        index = (2 * head + 1) * HEAD + (column & (HEAD - 1))
        index = jnp.where(column & WIDE == 0, -1, index)
    else:
        index = 2 * (column >> log2(HEAD)) * HEAD + (column & (HEAD - 1))
    here = (index >> shift == device) & (index & (size - 1) == entry)
    return dot(vector.astype(BF), here.astype(F32).astype(BF))


def joint_columns():
    blocks = [3 * head for head in range(H)]
    for pair in range(PAIRS):
        blocks += [3 * head + kind for kind in (1, 2) for head in (2 * pair, 2 * pair + 1)]
    return blocks


def begin_kernel(bits_dp, bits_seq, parts, packed, *refs):
    (
        tokens,
        joint_wide,
        up_wide,
        down_wide,
        out_wide,
        pair_bias,
        out_bias,
        gain_one,
        shift_one,
        up_bias,
        down_bias,
        gain_two,
        shift_two,
        tokens_low,
        tokens_t,
        tokens_rest,
        joint_out,
        vec,
        up_w,
        down_w,
        out_w,
        query,
        pair_own,
        wide,
        narrow,
        narrow_t,
        joint_here,
        joint_shard,
        up_shard,
        down_shard,
        out_shard,
        vec_sent,
        vec_landing,
        query_here,
        pair_here,
        own_sem,
        send_sem,
        recv_sem,
    ) = refs
    joint_w = joint_here if packed else joint_out
    net = Net(bits_dp, bits_seq)
    links = Links(net, send_sem, recv_sem)
    beside, upper, next_to, cores = stages_of(bits_dp, bits_seq)
    order = beside + upper + next_to + cores
    groups, local, width = tokens.shape
    due = net.greet(order)
    for other in range(1, parts):
        net.signal(ring(net, parts, other))
        due += 1
    loads = [
        pltpu.make_async_copy(tokens.at[g], wide.at[g], own_sem.at[g]) for g in range(groups)
    ]
    stores = [
        pltpu.make_async_copy(narrow.at[g], tokens_low.at[g], own_sem.at[groups + g])
        for g in range(groups)
    ]
    turned_stores = [pltpu.make_async_copy(narrow_t, tokens_t, own_sem.at[4 * groups + 7])]
    mine = net.place(())
    placed = [
        pltpu.make_async_copy(shard, full.at[mine], own_sem.at[2 * groups + i])
        for i, (shard, full) in enumerate(
            ((joint_shard, joint_w), (up_shard, up_w), (down_shard, down_w), (out_shard, out_w))
        )
    ]
    start(loads)
    joint = joint_wide[...]
    turned = [joint[:, b * HEAD : (b + 1) * HEAD] for b in joint_columns()]
    joint_shard[...] = jnp.concatenate(turned, axis=1).astype(BF)
    start(placed[:1])
    pl.semaphore_wait(pltpu.get_barrier_semaphore(), due)

    def prepare():
        up_shard[...] = up_wide[...].astype(BF)
        down_shard[...] = down_wide[...].astype(BF)
        out_shard[...] = out_wide[...].astype(BF)
        start(placed[1:])
        device = net.dp * parts + net.seq
        vec[...] = jnp.zeros_like(vec)
        lines = (out_bias, gain_one, shift_one, down_bias, gain_two, shift_two)
        for row, vector in enumerate(lines):
            vec[row : row + 1] = owned_row(vector[...], 0, device)
        for row in range(4):
            vec[6 + row : 7 + row] = owned_row(up_bias[...], row, device)
        for row in range(3):
            vec[10 + row : 11 + row] = owned_pair(pair_bias[...], row, device)
        wait(placed)

    def narrowed(g):
        wait(loads[g : g + 1])
        narrow[g] = wide[g].astype(BF)
        start(stores[g : g + 1])

    def turned_tokens():
        block = min(256, local)
        for g in range(groups):
            for at in range(0, local, block):
                rows = slice(at, at + block)
                narrow_t[g, :, rows] = narrow[g, rows].T
        start(turned_stores)

    cut = width + 2 * WIDE
    columns = (slice(0, cut), slice(cut, 3 * width))
    dones = [flat(order[:stage]) for stage in range(len(order))]
    ahead, behind = [
        [
            links.spread(joint_w, done, group, c, None if done else joint_shard)
            for done, group in zip(dones, order)
        ]
        for c in columns
    ]
    small = [
        [
            links.copy(
                functools.partial(Everywhere.line, vec_sent, stage),
                functools.partial(Everywhere.line, vec_landing, stage, i),
                functools.partial(net.partner, flips),
            )
            for i, flips in enumerate(subsets(group))
        ]
        for stage, group in enumerate(order)
    ]

    def small_start(stage):
        vec_sent[stage] = vec[...].astype(BF)
        start(small[stage])

    def small_add(stage):
        wait(small[stage])
        for i in range(len(small[stage])):
            vec[...] += vec_landing[stage, i].astype(F32)

    exchange = [
        links.copy(
            functools.partial(Everywhere.line, narrow, 0),
            functools.partial(Everywhere.line, tokens_rest, other - 1, 0),
            functools.partial(ring, net, parts, other),
        )
        for other in range(1, parts)
    ]
    some = slice(0, local // AHEAD)
    exchange_next = [
        links.copy(
            functools.partial(Everywhere.line, narrow, 1, some),
            functools.partial(Everywhere.line, tokens_rest, other - 1, 1, some),
            functools.partial(ring, net, parts, other),
        )
        for other in range(1, parts)
    ]

    def projected(part):
        bias = jnp.concatenate([vec[10 + i : 11 + i] for i in range(3)], axis=1)[:, columns[part]]
        block = min(512, local)
        for g in range(groups):

            def rows_of(b, carry):
                rows = pl.ds(pl.multiple_of(b * block, block), block)
                full = joint_w[..., columns[part]].reshape(width, -1)
                joint = (dot(narrow[g, rows], full) + bias).astype(BF)
                if part == 0:
                    query_here[g, rows] = joint[:, :width]
                    pair_here[g, rows, : cut - width] = joint[:, width:]
                else:
                    pair_here[g, rows, cut - width :] = joint
                return carry

            lax.fori_loop(0, local // block, rows_of, 0)

    late, rest = [], []
    last = len(order) - 1
    start(ahead[0])
    start(behind[0])
    prepare()
    small_start(0)
    for stage in range(last):
        done, group = dones[stage], order[stage]
        if stage < len(beside):
            for copies in rest:
                wait(copies)
            rest = [links.spread(full, done, group) for full in (up_w, down_w, out_w)]
            for copies in rest:
                start(copies)
        if stage == len(beside) - 1:
            narrowed(0)
            start(exchange)
        elif stage == len(beside):
            for g in range(1, groups):
                narrowed(g)
            start(exchange_next)
            turned_tokens()
        wait(ahead[stage])
        small_add(stage)
        start(ahead[stage + 1])
        small_start(stage + 1)
        if stage + 1 < last:
            wait(behind[stage])
            start(behind[stage + 1])
        if len(beside) <= stage < len(beside) + len(upper):
            for copies in rest:
                wait(copies)
            rest = []
            wait(late)
            late = links.spread(up_w, done, group)
            start(late)
    wait(ahead[last])
    small_add(last)
    if packed:
        projected(0)
    wait(behind[last - 1])
    start(behind[last])
    wait(behind[last])
    if packed:
        results = [
            pltpu.make_async_copy(joint_here, joint_out, own_sem.at[4 * groups + 4]),
            pltpu.make_async_copy(query_here, query, own_sem.at[4 * groups + 5]),
        ]
        start(results)
        projected(1)
        results.append(pltpu.make_async_copy(pair_here, pair_own, own_sem.at[4 * groups + 6]))
        start(results[2:])
        wait(results)
    wait(late)
    wait(exchange)
    wait(exchange_next)
    wait(stores)
    wait(turned_stores)


def begin(tokens, joint, up, down, out, vectors, parts):
    bits_dp, bits_seq = mesh_bits()
    bits = bits_dp + bits_seq
    groups, local, width = tokens.shape
    packed = joint.shape[0] % 16 == 0
    beside, upper, next_to, cores = stages_of(bits_dp, bits_seq)
    order = beside + upper + next_to + cores
    sends = sum(2 ** len(group) - 1 for group in order)
    copies = 3 * sends + 4 * sends + 2 * parts
    split = (2,) * bits
    hbm = pl.BlockSpec(memory_space=pl.ANY)
    vmem = pl.BlockSpec(memory_space=pltpu.VMEM)
    return pl.pallas_call(
        functools.partial(begin_kernel, bits_dp, bits_seq, parts, packed),
        in_specs=[hbm] + [vmem] * (4 + len(vectors)),
        out_specs=[hbm, hbm, hbm, hbm, vmem] + [hbm] * 5,
        out_shape=[
            jax.ShapeDtypeStruct((groups, local, width), BF),
            jax.ShapeDtypeStruct((groups, width, local), BF),
            jax.ShapeDtypeStruct((parts - 1, groups, local, width), BF),
            jax.ShapeDtypeStruct(split + joint.shape, BF),
            jax.ShapeDtypeStruct((16, width), F32),
            jax.ShapeDtypeStruct(split + up.shape, BF),
            jax.ShapeDtypeStruct(split + down.shape, BF),
            jax.ShapeDtypeStruct(split + out.shape, BF),
            jax.ShapeDtypeStruct((groups, local, width), BF),
            jax.ShapeDtypeStruct((groups, local, 2 * width), BF),
        ],
        scratch_shapes=[
            pltpu.VMEM((groups, local, width), F32),
            pltpu.VMEM((groups, local, width), BF),
            pltpu.VMEM((groups, width, local), BF),
            pltpu.VMEM(split + joint.shape if packed else (16, 128), BF),
            pltpu.VMEM(joint.shape, BF),
            pltpu.VMEM(up.shape, BF),
            pltpu.VMEM(down.shape, BF),
            pltpu.VMEM(out.shape, BF),
            pltpu.VMEM((len(order), 16, width), BF),
            pltpu.VMEM((len(order), 3, 16, width), BF),
            pltpu.VMEM((groups, local, width), BF),
            pltpu.VMEM((groups, local, 2 * width), BF),
            pltpu.SemaphoreType.DMA((4 * groups + 8,)),
            pltpu.SemaphoreType.DMA((copies,)),
            pltpu.SemaphoreType.DMA((copies,)),
        ],
        compiler_params=pltpu.CompilerParams(
            vmem_limit_bytes=62 * MIB, collective_id=0, has_side_effects=True
        ),
        name="begin",
    )(tokens, joint, up, down, out, *vectors)


def matrix_of(full):
    return full.reshape((-1,) + full.shape[-1:])


def owner_sums(arrays):
    size_dp, size_seq = lax.axis_size("dp"), lax.axis_size("seq")
    bits_dp, bits_seq = log2(size_dp), log2(size_seq)
    bits = bits_dp + bits_seq
    dp, seq = lax.axis_index("dp"), lax.axis_index("seq")
    arrays = [a.reshape((2,) * bits + (-1,) + a.shape[1:]) for a in arrays]
    left = list(range(bits))
    for bit in [bits_dp - 1] + list(range(bits_dp, bits)) + list(range(bits_dp - 2, -1, -1)):
        axis = left.index(bit)
        left.remove(bit)
        if bit < bits_dp:
            name, size, step, me = "dp", size_dp, 2 ** (bits_dp - 1 - bit), dp
        else:
            name, size, step, me = "seq", size_seq, 2 ** (bits - 1 - bit), seq
        mine = me // step % 2
        pairs = [(i, i ^ step) for i in range(size)]
        sent = [
            lax.dynamic_index_in_dim(a, 1 - mine, axis, keepdims=False).astype(BF) for a in arrays
        ]
        kept = [lax.dynamic_index_in_dim(a, mine, axis, keepdims=False) for a in arrays]
        arrived = [lax.ppermute(v, name, pairs) for v in sent]
        arrays = [k + a.astype(F32) for k, a in zip(kept, arrived)]
    return arrays


class Halving:
    def __init__(self, net, links, groups, held, landing, source=None):
        self.net, self.groups, self.held, self.landing = net, groups, held, landing
        self.gone = groups[0] if source is not None else ()
        self.rounds = []
        for stage, group in enumerate(groups):
            copies = []
            for i, flips in enumerate(subsets(group)):
                copies.append(
                    links.copy(
                        functools.partial(self.part, stage, flips, source),
                        functools.partial(self.slot, stage, i),
                        functools.partial(net.partner, flips),
                    )
                )
            self.rounds.append(copies)

    def place(self, stage, turned):
        done, group = flat(self.groups[:stage]), self.groups[stage]
        at = []
        for bit, mine in enumerate(self.net.mine):
            if bit in done or bit in group:
                at.append(1 - mine if bit in turned else mine)
            else:
                at.append(slice(None))
        return tuple(at)

    def part(self, stage, flips, source):
        at = self.place(stage, flips)
        return source.at[at] if stage == 0 and source is not None else self.held.at[self.cut(at)]

    def slot(self, stage, i):
        return self.landing[stage].at[i]

    def cut(self, at):
        return tuple(a for bit, a in enumerate(at) if bit not in self.gone)

    def start(self, stage):
        start(self.rounds[stage])

    def add(self, stage, out=None):
        wait(self.rounds[stage])
        at = self.cut(self.place(stage, ()))
        free = [i for i, a in enumerate(at) if isinstance(a, slice)]
        landing = self.landing[stage]

        def one(flat_index, carry):
            inner = [lax.rem(flat_index // 2 ** (len(free) - 1 - i), 2) for i in range(len(free))]
            there = list(at)
            for axis, value in zip(free, inner):
                there[axis] = value
            there = tuple(there)
            value = self.held[there].astype(F32)
            for i in range(landing.shape[0]):
                value += landing[(i,) + tuple(inner)].astype(F32)
            if out is None:
                self.held[there] = value.astype(BF)
            else:
                out[...] = value
            return carry

        if free:
            lax.fori_loop(0, 2 ** len(free), one, 0)
        else:
            one(0, 0)


class Everywhere:
    def __init__(self, net, links, groups, value, sent, landing):
        self.value, self.sent, self.landing = value, sent, landing
        self.rounds = [
            [
                links.copy(
                    functools.partial(self.line, sent, stage),
                    functools.partial(self.line, landing, stage, i),
                    functools.partial(net.partner, flips),
                )
                for i, flips in enumerate(subsets(group))
            ]
            for stage, group in enumerate(groups)
        ]

    @staticmethod
    def line(ref, *at):
        return ref.at[at]

    def start(self, stage):
        self.sent[stage] = self.value[...]
        start(self.rounds[stage])

    def add(self, stage, out=None):
        wait(self.rounds[stage])
        for i in range(len(self.rounds[stage])):
            self.value[...] += self.landing[stage, i]


def landing_shapes(groups, bits, rows, width):
    shapes, left = [], bits
    for group in groups:
        left -= len(group)
        shapes.append(pltpu.VMEM((2 ** len(group) - 1,) + (2,) * left + (rows, width), BF))
    return shapes


def sum_orders(bits_dp, bits_seq):
    beside, upper, next_to, cores = stages_of(bits_dp, bits_seq)
    far = upper[::-1]
    if len(beside) == 1 and len(beside[0]) == 1:
        near = [beside[0] + next_to[0]]
    else:
        near = beside + next_to
    return cores + beside + next_to + far, cores + next_to + beside + far, cores + near + far


def project_kernel(tokens, weight, bias, query, pair):
    x = tokens[...]
    width = x.shape[1]
    query[...] = (dot(x, weight[:, :width]) + bias[:, :width]).astype(BF)
    pair[...] = (dot(x, weight[:, width:]) + bias[:, width:]).astype(BF)


def project(tokens, weight, bias):
    count, width = tokens.shape
    block = min(512, count)

    def moving(columns):
        return pl.BlockSpec((block, columns), lambda b: (b, 0))

    def still(*shape):
        return pl.BlockSpec(shape, lambda b: (0, 0), pipeline_mode=pl.Buffered(1))

    return pl.pallas_call(
        project_kernel,
        grid=(count // block,),
        in_specs=[moving(width), still(width, 3 * width), still(1, 3 * width)],
        out_specs=[moving(width), moving(2 * width)],
        out_shape=[
            jax.ShapeDtypeStruct((count, width), BF),
            jax.ShapeDtypeStruct((count, 2 * width), BF),
        ],
        compiler_params=params(40, 1),
        name="project",
    )(tokens, weight, bias)


def attend_kernel(parts, groups, steps, blocks, bits_dp, bits_seq, *refs):
    (
        lengths,
        query,
        keys_own,
        values_own,
        weight,
        vec,
        tokens_low,
        _,
        _,
        _,
        _,
        e_out,
        mixed,
        mixed_t,
        inverse,
        pair_rest,
        tokens_rest,
        up_w,
        down_w,
        out_w,
        k_mask,
        v_ext,
        kept,
        tops,
        rest_here,
        pair_here,
        own_sem,
        send_sem,
        recv_sem,
    ) = refs
    local = keys_own.shape[1]
    block = query.shape[1]
    step = pl.program_id(0)
    chunk = min(256, local)

    net = Net(bits_dp, bits_seq)
    links = Links(net, send_sem, recv_sem)
    beside, upper, next_to, cores = stages_of(bits_dp, bits_seq)
    order = beside + upper + next_to + cores
    first, last = len(beside), len(order)
    lead = len(upper)
    rounds = []
    for stage in range(first, last):
        copies = []
        for full in (down_w, out_w):
            copies += links.spread(full, flat(order[:stage]), order[stage])
        ahead = stage + lead
        if ahead < last:
            copies += links.spread(up_w, flat(order[:ahead]), order[ahead])
        rounds.append(copies)
    if len(rounds) > 3:
        times = [i * steps // (len(rounds) + 1) for i in range(len(rounds) + 1)]
    else:
        times = [0, steps * 6 // 16, steps * 12 // 16, steps * 14 // 16]
    exchange = []
    for g in range(1, groups):
        left = slice(local // AHEAD if g == 1 else 0, local)
        exchange.append(
            [
                links.copy(
                    functools.partial(Everywhere.line, tokens_low, g, left),
                    functools.partial(Everywhere.line, tokens_rest, other - 1, g, left),
                    functools.partial(ring, net, parts, other),
                )
                for other in range(1, parts)
            ]
        )

    @pl.when(step == 0)
    def enter():
        due = net.greet(order[first:])
        for other in range(1, parts):
            net.signal(ring(net, parts, other))
            due += 1
        pl.semaphore_wait(pltpu.get_barrier_semaphore(), due)
        for copies in exchange:
            start(copies)
        start(rounds[0])

    for i in range(len(rounds)):
        @pl.when(step == times[i + 1])
        def advance():
            wait(rounds[i])
            if i + 1 < len(rounds):
                start(rounds[i + 1])

    stores = [
        pltpu.make_async_copy(pair_here.at[:, g], pair_rest.at[:, g], own_sem.at[groups + g])
        for g in range(groups)
    ]
    for group in range(groups):
        @pl.when(step == group * blocks * PAIRS)
        def other_keys():
            if group > 0:
                wait(exchange[group - 1])
            copy = pltpu.make_async_copy(tokens_rest.at[:, group], rest_here, own_sem.at[group])
            copy.start()
            width = weight.shape[0]
            bias = jnp.concatenate([vec[11:12], vec[12:13]], axis=1)
            for part in range(parts):
                rows = slice(part * local, (part + 1) * local)
                first_key = lax.rem(net.seq + part, parts) * local
                place = lax.broadcasted_iota(jnp.int32, (local, WIDE), 0) + first_key
                k_mask[rows] = jnp.where(place < lengths[group], 0.0, -1e30).astype(BF)
            copy.wait()
            for part in range(1, parts):
                for p in range(PAIRS):
                    columns = slice(2 * WIDE * p, 2 * WIDE * (p + 1))
                    both = dot(rest_here[part - 1], weight[:, width:][:, columns])
                    pair_here[part - 1, group, p] = (both + bias[:, columns]).astype(BF)
            start(stores[group : group + 1])

    @pl.when(step == steps)
    def leave():
        wait(stores)

    def decode(t):
        return lax.div(t, PAIRS * blocks), lax.rem(lax.div(t, blocks), PAIRS)

    group_then, pair_then = decode(jnp.maximum(step - 1, 0))

    @pl.when(lax.rem(step, blocks) == 1 % blocks)
    def prepare_values():
        for part in range(parts):
            rows = slice(part * local, (part + 1) * local)
            if part == 0:
                values = values_own[0]
            else:
                values = pair_here[part - 1, group_then, pair_then, :, WIDE:]
            turned = values.T
            v_ext[0, :HEAD, rows] = turned[:HEAD]
            v_ext[1, :HEAD, rows] = turned[HEAD:]

    @pl.when(step == 0)
    def ones():
        v_ext[:, HEAD:] = jnp.ones((2, HEAD, parts * local), BF)

    group_now, pair_now = decode(jnp.minimum(step, steps - 1))

    turned = query[0].T
    zero = jnp.zeros((HEAD, block), BF)
    one = (lax.broadcasted_iota(jnp.int32, (WIDE, block), 0) == 0).astype(F32).astype(BF)
    heads = []
    for head in range(2):
        if head == 0:
            picked = jnp.concatenate([turned[:HEAD], zero, one], axis=0)
        else:
            picked = jnp.concatenate([zero, turned[HEAD:], one], axis=0)
        top = tops[head : head + 1]
        out = None
        largest = None
        for at in range(0, parts * local, chunk):
            rows = slice(at, at + chunk)
            inside = slice(at % local, at % local + chunk)
            e = jnp.exp2((kept[head, rows] - top) * (SCALE * LOG2E)).astype(BF)
            e_out[at // local, 0, head, inside] = e
            add = dot(v_ext[head, :, rows], e)
            out = add if out is None else out + add
            if at < local:
                keys = keys_own[0, inside]
            else:
                keys = pair_here[at // local - 1, group_now, pair_now, inside, :WIDE]
            scores = dot(jnp.concatenate([keys, k_mask[rows]], axis=1), picked)
            kept[head, rows] = scores
            most = jnp.max(scores.reshape(chunk // 8, 8, block), axis=0)
            largest = most if largest is None else jnp.maximum(largest, most)
        tops[head : head + 1] = jnp.max(largest, axis=0, keepdims=True)
        inv = 1.0 / out[HEAD : HEAD + 1]
        inverse[0, 0, head : head + 1] = inv
        heads.append(out[:HEAD] * inv)
    both = jnp.concatenate(heads, axis=0).astype(BF)
    mixed_t[0] = both
    mixed[0] = both.T


def attend(lengths, query, pair_own, weight, vec, tokens_low, tokens_rest, up_w, down_w, out_w):
    groups, local, width = query.shape
    others = tokens_rest.shape[0]
    parts = others + 1
    block = min(512, local)
    blocks = local // block
    steps = groups * PAIRS * blocks
    bits_dp, bits_seq = mesh_bits()
    beside, upper, next_to, cores = stages_of(bits_dp, bits_seq)
    sends = sum(2 ** len(group) - 1 for group in upper + next_to + cores)
    copies = 3 * sends + groups * others

    def decode(t, place):
        return place(
            lax.div(t, PAIRS * blocks), lax.rem(lax.div(t, blocks), PAIRS), lax.rem(t, blocks)
        )

    def now(place):
        return lambda t: decode(jnp.minimum(t, steps - 1), place)

    def before(place):
        return lambda t: decode(jnp.maximum(t - 1, 0), place)

    def still(*shape):
        return pl.BlockSpec(shape, lambda t: (0,) * len(shape), pipeline_mode=pl.Buffered(1))

    hbm = pl.BlockSpec(memory_space=pl.ANY)
    passed = (tokens_rest, up_w, down_w, out_w)
    return pl.pallas_call(
        functools.partial(attend_kernel, parts, groups, steps, blocks, bits_dp, bits_seq),
        grid=(steps + 1,),
        in_specs=[
            pl.BlockSpec(memory_space=pltpu.SMEM),
            pl.BlockSpec((1, block, WIDE), now(lambda g, p, b: (g, b, p))),
            pl.BlockSpec((1, local, WIDE), now(lambda g, p, b: (g, 0, 2 * p))),
            pl.BlockSpec((1, local, WIDE), before(lambda g, p, b: (g, 0, 2 * p + 1))),
            still(width, 3 * width),
            still(*vec.shape),
        ]
        + [hbm] * 5,
        out_specs=[
            pl.BlockSpec((parts, 1, 2, local, block), before(lambda g, p, b: (0, g, p, 0, b))),
            pl.BlockSpec((1, block, WIDE), before(lambda g, p, b: (g, b, p))),
            pl.BlockSpec((1, WIDE, block), before(lambda g, p, b: (g, p, b))),
            pl.BlockSpec((1, 1, 2, block), before(lambda g, p, b: (g, p, 0, b))),
            hbm,
        ]
        + [hbm] * 4,
        out_shape=[
            jax.ShapeDtypeStruct((parts, groups, H, local, local), BF),
            jax.ShapeDtypeStruct((groups, local, width), BF),
            jax.ShapeDtypeStruct((groups, width, local), BF),
            jax.ShapeDtypeStruct((groups, PAIRS, 2, local), F32),
            jax.ShapeDtypeStruct((others, groups, PAIRS, local, 2 * WIDE), BF),
        ]
        + [jax.ShapeDtypeStruct(v.shape, v.dtype) for v in passed],
        input_output_aliases={7: 5, 8: 6, 9: 7, 10: 8},
        scratch_shapes=[
            pltpu.VMEM((parts * local, WIDE), BF),
            pltpu.VMEM((2, WIDE, parts * local), BF),
            pltpu.VMEM((2, parts * local, block), F32),
            pltpu.VMEM((8, block), F32),
            pltpu.VMEM((others, local, width), BF),
            pltpu.VMEM((others, groups, PAIRS, local, 2 * WIDE), BF),
            pltpu.SemaphoreType.DMA((2 * groups,)),
            pltpu.SemaphoreType.DMA((copies,)),
            pltpu.SemaphoreType.DMA((copies,)),
        ],
        compiler_params=pltpu.CompilerParams(
            vmem_limit_bytes=62 * MIB,
            dimension_semantics=("arbitrary",),
            collective_id=1,
            has_side_effects=True,
        ),
        name="attend",
    )(lengths, query, pair_own, pair_own, weight, vec, tokens_low, *passed)


def middle_kernel(
    packed,
    tokens,
    cotangent,
    mixed,
    out_w,
    up_w,
    down_w,
    rows,
    result,
    partial,
    mixed_grad,
    upper_sums,
    lower_sums,
    vec_sums,
    out_wg,
    up_wg,
    down_wg,
    row_sums,
    up_bias_sum,
):
    first = pl.program_id(0) == 0

    @pl.when(first)
    def clear():
        out_wg[...] = jnp.zeros_like(out_wg)
        up_wg[...] = jnp.zeros_like(up_wg)
        down_wg[...] = jnp.zeros_like(down_wg)
        row_sums[...] = jnp.zeros_like(row_sums)
        up_bias_sum[...] = jnp.zeros_like(up_bias_sum)

    pieces = up_w.shape[1] // tokens.shape[1]
    up_bias = jnp.concatenate([rows[6 + i : 7 + i] for i in range(pieces)], axis=1)
    out_bias, gain_one, shift_one = rows[0:1], rows[1:2], rows[2:3]
    down_bias, gain_two, shift_two = rows[3:4], rows[4:5], rows[5:6]

    def mean(v):
        return jnp.mean(v, axis=-1, keepdims=True)

    def total(v):
        return jnp.sum(v, axis=0, keepdims=True)

    x = tokens[...]
    heads = mixed[...]
    hidden = x + (dot(heads, out_w[...]) + out_bias)
    centred = hidden - mean(hidden)
    r_one = lax.rsqrt(mean(centred * centred) + EPS)
    n_one = centred * r_one
    normal = n_one * gain_one + shift_one
    normal_low = normal.astype(BF)
    inner = dot(normal_low, up_w[...]) + up_bias
    square = inner * inner
    tanh = jnp.tanh(inner * (GELU_A + (GELU_A * GELU_B) * square))
    half = 0.5 + 0.5 * tanh
    active = (inner * half).astype(BF)
    slope = half + (0.5 * inner) * (1.0 - tanh * tanh) * (
        GELU_A + (3.0 * GELU_A * GELU_B) * square
    )
    branch = dot(active, down_w[...]) + down_bias
    last = normal + branch + x
    centred = last - mean(last)
    r_two = lax.rsqrt(mean(centred * centred) + EPS)
    n_two = centred * r_two
    result[...] = n_two * gain_two + shift_two
    grad = cotangent[...]
    e_two = grad * gain_two
    back = r_two * (e_two - mean(e_two) - n_two * mean(e_two * n_two))
    branch_grad = back.astype(BF)
    down_wg[...] += dot(active, branch_grad, "tn")
    inner_grad_wide = slope * dot(branch_grad, down_w[...], "nt")
    inner_grad = inner_grad_wide.astype(BF)
    up_wg[...] += dot(normal_low, inner_grad, "tn")
    up_bias_sum[...] += total(inner_grad.astype(F32))
    norm_grad = back + dot(inner_grad, up_w[...], "nt")
    e_one = norm_grad * gain_one
    hidden_grad = r_one * (e_one - mean(e_one) - n_one * mean(e_one * n_one))
    attn_grad = hidden_grad.astype(BF)
    partial[...] = back + hidden_grad
    out_wg[...] += dot(heads, attn_grad, "tn")
    mixed_grad[...] = dot(attn_grad, out_w[...], "nt").astype(BF)
    row_sums[0:1] += total(attn_grad.astype(F32))
    row_sums[1:2] += total(norm_grad * n_one)
    row_sums[2:3] += total(norm_grad)
    row_sums[3:4] += total(branch_grad.astype(F32))
    row_sums[4:5] += total(grad * n_two)
    row_sums[5:6] += total(grad)

    @pl.when(pl.program_id(0) == pl.num_programs(0) - 1)
    def pack():
        width = tokens.shape[1]
        pieces = up_wg.shape[1] // width
        vec_sums[...] = jnp.zeros_like(vec_sums)
        vec_sums[0:8] = row_sums[...]
        for piece in range(pieces):
            columns = slice(piece * width, (piece + 1) * width)
            vec_sums[8 + piece : 9 + piece] = up_bias_sum[:, columns]
        if not packed:
            upper_sums[:, :width] = out_wg[...]
            upper_sums[:, width:] = up_wg[...]
            lower_sums[...] = down_wg[...]
            return
        owners = upper_sums.shape[0]
        rows_out = out_wg.shape[0] // owners
        rows_down = down_wg.shape[0] // owners

        def one(owner, carry):
            near = pl.ds(pl.multiple_of(owner * rows_out, rows_out), rows_out)
            upper_sums[owner, :rows_out] = out_wg[near].astype(BF)
            for piece in range(pieces):
                columns = slice(piece * width, (piece + 1) * width)
                to = slice((piece + 1) * rows_out, (piece + 2) * rows_out)
                upper_sums[owner, to] = up_wg[near, columns].astype(BF)
            far = pl.ds(pl.multiple_of(owner * rows_down, rows_down), rows_down)
            lower_sums[owner] = down_wg[far].astype(BF)
            return carry

        lax.fori_loop(0, owners, one, 0)


def middle(tokens, cotangent, mixed, out_w, up_w, down_w, rows, owners):
    count, width = tokens.shape
    hidden = up_w.shape[1]
    block = min(512, count)
    packed = whole_tiles(width, owners)

    def moving(columns=width):
        return pl.BlockSpec((block, columns), lambda b: (b, 0))

    def still(*shape):
        return pl.BlockSpec(shape, lambda b: (0,) * len(shape), pipeline_mode=pl.Buffered(1))

    rows_upper = width // owners * (1 + hidden // width)
    rows_lower = hidden // owners
    if packed:
        sums = [((owners, rows_upper, width), BF), ((owners, rows_lower, width), BF)]
    else:
        sums = [((width, width + hidden), F32), ((hidden, width), F32)]
    return pl.pallas_call(
        functools.partial(middle_kernel, packed),
        grid=(count // block,),
        in_specs=[
            moving(),
            moving(),
            moving(),
            still(width, width),
            still(width, hidden),
            still(hidden, width),
            still(16, width),
        ],
        out_specs=[
            moving(),
            moving(),
            moving(),
        ]
        + [still(*shape) for shape, _ in sums]
        + [still(16, width)],
        out_shape=[
            jax.ShapeDtypeStruct((count, width), F32),
            jax.ShapeDtypeStruct((count, width), F32),
            jax.ShapeDtypeStruct((count, width), BF),
        ]
        + [jax.ShapeDtypeStruct(shape, kind) for shape, kind in sums]
        + [jax.ShapeDtypeStruct((16, width), F32)],
        scratch_shapes=[
            pltpu.VMEM((width, width), F32),
            pltpu.VMEM((width, hidden), F32),
            pltpu.VMEM((hidden, width), F32),
            pltpu.VMEM((8, width), F32),
            pltpu.VMEM((1, hidden), F32),
        ],
        compiler_params=params(62, 1),
        name="middle",
    )(tokens, cotangent, mixed, out_w, up_w, down_w, rows)


def pull_kernel(parts, groups, bits_dp, bits_seq, packed, *refs):
    taken = 0

    def take(count):
        nonlocal taken
        taken += count
        return refs[taken - count : taken]

    e_part, query, pair_own, pair_rest, mixed_grad, mixed_t, inverse = take(7)
    tokens_t, tokens_rest, weight, partial = take(4)
    sources = take(2) if packed else ()
    (vec_in,) = take(1)
    share_own, arrived, joint_out, vec_out = take(4)
    owned = take(2) if packed else ()
    d_scores, joint_grad, total, dq_sums, weight_grad, bias_grad, shares = take(7)
    share_send, share_recv, own_sem = take(3)
    step = pl.program_id(0)
    steps = pl.num_programs(0)
    each = groups * PAIRS
    part = lax.rem(lax.div(step, each) + 1, parts)
    own = part == 0
    inside = lax.rem(step, each)
    group = jnp.where(own, lax.rem(inside, groups), lax.div(inside, PAIRS))
    pair = jnp.where(own, lax.div(inside, groups), lax.rem(inside, PAIRS))

    net = Net(bits_dp, bits_seq)
    bits = net.bits
    orders = sum_orders(bits_dp, bits_seq)
    streams, loads = [], []
    if packed:
        upper_held, lower_held = take(2)
        joint_helds = take(len(JOINT_PARTS))
        vec_sent, vec_landing, bias_sent, bias_landing = take(4)
        send_sem, recv_sem = take(2)
        links = Links(net, send_sem, recv_sem)
        upper, lower = streams = [
            Halving(net, links, orders[i], held, take(len(orders[i])), sources[i])
            for i, held in enumerate((upper_held, lower_held))
        ]
        joint = [Halving(net, links, orders[2], h, take(len(orders[2]))) for h in joint_helds]
        early_vec = Everywhere(net, links, orders[2], vec_out.at[0:16], vec_sent, vec_landing)
        late_vec = Everywhere(net, links, orders[2], bias_grad, bias_sent, bias_landing)
        for i, stream in enumerate(streams):
            at = stream.place(0, ())
            loads.append(pltpu.make_async_copy(sources[i].at[at], stream.held, own_sem.at[i]))
    stores = [
        pltpu.make_async_copy(total.at[g], share_own.at[g], own_sem.at[2 + g])
        for g in range(groups)
    ]
    partials = [
        pltpu.make_async_copy(partial.at[g], total.at[g], own_sem.at[2 + groups + g])
        for g in range(groups)
    ]

    def share_copy(other, g):
        return pltpu.make_async_remote_copy(
            src_ref=shares.at[other - 1, g],
            dst_ref=arrived.at[other - 1, g],
            send_sem=share_send.at[other - 1, g],
            recv_sem=share_recv.at[other - 1, g],
            device_id=(net.dp, lax.rem(net.seq + other, parts)),
            device_id_type=MESH,
        )

    @pl.when(step == 0)
    def enter():
        due = parts - 1
        for other in range(1, parts):
            net.signal((net.dp, lax.rem(net.seq + other, parts)))
        if packed:
            due += net.greet(orders[0]) + net.greet(orders[2])
        start(loads)
        start(partials)
        pl.semaphore_wait(pltpu.get_barrier_semaphore(), due)
        for stream in streams:
            stream.start(0)

    def advance(streams, stage, outs, count):
        for stream, out in zip(streams, outs):
            stream.add(stage, out if stage == count - 1 else None)
            if stage < count - 1:
                stream.start(stage + 1)

    def pack(index):
        first, count = JOINT_PARTS[index]
        held = joint[index].held
        rows_each, width = weight_grad.shape[0] // 2**bits, weight_grad.shape[0]
        columns = slice(first * WIDE, (first + count) * WIDE)
        doubled = slice(width + 2 * first * WIDE, width + 2 * (first + count) * WIDE)

        def one(flat_index, carry):
            place = tuple(lax.rem(flat_index // 2 ** (bits - 1 - i), 2) for i in range(bits))
            near = pl.ds(pl.multiple_of(flat_index * rows_each, rows_each), rows_each)
            held[place + (slice(None), slice(0, count * WIDE))] = weight_grad[near, columns].astype(BF)
            held[place + (slice(None), slice(count * WIDE, 3 * count * WIDE))] = weight_grad[
                near, doubled
            ].astype(BF)
            return carry

        lax.fori_loop(0, 2**bits, one, 0)

    def joint_place(index):
        first, count = JOINT_PARTS[index]
        return joint_out.at[:, 3 * first * WIDE : 3 * (first + count) * WIDE]

    if packed:
        last = len(orders[2])
        for stage, when in enumerate((1, 5, 9, 12)):
            @pl.when(step == when)
            def ffn():
                if stage == 0:
                    wait(loads)
                advance(streams, stage, owned, len(orders[0]))

        @pl.when(step == steps - 2 * groups)
        def joint_early():
            pack(0)
            vec_out[...] = vec_in[...]
            joint[0].start(0)
            early_vec.start(0)

        @pl.when(step == steps - 2 * groups + 1)
        def joint_early_near():
            advance((joint[0], early_vec), 0, (None, None), last)

        @pl.when(step == steps - groups)
        def joint_middle():
            pack(1)
            joint[1].start(0)

        @pl.when(step == steps - 1)
        def joint_middle_near():
            advance((joint[0], early_vec), 1, (None, None), last)
            advance((joint[1],), 0, (None,), last)

    local = query.shape[1]
    chunk = min(256, local)
    turned = mixed_grad[0].astype(F32).T
    mixed = mixed_t[0].astype(F32)
    values = jnp.where(own, pair_own[0, :, WIDE:], pair_rest[0, 0, 0, :, WIDE:])
    keys_t = jnp.where(own, pair_own[0, :, :WIDE], pair_rest[0, 0, 0, :, :WIDE]).T
    query_now = query[0]
    lane = lax.broadcasted_iota(jnp.int32, (local, WIDE), 1)
    zero = jnp.zeros((HEAD, local), BF)
    grad_t, grad, centre, picked = [], [], [], []
    for head in range(2):
        side = slice(head * HEAD, (head + 1) * HEAD)
        inv = inverse[0, 0, head : head + 1]
        centre.append(inv * jnp.sum(turned[side] * mixed[side], axis=0, keepdims=True))
        scaled = (turned[side] * inv).astype(BF)
        grad_t.append(jnp.concatenate([scaled, zero] if head == 0 else [zero, scaled], axis=0))
        grad.append(grad_t[head].T)
        kept = lane < HEAD if head == 0 else lane >= HEAD
        picked.append(jnp.where(kept, query_now, jnp.zeros_like(query_now)))

    width = weight.shape[0]
    at_queries = pl.ds(pl.multiple_of(pair * WIDE, WIDE), WIDE)
    start_at = width + pair * (2 * WIDE)
    at_keys = pl.ds(pl.multiple_of(start_at, WIDE), WIDE)
    at_values = pl.ds(pl.multiple_of(start_at + WIDE, WIDE), WIDE)
    at_both = pl.ds(pl.multiple_of(start_at, WIDE), 2 * WIDE)

    def key_grad(rows):
        sums = dot(d_scores[0, rows], picked[0]) + dot(d_scores[1, rows], picked[1])
        joint_grad[group, rows, at_keys] = (sums * SCALE).astype(BF)

    @pl.when(step == 0)
    def clear():
        weight_grad[...] = jnp.zeros_like(weight_grad)
        bias_grad[...] = jnp.zeros_like(bias_grad)
        dq_sums[...] = jnp.zeros_like(dq_sums)

    column = group * PAIRS + pair
    value_sums = jnp.zeros((1, WIDE), F32)
    last_rows = None
    for at in range(0, local, chunk):
        rows = slice(at, at + chunk)
        for head in range(2):
            pulled = dot(values[rows], grad_t[head])
            e = e_part[0, 0, head, rows].astype(F32)
            d_scores[head, rows] = (e * (pulled - centre[head])).astype(BF)
        sums = dot(e_part[0, 0, 0, rows], grad[0]) + dot(e_part[0, 0, 1, rows], grad[1])
        sums = sums.astype(BF)
        joint_grad[group, rows, at_values] = sums
        value_sums += jnp.sum(sums.astype(F32), axis=0, keepdims=True)
        if last_rows is not None:
            key_grad(last_rows)
        last_rows = rows
    key_grad(last_rows)
    for head in range(2):
        side = slice(head * HEAD, (head + 1) * HEAD)
        dq_sums[column, side] += dot(keys_t, d_scores[head])[side]
    bias_grad[1:2, at_queries] += value_sums

    @pl.when(own)
    def near():
        dq = (dq_sums[column] * SCALE).astype(BF).T
        joint_grad[group, :, at_queries] = dq
        bias_grad[0:1, at_queries] += jnp.sum(dq.astype(F32), axis=0, keepdims=True)
        weight_grad[:, at_queries] += dot(tokens_t[group], dq)
        weight_grad[:, at_both] += dot(tokens_t[group], joint_grad[group, :, at_both])

    for other in range(1, parts):
        for g in range(groups):
            @pl.when(step == ((other - 1) * groups + g + 1) * PAIRS - 1)
            def finish_far():
                for at in range(0, local, chunk):
                    rows = slice(at, at + chunk)
                    part_share = dot(joint_grad[g, rows, width:], weight[:, width:], "nt")
                    shares[other - 1, g, rows] = part_share.astype(BF)
                share_copy(other, g).start()
                weight_grad[:, width:] += dot(tokens_rest[0, 0], joint_grad[g, :, width:], "tn")

    def input_grads(g):
        for at in range(0, local, chunk):
            rows = slice(at, at + chunk)
            total[g, rows] += dot(joint_grad[g, rows], weight[...], "nt")
        start(stores[g : g + 1])

    @pl.when(step == steps - 1)
    def finish():
        work = list(range(groups))
        if packed:
            pack(2)
            joint[2].start(0)
            late_vec.start(0)
            advance((joint[1],), 1, (None,), last)
        wait(partials)
        if packed:
            for stage in range(last):
                if work:
                    input_grads(work.pop(0))
                outs = (joint_place(2), None)
                advance((joint[2], late_vec), stage, outs, last)
                if stage == 0:
                    advance((joint[0], early_vec), last - 1, (joint_place(0), None), last)
            joint[1].add(last - 1, joint_place(1))
        else:
            vec_out[...] = vec_in[...]
            joint_out[...] = weight_grad[...]
        for g in work:
            input_grads(g)
        vec_out[12:14] = bias_grad[0:2]
        for g in range(groups):
            for other in range(1, parts):
                share_copy(other, g).wait()
        wait(stores)


def pull(
    e_all,
    query,
    pair_own,
    pair_rest,
    mixed_grad,
    mixed_t,
    inverse,
    own,
    rest,
    weight,
    partial,
    upper_sums,
    lower_sums,
    vec_sums,
):
    parts, groups, _, local, _ = e_all.shape
    width = H * HEAD
    each = groups * PAIRS
    bits_dp, bits_seq = mesh_bits()
    bits = bits_dp + bits_seq
    orders = sum_orders(bits_dp, bits_seq)
    packed = whole_tiles(width, 2**bits)
    split = (2,) * bits
    sums, out_blocks, extra = [], [], []
    if packed:
        rows_upper, rows_lower = upper_sums.shape[1], lower_sums.shape[1]
        rows_joint = width // 2**bits
        sums = [v.reshape(split + v.shape[1:]) for v in (upper_sums, lower_sums)]
        out_blocks = [(rows_joint, 3 * width), (16, width), (rows_upper, width), (rows_lower, width)]
        joint_widths = [3 * count * WIDE for _, count in JOINT_PARTS]
        last = len(orders[2])
        sends = sum(2 ** len(g) - 1 for order in orders for g in order)
        sends += 4 * sum(2 ** len(g) - 1 for g in orders[2])
        extra = [
            pltpu.VMEM((2,) * (bits - 1) + (rows_upper, width), BF),
            pltpu.VMEM((2,) * (bits - 1) + (rows_lower, width), BF),
        ]
        extra += [pltpu.VMEM(split + (rows_joint, columns), BF) for columns in joint_widths]
        extra += [
            pltpu.VMEM((last, 16, width), F32),
            pltpu.VMEM((last, 3, 16, width), F32),
            pltpu.VMEM((last, 8, width), F32),
            pltpu.VMEM((last, 3, 8, width), F32),
            pltpu.SemaphoreType.DMA((sends,)),
            pltpu.SemaphoreType.DMA((sends,)),
        ]
        extra += landing_shapes(orders[0], bits, rows_upper, width)
        extra += landing_shapes(orders[1], bits, rows_lower, width)
        for columns in joint_widths:
            extra += landing_shapes(orders[2], bits, rows_joint, columns)
    else:
        out_blocks = [(width, 3 * width), (16, width)]

    def decode(t):
        part, inside = lax.rem(lax.div(t, each) + 1, parts), lax.rem(t, each)
        own = part == 0
        group = jnp.where(own, lax.rem(inside, groups), lax.div(inside, PAIRS))
        pair = jnp.where(own, lax.div(inside, groups), lax.rem(inside, PAIRS))
        return part, group, pair

    def at(place):
        return lambda t: place(*decode(t))

    def own_at(place):
        def index(t):
            part, group, pair = decode(t)
            return place(jnp.where(part == 0, group, 0), jnp.where(part == 0, pair, 0))

        return index

    def rest_at(place):
        def index(t):
            t = jnp.minimum(t, (parts - 1) * each - 1)
            return place(
                lax.div(t, each), lax.rem(lax.div(t, PAIRS), groups), lax.rem(t, PAIRS)
            )

        return index

    def still(*shape):
        return pl.BlockSpec(shape, lambda t: (0,) * len(shape), pipeline_mode=pl.Buffered(1))

    once = pl.Buffered(1)
    return pl.pallas_call(
        functools.partial(pull_kernel, parts, groups, bits_dp, bits_seq, packed),
        grid=(parts * each,),
        in_specs=[
            pl.BlockSpec((1, 1, 2, local, local), at(lambda j, g, p: (j, g, p, 0, 0))),
            pl.BlockSpec((1, local, WIDE), at(lambda j, g, p: (g, 0, p))),
            pl.BlockSpec((1, local, 2 * WIDE), own_at(lambda g, p: (g, 0, p))),
            pl.BlockSpec((1, 1, 1, local, 2 * WIDE), rest_at(lambda j, g, p: (j, g, p, 0, 0))),
            pl.BlockSpec((1, local, WIDE), at(lambda j, g, p: (g, 0, p))),
            pl.BlockSpec((1, WIDE, local), at(lambda j, g, p: (g, p, 0))),
            pl.BlockSpec((1, 1, 2, local), at(lambda j, g, p: (g, p, 0, 0))),
            still(groups, width, local),
            pl.BlockSpec(
                (1, 1, local, width), rest_at(lambda j, g, p: (j, g, 0, 0)), pipeline_mode=once
            ),
            still(width, 3 * width),
            pl.BlockSpec(memory_space=pl.ANY),
        ]
        + [pl.BlockSpec(memory_space=pl.ANY)] * len(sums)
        + [still(16, width)],
        out_specs=[
            pl.BlockSpec(memory_space=pl.ANY),
            pl.BlockSpec(memory_space=pl.ANY),
        ]
        + [still(*shape) for shape in out_blocks],
        out_shape=[
            jax.ShapeDtypeStruct((groups, local, width), F32),
            jax.ShapeDtypeStruct((parts - 1, groups, local, width), BF),
        ]
        + [jax.ShapeDtypeStruct(shape, F32) for shape in out_blocks],
        scratch_shapes=[
            pltpu.VMEM((2, local, local), BF),
            pltpu.VMEM((groups, local, 3 * width), BF),
            pltpu.VMEM((groups, local, width), F32),
            pltpu.VMEM((each, WIDE, local), F32),
            pltpu.VMEM((width, 3 * width), F32),
            pltpu.VMEM((8, width), F32),
            pltpu.VMEM((parts - 1, groups, local, width), BF),
            pltpu.SemaphoreType.DMA((parts - 1, groups)),
            pltpu.SemaphoreType.DMA((parts - 1, groups)),
            pltpu.SemaphoreType.DMA((2 + 2 * groups,)),
        ]
        + extra,
        compiler_params=pltpu.CompilerParams(
            vmem_limit_bytes=63 * MIB,
            dimension_semantics=("arbitrary",),
            collective_id=2,
            has_side_effects=True,
        ),
        name="pull",
    )(
        e_all,
        query,
        pair_own,
        pair_rest,
        mixed_grad,
        mixed_t,
        inverse,
        own,
        rest,
        weight,
        partial,
        *sums,
        vec_sums,
    )


def finish_kernel(bits_dp, bits_seq, share, arrived, joint, vec, upper, lower, *outs):
    (
        input_grad,
        joint_sum,
        pair_sum,
        out_sum,
        out_bias,
        gain_one,
        shift_one,
        up_sum,
        up_bias,
        down_sum,
        down_bias,
        gain_two,
        shift_two,
    ) = outs
    value = share[...]
    for other in range(arrived.shape[0]):
        value += arrived[other].astype(F32)
    input_grad[...] = value

    @pl.when(pl.program_id(0) == 0)
    def small():
        net = Net(bits_dp, bits_seq)
        device = net.dp * 2**bits_seq + net.seq
        rows, width = out_sum.shape
        summed = joint[...]
        turned = []
        for head in range(H):
            pair = head // 2
            for first, count in JOINT_PARTS:
                if first <= pair < first + count:
                    base = 3 * first * WIDE + head % 2 * HEAD
                    both = base + (count + 2 * (pair - first)) * WIDE
                    for at in (base + (pair - first) * WIDE, both, both + WIDE):
                        turned.append(summed[:, at : at + HEAD])
        joint_sum[...] = jnp.concatenate(turned, axis=1)
        out_sum[...] = upper[:rows]
        for piece in range(up_sum.shape[1] // width):
            up_sum[:, piece * width : (piece + 1) * width] = upper[
                (piece + 1) * rows : (piece + 2) * rows
            ]
        down_sum[...] = lower[...]
        lines = vec[...]
        which = lax.broadcasted_iota(jnp.int32, lines.shape, 0)

        def entries(out, row, column):
            line = jnp.sum(jnp.where(which == row, lines, 0.0), axis=0, keepdims=True)
            line = jnp.broadcast_to(line, (8, width))
            out[...] = pltpu.roll(line, lax.rem(width - column, width), 1)[:1, : out.shape[1]]

        plain = (out_bias, gain_one, shift_one, down_bias, gain_two, shift_two)
        for row, out in enumerate(plain):
            entries(out, row, device * out.shape[1])
        first = device * up_bias.shape[1]
        entries(up_bias, 8 + first // width, lax.rem(first, width))
        first = device * pair_sum.shape[1]
        kind = lax.rem(first // HEAD, 2)
        entries(pair_sum, 12 + kind, first // WIDE * HEAD + lax.rem(first, HEAD))


def finish(share, arrived, joint, vec, upper, lower, shards):
    groups, local, width = share.shape
    block = min(1024, local)
    each = local // block

    def moving(*lead):
        return pl.BlockSpec(
            (1,) * len(lead) + (block, width), lambda b: (b // each, b % each, 0)
        )

    def still(shape):
        return pl.BlockSpec(shape, lambda b: (0,) * len(shape), pipeline_mode=pl.Buffered(1))

    bits_dp, bits_seq = mesh_bits()
    others = arrived.shape[0]
    small = (joint, vec, upper, lower)
    outs = pl.pallas_call(
        functools.partial(finish_kernel, bits_dp, bits_seq),
        grid=(groups * each,),
        in_specs=[
            moving(1),
            pl.BlockSpec((others, 1, block, width), lambda b: (0, b // each, b % each, 0)),
        ]
        + [still(v.shape) for v in small],
        out_specs=[moving(1)] + [still(shape) for shape in shards],
        out_shape=[jax.ShapeDtypeStruct(share.shape, F32)]
        + [jax.ShapeDtypeStruct(shape, F32) for shape in shards],
        compiler_params=params(62, 1),
        name="finish",
    )(share, arrived, *small)
    return [outs[0]] + [
        v.reshape(v.shape[1:]) if v.shape[0] == 1 else v for v in outs[1:]
    ]


def per_device(
    tokens,
    lengths,
    joint_weight,
    joint_bias,
    out_weight,
    out_bias,
    gain_first,
    shift_first,
    up_weight,
    up_bias,
    down_weight,
    down_bias,
    gain_second,
    shift_second,
    cotangent,
):
    groups, local, width = tokens.shape
    parts = lax.axis_size("seq")
    devices = lax.axis_size("dp") * parts
    me = lax.axis_index("seq")
    rows = groups * local
    own_rows = joint_weight.shape[0]
    vectors = [
        joint_bias,
        out_bias,
        gain_first,
        shift_first,
        up_bias,
        down_bias,
        gain_second,
        shift_second,
    ]
    lens = [v.shape[0] for v in vectors]
    tokens_low, tokens_t, tokens_rest, joint_w, vec, up_w, down_w, out_w, query, pair_own = begin(
        tokens,
        joint_weight,
        up_weight,
        down_weight,
        out_weight,
        [v.reshape(1, -1) for v in vectors],
        parts,
    )
    joint_w = matrix_of(joint_w)
    pieces = up_weight.shape[1] // width
    if not whole_tiles(width, devices):
        query, pair_own = project(
            tokens_low.reshape(rows, width), joint_w, vec[10:13].reshape(1, -1)
        )
        query = query.reshape(groups, local, width)
        pair_own = pair_own.reshape(groups, local, 2 * width)

    e_all, mixed, mixed_t, inverse, pair_rest, tokens_rest, up_w, down_w, out_w = attend(
        lengths, query, pair_own, joint_w, vec, tokens_low, tokens_rest, up_w, down_w, out_w
    )
    out_w, up_w, down_w = matrix_of(out_w), matrix_of(up_w), matrix_of(down_w)

    result, partial, mixed_grad, upper_sums, lower_sums, vec_sums = middle(
        tokens.reshape(rows, width),
        cotangent.reshape(rows, width),
        mixed.reshape(rows, width),
        out_w,
        up_w,
        down_w,
        vec,
        devices,
    )
    mixed_grad = mixed_grad.reshape(groups, local, width)
    share, arrived, joint, vec, *owned = pull(
        e_all,
        query,
        pair_own,
        pair_rest,
        mixed_grad,
        mixed_t,
        inverse,
        tokens_t,
        tokens_rest,
        joint_w,
        partial.reshape(groups, local, width),
        upper_sums,
        lower_sums,
        vec_sums,
    )
    if owned:
        upper, lower = owned
        shards = [
            (1, v.shape[0]) if v.ndim == 1 else v.shape
            for v in (
                joint_weight,
                joint_bias,
                out_weight,
                out_bias,
                gain_first,
                shift_first,
                up_weight,
                up_bias,
                down_weight,
                down_bias,
                gain_second,
                shift_second,
            )
        ]
        outs = finish(share, arrived, joint, vec, upper, lower, shards)
        return (result.reshape(groups, local, width), *outs)
    input_grad = share + jnp.sum(arrived.astype(F32), axis=0)
    joint_sum, upper, lower = owner_sums([joint, upper_sums, lower_sums])
    out_sum, up_sum = upper[:, :width], upper[:, width:]
    vec = lax.psum(vec, ("dp", "seq"))
    device = lax.axis_index("dp") * parts + me
    back = [joint_columns().index(block) for block in range(3 * H)]
    joint_sum = joint_sum.reshape(own_rows, 3 * H, HEAD)
    joint_sum = jnp.stack([joint_sum[:, b] for b in back], axis=1).reshape(own_rows, 3 * width)
    pair_grad = jnp.stack(
        [vec[12].reshape(H, HEAD), vec[13].reshape(H, HEAD)], axis=1
    ).reshape(2 * width)
    sums = [
        pair_grad,
        vec[0],
        vec[1],
        vec[2],
        vec[8 : 8 + pieces].reshape(-1),
        vec[3],
        vec[4],
        vec[5],
    ]
    small = [
        lax.dynamic_slice_in_dim(v, device * size, size, 0) for v, size in zip(sums, lens)
    ]
    return (
        result.reshape(groups, local, width),
        input_grad,
        joint_sum,
        small[0],
        out_sum,
        small[1],
        small[2],
        small[3],
        up_sum,
        small[4],
        lower,
        small[5],
        small[6],
        small[7],
    )


def solution(mesh):
    both = ("dp", "seq")
    matrix, vector, whole = P(both, None), P(both), P("dp", "seq", None)
    return jax.shard_map(
        per_device,
        mesh=mesh,
        in_specs=(
            whole,
            P("dp"),
            matrix,
            vector,
            matrix,
            vector,
            vector,
            vector,
            matrix,
            vector,
            matrix,
            vector,
            vector,
            vector,
            whole,
        ),
        out_specs=(
            whole,
            whole,
            matrix,
            vector,
            matrix,
            vector,
            vector,
            vector,
            matrix,
            vector,
            matrix,
            vector,
            vector,
            vector,
        ),
        check_vma=False,
    )
```
